32 devices in a mesh: fsdp: 8 (over z, x), dp: 4 (over y, core).
Axes of the slice: x: 2, y: 2, z: 4, core: 2. Of those that a mesh axis runs over, the one named last changes fastest.
Arguments:
- patches: bfloat16 [160, 197, 768], P(('fsdp', 'dp')), may hold values from -6 to 6
- keep: int32 [160, 197], P(('fsdp', 'dp')), may hold values from -1 to 196, as said below
- ln1_gain: bfloat16 [768], P('fsdp'), may hold values from 0.5 to 1.5
- ln1_bias: bfloat16 [768], P('fsdp'), may hold values from -1.1953125 to 1.1953125
- w_qkv: bfloat16 [768, 2304], P('fsdp'), may hold values from -0.21875 to 0.21875
- b_query: bfloat16 [768], P('fsdp'), may hold values from -1.1953125 to 1.1953125
- b_value: bfloat16 [768], P('fsdp'), may hold values from -1.1953125 to 1.1953125
- w_out: bfloat16 [768, 768], P('fsdp'), may hold values from -1.75 to 1.75
- b_out: bfloat16 [768], P('fsdp'), may hold values from -1.1953125 to 1.1953125
- ln2_gain: bfloat16 [768], P('fsdp'), may hold values from 0.5 to 1.5
- ln2_bias: bfloat16 [768], P('fsdp'), may hold values from -1.1953125 to 1.1953125
- w_up: bfloat16 [768, 3072], P('fsdp'), may hold values from -0.21875 to 0.21875
- b_up: bfloat16 [3072], P('fsdp'), may hold values from -1.1953125 to 1.1953125
- w_down: bfloat16 [3072, 768], P('fsdp'), may hold values from -0.109375 to 0.109375
- b_down: bfloat16 [768], P('fsdp'), may hold values from -1.1953125 to 1.1953125
- cotangent: bfloat16 [160, 197, 768], P(('fsdp', 'dp')), may hold values from -6 to 6
Outputs:
- out_tokens: bfloat16 [160, 197, 768], P(('fsdp', 'dp'))
- grad_patches: float32 [160, 197, 768], P(('fsdp', 'dp'))
- g_ln1_gain: float32 [768], P('fsdp')
- g_ln1_bias: float32 [768], P('fsdp')
- g_w_qkv: float32 [768, 2304], P('fsdp')
- g_b_query: float32 [768], P('fsdp')
- g_b_value: float32 [768], P('fsdp')
- g_w_out: float32 [768, 768], P('fsdp')
- g_b_out: float32 [768], P('fsdp')
- g_ln2_gain: float32 [768], P('fsdp')
- g_ln2_bias: float32 [768], P('fsdp')
- g_w_up: float32 [768, 3072], P('fsdp')
- g_b_up: float32 [3072], P('fsdp')
- g_w_down: float32 [3072, 768], P('fsdp')
- g_b_down: float32 [768], P('fsdp')
The draws below stay inside these ranges and needn't reach their ends.
Inputs may be any that keep to these rules, and one draw needn't show every extreme that they name: `keep`: each row holds the class token 0 first, then that image's kept patch positions in rising order, then -1 in the remaining slots. Every image keeps 197 // 4 or more positions, and some image keeps all 197.
All inputs are finite; a program needn't handle non-finite values.
Results may differ from the reference program's by a relative error of at most 0.018.
Values may be sent and summed in bfloat16 or wider, within the bound.
A program may use at most 192 MiB of HBM per device.

```python
import math
from functools import partial
import jax
import jax.numpy as jnp
from jax import lax

D = 768
H = 12
HD = 64
FF = 3072
P_SIZE = 197
IMG_DEV = 5
IMAGES = 160


def draw_keep(key, part):
    key = jax.random.fold_in(key, 11)
    count_key, order_key = jax.random.split(key)
    counts = jax.random.randint(count_key, (IMAGES,), P_SIZE // 4, P_SIZE)
    counts = counts.at[0].set(P_SIZE)
    random_bits = jax.random.randint(order_key, (IMAGES, P_SIZE - 1), 0, 1 << 20)
    ranking = random_bits * P_SIZE + jnp.arange(P_SIZE - 1)[None, :]
    ranks = jnp.argsort(jnp.argsort(ranking, axis=1), axis=1)
    chosen = ranks < (counts - 1)[:, None]
    positions = jnp.arange(1, P_SIZE)[None, :]
    keyed = jnp.where(chosen, positions, P_SIZE + positions)
    ordered = jnp.sort(keyed, axis=1)
    kept_patches = jnp.where(ordered < P_SIZE, ordered, -1)
    leading = jnp.zeros((IMAGES, 1), jnp.int32)
    return jnp.concatenate([leading, kept_patches.astype(jnp.int32)], axis=1).astype(jnp.int32)


def shard_levels(key, dims, cuts, low, top_value):
    level = 1.0
    for dim, blocks in cuts:
        steps = jax.random.uniform(jax.random.fold_in(jax.random.fold_in(key, 6), dim), (blocks,), jnp.float32, low / len(cuts), top_value / len(cuts))
        level = level * jnp.repeat(jnp.exp(steps), dims[dim] // blocks).reshape((-1,) + (1,) * (len(dims) - 1 - dim))
    return level


def centred(key, dims, scale, limit, cuts=(), dtype=jnp.bfloat16):
    factor_of = shard_levels(key, dims, cuts, -0.22, 0.18) if cuts else 1.0
    array = jax.random.normal(key, dims, jnp.float32) * scale * factor_of
    return jnp.minimum(jnp.maximum(array, -limit), limit).astype(dtype)


def setup_inputs(seed: int = 0) -> dict:
    splits = jax.random.split(jax.random.key(seed), 17)
    return {
        "patches": centred(splits[0], (IMAGES, P_SIZE, D), 1.0, 6.0, ((0, 32),)),
        "keep": draw_keep(jax.random.fold_in(splits[16], 71), 0),
        "ln1_gain": jnp.clip(1.0 + 0.1 * jax.random.normal(splits[2], (D,), jnp.float32), 0.5, 1.5).astype(jnp.bfloat16),
        "ln1_bias": centred(splits[3], (D,), 0.3, 1.1953125, ((0, 8),)),
        "w_qkv": centred(splits[4], (D, 3 * D), D ** -0.5, 0.21875, ((0, 8),)),
        "b_query": centred(splits[5], (D,), 0.3, 1.1953125, ((0, 8),)),
        "b_value": centred(splits[6], (D,), 0.3, 1.1953125, ((0, 8),)),
        "w_out": centred(splits[7], (D, D), (D // 64) ** -0.5, 1.75, ((0, 8),)),
        "b_out": centred(splits[8], (D,), 0.3, 1.1953125, ((0, 8),)),
        "ln2_gain": jnp.clip(1.0 + 0.1 * jax.random.normal(splits[9], (D,), jnp.float32), 0.5, 1.5).astype(jnp.bfloat16),
        "ln2_bias": centred(splits[10], (D,), 0.3, 1.1953125, ((0, 8),)),
        "w_up": centred(splits[11], (D, FF), D ** -0.5, 0.21875, ((0, 8),)),
        "b_up": centred(splits[12], (FF,), 0.3, 1.1953125, ((0, 8),)),
        "w_down": centred(splits[13], (FF, D), FF ** -0.5, 0.109375, ((0, 8),)),
        "b_down": centred(splits[14], (D,), 0.3, 1.1953125, ((0, 8),)),
        "cotangent": centred(splits[15], (IMAGES, P_SIZE, D), 1.0, 6.0, ((0, 32),)),
    }


@jax.custom_vjp
def low(v):
    return lax.optimization_barrier(v.astype(jnp.bfloat16)).astype(jnp.float32)

@jax.custom_vjp
def low_back(v):
    return v

def low_keep(v):
    return (low(v), None)

def low_pass(kept, grad):
    return (grad,)

def back_keep(v):
    return (v, None)

def back_low(kept, grad):
    return (low(grad),)
low.defvjp(low_keep, low_pass)
low_back.defvjp(back_keep, back_low)
EPSILON = 1e-06
HIGHEST = lax.Precision.HIGHEST

def layer_norm(values, gain, shift):
    centre = values - lax.optimization_barrier(jnp.mean(values, axis=-1, keepdims=True))
    spread = lax.optimization_barrier(jnp.mean(centre * centre, axis=-1, keepdims=True))
    return centre * lax.rsqrt(spread + EPSILON) * gain + shift

def group_forward(params, group_data):
    tokens_in, live_slots = group_data
    gain_one, shift_one, qkv_full, query_bias, value_bias, out_full, out_bias, gain_two, shift_two, up_full, up_bias, down_full, down_bias = params
    images = tokens_in.shape[0]
    normed_one = low(layer_norm(tokens_in, gain_one, shift_one))
    bias_all = jnp.concatenate([query_bias, jnp.zeros_like(query_bias), value_bias])
    projected = low(low_back(jnp.einsum('ipd,de->ipe', normed_one, qkv_full, precision=HIGHEST) + bias_all))
    queries = projected[..., :D].reshape(images, P_SIZE, H, HD)
    key_heads = projected[..., D:2 * D].reshape(images, P_SIZE, H, HD)
    value_heads = projected[..., 2 * D:].reshape(images, P_SIZE, H, HD)
    factor = 1.0 / math.sqrt(HD)
    scores = low_back(jnp.einsum('iqhd,ikhd->ihqk', queries, key_heads, precision=HIGHEST) * factor)
    scores = jnp.where(live_slots[:, None, None, :], scores, -1e+30)
    highest = lax.optimization_barrier(jnp.max(scores, axis=-1, keepdims=True))
    exponent = jnp.exp(scores - highest)
    attention_low = low(exponent / lax.optimization_barrier(jnp.sum(exponent, axis=-1, keepdims=True)))
    attended = low(low_back(jnp.einsum('ihqk,ikhd->iqhd', attention_low, value_heads, precision=HIGHEST)))
    attended = attended.reshape(images, P_SIZE, D)
    branch = low_back(jnp.einsum('ipd,de->ipe', attended, out_full, precision=HIGHEST) + out_bias)
    middle = tokens_in + branch
    normed_two = low(layer_norm(middle, gain_two, shift_two))
    hidden = low_back(jnp.einsum('ipd,df->ipf', normed_two, up_full, precision=HIGHEST) + up_bias)
    activated = low(jax.nn.gelu(hidden, approximate=False))
    mlp_out = low_back(jnp.einsum('ipf,fd->ipd', activated, down_full, precision=HIGHEST) + down_bias)
    return (middle + mlp_out) * live_slots[..., None].astype(jnp.float32)

def reference(patches, keep, ln1_gain, ln1_bias, w_qkv, b_query, b_value, w_out, b_out, ln2_gain, ln2_bias, w_up, b_up, w_down, b_down, cotangent):
    live_slots = keep >= 0
    slot_index = jnp.maximum(keep, 0).astype(jnp.int32)
    params = tuple((member.astype(jnp.float32) for member in (ln1_gain, ln1_bias, w_qkv, b_query, b_value, w_out, b_out, ln2_gain, ln2_bias, w_up, b_up, w_down, b_down)))
    group_size = 4 * IMG_DEV
    group_count = IMAGES // group_size

    def whole(inputs, weights):
        gathered = jnp.take_along_axis(inputs, slot_index[..., None], axis=1)
        shaped = gathered.reshape(group_count, group_size, P_SIZE, D)
        live_groups = live_slots.reshape(group_count, group_size, P_SIZE)
        outputs = lax.map(jax.checkpoint(partial(group_forward, weights)), (shaped, live_groups))
        return outputs.reshape(IMAGES, P_SIZE, D)
    outputs, pullback = jax.vjp(whole, patches.astype(jnp.float32), params)
    grad_inputs, grad_weights = pullback(cotangent.astype(jnp.float32))
    return (outputs.astype(jnp.bfloat16), grad_inputs, grad_weights[0], grad_weights[1], grad_weights[2], grad_weights[3], grad_weights[4], grad_weights[5], grad_weights[6], grad_weights[7], grad_weights[8], grad_weights[9], grad_weights[10], grad_weights[11], grad_weights[12])
```

```python
import functools
import math

import jax
import jax.numpy as jnp
from jax import lax
from jax.experimental import pallas as pl
from jax.experimental.pallas import tpu as pltpu
from jax.sharding import PartitionSpec as P

H = 12
HD = 64
EPSILON = 1e-06
F32 = jnp.float32
BF16 = jnp.bfloat16
SLOT = 200
ROWS = 1024
BLOCK = 128
TILE = 256
NT = (((1,), (1,)), ((), ()))


def dot(left, right):
    return jnp.dot(left, right, preferred_element_type=F32)


def dot_nt(left, right):
    return lax.dot_general(left, right, NT, preferred_element_type=F32)


def tile_at(index, size):
    return pl.ds(pl.multiple_of(index * size, size), size)


def norm_parts(values):
    centre = values - jnp.mean(values, axis=-1, keepdims=True)
    spread = jnp.mean(centre * centre, axis=-1, keepdims=True)
    inverse = lax.rsqrt(spread + EPSILON)
    return centre * inverse, inverse


def norm_back(hat, inverse, gain, grad):
    scaled = grad * gain
    along = jnp.mean(scaled * hat, axis=-1, keepdims=True)
    return inverse * (scaled - jnp.mean(scaled, axis=-1, keepdims=True) - hat * along)


def gelu_parts(hidden):
    size = jnp.abs(hidden)
    bell = jnp.exp(hidden * hidden * -0.5)
    t = 1.0 / (1.0 + size * (0.3275911 / math.sqrt(2.0)))
    tail = 1.061405429 * 0.5
    for term in (-1.453152027, 1.421413741, -0.284496736, 0.254829592):
        tail = tail * t + term * 0.5
    tail = tail * t * bell
    below = jnp.where(hidden >= 0, 1.0 - tail, tail)
    slope = below + hidden * (bell * (1.0 / math.sqrt(2.0 * math.pi)))
    return hidden * below, slope


def first_lanes(rows):
    return lax.broadcasted_iota(jnp.int32, (rows, 2 * HD), 1) < HD


def stage_gather(images, slots, patches, keep, stack, live, mask):
    stack[...] = jnp.zeros_like(stack)
    live[...] = jnp.zeros_like(live)

    def gather(i, _):
        row = keep[i]
        column = jnp.broadcast_to(row, (SLOT, SLOT)).T
        mask[i] = jnp.where(column >= 0, 0.0, -1e30)
        alive = (column >= 0).astype(F32)
        chosen = (column[:, :slots] == lax.broadcasted_iota(jnp.int32, (SLOT, slots), 1)).astype(F32).astype(BF16)
        rows = pl.ds(pl.multiple_of(i * SLOT, 8), SLOT)
        stack[rows, :] = dot(chosen, patches[i])
        live[rows, :] = alive[:, :BLOCK]
        return 0

    lax.fori_loop(0, images, gather, 0)


def stage_norm(stack, gain, shift, token, normed, normed_t):
    def norm(b, _):
        rows = tile_at(b, BLOCK)
        values = stack[rows, :]
        token[rows, :] = values.astype(BF16)
        hat, _ = norm_parts(values)
        low = (hat * gain + shift).astype(BF16)
        normed[rows, :] = low
        normed_t[:, rows] = low.T
        return 0

    lax.fori_loop(0, ROWS // BLOCK, norm, 0)


def stage_grads(images, slots, width, cot, stack, live, dm, dm_t):
    stack[...] = jnp.zeros_like(stack)
    for i in range(images):
        stack[i * SLOT : i * SLOT + slots, :] = cot[i].astype(F32)

    def grads(b, _):
        rows = tile_at(b, BLOCK)
        low = (stack[rows, :] * jnp.concatenate([live[rows, :]] * (width // BLOCK), axis=1)).astype(BF16)
        dm[rows, :] = low
        dm_t[:, rows] = low.T
        return 0

    lax.fori_loop(0, ROWS // BLOCK, grads, 0)


def stage_qkv(images, width, normed, w_qkv, bias, qkv):
    def body(c, _):
        cols = tile_at(c, TILE)
        scale = jnp.where(c < width // TILE, 1.0 / math.sqrt(HD), 1.0)
        values = (dot(normed[...], w_qkv[:, cols]) + bias[:, cols]) * scale
        for i in range(images):
            qkv[i, :, cols] = values[i * SLOT : (i + 1) * SLOT].astype(BF16)
        return 0

    lax.fori_loop(0, 3 * width // TILE, body, 0)


def stage_attention(images, width, qkv, mask, probs, stack, begin, end):
    pairs = H // 2

    def body(step, _):
        i, p = step // pairs, lax.rem(step, pairs)
        q2 = qkv[i, :, pl.ds(pl.multiple_of(p * 128, 128), 128)]
        k2 = qkv[i, :, pl.ds(pl.multiple_of(width + p * 128, 128), 128)]
        v2_t = qkv[i, :, pl.ds(pl.multiple_of(2 * width + p * 128, 128), 128)].T
        low = first_lanes(SLOT)
        outs = []
        for h in range(2):
            qh = jnp.where(low if h == 0 else ~low, q2, jnp.zeros_like(q2))
            scores = dot_nt(k2, qh) + mask[i]
            exponent = jnp.exp(scores - jnp.max(scores, axis=0, keepdims=True))
            share = 1.0 / jnp.sum(exponent, axis=0, keepdims=True)
            prob = (exponent * share).astype(BF16)
            probs[2 * step + h] = prob
            outs.append(dot(v2_t[h * HD : (h + 1) * HD], prob))
        stack[pl.ds(pl.multiple_of(i * SLOT, 8), SLOT), pl.ds(pl.multiple_of(p * 128, 128), 128)] = jnp.concatenate(outs, axis=0).T
        return 0

    lax.fori_loop(begin * pairs, end * pairs, body, 0)


def stage_out(width, stack, w_out, bias, token, gain, shift, att, att_t, middle, normed, normed_t):
    def low(b, _):
        rows = tile_at(b, BLOCK)
        values = stack[rows, :].astype(BF16)
        att[rows, :] = values
        att_t[:, rows] = values.T
        return 0

    lax.fori_loop(0, ROWS // BLOCK, low, 0)

    def body(c, _):
        cols = tile_at(c, TILE)
        middle[:, cols] = token[:, cols].astype(F32) + (dot(att[...], w_out[:, cols]) + bias[:, cols])
        return 0

    lax.fori_loop(0, width // TILE, body, 0)

    def norm(b, _):
        rows = tile_at(b, BLOCK)
        hat, _ = norm_parts(middle[rows, :])
        values = (hat * gain[...] + shift[...]).astype(BF16)
        normed[rows, :] = values
        normed_t[:, rows] = values.T
        return 0

    lax.fori_loop(0, ROWS // BLOCK, norm, 0)


def stage_mlp(width, hidden_width, normed, normed_t, dm, dm_t, w_up, b_up, w_down, act, dh, g_up, g_down_t, g_b_up):
    def body(c, _):
        cols = tile_at(c, TILE)
        hidden = dot(normed[...], w_up[:, cols]) + b_up[:, cols]
        d_act = dot_nt(dm[...], w_down[cols, :])
        value, slope = gelu_parts(hidden)
        value = value.astype(BF16)
        grad = (d_act * slope).astype(BF16)
        act[:, cols] = value
        dh[:, cols] = grad
        g_b_up[:, cols] = jnp.sum(grad.astype(F32), axis=0, keepdims=True)
        g_up[:, cols] = dot(normed_t[...], grad).astype(BF16)
        g_down_t[:, cols] = dot(dm_t[...], value).astype(BF16)
        return 0

    lax.fori_loop(0, hidden_width // TILE, body, 0)


def stage_mlp_out(images, slots, width, act, dh, w_up, w_down, b_down, middle, live, gain, dm, stack, out, d_mid_low, g_gain, g_shift, g_b_down, g_b_out):
    def body(c, _):
        cols = tile_at(c, TILE)
        stack[:, cols] = dot(act[...], w_down[:, cols])
        return 0

    lax.fori_loop(0, width // TILE, body, 0)

    def final(b, _):
        rows = tile_at(b, BLOCK)
        stack[rows, :] = (middle[rows, :] + (stack[rows, :] + b_down[...])) * jnp.concatenate([live[rows, :]] * (width // BLOCK), axis=1)
        return 0

    lax.fori_loop(0, ROWS // BLOCK, final, 0)
    for i in range(images):
        out[i] = stack[i * SLOT : i * SLOT + slots, :].astype(BF16)

    def body2(c, _):
        cols = tile_at(c, TILE)
        stack[:, cols] = dot_nt(dh[...], w_up[cols, :])
        return 0

    lax.fori_loop(0, width // TILE, body2, 0)
    for ref in (g_gain, g_shift, g_b_down, g_b_out):
        ref[...] = jnp.zeros_like(ref)

    def back(b, _):
        rows = tile_at(b, BLOCK)
        grad = stack[rows, :]
        hat, inverse = norm_parts(middle[rows, :])
        g_gain[...] += jnp.sum(grad * hat, axis=0, keepdims=True)
        g_shift[...] += jnp.sum(grad, axis=0, keepdims=True)
        own = dm[rows, :].astype(F32)
        g_b_down[...] += jnp.sum(own, axis=0, keepdims=True)
        total = own + norm_back(hat, inverse, gain[...], grad)
        middle[rows, :] = total
        low = total.astype(BF16)
        d_mid_low[rows, :] = low
        g_b_out[...] += jnp.sum(low.astype(F32), axis=0, keepdims=True)
        return 0

    lax.fori_loop(0, ROWS // BLOCK, back, 0)


def stage_out_back(width, att_t, d_mid_low, w_out, g_out, stack):
    def body(c, _):
        cols = tile_at(c, TILE)
        g_out[:, cols] = dot(att_t[...], d_mid_low[:, cols]).astype(BF16)
        stack[:, cols] = dot_nt(d_mid_low[...], w_out[cols, :])
        return 0

    lax.fori_loop(0, width // TILE, body, 0)


def stage_attention_back(images, width, qkv, probs, stack, d_qkv):
    pairs = H // 2

    def body(step, _):
        i, p = step // pairs, lax.rem(step, pairs)
        at_q = pl.ds(pl.multiple_of(p * 128, 128), 128)
        at_k = pl.ds(pl.multiple_of(width + p * 128, 128), 128)
        at_v = pl.ds(pl.multiple_of(2 * width + p * 128, 128), 128)
        q2, k2, v2 = qkv[i, :, at_q], qkv[i, :, at_k], qkv[i, :, at_v]
        k2_t = k2.T
        da = stack[pl.ds(pl.multiple_of(i * SLOT, 8), SLOT), at_q].astype(BF16)
        low = first_lanes(SLOT)
        dq, dk, dv = [], 0.0, 0.0
        for h in range(2):
            pick = lambda m: jnp.where(low if h == 0 else ~low, m, jnp.zeros_like(m))
            prob = probs[2 * step + h]
            d_prob = dot_nt(pick(v2), da)
            mixed = prob.astype(F32)
            moved = mixed * d_prob
            total = jnp.sum(moved, axis=0, keepdims=True)
            ds = (moved - mixed * total).astype(BF16)
            dq.append(dot(k2_t[h * HD : (h + 1) * HD], ds))
            dk = dk + dot(ds, pick(q2))
            dv = dv + dot(prob, pick(da))
        d_qkv[i, :, at_q] = (jnp.concatenate(dq, axis=0).T * (1.0 / math.sqrt(HD))).astype(BF16)
        d_qkv[i, :, at_k] = dk.astype(BF16)
        d_qkv[i, :, at_v] = dv.astype(BF16)
        return 0

    lax.fori_loop(0, images * pairs, body, 0)


def stage_qkv_back(images, width, d_qkv, normed_t, w_qkv, tile, flat, g_qkv, g_b_qkv, stack):
    tile[...] = jnp.zeros_like(tile)

    def body(c, _):
        cols = tile_at(c, TILE)
        for i in range(images):
            tile[i * SLOT : (i + 1) * SLOT, :] = d_qkv[i, :, cols].astype(F32)
        values = tile[...]
        g_b_qkv[:, cols] = jnp.sum(values, axis=0, keepdims=True)
        low = values.astype(BF16)
        flat[:, cols] = low
        g_qkv[:, cols] = dot(normed_t[...], low).astype(BF16)
        return 0

    lax.fori_loop(0, 3 * width // TILE, body, 0)

    def body2(c, _):
        cols = tile_at(c, TILE)
        stack[:, cols] = dot_nt(flat[:, : 3 * width], w_qkv[cols, :])
        return 0

    lax.fori_loop(0, width // TILE, body2, 0)


def stage_end(images, slots, width, keep, token, gain, middle, live, stack, g_gain, g_shift, grad_patches):
    for ref in (g_gain, g_shift):
        ref[...] = jnp.zeros_like(ref)

    def back(b, _):
        rows = tile_at(b, BLOCK)
        grad = stack[rows, :]
        hat, inverse = norm_parts(token[rows, :].astype(F32))
        g_gain[...] += jnp.sum(grad * hat, axis=0, keepdims=True)
        g_shift[...] += jnp.sum(grad, axis=0, keepdims=True)
        total = middle[rows, :] + norm_back(hat, inverse, gain[...], grad)
        stack[rows, :] = total * jnp.concatenate([live[rows, :]] * (width // BLOCK), axis=1)
        return 0

    lax.fori_loop(0, ROWS // BLOCK, back, 0)

    def scatter(i, _):
        chosen = (lax.broadcasted_iota(jnp.int32, (slots, SLOT), 0) == keep[i]).astype(F32).astype(BF16)
        values = stack[pl.ds(pl.multiple_of(i * SLOT, 8), SLOT), :]
        high = values.astype(BF16)
        rest = (values - high.astype(F32)).astype(BF16)
        grad_patches[i] = dot(chosen, high) + dot(chosen, rest)
        return 0

    lax.fori_loop(0, images, scatter, 0)


MESH = pl.DeviceIdType.MESH


class Place:
    def __init__(self):
        f, d = lax.axis_index("fsdp"), lax.axis_index("dp")
        self.z, self.x = f // 2, lax.rem(f, 2)
        self.y, self.c = d // 2, lax.rem(d, 2)
        z = self.z
        self.zs = [z, z + 1 - 2 * lax.rem(z, 2), lax.rem(z + 2, 4), 3 - z]

    def to(self, z=None, x=None, y=None, c=None):
        z, x, y, c = (own if new is None else new for new, own in ((z, self.z), (x, self.x), (y, self.y), (c, self.c)))
        return (z * 2 + x, y * 2 + c)

    def sides(self):
        return self.to(x=1 - self.x), self.to(y=1 - self.y), self.to(c=1 - self.c)


def enter(peers):
    barrier = pltpu.get_barrier_semaphore()
    for peer in peers:
        pl.semaphore_signal(barrier, inc=1, device_id=peer, device_id_type=MESH)
    pl.semaphore_wait(barrier, len(peers))


class Gather:
    def __init__(self, place, shard, full, first_cols, send, recv):
        self.place, self.shard, self.full, self.send, self.recv = place, shard, full, send, recv
        self.rows, cols = shard.shape
        self.half, self.wide, self.cut = self.rows // 2, cols // 2, first_cols
        self.started = []

    def spot(self, z, x, y, part=None, local=False):
        p = self.place
        base = 0 if local else (z * 2 + x) * self.rows
        rows = pl.ds(pl.multiple_of(base + p.c * self.half, 16), self.half)
        if y is None:
            return rows, slice(None)
        start, size = (y * self.wide, self.wide) if part is None else ((y * self.wide, self.cut) if part == 0 else (y * self.wide + self.cut, self.wide - self.cut))
        return rows, pl.ds(pl.multiple_of(start, 128), size)

    def copy(self, spot, sem, peer, local=None):
        src = self.full.at[spot] if local is None else self.shard.at[local]
        return pltpu.make_async_remote_copy(
            src_ref=src, dst_ref=self.full.at[spot], send_sem=self.send.at[sem], recv_sem=self.recv.at[sem], device_id=peer, device_id_type=MESH
        )

    def start(self, spot, sem, peer, local=None):
        copy = self.copy(spot, sem, peer, local)
        copy.start()
        self.started.append(copy)

    def arrived(self, spot, sem):
        self.copy(spot, sem, self.place.sides()[0]).wait_recv()

    def own(self, sem):
        p = self.place
        rows = pl.ds(pl.multiple_of((p.z * 2 + p.x) * self.rows, 16), self.rows)
        return pltpu.make_async_copy(self.shard, self.full.at[rows, :], sem)

    def begin(self):
        p = self.place
        side_x, side_y, _ = p.sides()
        spot, local = self.spot(p.z, p.x, p.y), self.spot(p.z, p.x, p.y, None, True)
        for k in (1, 2, 3):
            self.start(spot, k, p.to(z=p.zs[k]), local)
        self.start(spot, 4, side_x, local)
        self.start(self.spot(p.z, p.x, 1 - p.y, 1), 16, side_x, self.spot(p.z, p.x, 1 - p.y, 1, True))

    def spread(self, k):
        p = self.place
        side_x, side_y, _ = p.sides()
        spot = self.spot(p.zs[k], p.x, p.y)
        self.arrived(spot, k)
        self.start(spot, 4 + k, side_x)
        self.start(spot, 8 + k, side_y)

    def cross(self, k):
        p = self.place
        side_x, side_y, _ = p.sides()
        self.arrived(self.spot(p.zs[k], 1 - p.x, p.y), 4 + k)
        self.start(self.spot(p.zs[k], 1 - p.x, p.y, 0), 12 + k, side_y)
        if k:
            self.arrived(self.spot(p.zs[k], p.x, 1 - p.y), 8 + k)
            self.start(self.spot(p.zs[k], p.x, 1 - p.y, 1), 16 + k, side_x)

    def share(self, k):
        p = self.place
        core = p.sides()[2]
        if k:
            self.start(self.spot(p.zs[k], p.x, None), 20 + k, core)
        self.arrived(self.spot(p.zs[k], 1 - p.x, 1 - p.y, 0), 12 + k)
        self.arrived(self.spot(p.zs[k], 1 - p.x, 1 - p.y, 1), 16 + k)
        self.start(self.spot(p.zs[k], 1 - p.x, None), 24 + k, core)

    def finish(self):
        p = self.place

        def other(z, x):
            return pl.ds(pl.multiple_of((z * 2 + x) * self.rows + (1 - p.c) * self.half, 16), self.half), slice(None)

        for k in range(4):
            if k:
                self.arrived(other(p.zs[k], p.x), 20 + k)
            self.arrived(other(p.zs[k], 1 - p.x), 24 + k)

    def drain(self):
        for copy in self.started:
            copy.wait_send()
VMEM = pl.BlockSpec(memory_space=pltpu.VMEM)
ANY = pl.BlockSpec(memory_space=pl.ANY)
LIMIT = 61 * 1024 * 1024


def call(body, outs, scratch, args, name):
    return pl.pallas_call(
        body,
        out_shape=[jax.ShapeDtypeStruct(*o) for o in outs],
        in_specs=[VMEM] * len(args),
        out_specs=[VMEM] * len(outs),
        scratch_shapes=[pltpu.VMEM(*s) for s in scratch],
        compiler_params=pltpu.CompilerParams(vmem_limit_bytes=LIMIT),
        name=name,
    )(*args)


def first_plain(
    images, slots, width, patches, keep, cot, vectors, w_qkv, w_out,
    token, n1t, dm, dmt, live, qkv, probs, att_t, middle, n2, n2t, stack, normed, mask, att, bias,
):
    bias[...] = jnp.concatenate([vectors[2:3, :], jnp.zeros((1, width), F32), vectors[3:4, :]], axis=1)
    stage_gather(images, slots, patches, keep, stack, live, mask)
    stage_norm(stack, vectors[0:1, :], vectors[1:2, :], token, normed, n1t)
    stage_grads(images, slots, width, cot, stack, live, dm, dmt)
    stage_qkv(images, width, normed, w_qkv, bias, qkv)
    stage_attention(images, width, qkv, mask, probs, stack, 0, images)
    stage_out(width, stack, w_out, vectors.at[4:5, :], token, vectors.at[5:6, :], vectors.at[6:7, :], att, att_t, middle, n2, n2t)


def first_kernel(
    images, slots, width,
    patches, keep, cot, vec, s_qkv, s_out, s_up, s_down,
    token, n1t, dm, dmt, live, qkv, probs, att_t, middle, n2, n2t, vectors, b_up, o_qkv, o_out, f_up, f_down,
    stack, normed, mask, att, f_qkv, f_out, vecs, bias, q_send, q_recv, o_send, o_recv, u_send, u_recv, d_send, d_recv, v_send, v_recv, own,
):
    place = Place()
    side_x, side_y, side_c = place.sides()
    flat = [place.to(z=place.zs[k], x=x) for k in range(4) for x in (place.x, 1 - place.x)][1:]
    enter(flat + [side_y, side_c])
    g_qkv = Gather(place, s_qkv, f_qkv, 640, q_send, q_recv)
    g_out = Gather(place, s_out, f_out, 256, o_send, o_recv)
    g_up = Gather(place, s_up, f_up, 896, u_send, u_recv)
    g_down = Gather(place, s_down, f_down, 256, d_send, d_recv)
    mine = place.z * 2 + place.x
    tiny = []
    for j, peer in enumerate(flat):
        copy = pltpu.make_async_remote_copy(src_ref=vec, dst_ref=vecs.at[mine], send_sem=v_send.at[j], recv_sem=v_recv.at[j], device_id=peer, device_id_type=MESH)
        copy.start()
        tiny.append(copy)
    g_qkv.begin()
    locals_ = [g.own(own.at[j]) for j, g in enumerate((g_qkv, g_out, g_up, g_down))]
    for copy in locals_:
        copy.start()
    vecs[mine] = vec[...]
    stage_gather(images, slots, patches, keep, stack, live, mask)
    g_out.begin()
    for copy in tiny:
        copy.wait_recv()
    rows = jnp.concatenate([vecs[f][:, :96] for f in range(8)], axis=1).astype(F32)
    vectors[...] = rows
    b_up[...] = jnp.concatenate([vecs[f][8 + j : 9 + j, :96].astype(F32) for f in range(8) for j in range(4)], axis=1)
    for k in (1, 2, 3):
        g_qkv.spread(k)
    g_up.begin()
    stage_norm(stack, vectors[0:1, :], vectors[1:2, :], token, normed, n1t)
    for k in range(4):
        g_qkv.cross(k)
    for k in (1, 2, 3):
        g_out.spread(k)
    g_down.begin()
    stage_grads(images, slots, width, cot, stack, live, dm, dmt)
    for k in range(4):
        g_qkv.share(k)
    for k in range(4):
        g_out.cross(k)
    for k in (1, 2, 3):
        g_up.spread(k)
    locals_[0].wait()
    g_qkv.finish()
    keep_qkv = pltpu.make_async_copy(f_qkv, o_qkv, own.at[4])
    keep_qkv.start()
    bias[...] = jnp.concatenate([vectors[2:3, :], jnp.zeros((1, width), F32), vectors[3:4, :]], axis=1)
    stage_qkv(images, width, normed, f_qkv, bias, qkv)
    for k in range(4):
        g_out.share(k)
    for k in (1, 2, 3):
        g_down.spread(k)
    stage_attention(images, width, qkv, mask, probs, stack, 0, 1)
    for k in range(4):
        g_up.cross(k)
    stage_attention(images, width, qkv, mask, probs, stack, 1, 2)
    for k in range(4):
        g_up.share(k)
    stage_attention(images, width, qkv, mask, probs, stack, 2, 3)
    for k in range(4):
        g_down.cross(k)
    stage_attention(images, width, qkv, mask, probs, stack, 3, 4)
    stage_attention(images, width, qkv, mask, probs, stack, 4, images)
    locals_[1].wait()
    g_out.finish()
    keep_out = pltpu.make_async_copy(f_out, o_out, own.at[5])
    keep_out.start()
    stage_out(width, stack, f_out, vectors.at[4:5, :], token, vectors.at[5:6, :], vectors.at[6:7, :], att, att_t, middle, n2, n2t)
    for k in range(4):
        g_down.share(k)
    g_up.finish()
    g_down.finish()
    for copy in locals_[2:] + [keep_qkv, keep_out]:
        copy.wait()
    for copy in tiny:
        copy.wait_send()
    for g in (g_qkv, g_out, g_up, g_down):
        g.drain()


def shards(
    linked,
    patches, keep, ln1_gain, ln1_bias, w_qkv, b_query, b_value, w_out, b_out,
    ln2_gain, ln2_bias, w_up, b_up, w_down, b_down, cotangent,
):
    images, slots = keep.shape
    width = patches.shape[2]
    hidden_width = w_up.shape[1]
    keep_pad = jnp.pad(keep, ((0, 0), (0, SLOT - slots)), constant_values=-1).reshape(images, 1, SLOT)
    part = ln1_gain.shape[0]
    singles = [v.reshape(1, part) for v in (ln1_gain, ln1_bias, b_query, b_value, b_out, ln2_gain, ln2_bias, b_down)]
    rows_low, rows_wide = ((ROWS, width), BF16), ((ROWS, width), F32)
    cols_low = ((width, ROWS), BF16)
    live_like, mask_like = ((ROWS, BLOCK), F32), ((images, SLOT, SLOT), F32)
    heads_like = ((images, SLOT, 3 * width), BF16)
    probs_like = ((images * H, SLOT, SLOT), BF16)
    row_like = ((1, width), F32)

    if linked:
        vec = jnp.concatenate(singles + [b_up.reshape(4, part)], axis=0)
        vec = jnp.pad(vec, ((0, 4), (0, BLOCK - part)))
        full = lambda v: ((v.shape[0] * 8, v.shape[1]), BF16)
        outs = [
            rows_low, cols_low, rows_low, cols_low, live_like, heads_like, probs_like, cols_low, rows_wide, rows_low, cols_low,
            ((16, width), F32), ((1, hidden_width), F32), full(w_qkv), full(w_out), full(w_up), full(w_down),
        ]
        scratch = [rows_wide, rows_low, mask_like, rows_low, full(w_qkv), full(w_out), ((8, 16, BLOCK), BF16), ((1, 3 * width), F32)]
        token, n1t, dm, dmt, live, qkv, probs, att_t, middle, n2, n2t, vectors, bias_up, qkv_full, out_full, up_full, down_full = pl.pallas_call(
            functools.partial(first_kernel, images, slots, width),
            out_shape=[jax.ShapeDtypeStruct(*o) for o in outs],
            in_specs=[VMEM] * 8,
            out_specs=[VMEM] * 13 + [ANY] * 4,
            scratch_shapes=[pltpu.VMEM(*s) for s in scratch]
            + [pltpu.SemaphoreType.DMA((28,))] * 8
            + [pltpu.SemaphoreType.DMA((7,))] * 2
            + [pltpu.SemaphoreType.DMA((6,))],
            compiler_params=pltpu.CompilerParams(vmem_limit_bytes=LIMIT, collective_id=0, has_side_effects=True),
            name="first",
        )(patches, keep_pad, cotangent, vec, w_qkv, w_out, w_up, w_down)
    else:
        gather = lambda v: lax.all_gather(v, "fsdp", axis=0, tiled=True)
        vectors = jnp.pad(gather(jnp.concatenate(singles, axis=0).T).T.astype(F32), ((0, 8), (0, 0)))
        bias_up = gather(b_up).astype(F32).reshape(1, hidden_width)
        qkv_full, out_full, up_full, down_full = gather(w_qkv), gather(w_out), gather(w_up), gather(w_down)
        outs = [rows_low, cols_low, rows_low, cols_low, live_like, heads_like, probs_like, cols_low, rows_wide, rows_low, cols_low]
        scratch = [rows_wide, rows_low, mask_like, rows_low, ((1, 3 * width), F32)]
        token, n1t, dm, dmt, live, qkv, probs, att_t, middle, n2, n2t = call(
            functools.partial(first_plain, images, slots, width),
            outs, scratch, (patches, keep_pad, cotangent, vectors, qkv_full, out_full), "first",
        )
    gain1, gain2, b_d = vectors[0:1], vectors[5:6], vectors[7:8]

    def second(n2, n2t, dm, dmt, w_up, b_up, w_down, b_d, middle_in, live, gain2, out, middle, d_low, g_up, g_down_t, g_b_up, g_g2, g_s2, g_bd, g_bo, act, dh, stack):
        middle[...] = middle_in[...]
        stage_mlp(width, hidden_width, n2, n2t, dm, dmt, w_up, b_up, w_down, act, dh, g_up, g_down_t, g_b_up)
        stage_mlp_out(images, slots, width, act, dh, w_up, w_down, b_d, middle, live, gain2, dm, stack, out, d_low, g_g2, g_s2, g_bd, g_bo)

    hid = ((ROWS, hidden_width), BF16)
    out_tokens, d_mid, d_low, g_up, g_down_t, g_b_up, g_g2, g_s2, g_bd, g_bo = call(
        second,
        [((images, slots, width), BF16), rows_wide, rows_low, ((width, hidden_width), BF16), ((width, hidden_width), BF16), ((1, hidden_width), F32)] + [row_like] * 4,
        [hid, hid, rows_wide],
        (n2, n2t, dm, dmt, up_full, bias_up, down_full, b_d, middle, live, gain2),
        "second",
    )

    def third(d_low, att_t, w_out, qkv, probs, n1t, w_qkv, token, gain1, d_mid, live, keep, g_out, g_qkv, g_b, g_g1, g_s1, gp, stack, tile, flat, d_qkv):
        stage_out_back(width, att_t, d_low, w_out, g_out, stack)
        stage_attention_back(images, width, qkv, probs, stack, d_qkv)
        stage_qkv_back(images, width, d_qkv, n1t, w_qkv, tile, flat, g_qkv, g_b, stack)
        stage_end(images, slots, width, keep, token, gain1, d_mid, live, stack, g_g1, g_s1, gp)

    g_out, g_qkv, g_b, g_g1, g_s1, grad_patches = call(
        third,
        [((width, width), BF16), ((width, 3 * width), BF16), ((1, 3 * width), F32), row_like, row_like, ((images, slots, width), F32)],
        [rows_wide, ((ROWS, TILE), F32), ((ROWS, 3 * width), BF16), heads_like],
        (d_low, att_t, out_full, qkv, probs, n1t, qkv_full, token, gain1, d_mid, live, keep_pad),
        "third",
    )
    both = ("fsdp", "dp")
    scat = lambda v, dim=0: lax.psum(lax.psum_scatter(v, "fsdp", scatter_dimension=dim, tiled=True), "dp").astype(F32)
    small = jnp.concatenate([g_g1, g_s1, g_b[:, :width], g_b[:, 2 * width :], g_bo, g_g2, g_s2, g_bd], axis=0).astype(BF16)
    small = scat(small, 1)
    b_up_sum = scat(g_b_up.astype(BF16), 1)[0]
    return (
        out_tokens, grad_patches, small[0], small[1], scat(g_qkv), small[2], small[3], scat(g_out), small[4],
        small[5], small[6], scat(g_up), b_up_sum, scat(g_down_t, 1).T, small[7],
    )


def solution(mesh):
    linked = (mesh.shape["fsdp"], mesh.shape["dp"]) == (8, 4)
    many, one, two = P(("fsdp", "dp"), None, None), P("fsdp"), P("fsdp", None)
    in_specs = (many, P(("fsdp", "dp"), None), one, one, two, one, one, two, one, one, one, two, one, two, one, many)
    out_specs = (many, many, one, one, two, one, one, two, one, one, one, two, one, two, one)
    return jax.shard_map(functools.partial(shards, linked), mesh=mesh, in_specs=in_specs, out_specs=out_specs, check_vma=False)
```

```python
import functools
import math

import jax
import jax.numpy as jnp
from jax import lax
from jax.experimental import pallas as pl
from jax.experimental.pallas import tpu as pltpu
from jax.sharding import PartitionSpec as P

H = 12
HD = 64
EPSILON = 1e-06
F32 = jnp.float32
BF16 = jnp.bfloat16
SLOT = 200
ROWS = 1024
BLOCK = 128
TILE = 256
NT = (((1,), (1,)), ((), ()))


def dot(left, right):
    return jnp.dot(left, right, preferred_element_type=F32)


def dot_nt(left, right):
    return lax.dot_general(left, right, NT, preferred_element_type=F32)


def tile_at(index, size):
    return pl.ds(pl.multiple_of(index * size, size), size)


def norm_parts(values):
    centre = values - jnp.mean(values, axis=-1, keepdims=True)
    spread = jnp.mean(centre * centre, axis=-1, keepdims=True)
    inverse = lax.rsqrt(spread + EPSILON)
    return centre * inverse, inverse


def norm_back(hat, inverse, gain, grad):
    scaled = grad * gain
    along = jnp.mean(scaled * hat, axis=-1, keepdims=True)
    return inverse * (scaled - jnp.mean(scaled, axis=-1, keepdims=True) - hat * along)


def gelu_parts(hidden):
    size = jnp.abs(hidden)
    bell = jnp.exp(hidden * hidden * -0.5)
    t = 1.0 / (1.0 + size * (0.3275911 / math.sqrt(2.0)))
    tail = 1.061405429 * 0.5
    for term in (-1.453152027, 1.421413741, -0.284496736, 0.254829592):
        tail = tail * t + term * 0.5
    tail = tail * t * bell
    below = jnp.where(hidden >= 0, 1.0 - tail, tail)
    slope = below + hidden * (bell * (1.0 / math.sqrt(2.0 * math.pi)))
    return hidden * below, slope


def first_lanes(rows):
    return lax.broadcasted_iota(jnp.int32, (rows, 2 * HD), 1) < HD


def stage_gather(images, slots, patches, keep, stack, live, mask):
    stack[...] = jnp.zeros_like(stack)
    live[...] = jnp.zeros_like(live)

    def gather(i, _):
        row = keep[i]
        column = jnp.broadcast_to(row, (SLOT, SLOT)).T
        mask[i] = jnp.where(column >= 0, 0.0, -1e30)
        alive = (column >= 0).astype(F32)
        chosen = (column[:, :slots] == lax.broadcasted_iota(jnp.int32, (SLOT, slots), 1)).astype(F32).astype(BF16)
        rows = pl.ds(pl.multiple_of(i * SLOT, 8), SLOT)
        stack[rows, :] = dot(chosen, patches[i])
        live[rows, :] = alive[:, :BLOCK]
        return 0

    lax.fori_loop(0, images, gather, 0)


def stage_norm(stack, gain, shift, token, normed, normed_t):
    def norm(b, _):
        rows = tile_at(b, BLOCK)
        values = stack[rows, :]
        token[rows, :] = values.astype(BF16)
        hat, _ = norm_parts(values)
        low = (hat * gain + shift).astype(BF16)
        normed[rows, :] = low
        normed_t[:, rows] = low.T
        return 0

    lax.fori_loop(0, ROWS // BLOCK, norm, 0)


def stage_grads(images, slots, width, cot, stack, live, dm, dm_t):
    stack[...] = jnp.zeros_like(stack)
    for i in range(images):
        stack[i * SLOT : i * SLOT + slots, :] = cot[i].astype(F32)

    def grads(b, _):
        rows = tile_at(b, BLOCK)
        low = (stack[rows, :] * jnp.concatenate([live[rows, :]] * (width // BLOCK), axis=1)).astype(BF16)
        dm[rows, :] = low
        dm_t[:, rows] = low.T
        return 0

    lax.fori_loop(0, ROWS // BLOCK, grads, 0)


def stage_qkv(images, width, normed, w_qkv, bias, qkv):
    def body(c, _):
        cols = tile_at(c, TILE)
        scale = jnp.where(c < width // TILE, 1.0 / math.sqrt(HD), 1.0)
        values = (dot(normed[...], w_qkv[:, cols]) + bias[:, cols]) * scale
        for i in range(images):
            qkv[i, :, cols] = values[i * SLOT : (i + 1) * SLOT].astype(BF16)
        return 0

    lax.fori_loop(0, 3 * width // TILE, body, 0)


def stage_attention(images, width, qkv, mask, probs, stack, begin, end):
    pairs = H // 2

    def body(step, _):
        i, p = step // pairs, lax.rem(step, pairs)
        q2 = qkv[i, :, pl.ds(pl.multiple_of(p * 128, 128), 128)]
        k2 = qkv[i, :, pl.ds(pl.multiple_of(width + p * 128, 128), 128)]
        v2_t = qkv[i, :, pl.ds(pl.multiple_of(2 * width + p * 128, 128), 128)].T
        low = first_lanes(SLOT)
        outs = []
        for h in range(2):
            qh = jnp.where(low if h == 0 else ~low, q2, jnp.zeros_like(q2))
            scores = dot_nt(k2, qh) + mask[i]
            exponent = jnp.exp(scores - jnp.max(scores, axis=0, keepdims=True))
            share = 1.0 / jnp.sum(exponent, axis=0, keepdims=True)
            prob = (exponent * share).astype(BF16)
            probs[2 * step + h] = prob
            outs.append(dot(v2_t[h * HD : (h + 1) * HD], prob))
        stack[pl.ds(pl.multiple_of(i * SLOT, 8), SLOT), pl.ds(pl.multiple_of(p * 128, 128), 128)] = jnp.concatenate(outs, axis=0).T
        return 0

    lax.fori_loop(begin * pairs, end * pairs, body, 0)


def stage_out(width, stack, w_out, bias, token, gain, shift, att, att_t, middle, normed, normed_t):
    def low(b, _):
        rows = tile_at(b, BLOCK)
        values = stack[rows, :].astype(BF16)
        att[rows, :] = values
        att_t[:, rows] = values.T
        return 0

    lax.fori_loop(0, ROWS // BLOCK, low, 0)

    def body(c, _):
        cols = tile_at(c, TILE)
        middle[:, cols] = token[:, cols].astype(F32) + (dot(att[...], w_out[:, cols]) + bias[:, cols])
        return 0

    lax.fori_loop(0, width // TILE, body, 0)

    def norm(b, _):
        rows = tile_at(b, BLOCK)
        hat, _ = norm_parts(middle[rows, :])
        values = (hat * gain[...] + shift[...]).astype(BF16)
        normed[rows, :] = values
        normed_t[:, rows] = values.T
        return 0

    lax.fori_loop(0, ROWS // BLOCK, norm, 0)


def stage_mlp(width, hidden_width, normed, normed_t, dm, dm_t, w_up, b_up, w_down, act, dh, put_up, put_down, g_b_up):
    def body(c, _):
        cols = tile_at(c, TILE)
        hidden = dot(normed[...], w_up[:, cols]) + b_up[:, cols]
        d_act = dot_nt(dm[...], w_down[cols, :])
        value, slope = gelu_parts(hidden)
        value = value.astype(BF16)
        grad = (d_act * slope).astype(BF16)
        act[:, cols] = value
        dh[:, cols] = grad
        g_b_up[:, cols] = jnp.sum(grad.astype(F32), axis=0, keepdims=True)
        put_up(c, dot(normed_t[...], grad).astype(BF16))
        put_down(c, dot(dm_t[...], value).astype(BF16))
        return 0

    lax.fori_loop(0, hidden_width // TILE, body, 0)


def stage_mlp_out(images, slots, width, act, dh, w_up, w_down, b_down, middle, live, gain, dm, stack, out, d_mid_low, g_gain, g_shift, g_b_down, g_b_out):
    def body(c, _):
        cols = tile_at(c, TILE)
        stack[:, cols] = dot(act[...], w_down[:, cols])
        return 0

    lax.fori_loop(0, width // TILE, body, 0)

    def final(b, _):
        rows = tile_at(b, BLOCK)
        stack[rows, :] = (middle[rows, :] + (stack[rows, :] + b_down[...])) * jnp.concatenate([live[rows, :]] * (width // BLOCK), axis=1)
        return 0

    lax.fori_loop(0, ROWS // BLOCK, final, 0)
    for i in range(images):
        out[i] = stack[i * SLOT : i * SLOT + slots, :].astype(BF16)

    def body2(c, _):
        cols = tile_at(c, TILE)
        stack[:, cols] = dot_nt(dh[...], w_up[cols, :])
        return 0

    lax.fori_loop(0, width // TILE, body2, 0)
    for ref in (g_gain, g_shift, g_b_down, g_b_out):
        ref[...] = jnp.zeros_like(ref)

    def back(b, _):
        rows = tile_at(b, BLOCK)
        grad = stack[rows, :]
        hat, inverse = norm_parts(middle[rows, :])
        g_gain[...] += jnp.sum(grad * hat, axis=0, keepdims=True)
        g_shift[...] += jnp.sum(grad, axis=0, keepdims=True)
        own = dm[rows, :].astype(F32)
        g_b_down[...] += jnp.sum(own, axis=0, keepdims=True)
        total = own + norm_back(hat, inverse, gain[...], grad)
        middle[rows, :] = total
        low = total.astype(BF16)
        d_mid_low[rows, :] = low
        g_b_out[...] += jnp.sum(low.astype(F32), axis=0, keepdims=True)
        return 0

    lax.fori_loop(0, ROWS // BLOCK, back, 0)


def stage_out_back(width, att_t, d_mid_low, w_out, put_out, stack):
    def body(c, _):
        cols = tile_at(c, TILE)
        put_out(c, dot(att_t[...], d_mid_low[:, cols]).astype(BF16))
        stack[:, cols] = dot_nt(d_mid_low[...], w_out[cols, :])
        return 0

    lax.fori_loop(0, width // TILE, body, 0)


def stage_attention_back(width, qkv, probs, stack, i, begin, end):
    def body(p, _):
        at_q = pl.ds(pl.multiple_of(p * 128, 128), 128)
        at_k = pl.ds(pl.multiple_of(width + p * 128, 128), 128)
        at_v = pl.ds(pl.multiple_of(2 * width + p * 128, 128), 128)
        q2, k2, v2 = qkv[i, :, at_q], qkv[i, :, at_k], qkv[i, :, at_v]
        k2_t = k2.T
        da = stack[pl.ds(pl.multiple_of(i * SLOT, 8), SLOT), at_q].astype(BF16)
        low = first_lanes(SLOT)
        dq, dk, dv = [], 0.0, 0.0
        for h in range(2):
            pick = lambda m: jnp.where(low if h == 0 else ~low, m, jnp.zeros_like(m))
            prob = probs[2 * p + h]
            d_prob = dot_nt(pick(v2), da)
            mixed = prob.astype(F32)
            moved = mixed * d_prob
            total = jnp.sum(moved, axis=0, keepdims=True)
            ds = (moved - mixed * total).astype(BF16)
            dq.append(dot(k2_t[h * HD : (h + 1) * HD], ds))
            dk = dk + dot(ds, pick(q2))
            dv = dv + dot(prob, pick(da))
        qkv[i, :, at_q] = (jnp.concatenate(dq, axis=0).T * (1.0 / math.sqrt(HD))).astype(BF16)
        qkv[i, :, at_k] = dk.astype(BF16)
        qkv[i, :, at_v] = dv.astype(BF16)
        return 0

    lax.fori_loop(begin, end, body, 0)


def stage_qkv_back(images, width, d_qkv, normed_t, tile, flat, put_qkv, g_b_qkv, begin, end):
    def body(c, _):
        cols = tile_at(c, TILE)
        for i in range(images):
            tile[i * SLOT : (i + 1) * SLOT, :] = d_qkv[i, :, cols].astype(F32)
        values = tile[...]
        g_b_qkv[:, cols] = jnp.sum(values, axis=0, keepdims=True)
        low = values.astype(BF16)
        flat[:, cols] = low
        put_qkv(c, dot(normed_t[...], low).astype(BF16))
        return 0

    lax.fori_loop(begin, end, body, 0)


def stage_norm_back(width, flat, w_qkv, stack):
    def body(c, _):
        cols = tile_at(c, TILE)
        stack[:, cols] = dot_nt(flat[...], w_qkv[cols, :])
        return 0

    lax.fori_loop(0, width // TILE, body, 0)


def stage_end(images, slots, width, keep, token, gain, middle, live, stack, g_gain, g_shift, put_patches):
    for ref in (g_gain, g_shift):
        ref[...] = jnp.zeros_like(ref)

    def back(b, _):
        rows = tile_at(b, BLOCK)
        grad = stack[rows, :]
        hat, inverse = norm_parts(token[rows, :].astype(F32))
        g_gain[...] += jnp.sum(grad * hat, axis=0, keepdims=True)
        g_shift[...] += jnp.sum(grad, axis=0, keepdims=True)
        total = middle[rows, :] + norm_back(hat, inverse, gain[...], grad)
        stack[rows, :] = total * jnp.concatenate([live[rows, :]] * (width // BLOCK), axis=1)
        return 0

    lax.fori_loop(0, ROWS // BLOCK, back, 0)

    def scatter(i, _):
        chosen = (lax.broadcasted_iota(jnp.int32, (slots, SLOT), 0) == keep[i]).astype(F32).astype(BF16)
        values = stack[pl.ds(pl.multiple_of(i * SLOT, 8), SLOT), :]
        high = values.astype(BF16)
        rest = (values - high.astype(F32)).astype(BF16)
        put_patches(i, dot(chosen, high) + dot(chosen, rest))
        return 0

    for i in range(images):
        scatter(i, 0)


MESH = pl.DeviceIdType.MESH


class Place:
    def __init__(self):
        f, d = lax.axis_index("fsdp"), lax.axis_index("dp")
        self.z, self.x = f // 2, lax.rem(f, 2)
        self.y, self.c = d // 2, lax.rem(d, 2)
        z = self.z
        self.zs = [z, z + 1 - 2 * lax.rem(z, 2), lax.rem(z + 2, 4), 3 - z]

    def to(self, z=None, x=None, y=None, c=None):
        z, x, y, c = (own if new is None else new for new, own in ((z, self.z), (x, self.x), (y, self.y), (c, self.c)))
        return (z * 2 + x, y * 2 + c)

    def sides(self):
        return self.to(x=1 - self.x), self.to(y=1 - self.y), self.to(c=1 - self.c)


def enter(peers):
    barrier = pltpu.get_barrier_semaphore()
    for peer in peers:
        pl.semaphore_signal(barrier, inc=1, device_id=peer, device_id_type=MESH)
    pl.semaphore_wait(barrier, len(peers))


class Gather:
    def __init__(self, place, shard, full, first_cols, send, recv):
        self.place, self.shard, self.full, self.send, self.recv = place, shard, full, send, recv
        self.rows, cols = shard.shape
        self.half, self.wide, self.cut = self.rows // 2, cols // 2, first_cols
        self.started = []

    def spot(self, z, x, y, part=None, local=False):
        p = self.place
        base = 0 if local else (z * 2 + x) * self.rows
        rows = pl.ds(pl.multiple_of(base + p.c * self.half, 16), self.half)
        if y is None:
            return rows, slice(None)
        start, size = (y * self.wide, self.wide) if part is None else ((y * self.wide, self.cut) if part == 0 else (y * self.wide + self.cut, self.wide - self.cut))
        return rows, pl.ds(pl.multiple_of(start, 128), size)

    def copy(self, spot, sem, peer, local=None):
        src = self.full.at[spot] if local is None else self.shard.at[local]
        return pltpu.make_async_remote_copy(
            src_ref=src, dst_ref=self.full.at[spot], send_sem=self.send.at[sem], recv_sem=self.recv.at[sem], device_id=peer, device_id_type=MESH
        )

    def start(self, spot, sem, peer, local=None):
        copy = self.copy(spot, sem, peer, local)
        copy.start()
        self.started.append(copy)

    def arrived(self, spot, sem):
        self.copy(spot, sem, self.place.sides()[0]).wait_recv()

    def own(self, sem):
        p = self.place
        rows = pl.ds(pl.multiple_of((p.z * 2 + p.x) * self.rows, 16), self.rows)
        return pltpu.make_async_copy(self.shard, self.full.at[rows, :], sem)

    def begin(self):
        p = self.place
        side_x, side_y, _ = p.sides()
        spot, local = self.spot(p.z, p.x, p.y), self.spot(p.z, p.x, p.y, None, True)
        for k in (1, 2, 3):
            self.start(spot, k, p.to(z=p.zs[k]), local)
        self.start(spot, 4, side_x, local)
        self.start(self.spot(p.z, p.x, 1 - p.y, 1), 16, side_x, self.spot(p.z, p.x, 1 - p.y, 1, True))

    def spread(self, k):
        p = self.place
        side_x, side_y, _ = p.sides()
        spot = self.spot(p.zs[k], p.x, p.y)
        self.arrived(spot, k)
        self.start(spot, 4 + k, side_x)
        self.start(spot, 8 + k, side_y)

    def cross(self, k):
        p = self.place
        side_x, side_y, _ = p.sides()
        self.arrived(self.spot(p.zs[k], 1 - p.x, p.y), 4 + k)
        self.start(self.spot(p.zs[k], 1 - p.x, p.y, 0), 12 + k, side_y)
        if k:
            self.arrived(self.spot(p.zs[k], p.x, 1 - p.y), 8 + k)
            self.start(self.spot(p.zs[k], p.x, 1 - p.y, 1), 16 + k, side_x)

    def share(self, k):
        p = self.place
        core = p.sides()[2]
        if k:
            self.start(self.spot(p.zs[k], p.x, None), 20 + k, core)
        self.arrived(self.spot(p.zs[k], 1 - p.x, 1 - p.y, 0), 12 + k)
        self.arrived(self.spot(p.zs[k], 1 - p.x, 1 - p.y, 1), 16 + k)
        self.start(self.spot(p.zs[k], 1 - p.x, None), 24 + k, core)

    def finish(self):
        p = self.place

        def other(z, x):
            return pl.ds(pl.multiple_of((z * 2 + x) * self.rows + (1 - p.c) * self.half, 16), self.half), slice(None)

        for k in range(4):
            if k:
                self.arrived(other(p.zs[k], p.x), 20 + k)
            self.arrived(other(p.zs[k], 1 - p.x), 24 + k)

    def drain(self):
        for copy in self.started:
            copy.wait_send()


class Reduce:
    def __init__(self, place, source, held, core, diag_x, diag_y, side_x, side_y, line, final, send, recv):
        self.place, self.source, self.held, self.core = place, source, held, core
        self.diag_x, self.diag_y, self.side_x, self.side_y, self.line, self.final = diag_x, diag_y, side_x, side_y, line, final
        self.send, self.recv, self.started = send, recv, []
        self.by_rows = diag_y.shape[2] == final.shape[3]
        self.cut = diag_y.shape[1] if self.by_rows else diag_y.shape[2]

    def part(self, second):
        bounds = pl.ds(self.cut, (self.final.shape[2] if self.by_rows else self.final.shape[3]) - self.cut) if second else pl.ds(0, self.cut)
        return (bounds, slice(None)) if self.by_rows else (slice(None), bounds)

    def hold(self, z, x, y, *rest):
        if self.held is None:
            return (z, x, self.place.c, y) + rest
        return (z, x, y) + rest

    @property
    def home(self):
        return self.source if self.held is None else self.held

    def copy(self, src, dst, sem, peer):
        return pltpu.make_async_remote_copy(src_ref=src, dst_ref=dst, send_sem=self.send.at[sem], recv_sem=self.recv.at[sem], device_id=peer, device_id_type=MESH)

    def start(self, src, dst, sem, peer):
        copy = self.copy(src, dst, sem, peer)
        copy.start()
        self.started.append(copy)

    def arrived(self, dst, sem):
        self.copy(dst, dst, sem, self.place.sides()[0]).wait_recv()

    def begin(self, own=None):
        p = self.place
        self.start(self.source.at[:, :, 1 - p.c], self.core, 0, p.sides()[2])
        self.own = own
        if own is not None:
            own.start()

    def add_core(self, x, y):
        def body(z, _):
            spot = self.hold(z, x, y)
            self.home[spot] = self.home[spot] + self.core[z, x, y]
            return 0

        lax.fori_loop(0, 4, body, 0)

    def add(self, x, y, part, buffer):
        def body(z, _):
            spot = self.hold(z, x, y, *part)
            self.home[spot] = self.home[spot] + buffer[z]
            return 0

        lax.fori_loop(0, 4, body, 0)

    def step_core(self):
        p = self.place
        side_x, side_y, _ = p.sides()
        if self.own is not None:
            self.own.wait()
        self.arrived(self.core, 0)
        self.add_core(1 - p.x, 1 - p.y)
        every = slice(None)
        self.start(self.home.at[self.hold(every, 1 - p.x, 1 - p.y, *self.part(True))], self.diag_x, 1, side_x)
        self.start(self.home.at[self.hold(every, 1 - p.x, 1 - p.y, *self.part(False))], self.diag_y, 2, side_y)
        self.add_core(1 - p.x, p.y)
        self.add_core(p.x, 1 - p.y)
        self.add_core(p.x, p.y)

    def step_diag(self):
        p = self.place
        side_x, side_y, _ = p.sides()
        every = slice(None)
        self.arrived(self.diag_y, 2)
        self.add(1 - p.x, p.y, self.part(False), self.diag_y)
        self.start(self.home.at[self.hold(every, 1 - p.x, p.y)], self.side_x, 3, side_x)
        self.arrived(self.diag_x, 1)
        self.add(p.x, 1 - p.y, self.part(True), self.diag_x)
        self.start(self.home.at[self.hold(every, p.x, 1 - p.y)], self.side_y, 4, side_y)

    def step_side(self):
        p = self.place
        whole = (slice(None), slice(None))
        self.arrived(self.side_x, 3)
        self.add(p.x, p.y, whole, self.side_x)
        self.arrived(self.side_y, 4)
        self.add(p.x, p.y, whole, self.side_y)
        for k in (1, 2, 3):
            self.start(self.home.at[self.hold(p.zs[k], p.x, p.y)], self.line.at[k - 1], 4 + k, p.to(z=p.zs[k]))

    def step_line(self):
        p = self.place
        total = self.home[self.hold(p.z, p.x, p.y)].astype(F32)
        for k in (1, 2, 3):
            self.arrived(self.line.at[k - 1], 4 + k)
            total = total + self.line[k - 1].astype(F32)
        self.final[p.c, p.y] = total.astype(BF16)
        self.start(self.final.at[p.c, p.y], self.final.at[p.c, p.y], 8, p.sides()[1])

    def step_share(self):
        p = self.place
        self.arrived(self.final.at[p.c, 1 - p.y], 8)
        self.start(self.final.at[p.c], self.final.at[p.c], 9, p.sides()[2])

    def finish(self):
        self.arrived(self.final.at[1 - self.place.c], 9)

    def drain(self):
        for copy in self.started:
            copy.wait_send()


class SmallReduce:
    def __init__(self, place, home, core, side_y, side_x, line, send, recv):
        self.place, self.home, self.core, self.side_y, self.side_x, self.line = place, home, core, side_y, side_x, line
        self.send, self.recv, self.started = send, recv, []

    copy, start, arrived, drain = Reduce.copy, Reduce.start, Reduce.arrived, Reduce.drain

    def begin(self):
        self.start(self.home, self.core, 0, self.place.sides()[2])

    def step_core(self, sent):
        p = self.place
        self.arrived(self.core, 0)
        sent[...] = self.home[...] + self.core[...]
        self.start(sent, self.side_y, 1, p.sides()[1])

    def step_y(self, sent, total):
        p = self.place
        self.arrived(self.side_y, 1)
        total[...] = sent[...] + self.side_y[...]
        self.start(total.at[:, 1 - p.x], self.side_x, 2, p.sides()[0])

    def step_x(self, total):
        p = self.place
        self.arrived(self.side_x, 2)
        for z in range(4):
            self.side_x[z] = self.side_x[z] + total[z, p.x]
        for k in (1, 2, 3):
            self.start(self.side_x.at[p.zs[k]], self.line.at[k - 1], 2 + k, p.to(z=p.zs[k]))

    def step_line(self, out):
        total = self.side_x[self.place.z]
        for k in (1, 2, 3):
            self.arrived(self.line.at[k - 1], 2 + k)
            total = total + self.line[k - 1]
        out[...] = total
VMEM = pl.BlockSpec(memory_space=pltpu.VMEM)
ANY = pl.BlockSpec(memory_space=pl.ANY)
LIMIT = 61 * 1024 * 1024


def call(body, outs, scratch, args, name):
    return pl.pallas_call(
        body,
        out_shape=[jax.ShapeDtypeStruct(*o) for o in outs],
        in_specs=[VMEM] * len(args),
        out_specs=[VMEM] * len(outs),
        scratch_shapes=[pltpu.VMEM(*s) for s in scratch],
        compiler_params=pltpu.CompilerParams(vmem_limit_bytes=LIMIT),
        name=name,
    )(*args)


def first_plain(
    images, slots, width, patches, keep, cot, vectors, w_qkv, w_out,
    token, n1t, dm, dmt, live, qkv, probs, att_t, middle, n2, n2t, stack, normed, mask, att, bias,
):
    bias[...] = jnp.concatenate([vectors[2:3, :], jnp.zeros((1, width), F32), vectors[3:4, :]], axis=1)
    stage_gather(images, slots, patches, keep, stack, live, mask)
    stage_norm(stack, vectors[0:1, :], vectors[1:2, :], token, normed, n1t)
    stage_grads(images, slots, width, cot, stack, live, dm, dmt)
    stage_qkv(images, width, normed, w_qkv, bias, qkv)
    stage_attention(images, width, qkv, mask, probs, stack, 0, images)
    stage_out(width, stack, w_out, vectors.at[4:5, :], token, vectors.at[5:6, :], vectors.at[6:7, :], att, att_t, middle, n2, n2t)


def first_kernel(
    images, slots, width,
    patches, keep, cot, vec, s_qkv, s_out, s_up, s_down,
    token, n1t, dm, dmt, live, qkv, probs, att_t, middle, n2, n2t, vectors, b_up, o_qkv, o_out, f_up, f_down,
    stack, normed, mask, att, f_qkv, f_out, vecs, bias, q_send, q_recv, o_send, o_recv, u_send, u_recv, d_send, d_recv, v_send, v_recv, own,
):
    place = Place()
    side_x, side_y, side_c = place.sides()
    flat = [place.to(z=place.zs[k], x=x) for k in range(4) for x in (place.x, 1 - place.x)][1:]
    enter(flat + [side_y, side_c])
    g_qkv = Gather(place, s_qkv, f_qkv, 640, q_send, q_recv)
    g_out = Gather(place, s_out, f_out, 256, o_send, o_recv)
    g_up = Gather(place, s_up, f_up, 896, u_send, u_recv)
    g_down = Gather(place, s_down, f_down, 256, d_send, d_recv)
    mine = place.z * 2 + place.x
    tiny = []
    for j, peer in enumerate(flat):
        copy = pltpu.make_async_remote_copy(src_ref=vec, dst_ref=vecs.at[mine], send_sem=v_send.at[j], recv_sem=v_recv.at[j], device_id=peer, device_id_type=MESH)
        copy.start()
        tiny.append(copy)
    g_qkv.begin()
    locals_ = [g.own(own.at[j]) for j, g in enumerate((g_qkv, g_out, g_up, g_down))]
    for copy in locals_:
        copy.start()
    vecs[mine] = vec[...]
    stage_gather(images, slots, patches, keep, stack, live, mask)
    g_out.begin()
    for copy in tiny:
        copy.wait_recv()
    rows = jnp.concatenate([vecs[f][:, :96] for f in range(8)], axis=1).astype(F32)
    vectors[...] = rows
    b_up[...] = jnp.concatenate([vecs[f][8 + j : 9 + j, :96].astype(F32) for f in range(8) for j in range(4)], axis=1)
    for k in (1, 2, 3):
        g_qkv.spread(k)
    g_up.begin()
    stage_norm(stack, vectors[0:1, :], vectors[1:2, :], token, normed, n1t)
    for k in range(4):
        g_qkv.cross(k)
    for k in (1, 2, 3):
        g_out.spread(k)
    g_down.begin()
    stage_grads(images, slots, width, cot, stack, live, dm, dmt)
    for k in range(4):
        g_qkv.share(k)
    for k in range(4):
        g_out.cross(k)
    for k in (1, 2, 3):
        g_up.spread(k)
    locals_[0].wait()
    g_qkv.finish()
    keep_qkv = pltpu.make_async_copy(f_qkv, o_qkv, own.at[4])
    keep_qkv.start()
    bias[...] = jnp.concatenate([vectors[2:3, :], jnp.zeros((1, width), F32), vectors[3:4, :]], axis=1)
    stage_qkv(images, width, normed, f_qkv, bias, qkv)
    for k in range(4):
        g_out.share(k)
    for k in (1, 2, 3):
        g_down.spread(k)
    stage_attention(images, width, qkv, mask, probs, stack, 0, 1)
    for k in range(4):
        g_up.cross(k)
    stage_attention(images, width, qkv, mask, probs, stack, 1, 2)
    for k in range(4):
        g_up.share(k)
    stage_attention(images, width, qkv, mask, probs, stack, 2, 3)
    for k in range(4):
        g_down.cross(k)
    stage_attention(images, width, qkv, mask, probs, stack, 3, 4)
    stage_attention(images, width, qkv, mask, probs, stack, 4, images)
    locals_[1].wait()
    g_out.finish()
    keep_out = pltpu.make_async_copy(f_out, o_out, own.at[5])
    keep_out.start()
    stage_out(width, stack, f_out, vectors.at[4:5, :], token, vectors.at[5:6, :], vectors.at[6:7, :], att, att_t, middle, n2, n2t)
    for k in range(4):
        g_down.share(k)
    g_up.finish()
    g_down.finish()
    for copy in locals_[2:] + [keep_qkv, keep_out]:
        copy.wait()
    for copy in tiny:
        copy.wait_send()
    for g in (g_qkv, g_out, g_up, g_down):
        g.drain()


def second_kernel(
    linked, images, slots, width, hidden_width,
    n2, n2t, dm, dmt, w_up, b_up, w_down, b_d, middle_in, live, gain2,
    out, middle, d_low, g_up, g_down, g_b_up, g_g2, g_s2, g_bd, g_bo, act, dh, stack,
):
    middle[...] = middle_in[...]

    def put_up(c, value):
        if linked:
            per = 2 * width // TILE
            g_up[:, :, :, c // per, :, tile_at(lax.rem(c, per), TILE)] = value.reshape(4, 2, 2, 48, TILE)
        else:
            g_up[:, tile_at(c, TILE)] = value

    def put_down(c, value):
        if linked:
            for j in range(2):
                col = 2 * c + j
                f = col // 3
                g_down[f // 2, lax.rem(f, 2), :, :, :, tile_at(lax.rem(col, 3), 128)] = value[:, j * 128 : (j + 1) * 128].reshape(2, 2, 192, 128)
        else:
            g_down[:, tile_at(c, TILE)] = value

    stage_mlp(width, hidden_width, n2, n2t, dm, dmt, w_up, b_up, w_down, act, dh, put_up, put_down, g_b_up)
    stage_mlp_out(images, slots, width, act, dh, w_up, w_down, b_d, middle, live, gain2, dm, stack, out, d_low, g_g2, g_s2, g_bd, g_bo)


def third_plain(
    images, slots, width, d_low, att_t, w_out, qkv_in, probs, n1t, w_qkv, token, gain, mid, live, keep,
    g_out, g_qkv, g_b, g_g1, g_s1, gp, stack, tile, flat, qkv,
):
    def put(ref, c, value):
        ref[:, tile_at(c, TILE)] = value

    def put_patches(i, value):
        gp[i] = value

    qkv[...] = qkv_in[...]
    tile[...] = jnp.zeros_like(tile)
    stage_out_back(width, att_t, d_low, w_out, functools.partial(put, g_out), stack)
    for i in range(images):
        stage_attention_back(width, qkv, probs.at[pl.ds(i * H, H)], stack, i, 0, H // 2)
    stage_qkv_back(images, width, qkv, n1t, tile, flat, functools.partial(put, g_qkv), g_b, 0, 3 * width // TILE)
    stage_norm_back(width, flat, w_qkv, stack)
    stage_end(images, slots, width, keep, token, gain, mid, live, stack, g_g1, g_s1, put_patches)


def third_kernel(
    images, slots, width,
    d_low, att_t, w_out, keep, gain, s_bup, s_g2, s_s2, s_bd, s_bo, h_qkv, h_probs, h_n1t, h_wqkv, h_token, h_mid, h_live, g_up, g_down,
    gp, e_up, e_down, e_out, e_q, e_k, e_v, e_small,
    stack, tile, flat, qkv, probs, n1t, w_qkv, token, mid, live, stage, g_b, g_g1, g_s1, g_attn,
    up_held, up_core, up_dx, up_dy, up_sx, up_sy, up_ln, dn_held, dn_core, dn_dx, dn_dy, dn_sx, dn_sy, dn_ln,
    core4, dx4, dy4, sx4, sy4, ln4, v_home, v_core, v_sy, v_sx, v_ln, v_sent, v_total,
    send6, recv6, v_send, v_recv, own, probs_sem, out_sem,
):
    place = Place()
    side_x, side_y, side_c = place.sides()
    enter([place.to(z=place.zs[k]) for k in (1, 2, 3)] + [side_x, side_y, side_c])
    r_up = Reduce(place, g_up, up_held, up_core, up_dx, up_dy, up_sx, up_sy, up_ln, e_up, send6.at[0], recv6.at[0])
    r_down = Reduce(place, g_down, dn_held, dn_core, dn_dx, dn_dy, dn_sx, dn_sy, dn_ln, e_down, send6.at[1], recv6.at[1])
    r_q, r_k, r_v, r_out = (
        Reduce(place, g_attn.at[m], None, core4.at[m], dx4.at[m], dy4.at[m], sx4.at[m], sy4.at[m], ln4.at[m], e, send6.at[2 + m], recv6.at[2 + m])
        for m, e in enumerate((e_q, e_k, e_v, e_out))
    )
    small = SmallReduce(place, v_home, v_core, v_sy, v_sx, v_ln, v_send, v_recv)
    r_down.begin(pltpu.make_async_copy(g_down.at[:, :, place.c], dn_held, own.at[0]))
    r_up.begin(pltpu.make_async_copy(g_up.at[:, :, place.c], up_held, own.at[1]))
    fetch = {}
    for j, (name, src, dst) in enumerate(
        (("qkv", h_qkv, qkv), ("n1t", h_n1t, n1t), ("w_qkv", h_wqkv, w_qkv), ("token", h_token, token), ("mid", h_mid, mid), ("live", h_live, live))
    ):
        fetch[name] = pltpu.make_async_copy(src, dst, own.at[2 + j])

    def load_probs(i):
        return pltpu.make_async_copy(h_probs.at[pl.ds(i * H, H)], probs.at[i % 2], probs_sem.at[i % 2])

    fetch["qkv"].start()
    load_probs(0).start()
    for name in ("n1t", "w_qkv", "token", "mid", "live"):
        fetch[name].start()

    def put(m, c, value):
        for j in range(2):
            col = 2 * c + j
            y, off = lax.rem(col, 6) // 3, lax.rem(col, 3)
            at = pl.ds(pl.multiple_of(off * 128, 128), 128)
            g_attn[col // 6 if m is None else m, :, :, :, y, :, at] = value[:, j * 128 : (j + 1) * 128].reshape(4, 2, 2, 48, 128)

    stage_out_back(width, att_t, d_low, w_out, functools.partial(put, 3), stack)
    r_out.begin()
    r_down.step_core()
    r_up.step_core()
    fetch["qkv"].wait()
    steps = {
        1: [r_out.step_core],
        3: [r_down.step_diag],
        6: [r_up.step_diag],
        7: [r_out.step_diag],
    }
    for i in range(images):
        load_probs(i).wait()
        if i + 1 < images:
            load_probs(i + 1).start()
        for h in range(2):
            stage_attention_back(width, qkv, probs.at[i % 2], stack, i, h * 3, h * 3 + 3)
            for step in steps.get(2 * i + h, []):
                step()
    fetch["n1t"].wait()
    tile[...] = jnp.zeros_like(tile)
    back = functools.partial(stage_qkv_back, images, width, qkv, n1t, tile, flat, functools.partial(put, None), g_b)
    third = width // TILE
    back(0, third)
    r_q.begin()
    r_down.step_side()
    back(third, 2 * third)
    r_k.begin()
    r_q.step_core()
    back(2 * third, 3 * third)
    r_v.begin()
    r_k.step_core()
    for name in ("w_qkv", "token", "mid", "live"):
        fetch[name].wait()
    stage_norm_back(width, flat, w_qkv, stack)
    r_v.step_core()
    r_up.step_side()
    r_q.step_diag()
    flights = []

    def put_patches(i, value):
        if i >= 2:
            flights[i - 2].wait()
        stage[i % 2] = value
        copy = pltpu.make_async_copy(stage.at[i % 2], gp.at[i], out_sem.at[i % 2])
        copy.start()
        flights.append(copy)

    stage_end(images, slots, width, keep, token, gain, mid, live, stack, g_g1, g_s1, put_patches)
    v_home[...] = jnp.zeros_like(v_home)
    for j, (ref, base) in enumerate(((g_g1, 0), (g_s1, 0), (g_b, 0), (g_b, 2 * width), (s_bo, 0), (s_g2, 0), (s_s2, 0), (s_bd, 0))):
        row = ref[:, base : base + width]
        for f in range(8):
            v_home[f // 2, f % 2, j : j + 1, :96] = row[:, 96 * f : 96 * f + 96]
    row = s_bup[...]
    for f in range(8):
        for j in range(4):
            v_home[f // 2, f % 2, 8 + j : 9 + j, :96] = row[:, 384 * f + 96 * j : 384 * f + 96 * j + 96]
    small.begin()
    r_down.step_line()
    r_k.step_diag()
    small.step_core(v_sent)
    r_out.step_side()
    r_v.step_diag()
    small.step_y(v_sent, v_total)
    r_q.step_side()
    r_up.step_line()
    r_down.step_share()
    small.step_x(v_total)
    r_k.step_side()
    r_out.step_line()
    r_v.step_side()
    r_up.step_share()
    small.step_line(e_small)
    for r in (r_q, r_k, r_v):
        r.step_line()
    for r in (r_out, r_q, r_k, r_v):
        r.step_share()
    for r in (r_down, r_up, r_out, r_q, r_k, r_v):
        r.finish()
    for copy in flights[-2:]:
        copy.wait()
    for r in (r_down, r_up, r_out, r_q, r_k, r_v, small):
        r.drain()


def shards(
    linked,
    patches, keep, ln1_gain, ln1_bias, w_qkv, b_query, b_value, w_out, b_out,
    ln2_gain, ln2_bias, w_up, b_up, w_down, b_down, cotangent,
):
    images, slots = keep.shape
    width = patches.shape[2]
    hidden_width = w_up.shape[1]
    keep_pad = jnp.pad(keep, ((0, 0), (0, SLOT - slots)), constant_values=-1).reshape(images, 1, SLOT)
    part = ln1_gain.shape[0]
    singles = [v.reshape(1, part) for v in (ln1_gain, ln1_bias, b_query, b_value, b_out, ln2_gain, ln2_bias, b_down)]
    rows_low, rows_wide = ((ROWS, width), BF16), ((ROWS, width), F32)
    cols_low = ((width, ROWS), BF16)
    live_like, mask_like = ((ROWS, BLOCK), F32), ((images, SLOT, SLOT), F32)
    heads_like = ((images, SLOT, 3 * width), BF16)
    probs_like = ((images * H, SLOT, SLOT), BF16)
    row_like = ((1, width), F32)

    if linked:
        vec = jnp.concatenate(singles + [b_up.reshape(4, part)], axis=0)
        vec = jnp.pad(vec, ((0, 4), (0, BLOCK - part)))
        full = lambda v: ((v.shape[0] * 8, v.shape[1]), BF16)
        outs = [
            rows_low, cols_low, rows_low, cols_low, live_like, heads_like, probs_like, cols_low, rows_wide, rows_low, cols_low,
            ((16, width), F32), ((1, hidden_width), F32), full(w_qkv), full(w_out), full(w_up), full(w_down),
        ]
        scratch = [rows_wide, rows_low, mask_like, rows_low, full(w_qkv), full(w_out), ((8, 16, BLOCK), BF16), ((1, 3 * width), F32)]
        token, n1t, dm, dmt, live, qkv, probs, att_t, middle, n2, n2t, vectors, bias_up, qkv_full, out_full, up_full, down_full = pl.pallas_call(
            functools.partial(first_kernel, images, slots, width),
            out_shape=[jax.ShapeDtypeStruct(*o) for o in outs],
            in_specs=[VMEM] * 8,
            out_specs=[VMEM] * 13 + [ANY] * 4,
            scratch_shapes=[pltpu.VMEM(*s) for s in scratch]
            + [pltpu.SemaphoreType.DMA((28,))] * 8
            + [pltpu.SemaphoreType.DMA((7,))] * 2
            + [pltpu.SemaphoreType.DMA((6,))],
            compiler_params=pltpu.CompilerParams(vmem_limit_bytes=LIMIT, collective_id=0, has_side_effects=True),
            name="first",
        )(patches, keep_pad, cotangent, vec, w_qkv, w_out, w_up, w_down)
    else:
        gather = lambda v: lax.all_gather(v, "fsdp", axis=0, tiled=True)
        vectors = jnp.pad(gather(jnp.concatenate(singles, axis=0).T).T.astype(F32), ((0, 8), (0, 0)))
        bias_up = gather(b_up).astype(F32).reshape(1, hidden_width)
        qkv_full, out_full, up_full, down_full = gather(w_qkv), gather(w_out), gather(w_up), gather(w_down)
        outs = [rows_low, cols_low, rows_low, cols_low, live_like, heads_like, probs_like, cols_low, rows_wide, rows_low, cols_low]
        scratch = [rows_wide, rows_low, mask_like, rows_low, ((1, 3 * width), F32)]
        token, n1t, dm, dmt, live, qkv, probs, att_t, middle, n2, n2t = call(
            functools.partial(first_plain, images, slots, width),
            outs, scratch, (patches, keep_pad, cotangent, vectors, qkv_full, out_full), "first",
        )
    gain1, gain2, b_d = vectors[0:1], vectors[5:6], vectors[7:8]

    hid = ((ROWS, hidden_width), BF16)
    if linked:
        grads_like = [((4, 2, 2, 2, 48, 2 * width), BF16), ((4, 2, 2, 2, 192, width // 2), BF16)]
    else:
        grads_like = [((width, hidden_width), BF16)] * 2
    out_tokens, d_mid, d_low, g_up, g_down, g_b_up, g_g2, g_s2, g_bd, g_bo = call(
        functools.partial(second_kernel, linked, images, slots, width, hidden_width),
        [((images, slots, width), BF16), rows_wide, rows_low] + grads_like + [((1, hidden_width), F32)] + [row_like] * 4,
        [hid, hid, rows_wide],
        (n2, n2t, dm, dmt, up_full, bias_up, down_full, b_d, middle, live, gain2),
        "second",
    )
    if linked:
        final = lambda r, w: ((2, 2, r, w), BF16)
        attn = final(48, width // 2)
        outs = [((images, slots, width), F32), final(48, 2 * width), final(192, width // 2), attn, attn, attn, attn, ((16, BLOCK), F32)]
        half = width // 2

        def buffers(r, w, by_rows, cut, lead=()):
            other = (4, r - cut, w) if by_rows else (4, r, w - cut)
            first = (4, cut, w) if by_rows else (4, r, cut)
            shapes = [(4, 2, 2, r, w), other, first, (4, r, w), (4, r, w), (3, r, w)]
            return [(lead + s, BF16) for s in shapes]

        scratch = [rows_wide, ((ROWS, TILE), F32), ((ROWS, 3 * width), BF16), heads_like, ((2, H, SLOT, SLOT), BF16), cols_low]
        scratch += [((width, 3 * width), BF16), rows_low, rows_wide, live_like, ((2, slots, width), F32), ((1, 3 * width), F32), row_like, row_like]
        scratch += [((4, 4, 2, 2, 2, 48, half), BF16)]
        scratch += [((4, 2, 2, 48, 2 * width), BF16)] + buffers(48, 2 * width, False, 512)
        scratch += [((4, 2, 2, 192, half), BF16)] + buffers(192, half, True, 64)
        scratch += buffers(48, half, False, 128, (4,))
        small_like, line_like = ((4, 2, 16, BLOCK), F32), ((3, 16, BLOCK), F32)
        scratch += [small_like, small_like, small_like, ((4, 16, BLOCK), F32), line_like, small_like, small_like]
        grad_patches, e_up, e_down, e_out, e_q, e_k, e_v, small = pl.pallas_call(
            functools.partial(third_kernel, images, slots, width),
            out_shape=[jax.ShapeDtypeStruct(*o) for o in outs],
            in_specs=[VMEM] * 10 + [ANY] * 9,
            out_specs=[ANY] + [VMEM] * 7,
            scratch_shapes=[pltpu.VMEM(*s) for s in scratch]
            + [pltpu.SemaphoreType.DMA((6, 10))] * 2
            + [pltpu.SemaphoreType.DMA((6,))] * 2
            + [pltpu.SemaphoreType.DMA((8,)), pltpu.SemaphoreType.DMA((2,)), pltpu.SemaphoreType.DMA((2,))],
            compiler_params=pltpu.CompilerParams(vmem_limit_bytes=LIMIT, collective_id=1, has_side_effects=True),
            name="third",
        )(d_low, att_t, out_full, keep_pad, gain1, g_b_up, g_g2, g_s2, g_bd, g_bo, qkv, probs, n1t, qkv_full, token, d_mid, live, g_up, g_down)
        rows = small[:8, :part]
        square = lambda e: e.transpose(0, 2, 1, 3).reshape(part, -1).astype(F32)
        sum_qkv = jnp.concatenate([square(e) for e in (e_q, e_k, e_v)], axis=1)
        sum_out, sum_up, sum_down = square(e_out), square(e_up), e_down.reshape(width, half).T.astype(F32)
        b_up_sum = small[8:12, :part].reshape(-1)
    else:
        g_out, g_qkv, g_b, g_g1, g_s1, grad_patches = call(
            functools.partial(third_plain, images, slots, width),
            [((width, width), BF16), ((width, 3 * width), BF16), ((1, 3 * width), F32), row_like, row_like, ((images, slots, width), F32)],
            [rows_wide, ((ROWS, TILE), F32), ((ROWS, 3 * width), BF16), heads_like],
            (d_low, att_t, out_full, qkv, probs, n1t, qkv_full, token, gain1, d_mid, live, keep_pad),
            "third",
        )
        scat = lambda v, dim=0: lax.psum(lax.psum_scatter(v, "fsdp", scatter_dimension=dim, tiled=True), "dp").astype(F32)
        rows = jnp.concatenate([g_g1, g_s1, g_b[:, :width], g_b[:, 2 * width :], g_bo, g_g2, g_s2, g_bd], axis=0).astype(BF16)
        rows = scat(rows, 1)
        b_up_sum = scat(g_b_up.astype(BF16), 1)[0]
        sum_qkv, sum_out, sum_up, sum_down = scat(g_qkv), scat(g_out), scat(g_up), scat(g_down, 1).T
    return (
        out_tokens, grad_patches, rows[0], rows[1], sum_qkv, rows[2], rows[3], sum_out, rows[4],
        rows[5], rows[6], sum_up, b_up_sum, sum_down, rows[7],
    )


def solution(mesh):
    linked = (mesh.shape["fsdp"], mesh.shape["dp"]) == (8, 4)
    many, one, two = P(("fsdp", "dp"), None, None), P("fsdp"), P("fsdp", None)
    in_specs = (many, P(("fsdp", "dp"), None), one, one, two, one, one, two, one, one, one, two, one, two, one, many)
    out_specs = (many, many, one, one, two, one, one, two, one, one, one, two, one, two, one)
    return jax.shard_map(functools.partial(shards, linked), mesh=mesh, in_specs=in_specs, out_specs=out_specs, check_vma=False)
```

```python
import functools
import math

import jax
import jax.numpy as jnp
from jax import lax
from jax.experimental import pallas as pl
from jax.experimental.pallas import tpu as pltpu
from jax.sharding import PartitionSpec as P

H = 12
HD = 64
EPSILON = 1e-06
F32 = jnp.float32
BF16 = jnp.bfloat16
SLOT = 200
ROWS = 1024
BLOCK = 128
TILE = 256
NT = (((1,), (1,)), ((), ()))


def dot(left, right):
    return jnp.dot(left, right, preferred_element_type=F32)


def dot_nt(left, right):
    return lax.dot_general(left, right, NT, preferred_element_type=F32)


def tile_at(index, size):
    if isinstance(index, int):
        return pl.ds(index * size, size)
    return pl.ds(pl.multiple_of(index * size, size), size)


def loop(begin, end, body, unroll):
    if (end - begin) == unroll:
        for j in range(begin, end):
            body(j, 0)
        return

    def group(t, _):
        for u in range(unroll):
            body(begin + t * unroll + u, 0)
        return 0

    lax.fori_loop(0, (end - begin) // unroll, group, 0)


def norm_parts(values):
    centre = values - jnp.mean(values, axis=-1, keepdims=True)
    spread = jnp.mean(centre * centre, axis=-1, keepdims=True)
    inverse = lax.rsqrt(spread + EPSILON)
    return centre * inverse, inverse


def norm_back(hat, inverse, gain, grad):
    scaled = grad * gain
    along = jnp.mean(scaled * hat, axis=-1, keepdims=True)
    return inverse * (scaled - jnp.mean(scaled, axis=-1, keepdims=True) - hat * along)


def gelu_parts(hidden):
    size = jnp.abs(hidden)
    bell = jnp.exp(hidden * hidden * -0.5)
    t = 1.0 / (1.0 + size * (0.3275911 / math.sqrt(2.0)))
    tail = 1.061405429 * 0.5
    for term in (-1.453152027, 1.421413741, -0.284496736, 0.254829592):
        tail = tail * t + term * 0.5
    tail = tail * t * bell
    below = jnp.where(hidden >= 0, 1.0 - tail, tail)
    slope = below + hidden * (bell * (1.0 / math.sqrt(2.0 * math.pi)))
    return hidden * below, slope


def first_lanes(rows):
    return lax.broadcasted_iota(jnp.int32, (rows, 2 * HD), 1) < HD


def stage_gather(images, slots, patches, keep, stack, live, mask):
    stack[...] = jnp.zeros_like(stack)
    live[...] = jnp.zeros_like(live)

    def gather(i, _):
        row = keep[i]
        column = jnp.broadcast_to(row, (SLOT, SLOT)).T
        mask[i] = jnp.where(column >= 0, 0.0, -1e30)
        alive = (column >= 0).astype(F32)
        chosen = (column[:, :slots] == lax.broadcasted_iota(jnp.int32, (SLOT, slots), 1)).astype(F32).astype(BF16)
        rows = pl.ds(pl.multiple_of(i * SLOT, 8), SLOT)
        stack[rows, :] = dot(chosen, patches[i])
        live[rows, :] = alive[:, :BLOCK]
        return 0

    loop(0, images, gather, 1)


def stage_norm(stack, gain, shift, token, normed, normed_t):
    def norm(b, _):
        rows = tile_at(b, BLOCK)
        values = stack[rows, :]
        token[rows, :] = values.astype(BF16)
        hat, _ = norm_parts(values)
        low = (hat * gain + shift).astype(BF16)
        normed[rows, :] = low
        normed_t[:, rows] = low.T
        return 0

    loop(0, ROWS // BLOCK, norm, 4)


def stage_grads(images, slots, width, cot, stack, live, dm, dm_t):
    stack[...] = jnp.zeros_like(stack)
    for i in range(images):
        stack[i * SLOT : i * SLOT + slots, :] = cot[i].astype(F32)

    def grads(b, _):
        rows = tile_at(b, BLOCK)
        low = (stack[rows, :] * jnp.concatenate([live[rows, :]] * (width // BLOCK), axis=1)).astype(BF16)
        dm[rows, :] = low
        dm_t[:, rows] = low.T
        return 0

    loop(0, ROWS // BLOCK, grads, 2)


def stage_qkv(images, width, normed, w_qkv, bias, qkv):
    def body(c, _):
        cols = tile_at(c, TILE)
        scale = jnp.where(c < width // TILE, 1.0 / math.sqrt(HD), 1.0)
        values = (dot(normed[...], w_qkv[:, cols]) + bias[:, cols]) * scale
        for i in range(images):
            qkv[i, :, cols] = values[i * SLOT : (i + 1) * SLOT].astype(BF16)
        return 0

    loop(0, 3 * width // TILE, body, 3)


def stage_attention(width, qkv, mask, probs, stack, i):
    low = first_lanes(SLOT)
    for p in range(H // 2):
        q2 = qkv[i, :, p * 128 : (p + 1) * 128]
        k2 = qkv[i, :, width + p * 128 : width + (p + 1) * 128]
        v2_t = qkv[i, :, 2 * width + p * 128 : 2 * width + (p + 1) * 128].T
        outs = []
        for h in range(2):
            qh = jnp.where(low if h == 0 else ~low, q2, jnp.zeros_like(q2))
            scores = dot_nt(k2, qh) + mask[i]
            exponent = jnp.exp(scores - jnp.max(scores, axis=0, keepdims=True))
            share = 1.0 / jnp.sum(exponent, axis=0, keepdims=True)
            prob = (exponent * share).astype(BF16)
            probs[2 * p + h] = prob
            outs.append(dot(v2_t[h * HD : (h + 1) * HD], prob))
        stack[pl.ds(pl.multiple_of(i * SLOT, 8), SLOT), p * 128 : (p + 1) * 128] = jnp.concatenate(outs, axis=0).T


def stage_out(width, stack, w_out, bias, token, gain, shift, att, att_t, middle, normed, normed_t):
    def low(b, _):
        rows = tile_at(b, BLOCK)
        values = stack[rows, :].astype(BF16)
        att[rows, :] = values
        att_t[:, rows] = values.T
        return 0

    loop(0, ROWS // BLOCK, low, 4)

    def body(c, _):
        cols = tile_at(c, TILE)
        middle[:, cols] = token[:, cols].astype(F32) + (dot(att[...], w_out[:, cols]) + bias[:, cols])
        return 0

    loop(0, width // TILE, body, 3)

    def norm(b, _):
        rows = tile_at(b, BLOCK)
        hat, _ = norm_parts(middle[rows, :])
        values = (hat * gain[...] + shift[...]).astype(BF16)
        normed[rows, :] = values
        normed_t[:, rows] = values.T
        return 0

    loop(0, ROWS // BLOCK, norm, 4)


def stage_mlp(width, begin, end, normed, normed_t, dm, dm_t, w_up, b_up, w_down, act, dh, put_up, put_down, g_b_up):
    def body(c, _):
        cols = tile_at(c, TILE)
        hidden = dot(normed[...], w_up[:, cols]) + b_up[:, cols]
        d_act = dot_nt(dm[...], w_down[cols, :])
        value, slope = gelu_parts(hidden)
        value = value.astype(BF16)
        grad = (d_act * slope).astype(BF16)
        act[:, cols] = value
        dh[:, cols] = grad
        g_b_up[:, cols] = jnp.sum(grad.astype(F32), axis=0, keepdims=True)
        put_up(c, dot(normed_t[...], grad).astype(BF16))
        put_down(c, dot(dm_t[...], value).astype(BF16))
        return 0

    loop(begin, end, body, 2)


def add_products(width, stack, fresh, product):
    def body(c, _):
        cols = tile_at(c, TILE)
        value = product(cols)
        stack[:, cols] = value if fresh else stack[:, cols] + value
        return 0

    loop(0, width // TILE, body, 1)


def stage_final(images, slots, width, middle, live, b_down, stack, out):
    def final(b, _):
        rows = tile_at(b, BLOCK)
        stack[rows, :] = (middle[rows, :] + (stack[rows, :] + b_down[...])) * jnp.concatenate([live[rows, :]] * (width // BLOCK), axis=1)
        return 0

    loop(0, ROWS // BLOCK, final, 2)
    for i in range(images):
        out[i] = stack[i * SLOT : i * SLOT + slots, :].astype(BF16)


def stage_middle_back(middle, gain, dm, stack, d_mid_low, g_gain, g_shift, g_b_down, g_b_out):
    for ref in (g_gain, g_shift, g_b_down, g_b_out):
        ref[...] = jnp.zeros_like(ref)

    def back(b, _):
        rows = tile_at(b, BLOCK)
        grad = stack[rows, :]
        hat, inverse = norm_parts(middle[rows, :])
        g_gain[...] += jnp.sum(grad * hat, axis=0, keepdims=True)
        g_shift[...] += jnp.sum(grad, axis=0, keepdims=True)
        own = dm[rows, :].astype(F32)
        g_b_down[...] += jnp.sum(own, axis=0, keepdims=True)
        total = own + norm_back(hat, inverse, gain[...], grad)
        middle[rows, :] = total
        low = total.astype(BF16)
        d_mid_low[rows, :] = low
        g_b_out[...] += jnp.sum(low.astype(F32), axis=0, keepdims=True)
        return 0

    loop(0, ROWS // BLOCK, back, 2)


def stage_out_back(width, att_t, d_mid_low, w_out, put_out, stack):
    def body(c, _):
        cols = tile_at(c, TILE)
        put_out(c, dot(att_t[...], d_mid_low[:, cols]).astype(BF16))
        stack[:, cols] = dot_nt(d_mid_low[...], w_out[cols, :])
        return 0

    loop(0, width // TILE, body, 3)


def stage_attention_back(width, qkv, probs, stack, i):
    low = first_lanes(SLOT)
    for p in range(H // 2):
        at_q = slice(p * 128, (p + 1) * 128)
        at_k = slice(width + p * 128, width + (p + 1) * 128)
        at_v = slice(2 * width + p * 128, 2 * width + (p + 1) * 128)
        q2, k2, v2 = qkv[i, :, at_q], qkv[i, :, at_k], qkv[i, :, at_v]
        k2_t = k2.T
        da = stack[pl.ds(pl.multiple_of(i * SLOT, 8), SLOT), at_q].astype(BF16)
        dq, dk, dv = [], 0.0, 0.0
        for h in range(2):
            pick = lambda m: jnp.where(low if h == 0 else ~low, m, jnp.zeros_like(m))
            prob = probs[2 * p + h]
            d_prob = dot_nt(pick(v2), da)
            mixed = prob.astype(F32)
            moved = mixed * d_prob
            total = jnp.sum(moved, axis=0, keepdims=True)
            ds = (moved - mixed * total).astype(BF16)
            dq.append(dot(k2_t[h * HD : (h + 1) * HD], ds))
            dk = dk + dot(ds, pick(q2))
            dv = dv + dot(prob, pick(da))
        qkv[i, :, at_q] = (jnp.concatenate(dq, axis=0).T * (1.0 / math.sqrt(HD))).astype(BF16)
        qkv[i, :, at_k] = dk.astype(BF16)
        qkv[i, :, at_v] = dv.astype(BF16)


def stage_qkv_back(images, width, d_qkv, normed_t, tile, flat, put_qkv, g_b_qkv, begin, end):
    def body(c, _):
        cols = tile_at(c, TILE)
        for i in range(images):
            tile[i * SLOT : (i + 1) * SLOT, :] = d_qkv[i, :, cols].astype(F32)
        values = tile[...]
        g_b_qkv[:, cols] = jnp.sum(values, axis=0, keepdims=True)
        low = values.astype(BF16)
        flat[:, cols] = low
        put_qkv(c, dot(normed_t[...], low).astype(BF16))
        return 0

    loop(begin, end, body, 3)


def stage_norm_back(width, flat, w_qkv, stack):
    def body(c, _):
        cols = tile_at(c, TILE)
        stack[:, cols] = dot_nt(flat[...], w_qkv[cols, :])
        return 0

    loop(0, width // TILE, body, 3)


def stage_end(images, slots, width, keep, token, gain, middle, live, stack, g_gain, g_shift, put_patches):
    for ref in (g_gain, g_shift):
        ref[...] = jnp.zeros_like(ref)

    def back(b, _):
        rows = tile_at(b, BLOCK)
        grad = stack[rows, :]
        hat, inverse = norm_parts(token[rows, :].astype(F32))
        g_gain[...] += jnp.sum(grad * hat, axis=0, keepdims=True)
        g_shift[...] += jnp.sum(grad, axis=0, keepdims=True)
        total = middle[rows, :] + norm_back(hat, inverse, gain[...], grad)
        stack[rows, :] = total * jnp.concatenate([live[rows, :]] * (width // BLOCK), axis=1)
        return 0

    loop(0, ROWS // BLOCK, back, 2)

    def scatter(i, _):
        chosen = (lax.broadcasted_iota(jnp.int32, (slots, SLOT), 0) == keep[i]).astype(F32).astype(BF16)
        values = stack[pl.ds(pl.multiple_of(i * SLOT, 8), SLOT), :]
        high = values.astype(BF16)
        rest = (values - high.astype(F32)).astype(BF16)
        put_patches(i, dot(chosen, high) + dot(chosen, rest))
        return 0

    for i in range(images):
        scatter(i, 0)


MESH = pl.DeviceIdType.MESH


class Place:
    def __init__(self):
        f, d = lax.axis_index("fsdp"), lax.axis_index("dp")
        self.z, self.x = f // 2, lax.rem(f, 2)
        self.y, self.c = d // 2, lax.rem(d, 2)
        z = self.z
        self.zs = [z, z + 1 - 2 * lax.rem(z, 2), lax.rem(z + 2, 4), 3 - z]
        self.ox, self.oy, self.oc = 1 - self.x, 1 - self.y, 1 - self.c
        self.beside = self.to(x=self.ox), self.to(y=self.oy), self.to(c=self.oc)
        self.along = [self.to(z=k) for k in self.zs]

    def to(self, z=None, x=None, y=None, c=None):
        z, x, y, c = (own if new is None else new for new, own in ((z, self.z), (x, self.x), (y, self.y), (c, self.c)))
        return (z * 2 + x, y * 2 + c)

    def sides(self):
        return self.beside


def enter(peers):
    barrier = pltpu.get_barrier_semaphore()
    for peer in peers:
        pl.semaphore_signal(barrier, inc=1, device_id=peer, device_id_type=MESH)
    pl.semaphore_wait(barrier, len(peers))


class Gather:
    def __init__(self, place, shard, full, first_cols, send, recv):
        self.place, self.shard, self.full, self.send, self.recv = place, shard, full, send, recv
        self.rows, cols = shard.shape
        self.half, self.wide, self.cut = self.rows // 2, cols // 2, first_cols
        self.started = []

    def spot(self, *args):
        return lambda: self.place_of(*args)

    def place_of(self, z, x, y, part=None, local=False):
        p = self.place
        base = 0 if local else (z * 2 + x) * self.rows
        rows = pl.ds(pl.multiple_of(base + p.c * self.half, 16), self.half)
        if y is None:
            return rows, slice(None)
        start, size = (y * self.wide, self.wide) if part is None else ((y * self.wide, self.cut) if part == 0 else (y * self.wide + self.cut, self.wide - self.cut))
        return rows, pl.ds(pl.multiple_of(start, 128), size)

    def copy(self, spot, sem, peer, local=None):
        src = self.full.at[spot] if local is None else self.shard.at[local]
        return pltpu.make_async_remote_copy(
            src_ref=src, dst_ref=self.full.at[spot], send_sem=self.send.at[sem], recv_sem=self.recv.at[sem], device_id=peer, device_id_type=MESH
        )

    def start(self, spot, sem, peer, local=None):
        def make():
            return self.copy(spot(), sem, peer, None if local is None else local())

        make().start()
        self.started.append(make)

    def arrived(self, spot, sem):
        self.copy(spot(), sem, self.place.sides()[0]).wait_recv()

    def own(self, sem):
        p = self.place
        rows = pl.ds(pl.multiple_of((p.z * 2 + p.x) * self.rows, 16), self.rows)
        return pltpu.make_async_copy(self.shard, self.full.at[rows, :], sem)

    def begin(self):
        p = self.place
        side_x, side_y, _ = p.sides()
        spot, local = self.spot(p.z, p.x, p.y), self.spot(p.z, p.x, p.y, None, True)
        for k in (1, 2, 3):
            self.start(spot, k, p.along[k], local)
        self.start(spot, 4, side_x, local)
        self.start(self.spot(p.z, p.x, p.oy, 1), 16, side_x, self.spot(p.z, p.x, p.oy, 1, True))

    def spread(self, k):
        p = self.place
        side_x, side_y, _ = p.sides()
        spot = self.spot(p.zs[k], p.x, p.y)
        self.arrived(spot, k)
        self.start(spot, 4 + k, side_x)
        self.start(spot, 8 + k, side_y)

    def cross(self, k):
        p = self.place
        side_x, side_y, _ = p.sides()
        self.arrived(self.spot(p.zs[k], p.ox, p.y), 4 + k)
        self.start(self.spot(p.zs[k], p.ox, p.y, 0), 12 + k, side_y)
        if k:
            self.arrived(self.spot(p.zs[k], p.x, p.oy), 8 + k)
            self.start(self.spot(p.zs[k], p.x, p.oy, 1), 16 + k, side_x)

    def share(self, k):
        p = self.place
        core = p.sides()[2]
        if k:
            self.start(self.spot(p.zs[k], p.x, None), 20 + k, core)
        self.arrived(self.spot(p.zs[k], p.ox, p.oy, 0), 12 + k)
        self.arrived(self.spot(p.zs[k], p.ox, p.oy, 1), 16 + k)
        self.start(self.spot(p.zs[k], p.ox, None), 24 + k, core)

    def finish(self):
        p = self.place

        def other(z, x):
            return lambda: (pl.ds(pl.multiple_of((z * 2 + x) * self.rows + (p.oc) * self.half, 16), self.half), slice(None))

        for k in range(4):
            if k:
                self.arrived(other(p.zs[k], p.x), 20 + k)
            self.arrived(other(p.zs[k], p.ox), 24 + k)

    def drain(self):
        for make in self.started:
            make().wait_send()


class Reduce:
    def __init__(self, place, source, held, core, diag_x, diag_y, side_x, side_y, line, final, send, recv):
        self.place, self.source, self.held, self.core = place, source, held, core
        self.diag_x, self.diag_y, self.side_x, self.side_y, self.line, self.final = diag_x, diag_y, side_x, side_y, line, final
        self.send, self.recv, self.started = send, recv, []
        self.by_rows = diag_y.shape[2] == final.shape[3]
        self.cut = diag_y.shape[1] if self.by_rows else diag_y.shape[2]

    def part(self, second):
        bounds = pl.ds(self.cut, (self.final.shape[2] if self.by_rows else self.final.shape[3]) - self.cut) if second else pl.ds(0, self.cut)
        return (bounds, slice(None)) if self.by_rows else (slice(None), bounds)

    def hold(self, z, x, y, *rest):
        if self.held is None:
            return (z, x, self.place.c, y) + rest
        return (z, x, y) + rest

    @property
    def home(self):
        return self.source if self.held is None else self.held

    def copy(self, src, dst, sem, peer):
        return pltpu.make_async_remote_copy(src_ref=src, dst_ref=dst, send_sem=self.send.at[sem], recv_sem=self.recv.at[sem], device_id=peer, device_id_type=MESH)

    def start(self, src, dst, sem, peer):
        def make():
            return self.copy(src(), dst() if callable(dst) else dst, sem, peer)

        make().start()
        self.started.append(make)

    def arrived(self, dst, sem):
        self.copy(dst, dst, sem, self.place.sides()[0]).wait_recv()

    def begin(self, own=None):
        p = self.place
        self.start(lambda: self.source.at[:, :, p.oc], self.core, 0, p.sides()[2])
        self.own = own
        if own is not None:
            own.start()

    def add_core(self, x, y):
        def body(z, _):
            spot = self.hold(z, x, y)
            self.home[spot] = self.home[spot] + self.core[z, x, y]
            return 0

        lax.fori_loop(0, 4, body, 0)

    def add(self, x, y, part, buffer):
        def body(z, _):
            spot = self.hold(z, x, y, *part)
            self.home[spot] = self.home[spot] + buffer[z]
            return 0

        lax.fori_loop(0, 4, body, 0)

    def step_core(self):
        p = self.place
        side_x, side_y, _ = p.sides()
        if self.own is not None:
            self.own.wait()
        self.arrived(self.core, 0)
        for x, y in ((p.ox, p.oy), (p.ox, p.y), (p.x, p.oy), (p.x, p.y)):
            self.add_core(x, y)

    def step_open(self):
        p = self.place
        side_x, side_y, _ = p.sides()
        every = slice(None)
        self.start(lambda: self.home.at[self.hold(every, p.ox, p.oy, *self.part(True))], self.diag_x, 1, side_x)
        self.start(lambda: self.home.at[self.hold(every, p.ox, p.oy, *self.part(False))], self.diag_y, 2, side_y)

    def step_diag(self):
        p = self.place
        side_x, side_y, _ = p.sides()
        every = slice(None)
        self.arrived(self.diag_y, 2)
        self.add(p.ox, p.y, self.part(False), self.diag_y)
        self.start(lambda: self.home.at[self.hold(every, p.ox, p.y)], self.side_x, 3, side_x)
        self.arrived(self.diag_x, 1)
        self.add(p.x, p.oy, self.part(True), self.diag_x)
        self.start(lambda: self.home.at[self.hold(every, p.x, p.oy)], self.side_y, 4, side_y)

    def step_side(self):
        p = self.place
        whole = (slice(None), slice(None))
        self.arrived(self.side_x, 3)
        self.add(p.x, p.y, whole, self.side_x)
        self.arrived(self.side_y, 4)
        self.add(p.x, p.y, whole, self.side_y)
        for k in (1, 2, 3):
            self.start(lambda k=k: self.home.at[self.hold(p.zs[k], p.x, p.y)], lambda k=k: self.line.at[k - 1], 4 + k, p.along[k])

    def step_line(self):
        p = self.place
        total = self.home[self.hold(p.z, p.x, p.y)].astype(F32)
        for k in (1, 2, 3):
            self.arrived(self.line.at[k - 1], 4 + k)
            total = total + self.line[k - 1].astype(F32)
        self.final[p.c, p.y] = total.astype(BF16)
        self.start(lambda: self.final.at[p.c, p.y], lambda: self.final.at[p.c, p.y], 8, p.sides()[1])

    def step_share(self):
        p = self.place
        self.arrived(self.final.at[p.c, p.oy], 8)
        self.start(lambda: self.final.at[p.c], lambda: self.final.at[p.c], 9, p.sides()[2])

    def finish(self):
        self.arrived(self.final.at[self.place.oc], 9)

    def drain(self):
        for make in self.started:
            make().wait_send()


class SmallReduce:
    def __init__(self, place, home, core, side_y, side_x, line, send, recv):
        self.place, self.home, self.core, self.side_y, self.side_x, self.line = place, home, core, side_y, side_x, line
        self.send, self.recv, self.started = send, recv, []

    copy, start, arrived, drain = Reduce.copy, Reduce.start, Reduce.arrived, Reduce.drain

    def begin(self):
        self.start(lambda: self.home, self.core, 0, self.place.sides()[2])

    def step_core(self, sent):
        p = self.place
        self.arrived(self.core, 0)
        sent[...] = self.home[...] + self.core[...]
        self.start(lambda: sent, self.side_y, 1, p.sides()[1])

    def step_y(self, sent, total):
        p = self.place
        self.arrived(self.side_y, 1)
        total[...] = sent[...] + self.side_y[...]
        self.start(lambda: total.at[:, p.ox], self.side_x, 2, p.sides()[0])

    def step_x(self, total):
        p = self.place
        self.arrived(self.side_x, 2)
        for z in range(4):
            self.side_x[z] = self.side_x[z] + total[z, p.x]
        for k in (1, 2, 3):
            self.start(lambda k=k: self.side_x.at[p.zs[k]], lambda k=k: self.line.at[k - 1], 2 + k, p.along[k])

    def step_line(self, out):
        total = self.side_x[self.place.z]
        for k in (1, 2, 3):
            self.arrived(self.line.at[k - 1], 2 + k)
            total = total + self.line[k - 1]
        out[...] = total


VMEM = pl.BlockSpec(memory_space=pltpu.VMEM)
ANY = pl.BlockSpec(memory_space=pl.ANY)
LIMIT = 61 * 1024 * 1024
THIRD = 1024


def call(body, outs, scratch, args, name):
    return pl.pallas_call(
        body,
        out_shape=[jax.ShapeDtypeStruct(*o) for o in outs],
        in_specs=[VMEM] * len(args),
        out_specs=[VMEM] * len(outs),
        scratch_shapes=[pltpu.VMEM(*s) for s in scratch],
        compiler_params=pltpu.CompilerParams(vmem_limit_bytes=LIMIT),
        name=name,
    )(*args)


class Later:
    def __init__(self, sems):
        self.sems, self.flights = sems, {}

    def start(self, name, src, dst):
        copy = pltpu.make_async_copy(src, dst, self.sems.at[len(self.flights)])
        copy.start()
        self.flights[name] = copy

    def wait(self, *names):
        for name in names:
            self.flights[name].wait()


def first_plain(
    images, slots, width, patches, keep, cot, vectors, w_qkv, w_out,
    token, n1t, dm, dmt, live, qkv, probs, att_t, middle, n2, n2t, stack, normed, mask, att, bias,
):
    bias[...] = jnp.concatenate([vectors[2:3, :], jnp.zeros((1, width), F32), vectors[3:4, :]], axis=1)
    stage_gather(images, slots, patches, keep, stack, live, mask)
    stage_norm(stack, vectors[0:1, :], vectors[1:2, :], token, normed, n1t)
    stage_grads(images, slots, width, cot, stack, live, dm, dmt)
    stage_qkv(images, width, normed, w_qkv, bias, qkv)
    for i in range(images):
        stage_attention(width, qkv, mask, probs.at[pl.ds(i * H, H)], stack, i)
    stage_out(width, stack, w_out, vectors.at[4:5, :], token, vectors.at[5:6, :], vectors.at[6:7, :], att, att_t, middle, n2, n2t)


def first_kernel(
    images, slots, width,
    patches, keep, cot, vec, s_qkv, s_out, s_up, s_down,
    vectors, g_b_up, h_token, h_n1t, h_dm, h_live, h_qkv, h_probs, h_att_t, h_middle, h_wqkv, h_wout, h_up, h_down, h_act, h_dh, h_gup, h_gdown, h_up01, h_down01,
    stack, normed, mask, token, n1t, dm, dmt, live, qkv, probs, att_t, middle, f_qkv, f_out, f_up, f_down, s_up3, act, dh, g_up, g_down, up_core, down_core,
    vecs, bias, b_up, q_send, q_recv, m_send, m_recv, v_send, v_recv, own, saves, probs_sem, r_send, r_recv,
):
    place = Place()
    _, side_y, side_c = place.sides()
    flat = [place.to(z=place.zs[k], x=x) for k in range(4) for x in (place.x, place.ox)][1:]
    enter(flat + [side_y, side_c])
    g_qkv = Gather(place, s_qkv, f_qkv, 640, q_send.at[0], q_recv.at[0])
    g_out = Gather(place, s_out, f_out, 256, q_send.at[1], q_recv.at[1])
    g_ups = [Gather(place, s_up3.at[t], f_up.at[t], (256, 384, 256)[t], m_send.at[t], m_recv.at[t]) for t in range(3)]
    g_downs = [Gather(place, s_down.at[t * 128 : t * 128 + 128], f_down.at[t], 256, m_send.at[3 + t], m_recv.at[3 + t]) for t in range(3)]
    mine = place.z * 2 + place.x
    tiny = []
    for j, peer in enumerate(flat):
        copy = pltpu.make_async_remote_copy(src_ref=vec, dst_ref=vecs.at[mine], send_sem=v_send.at[j], recv_sem=v_recv.at[j], device_id=peer, device_id_type=MESH)
        copy.start()
        tiny.append(copy)
    g_qkv.begin()
    for t in range(3):
        for f in range(8):
            s_up3[t, :, f * 128 : f * 128 + 128] = s_up[:, f * 384 + t * 128 : f * 384 + t * 128 + 128]
    every = [g_qkv, g_out] + [g for t in range(3) for g in (g_ups[t], g_downs[t])]
    locals_ = [g.own(own.at[j]) for j, g in enumerate(every)]
    for copy in locals_:
        copy.start()
    vecs[mine] = vec[...]
    later = Later(saves)

    def go(name, *group):
        for g in group:
            for k in range(4):
                if k or name != "spread":
                    getattr(g, name)(k)

    def begin(*group):
        for g in group:
            g.begin()

    pairs = [(g_ups[t], g_downs[t]) for t in range(3)]
    stage_gather(images, slots, patches, keep, stack, live, mask)
    later.start("live", live, h_live)
    for copy in tiny:
        copy.wait_recv()
    vectors[...] = jnp.concatenate([vecs[f][:, :96] for f in range(8)], axis=1).astype(F32)
    g_qkv.spread(1)
    g_qkv.cross(0)
    for f in range(8):
        row = jnp.concatenate([vecs[f][8 + j : 9 + j, :96] for j in range(4)], axis=1).astype(F32)
        for t in range(3):
            b_up[t, :, f * 128 : f * 128 + 128] = row[:, t * 128 : t * 128 + 128]
    bias[...] = jnp.concatenate([vectors[2:3, :], jnp.zeros((1, width), F32), vectors[3:4, :]], axis=1)
    g_qkv.spread(2)
    g_qkv.spread(3)
    begin(g_out, *pairs[0])
    stage_norm(stack, vectors[0:1, :], vectors[1:2, :], token, normed, n1t)
    later.start("token", token, h_token)
    later.start("n1t", n1t, h_n1t)
    for k in (1, 2, 3):
        g_qkv.cross(k)
    go("spread", g_out)
    stage_grads(images, slots, width, cot, stack, live, dm, dmt)
    later.start("dm", dm, h_dm)
    go("share", g_qkv)
    begin(*pairs[1])
    go("spread", *pairs[0])
    locals_[0].wait()
    g_qkv.finish()
    later.start("w_qkv", f_qkv, h_wqkv)
    stage_qkv(images, width, normed, f_qkv, bias, qkv)
    later.start("qkv", qkv, h_qkv)
    plan = [
        lambda: (go("cross", g_out), begin(*pairs[2])),
        lambda: go("spread", *pairs[1]),
        lambda: (go("share", g_out), go("cross", *pairs[0])),
        lambda: go("spread", *pairs[2]),
        lambda: go("share", *pairs[0]),
    ]

    def save_probs(slot, i):
        return pltpu.make_async_copy(probs.at[slot], h_probs.at[pl.ds(i * H, H)], probs_sem.at[slot])

    def attend(i, _):
        slot = lax.rem(i, 2)
        for j, step in enumerate(plan):
            pl.when(i == j)(lambda step=step: (step(), None)[1])
        pl.when(i >= 2)(lambda: save_probs(slot, i - 2).wait())
        stage_attention(width, qkv, mask, probs.at[slot], stack, i)
        save_probs(slot, i).start()
        return 0

    lax.fori_loop(0, images, attend, 0)
    for i in range(images - 2, images):
        save_probs(i % 2, i).wait()
    locals_[1].wait()
    g_out.finish()
    later.start("w_out", f_out, h_wout)
    later.wait("n1t")
    n2t = n1t
    stage_out(width, stack, f_out, vectors.at[4:5, :], token, vectors.at[5:6, :], vectors.at[6:7, :], normed, att_t, middle, normed, n2t)
    later.start("att_t", att_t, h_att_t)
    later.start("middle", middle, h_middle)
    go("cross", *pairs[1])
    core = place.sides()[2]
    swaps = {
        (name, t): pltpu.make_async_remote_copy(
            src_ref=g.at[t, :, :, place.oc], dst_ref=buffer.at[t], send_sem=r_send.at[2 * t + j], recv_sem=r_recv.at[2 * t + j], device_id=core, device_id_type=MESH
        )
        for t in range(2)
        for j, (name, g, buffer) in enumerate((("up", g_up, up_core), ("down", g_down, down_core)))
    }

    def merge(t):
        for name, g, buffer, h in (("up", g_up, up_core, h_up01), ("down", g_down, down_core, h_down01)):
            swaps[name, t].wait_recv()

            def body(z, _, g=g, buffer=buffer):
                g[t, z, :, place.c] = g[t, z, :, place.c] + buffer[t, z]
                return 0

            lax.fori_loop(0, 4, body, 0)
            later.start(f"{name}_sum{t}", g.at[t, :, :, place.c], h.at[t])

    for t in range(3):
        slot = t % 2
        locals_[2 + 2 * t].wait()
        locals_[3 + 2 * t].wait()
        g_ups[t].finish()
        g_downs[t].finish()
        later.start(f"up{t}", f_up.at[t], h_up.at[t])
        later.start(f"down{t}", f_down.at[t], h_down.at[t])

        def put_up(c, value):
            y, at = c // 2, tile_at(c % 2, TILE)
            g_up[slot, :, :, :, y, :, at] = value.reshape(4, 2, 2, 48, TILE)

        def put_down(c, value):
            for x in range(2):
                g_down[slot, c, x] = value[:, x * 128 : (x + 1) * 128].reshape(2, 2, 192, 128)

        for part in range(2):
            if t:
                later.wait(f"act{t - 1}{part}", f"dh{t - 1}{part}")
            if t == 2 and part == 0:
                for name in ("up", "down"):
                    swaps[name, 0].wait_send()
                    later.wait(f"{name}_sum0")
            stage_mlp(width, part * 2, part * 2 + 2, normed, n2t, dm, dmt, f_up.at[t], b_up.at[t], f_down.at[t], act, dh, put_up, put_down, g_b_up.at[t])
            cols = slice(part * 512, part * 512 + 512)
            later.start(f"act{t}{part}", act.at[:, cols], h_act.at[t, :, cols])
            later.start(f"dh{t}{part}", dh.at[:, cols], h_dh.at[t, :, cols])
            if part == 0:
                if t == 0:
                    go("share", *pairs[1])
                    go("cross", *pairs[2])
                else:
                    merge(t - 1)
                    if t == 1:
                        go("share", *pairs[2])
        if t < 2:
            swaps["up", t].start()
            swaps["down", t].start()
        else:
            later.start("g_up2", g_up.at[slot], h_gup)
            later.start("g_down2", g_down.at[slot], h_gdown)
    waited = {"n1t", "up_sum0", "down_sum0"} | {f"{n}{t}{p}" for n in ("act", "dh") for t in range(2) for p in range(2)}
    for name in ("up", "down"):
        swaps[name, 1].wait_send()
    later.wait(*(n for n in later.flights if n not in waited))
    for copy in tiny:
        copy.wait_send()
    for g in every:
        g.drain()


def second_plain(
    images, slots, width, hidden_width,
    n2, n2t, dm, dmt, w_up, b_up, w_down, b_d, middle_in, live, gain2,
    out, middle, d_low, g_up, g_down, g_b_up, g_g2, g_s2, g_bd, g_bo, act, dh, stack,
):
    middle[...] = middle_in[...]

    def put(ref, c, value):
        ref[:, tile_at(c, TILE)] = value

    stage_mlp(width, 0, hidden_width // TILE, n2, n2t, dm, dmt, w_up, b_up, w_down, act, dh, functools.partial(put, g_up), functools.partial(put, g_down), g_b_up)
    add_products(width, stack, True, lambda cols: dot(act[...], w_down[:, cols]))
    stage_final(images, slots, width, middle, live, b_d, stack, out)
    add_products(width, stack, True, lambda cols: dot_nt(dh[...], w_up[cols, :]))
    stage_middle_back(middle, gain2, dm, stack, d_low, g_g2, g_s2, g_bd, g_bo)


def third_plain(
    images, slots, width, d_low, att_t, w_out, qkv_in, probs, n1t, w_qkv, token, gain, mid, live, keep,
    g_out, g_qkv, g_b, g_g1, g_s1, gp, stack, tile, flat, qkv,
):
    def put(ref, c, value):
        ref[:, tile_at(c, TILE)] = value

    def put_patches(i, value):
        gp[i] = value

    qkv[...] = qkv_in[...]
    tile[...] = jnp.zeros_like(tile)
    stage_out_back(width, att_t, d_low, w_out, functools.partial(put, g_out), stack)
    for i in range(images):
        stage_attention_back(width, qkv, probs.at[pl.ds(i * H, H)], stack, i)
    stage_qkv_back(images, width, qkv, n1t, tile, flat, functools.partial(put, g_qkv), g_b, 0, 3 * width // TILE)
    stage_norm_back(width, flat, w_qkv, stack)
    stage_end(images, slots, width, keep, token, gain, mid, live, stack, g_g1, g_s1, put_patches)


def second_kernel(
    images, slots, width,
    keep, vectors, s_bup, h_token, h_n1t, h_dm, h_live, h_qkv, h_probs, h_att_t, h_middle, h_wqkv, h_wout, h_up, h_down, h_act, h_dh, h_gup, h_gdown, h_up01, h_down01,
    gp, out_tokens, o_qkv, o_out, o_up, o_down, e_small,
    e_up, e_down, e_out, e_q, e_k, e_v,
    stack, tile, flat, qkv, probs, t_a, t_b, r_a, r_b, mid, live, w_qkv, w_out, stage, g_b, g_g1, g_s1, g_g2, g_s2, g_bd, g_bo, g_attn,
    up_held, up_core, up_dx, up_dy, up_sx, up_sy, up_ln, dn_held, dn_core, dn_dx, dn_dy, dn_sx, dn_sy, dn_ln,
    core4, dx4, dy4, sx4, sy4, ln4, v_home, v_core, v_sy, v_sx, v_ln, v_sent, v_total,
    send, recv, v_send, v_recv, own, loads, probs_sem, out_sem,
):
    place = Place()
    enter(place.along[1:] + list(place.sides()))
    r_up = [
        Reduce(place, h_gup, up_held.at[t], up_core, up_dx.at[t], up_dy.at[t], up_sx.at[t], up_sy.at[t], up_ln.at[t], e_up.at[t], send.at[t], recv.at[t])
        for t in range(3)
    ]
    r_down = [
        Reduce(place, h_gdown, dn_held.at[t], dn_core, dn_dx.at[t], dn_dy.at[t], dn_sx.at[t], dn_sy.at[t], dn_ln.at[t], e_down.at[t], send.at[3 + t], recv.at[3 + t])
        for t in range(3)
    ]
    mlp = [(r_up[t], r_down[t]) for t in range(3)]
    r_q, r_k, r_v, r_out = (
        Reduce(place, g_attn.at[m], None, core4.at[m], dx4.at[m], dy4.at[m], sx4.at[m], sy4.at[m], ln4.at[m], e, send.at[6 + m], recv.at[6 + m])
        for m, e in enumerate((e_q, e_k, e_v, e_out))
    )
    small = SmallReduce(place, v_home, v_core, v_sy, v_sx, v_ln, v_send, v_recv)
    later = Later(loads)
    slots_ = [flat.at[:, 0:THIRD], flat.at[:, THIRD : 2 * THIRD]]
    held = [[pltpu.make_async_copy(h.at[t], into.at[t], own.at[2 * t + j]) for j, (h, into) in enumerate(((h_up01, up_held), (h_down01, dn_held)))] for t in range(2)]
    for copy in held[0]:
        copy.start()
    later.start("dh0", h_dh.at[0], slots_[0])
    later.start("up0", h_up.at[0], t_a)
    for copy in held[1]:
        copy.start()
    for j, (r, h, into) in enumerate(((r_up[2], h_gup, up_held), (r_down[2], h_gdown, dn_held))):
        r.begin(pltpu.make_async_copy(h.at[:, :, place.c], into.at[2], own.at[4 + j]))
    later.start("dh1", h_dh.at[1], slots_[1])
    later.start("up1", h_up.at[1], t_b)
    for copy, r in zip(held[0], mlp[0]):
        copy.wait()
        r.step_open()
    for copy, r in zip(held[1], mlp[1]):
        copy.wait()
        r.step_open()
    for name, src, dst in (("mid", h_middle, mid), ("dm", h_dm, r_a), ("live", h_live, live), ("w_out", h_wout, w_out), ("qkv", h_qkv, qkv), ("w_qkv", h_wqkv, w_qkv)):
        later.start(name, src, dst)

    def load_probs(i):
        slot = i % 2
        return pltpu.make_async_copy(h_probs.at[pl.ds(i * H, H)], probs.at[slot], probs_sem.at[slot])

    load_probs(0).start()
    later.wait("dh0", "up0")
    add_products(width, stack, True, lambda cols: dot_nt(slots_[0][...], t_a[cols, :]))
    later.start("dh2", h_dh.at[2], slots_[0])
    later.start("up2", h_up.at[2], t_a)
    later.wait("dh1", "up1")
    add_products(width, stack, False, lambda cols: dot_nt(slots_[1][...], t_b[cols, :]))
    later.start("att_t", h_att_t, t_b)
    for r in mlp[2]:
        r.step_core()
        r.step_open()
    later.wait("dh2", "up2")
    add_products(width, stack, False, lambda cols: dot_nt(slots_[0][...], t_a[cols, :]))
    later.start("n1t", h_n1t, t_a)
    for r in mlp[0]:
        r.step_diag()
    later.wait("mid", "dm")
    gain2 = vectors.at[5:6, :]
    stage_middle_back(mid, gain2, r_a, stack, r_b, g_g2, g_s2, g_bd, g_bo)
    later.start("token", h_token, r_a)

    def put(m, c, value):
        for j in range(2):
            col = 2 * c + j
            y, off = (col % 6) // 3, col % 3
            at = tile_at(off, 128)
            g_attn[col // 6 if m is None else m, :, :, :, y, :, at] = value[:, j * 128 : (j + 1) * 128].reshape(4, 2, 2, 48, 128)

    later.wait("att_t", "w_out", "qkv")
    stage_out_back(width, t_b, r_b, w_out, functools.partial(put, 3), stack)
    r_out.begin()
    for r in mlp[1]:
        r.step_diag()
    plan = {
        0: lambda: (r_out.step_core(), r_out.step_open()),
        1: lambda: [r.step_side() for r in mlp[0]],
        2: lambda: [r.step_diag() for r in mlp[2]],
        3: lambda: (r_out.step_diag(),),
        4: lambda: [r.step_side() for r in mlp[1]] + [r.step_line() for r in mlp[0]],
    }

    def back(i, _):
        load_probs(i).wait()
        pl.when(i + 1 < images)(lambda: load_probs(i + 1).start())
        stage_attention_back(width, qkv, probs.at[lax.rem(i, 2)], stack, i)
        for j, step in plan.items():
            pl.when(i == j)(lambda step=step: (step(), None)[1])
        return 0

    lax.fori_loop(0, images, back, 0)
    later.wait("n1t")
    tile[...] = jnp.zeros_like(tile)
    project = functools.partial(stage_qkv_back, images, width, qkv, t_a, tile, flat, functools.partial(put, None), g_b)
    third = width // TILE
    project(0, third)
    r_q.begin()
    project(third, 2 * third)
    r_k.begin()
    r_q.step_core()
    r_q.step_open()
    project(2 * third, 3 * third)
    r_v.begin()
    r_k.step_core()
    r_k.step_open()
    for r in mlp[0]:
        r.step_share()
    later.wait("w_qkv")
    stage_norm_back(width, flat, w_qkv, stack)
    r_v.step_core()
    r_v.step_open()
    for r in mlp[2]:
        r.step_side()
    r_out.step_side()
    later.start("act0", h_act.at[0], slots_[0])
    later.start("act1", h_act.at[1], slots_[1])
    later.start("down0", h_down.at[0], r_b)
    r_q.step_diag()
    for r in mlp[1]:
        r.step_line()
    later.wait("token", "live")
    flights = []

    def put_patches(i, value):
        if i >= 2:
            flights[i - 2].wait()
        stage[i % 2] = value
        copy = pltpu.make_async_copy(stage.at[i % 2], gp.at[i], out_sem.at[i % 2])
        copy.start()
        flights.append(copy)

    stage_end(images, slots, width, keep, r_a, vectors.at[0:1, :], mid, live, stack, g_g1, g_s1, put_patches)
    later.start("middle", h_middle, mid)
    later.start("down1", h_down.at[1], r_a)
    v_home[...] = jnp.zeros_like(v_home)
    for j, (ref, base) in enumerate(((g_g1, 0), (g_s1, 0), (g_b, 0), (g_b, 2 * width), (g_bo, 0), (g_g2, 0), (g_s2, 0), (g_bd, 0))):
        row = ref[:, base : base + width]
        for f in range(8):
            v_home[f // 2, f % 2, j : j + 1, :96] = row[:, 96 * f : 96 * f + 96]
    for f in range(8):
        row = jnp.concatenate([s_bup[t, :, f * 128 : f * 128 + 128] for t in range(3)], axis=1)
        for j in range(4):
            v_home[f // 2, f % 2, 8 + j : 9 + j, :96] = row[:, 96 * j : 96 * j + 96]
    small.begin()
    r_k.step_diag()
    for r in mlp[2] + (r_out,):
        r.step_line()
    for r in mlp[1]:
        r.step_share()
    small.step_core(v_sent)
    later.wait("act0", "down0")
    add_products(width, stack, True, lambda cols: dot(slots_[0][...], r_b[:, cols]))
    later.start("act2", h_act.at[2], slots_[0])
    later.start("down2", h_down.at[2], r_b)
    r_v.step_diag()
    small.step_y(v_sent, v_total)
    r_q.step_side()
    later.wait("act1", "down1")
    add_products(width, stack, False, lambda cols: dot(slots_[1][...], r_a[:, cols]))
    for r in mlp[2] + (r_out,):
        r.step_share()
    small.step_x(v_total)
    r_k.step_side()
    r_q.step_line()
    later.wait("act2", "down2", "middle")
    add_products(width, stack, False, lambda cols: dot(slots_[0][...], r_b[:, cols]))
    r_v.step_side()
    r_k.step_line()
    r_q.step_share()
    stage_final(images, slots, width, mid, live, vectors.at[7:8, :], stack, out_tokens)
    small.step_line(e_small)
    for r in r_up + r_down + [r_out]:
        r.finish()
    for t in range(3):
        for c in range(2):
            for y in range(2):
                for f in range(4):
                    col = (4 * y + f) * 384 + t * 128
                    o_up[48 * c : 48 * c + 48, col : col + 128] = e_up[t, c, y, :, f * 128 : f * 128 + 128]
        o_down[t * 128 : t * 128 + 128, :] = e_down[t].reshape(width, 128).T
    r_v.step_line()
    r_k.step_share()
    r_v.step_share()
    half = width // 2

    def place_blocks(ref, base, e):
        for c in range(2):
            for y in range(2):
                ref[48 * c : 48 * c + 48, base + y * half : base + y * half + half] = e[c, y]

    place_blocks(o_out, 0, e_out)
    for m, (r, e) in enumerate(((r_q, e_q), (r_k, e_k), (r_v, e_v))):
        r.finish()
        place_blocks(o_qkv, m * width, e)
    for copy in flights[-2:]:
        copy.wait()
    for r in r_up + r_down + [r_out, r_q, r_k, r_v, small]:
        r.drain()


def shards(
    linked,
    patches, keep, ln1_gain, ln1_bias, w_qkv, b_query, b_value, w_out, b_out,
    ln2_gain, ln2_bias, w_up, b_up, w_down, b_down, cotangent,
):
    images, slots = keep.shape
    width = patches.shape[2]
    hidden_width = w_up.shape[1]
    keep_pad = jnp.pad(keep, ((0, 0), (0, SLOT - slots)), constant_values=-1).reshape(images, 1, SLOT)
    part = ln1_gain.shape[0]
    singles = [v.reshape(1, part) for v in (ln1_gain, ln1_bias, b_query, b_value, b_out, ln2_gain, ln2_bias, b_down)]
    rows_low, rows_wide = ((ROWS, width), BF16), ((ROWS, width), F32)
    cols_low = ((width, ROWS), BF16)
    live_like, mask_like = ((ROWS, BLOCK), F32), ((images, SLOT, SLOT), F32)
    heads_like = ((images, SLOT, 3 * width), BF16)
    probs_like = ((images * H, SLOT, SLOT), BF16)
    row_like = ((1, width), F32)

    if linked:
        half = width // 2
        vec = jnp.concatenate(singles + [b_up.reshape(4, part)], axis=0)
        vec = jnp.pad(vec, ((0, 4), (0, BLOCK - part)))
        full = lambda v: ((v.shape[0] * 8, v.shape[1]), BF16)
        up3, down3, hid3 = ((3, width, THIRD), BF16), ((3, THIRD, width), BF16), ((3, ROWS, THIRD), BF16)
        gup_like, gdown_like = (4, 2, 2, 2, 48, THIRD // 2), (4, 2, 2, 2, width // 4, 128)
        outs = [
            ((16, width), F32), ((3, 1, THIRD), F32), rows_low, cols_low, rows_low, live_like, heads_like, probs_like, cols_low, rows_wide,
            full(w_qkv), full(w_out), up3, down3, hid3, hid3, (gup_like, BF16), (gdown_like, BF16), ((2, 4, 2) + gup_like[3:], BF16), ((2, 4, 2) + gdown_like[3:], BF16),
        ]
        scratch = [
            rows_wide, rows_low, mask_like, rows_low, cols_low, rows_low, cols_low, live_like, heads_like, ((2, H, SLOT, SLOT), BF16), cols_low,
            rows_wide, full(w_qkv), full(w_out), up3, down3, ((3, part, THIRD), BF16), hid3[0][1:], hid3[0][1:], (2,) + gup_like, (2,) + gdown_like,
            (2, 4, 2) + gup_like[3:], (2, 4, 2) + gdown_like[3:],
            ((8, 16, BLOCK), BF16), ((1, 3 * width), F32), ((3, 1, THIRD), F32),
        ]
        scratch = [s if isinstance(s[0], tuple) else (s, BF16) for s in scratch]
        vectors, g_b_up, token, n1t, dm, live, qkv, probs, att_t, middle, qkv_full, out_full, up_full, down_full, act, dh, g_up, g_down, up01, down01 = pl.pallas_call(
            functools.partial(first_kernel, images, slots, width),
            out_shape=[jax.ShapeDtypeStruct(*o) for o in outs],
            in_specs=[VMEM] * 8,
            out_specs=[VMEM] * 2 + [ANY] * 18,
            scratch_shapes=[pltpu.VMEM(*s) for s in scratch]
            + [pltpu.SemaphoreType.DMA((2, 28))] * 2
            + [pltpu.SemaphoreType.DMA((6, 28))] * 2
            + [pltpu.SemaphoreType.DMA((7,))] * 2
            + [pltpu.SemaphoreType.DMA((8,)), pltpu.SemaphoreType.DMA((33,)), pltpu.SemaphoreType.DMA((2,))]
            + [pltpu.SemaphoreType.DMA((4,))] * 2,
            compiler_params=pltpu.CompilerParams(vmem_limit_bytes=LIMIT, collective_id=0, has_side_effects=True),
            name="first",
        )(patches, keep_pad, cotangent, vec, w_qkv, w_out, w_up, w_down)
        final = lambda r, w, lead=(): (lead + (2, 2, r, w), BF16)
        attn = final(48, half)
        outs = [((images, slots, width), F32), ((images, slots, width), BF16), ((part, 3 * width), BF16), ((part, width), BF16), ((part, hidden_width), BF16), ((half, width), BF16), ((16, BLOCK), F32)]

        def buffers(r, w, by_rows, cut, lead):
            other = (4, r - cut, w) if by_rows else (4, r, w - cut)
            first = (4, cut, w) if by_rows else (4, r, cut)
            shapes = [other, first, (4, r, w), (4, r, w), (3, r, w)]
            return [((4, 2, 2, r, w) if len(lead) and lead[0] == 3 else lead + (4, 2, 2, r, w), BF16)] + [(lead + s, BF16) for s in shapes]

        scratch = [final(48, THIRD // 2, (3,)), final(width // 4, 128, (3,)), attn, attn, attn, attn]
        scratch += [rows_wide, ((ROWS, TILE), F32), ((ROWS, 3 * width), BF16), heads_like, ((2, H, SLOT, SLOT), BF16), cols_low, cols_low, rows_low, rows_low]
        scratch += [rows_wide, live_like, ((width, 3 * width), BF16), ((width, width), BF16), ((2, slots, width), F32), ((1, 3 * width), F32)] + [row_like] * 6
        scratch += [((4, 4, 2, 2, 2, 48, half), BF16)]
        scratch += [((3, 4, 2, 2, 48, THIRD // 2), BF16)] + buffers(48, THIRD // 2, False, 128, (3,))
        scratch += [((3, 4, 2, 2, width // 4, 128), BF16)] + buffers(width // 4, 128, True, 64, (3,))
        scratch += buffers(48, half, False, 128, (4,))
        small_like, line_like = ((4, 2, 16, BLOCK), F32), ((3, 16, BLOCK), F32)
        scratch += [small_like, small_like, small_like, ((4, 16, BLOCK), F32), line_like, small_like, small_like]
        grad_patches, out_tokens, o_qkv, o_out, o_up, o_down, small = pl.pallas_call(
            functools.partial(second_kernel, images, slots, width),
            out_shape=[jax.ShapeDtypeStruct(*o) for o in outs],
            in_specs=[VMEM] * 3 + [ANY] * 18,
            out_specs=[ANY] + [VMEM] * 6,
            scratch_shapes=[pltpu.VMEM(*s) for s in scratch]
            + [pltpu.SemaphoreType.DMA((10, 10))] * 2
            + [pltpu.SemaphoreType.DMA((6,))] * 2
            + [pltpu.SemaphoreType.DMA((6,)), pltpu.SemaphoreType.DMA((22,)), pltpu.SemaphoreType.DMA((2,)), pltpu.SemaphoreType.DMA((2,))],
            compiler_params=pltpu.CompilerParams(vmem_limit_bytes=LIMIT, collective_id=1, has_side_effects=True),
            name="second",
        )(keep_pad, vectors, g_b_up, token, n1t, dm, live, qkv, probs, att_t, middle, qkv_full, out_full, up_full, down_full, act, dh, g_up, g_down, up01, down01)
        rows = small[:8, :part]
        sum_qkv, sum_out, sum_up, sum_down = (o.astype(F32) for o in (o_qkv, o_out, o_up, o_down))
        b_up_sum = small[8:12, :part].reshape(-1)
    else:
        gather = lambda v: lax.all_gather(v, "fsdp", axis=0, tiled=True)
        vectors = jnp.pad(gather(jnp.concatenate(singles, axis=0).T).T.astype(F32), ((0, 8), (0, 0)))
        bias_up = gather(b_up).astype(F32).reshape(1, hidden_width)
        qkv_full, out_full, up_full, down_full = gather(w_qkv), gather(w_out), gather(w_up), gather(w_down)
        outs = [rows_low, cols_low, rows_low, cols_low, live_like, heads_like, probs_like, cols_low, rows_wide, rows_low, cols_low]
        scratch = [rows_wide, rows_low, mask_like, rows_low, ((1, 3 * width), F32)]
        token, n1t, dm, dmt, live, qkv, probs, att_t, middle, n2, n2t = call(
            functools.partial(first_plain, images, slots, width),
            outs, scratch, (patches, keep_pad, cotangent, vectors, qkv_full, out_full), "first",
        )
        gain1, gain2, b_d = vectors[0:1], vectors[5:6], vectors[7:8]
        hid = ((ROWS, hidden_width), BF16)
        out_tokens, d_mid, d_low, g_up, g_down, g_b_up, g_g2, g_s2, g_bd, g_bo = call(
            functools.partial(second_plain, images, slots, width, hidden_width),
            [((images, slots, width), BF16), rows_wide, rows_low] + [((width, hidden_width), BF16)] * 2 + [((1, hidden_width), F32)] + [row_like] * 4,
            [hid, hid, rows_wide],
            (n2, n2t, dm, dmt, up_full, bias_up, down_full, b_d, middle, live, gain2),
            "second",
        )
        g_out, g_qkv, g_b, g_g1, g_s1, grad_patches = call(
            functools.partial(third_plain, images, slots, width),
            [((width, width), BF16), ((width, 3 * width), BF16), ((1, 3 * width), F32), row_like, row_like, ((images, slots, width), F32)],
            [rows_wide, ((ROWS, TILE), F32), ((ROWS, 3 * width), BF16), heads_like],
            (d_low, att_t, out_full, qkv, probs, n1t, qkv_full, token, gain1, d_mid, live, keep_pad),
            "third",
        )
        scat = lambda v, dim=0: lax.psum(lax.psum_scatter(v, "fsdp", scatter_dimension=dim, tiled=True), "dp").astype(F32)
        rows = jnp.concatenate([g_g1, g_s1, g_b[:, :width], g_b[:, 2 * width :], g_bo, g_g2, g_s2, g_bd], axis=0).astype(BF16)
        rows = scat(rows, 1)
        b_up_sum = scat(g_b_up.astype(BF16), 1)[0]
        sum_qkv, sum_out, sum_up, sum_down = scat(g_qkv), scat(g_out), scat(g_up), scat(g_down, 1).T
    return (
        out_tokens, grad_patches, rows[0], rows[1], sum_qkv, rows[2], rows[3], sum_out, rows[4],
        rows[5], rows[6], sum_up, b_up_sum, sum_down, rows[7],
    )


def solution(mesh):
    linked = (mesh.shape["fsdp"], mesh.shape["dp"]) == (8, 4)
    many, one, two = P(("fsdp", "dp"), None, None), P("fsdp"), P("fsdp", None)
    in_specs = (many, P(("fsdp", "dp"), None), one, one, two, one, one, two, one, one, one, two, one, two, one, many)
    out_specs = (many, many, one, one, two, one, one, two, one, one, one, two, one, two, one)
    return jax.shard_map(functools.partial(shards, linked), mesh=mesh, in_specs=in_specs, out_specs=out_specs, check_vma=False)
```

```python
import functools
import math

import jax
import jax.numpy as jnp
from jax import lax
from jax.experimental import pallas as pl
from jax.experimental.pallas import tpu as pltpu
from jax.sharding import PartitionSpec as P

H = 12
HD = 64
EPSILON = 1e-06
F32 = jnp.float32
BF16 = jnp.bfloat16
SLOT = 200
ROWS = 1024
BLOCK = 128
TILE = 256
NT = (((1,), (1,)), ((), ()))


def dot(left, right):
    return jnp.dot(left, right, preferred_element_type=F32)


def dot_nt(left, right):
    return lax.dot_general(left, right, NT, preferred_element_type=F32)


def tile_at(index, size):
    if isinstance(index, int):
        return pl.ds(index * size, size)
    return pl.ds(pl.multiple_of(index * size, size), size)


def loop(begin, end, body, unroll):
    if (end - begin) == unroll:
        for j in range(begin, end):
            body(j, 0)
        return

    def group(t, _):
        for u in range(unroll):
            body(begin + t * unroll + u, 0)
        return 0

    lax.fori_loop(0, (end - begin) // unroll, group, 0)


def norm_parts(values):
    centre = values - jnp.mean(values, axis=-1, keepdims=True)
    spread = jnp.mean(centre * centre, axis=-1, keepdims=True)
    inverse = lax.rsqrt(spread + EPSILON)
    return centre * inverse, inverse


def norm_back(hat, inverse, gain, grad):
    scaled = grad * gain
    along = jnp.mean(scaled * hat, axis=-1, keepdims=True)
    return inverse * (scaled - jnp.mean(scaled, axis=-1, keepdims=True) - hat * along)


def gelu_parts(hidden):
    size = jnp.abs(hidden)
    bell = jnp.exp(hidden * hidden * -0.5)
    t = 1.0 / (1.0 + size * (0.3275911 / math.sqrt(2.0)))
    tail = 1.061405429 * 0.5
    for term in (-1.453152027, 1.421413741, -0.284496736, 0.254829592):
        tail = tail * t + term * 0.5
    tail = tail * t * bell
    below = jnp.where(hidden >= 0, 1.0 - tail, tail)
    slope = below + hidden * (bell * (1.0 / math.sqrt(2.0 * math.pi)))
    return hidden * below, slope


def first_lanes(rows):
    return lax.broadcasted_iota(jnp.int32, (rows, 2 * HD), 1) < HD


def stage_gather(images, slots, patches, keep, stack, live, mask, token):
    stack[...] = jnp.zeros_like(stack)
    live[...] = jnp.zeros_like(live)

    def gather(i, _):
        row = keep[i]
        column = jnp.broadcast_to(row, (SLOT, SLOT)).T
        mask[i] = jnp.where(column >= 0, 0.0, -1e30)
        alive = (column >= 0).astype(F32)
        chosen = (column[:, :slots] == lax.broadcasted_iota(jnp.int32, (SLOT, slots), 1)).astype(F32).astype(BF16)
        rows = pl.ds(pl.multiple_of(i * SLOT, 8), SLOT)
        stack[rows, :] = dot(chosen, patches[i])
        live[rows, :] = alive[:, :BLOCK]
        return 0

    loop(0, images, gather, 1)

    def narrow(b, _):
        rows = tile_at(b, BLOCK)
        token[rows, :] = stack[rows, :].astype(BF16)
        return 0

    loop(0, ROWS // BLOCK, narrow, 2)


def stage_norm(gain, shift, token, normed, normed_t):
    def norm(b, _):
        rows = tile_at(b, BLOCK)
        hat, _ = norm_parts(token[rows, :].astype(F32))
        low = (hat * gain + shift).astype(BF16)
        normed[rows, :] = low
        normed_t[:, rows] = low.T
        return 0

    loop(0, ROWS // BLOCK, norm, 4)


def stage_grads(images, slots, width, cot, stack, live, dm, dm_t):
    stack[...] = jnp.zeros_like(stack)
    for i in range(images):
        stack[i * SLOT : i * SLOT + slots, :] = cot[i].astype(F32)

    def grads(b, _):
        rows = tile_at(b, BLOCK)
        low = (stack[rows, :] * jnp.concatenate([live[rows, :]] * (width // BLOCK), axis=1)).astype(BF16)
        dm[rows, :] = low
        dm_t[:, rows] = low.T
        return 0

    loop(0, ROWS // BLOCK, grads, 2)


def stage_qkv(images, width, normed, w_qkv, bias, qkv, begin, end):
    def body(c, _):
        cols = tile_at(c, TILE)
        scale = jnp.where(c < width // TILE, 1.0 / math.sqrt(HD), 1.0)
        values = (dot(normed[...], w_qkv[:, cols]) + bias[:, cols]) * scale
        for i in range(images):
            qkv[i, :, cols] = values[i * SLOT : (i + 1) * SLOT].astype(BF16)
        return 0

    loop(begin, end, body, 1)


def stage_attention(width, qkv, mask, probs, stack, i):
    low = first_lanes(SLOT)
    for p in range(H // 2):
        q2 = qkv[i, :, p * 128 : (p + 1) * 128]
        k2 = qkv[i, :, width + p * 128 : width + (p + 1) * 128]
        v2_t = qkv[i, :, 2 * width + p * 128 : 2 * width + (p + 1) * 128].T
        outs = []
        for h in range(2):
            qh = jnp.where(low if h == 0 else ~low, q2, jnp.zeros_like(q2))
            scores = dot_nt(k2, qh) + mask[i]
            exponent = jnp.exp(scores - jnp.max(scores, axis=0, keepdims=True))
            share = 1.0 / jnp.sum(exponent, axis=0, keepdims=True)
            prob = (exponent * share).astype(BF16)
            probs[2 * p + h] = prob
            outs.append(dot(v2_t[h * HD : (h + 1) * HD], prob))
        stack[pl.ds(pl.multiple_of(i * SLOT, 8), SLOT), p * 128 : (p + 1) * 128] = jnp.concatenate(outs, axis=0).T


def stage_out(width, stack, w_out, bias, token, gain, shift, att, att_t, middle, normed, normed_t):
    def low(b, _):
        rows = tile_at(b, BLOCK)
        values = stack[rows, :].astype(BF16)
        att[rows, :] = values
        att_t[:, rows] = values.T
        return 0

    loop(0, ROWS // BLOCK, low, 4)

    def body(c, _):
        cols = tile_at(c, TILE)
        middle[:, cols] = token[:, cols].astype(F32) + (dot(att[...], w_out[:, cols]) + bias[:, cols])
        return 0

    loop(0, width // TILE, body, 1)

    def norm(b, _):
        rows = tile_at(b, BLOCK)
        hat, _ = norm_parts(middle[rows, :])
        values = (hat * gain[...] + shift[...]).astype(BF16)
        normed[rows, :] = values
        normed_t[:, rows] = values.T
        return 0

    loop(0, ROWS // BLOCK, norm, 4)


def stage_mlp(width, normed, normed_t, dm, dm_t, w_up, b_up, w_down, act, dh, put_up, put_down, g_b_up, c):
    cols = tile_at(c, TILE)
    hidden = dot(normed[...], w_up[:, cols]) + b_up[:, cols]
    d_act = dot_nt(dm[...], w_down[cols, :])
    value, slope = gelu_parts(hidden)
    value = value.astype(BF16)
    grad = (d_act * slope).astype(BF16)
    act[:, cols] = value
    dh[:, cols] = grad
    g_b_up[:, cols] = jnp.sum(grad.astype(F32), axis=0, keepdims=True)
    put_up(c, dot(normed_t[...], grad).astype(BF16))
    put_down(c, dot(dm_t[...], value).astype(BF16))


def add_products(width, stack, fresh, product):
    def body(c, _):
        cols = tile_at(c, TILE)
        value = product(cols)
        stack[:, cols] = value if fresh else stack[:, cols] + value
        return 0

    loop(0, width // TILE, body, 1)


def stage_final(images, slots, width, middle, live, b_down, stack, out):
    def final(b, _):
        rows = tile_at(b, BLOCK)
        stack[rows, :] = (middle[rows, :] + (stack[rows, :] + b_down[...])) * jnp.concatenate([live[rows, :]] * (width // BLOCK), axis=1)
        return 0

    loop(0, ROWS // BLOCK, final, 2)
    for i in range(images):
        out[i] = stack[i * SLOT : i * SLOT + slots, :].astype(BF16)


def stage_middle_back(middle, gain, dm, stack, d_mid_low, g_gain, g_shift, g_b_down, g_b_out):
    for ref in (g_gain, g_shift, g_b_down, g_b_out):
        ref[...] = jnp.zeros_like(ref)

    def back(b, _):
        rows = tile_at(b, BLOCK)
        grad = stack[rows, :]
        hat, inverse = norm_parts(middle[rows, :])
        g_gain[...] += jnp.sum(grad * hat, axis=0, keepdims=True)
        g_shift[...] += jnp.sum(grad, axis=0, keepdims=True)
        own = dm[rows, :].astype(F32)
        g_b_down[...] += jnp.sum(own, axis=0, keepdims=True)
        total = own + norm_back(hat, inverse, gain[...], grad)
        middle[rows, :] = total
        low = total.astype(BF16)
        d_mid_low[rows, :] = low
        g_b_out[...] += jnp.sum(low.astype(F32), axis=0, keepdims=True)
        return 0

    loop(0, ROWS // BLOCK, back, 2)


def stage_out_back(width, att_t, d_mid_low, w_out, put_out, stack):
    def body(c, _):
        cols = tile_at(c, TILE)
        put_out(c, dot(att_t[...], d_mid_low[:, cols]).astype(BF16))
        stack[:, cols] = dot_nt(d_mid_low[...], w_out[cols, :])
        return 0

    loop(0, width // TILE, body, 1)


def stage_attention_back(width, qkv, probs, stack, i):
    low = first_lanes(SLOT)
    for p in range(H // 2):
        at_q = slice(p * 128, (p + 1) * 128)
        at_k = slice(width + p * 128, width + (p + 1) * 128)
        at_v = slice(2 * width + p * 128, 2 * width + (p + 1) * 128)
        q2, k2, v2 = qkv[i, :, at_q], qkv[i, :, at_k], qkv[i, :, at_v]
        k2_t = k2.T
        da = stack[pl.ds(pl.multiple_of(i * SLOT, 8), SLOT), at_q].astype(BF16)
        dq, dk, dv = [], 0.0, 0.0
        for h in range(2):
            pick = lambda m: jnp.where(low if h == 0 else ~low, m, jnp.zeros_like(m))
            prob = probs[2 * p + h]
            d_prob = dot_nt(pick(v2), da)
            mixed = prob.astype(F32)
            moved = mixed * d_prob
            total = jnp.sum(moved, axis=0, keepdims=True)
            ds = (moved - mixed * total).astype(BF16)
            dq.append(dot(k2_t[h * HD : (h + 1) * HD], ds))
            dk = dk + dot(ds, pick(q2))
            dv = dv + dot(prob, pick(da))
        qkv[i, :, at_q] = (jnp.concatenate(dq, axis=0).T * (1.0 / math.sqrt(HD))).astype(BF16)
        qkv[i, :, at_k] = dk.astype(BF16)
        qkv[i, :, at_v] = dv.astype(BF16)


def stage_qkv_back(images, width, d_qkv, normed_t, tile, flat, put_qkv, g_b_qkv, c):
    cols = tile_at(c, TILE)
    for i in range(images):
        tile[i * SLOT : (i + 1) * SLOT, :] = d_qkv[i, :, cols].astype(F32)
    values = tile[...]
    g_b_qkv[:, cols] = jnp.sum(values, axis=0, keepdims=True)
    low = values.astype(BF16)
    flat[:, cols] = low
    put_qkv(c, dot(normed_t[...], low).astype(BF16))


def stage_norm_back(width, flat, w_qkv, stack):
    def body(c, _):
        cols = tile_at(c, TILE)
        stack[:, cols] = dot_nt(flat[...], w_qkv[cols, :])
        return 0

    loop(0, width // TILE, body, 1)


def stage_end(images, slots, width, keep, token, gain, middle, live, stack, g_gain, g_shift, put_patches):
    for ref in (g_gain, g_shift):
        ref[...] = jnp.zeros_like(ref)

    def back(b, _):
        rows = tile_at(b, BLOCK)
        grad = stack[rows, :]
        hat, inverse = norm_parts(token[rows, :].astype(F32))
        g_gain[...] += jnp.sum(grad * hat, axis=0, keepdims=True)
        g_shift[...] += jnp.sum(grad, axis=0, keepdims=True)
        total = middle[rows, :] + norm_back(hat, inverse, gain[...], grad)
        stack[rows, :] = total * jnp.concatenate([live[rows, :]] * (width // BLOCK), axis=1)
        return 0

    loop(0, ROWS // BLOCK, back, 2)

    def scatter(i, _):
        chosen = (lax.broadcasted_iota(jnp.int32, (slots, SLOT), 0) == keep[i]).astype(F32).astype(BF16)
        values = stack[pl.ds(pl.multiple_of(i * SLOT, 8), SLOT), :]
        high = values.astype(BF16)
        rest = (values - high.astype(F32)).astype(BF16)
        put_patches(i, dot(chosen, high) + dot(chosen, rest))
        return 0

    for i in range(images):
        scatter(i, 0)


MESH = pl.DeviceIdType.MESH


class Place:
    def __init__(self):
        f, d = lax.axis_index("fsdp"), lax.axis_index("dp")
        self.z, self.x = f // 2, lax.rem(f, 2)
        self.y, self.c = d // 2, lax.rem(d, 2)
        z = self.z
        self.zs = [z, z + 1 - 2 * lax.rem(z, 2), lax.rem(z + 2, 4), 3 - z]
        self.ox, self.oy, self.oc = 1 - self.x, 1 - self.y, 1 - self.c
        self.beside = self.to(x=self.ox), self.to(y=self.oy), self.to(c=self.oc)
        self.along = [self.to(z=k) for k in self.zs]

    def to(self, z=None, x=None, y=None, c=None):
        z, x, y, c = (own if new is None else new for new, own in ((z, self.z), (x, self.x), (y, self.y), (c, self.c)))
        return (z * 2 + x, y * 2 + c)

    def sides(self):
        return self.beside


def enter(peers, meanwhile=None):
    barrier = pltpu.get_barrier_semaphore()
    for peer in peers:
        pl.semaphore_signal(barrier, inc=1, device_id=peer, device_id_type=MESH)
    if meanwhile is not None:
        meanwhile()
    pl.semaphore_wait(barrier, len(peers))


class Gather:
    def __init__(self, place, shard, full, first_cols, send, recv):
        self.place, self.shard, self.full, self.send, self.recv = place, shard, full, send, recv
        self.rows, cols = shard.shape
        self.half, self.wide, self.cut = self.rows // 2, cols // 2, first_cols
        self.started = []

    def spot(self, *args):
        return lambda: self.place_of(*args)

    def place_of(self, z, x, y, part=None, local=False):
        p = self.place
        base = 0 if local else (z * 2 + x) * self.rows
        rows = pl.ds(pl.multiple_of(base + p.c * self.half, 16), self.half)
        if y is None:
            return rows, slice(None)
        start, size = (y * self.wide, self.wide) if part is None else ((y * self.wide, self.cut) if part == 0 else (y * self.wide + self.cut, self.wide - self.cut))
        return rows, pl.ds(pl.multiple_of(start, 128), size)

    def copy(self, spot, sem, peer, local=None):
        src = self.full.at[spot] if local is None else self.shard.at[local]
        return pltpu.make_async_remote_copy(
            src_ref=src, dst_ref=self.full.at[spot], send_sem=self.send.at[sem], recv_sem=self.recv.at[sem], device_id=peer, device_id_type=MESH
        )

    def start(self, spot, sem, peer, local=None):
        def make():
            return self.copy(spot(), sem, peer, None if local is None else local())

        make().start()
        self.started.append(make)

    def arrived(self, spot, sem):
        self.copy(spot(), sem, self.place.sides()[0]).wait_recv()

    def own(self, sem):
        p = self.place
        rows = pl.ds(pl.multiple_of((p.z * 2 + p.x) * self.rows, 16), self.rows)
        return pltpu.make_async_copy(self.shard, self.full.at[rows, :], sem)

    def lines(self, *ks):
        p = self.place
        spot, local = self.spot(p.z, p.x, p.y), self.spot(p.z, p.x, p.y, None, True)
        for k in ks:
            self.start(spot, k, p.along[k], local)

    def beside(self):
        p = self.place
        side_x, side_y, _ = p.sides()
        self.start(self.spot(p.z, p.x, p.y), 4, side_x, self.spot(p.z, p.x, p.y, None, True))
        self.start(self.spot(p.z, p.x, p.oy, 1), 16, side_x, self.spot(p.z, p.x, p.oy, 1, True))

    def phase(self, name):
        if name == "own":
            self.beside()
        elif name == "zs":
            self.lines(1, 2, 3)
        elif name[0] == "z":
            self.lines(int(name[1]))
        elif name in ("spread", "cross", "share"):
            for k in range(name == "spread", 4):
                getattr(self, name)(k)
        else:
            (self.spread if name[0] == "s" else self.cross)(int(name[1]))

    def spread(self, k):
        p = self.place
        side_x, side_y, _ = p.sides()
        spot = self.spot(p.zs[k], p.x, p.y)
        self.arrived(spot, k)
        self.start(spot, 4 + k, side_x)
        self.start(spot, 8 + k, side_y)

    def cross(self, k):
        p = self.place
        side_x, side_y, _ = p.sides()
        self.arrived(self.spot(p.zs[k], p.ox, p.y), 4 + k)
        self.start(self.spot(p.zs[k], p.ox, p.y, 0), 12 + k, side_y)
        if k:
            self.arrived(self.spot(p.zs[k], p.x, p.oy), 8 + k)
            self.start(self.spot(p.zs[k], p.x, p.oy, 1), 16 + k, side_x)

    def share(self, k):
        p = self.place
        core = p.sides()[2]
        if k:
            self.start(self.spot(p.zs[k], p.x, None), 20 + k, core)
        self.arrived(self.spot(p.zs[k], p.ox, p.oy, 0), 12 + k)
        self.arrived(self.spot(p.zs[k], p.ox, p.oy, 1), 16 + k)
        self.start(self.spot(p.zs[k], p.ox, None), 24 + k, core)

    def finish(self):
        p = self.place

        def other(z, x):
            return lambda: (pl.ds(pl.multiple_of((z * 2 + x) * self.rows + (p.oc) * self.half, 16), self.half), slice(None))

        for k in range(4):
            if k:
                self.arrived(other(p.zs[k], p.x), 20 + k)
            self.arrived(other(p.zs[k], p.ox), 24 + k)

    def drain(self):
        for make in self.started:
            make().wait_send()


class Reduce:
    def __init__(self, place, source, held, core, diag_x, diag_y, side_x, side_y, line, final, send, recv):
        self.place, self.source, self.held, self.core = place, source, held, core
        self.diag_x, self.diag_y, self.side_x, self.side_y, self.line, self.final = diag_x, diag_y, side_x, side_y, line, final
        self.send, self.recv, self.started = send, recv, []
        self.own4 = self.own = None
        if diag_y is not None:
            self.rows, self.wide = side_x.shape[1:]
            self.by_rows = diag_y.shape[2] == self.wide
            self.cut = diag_y.shape[1] if self.by_rows else diag_y.shape[2]

    def part(self, second):
        bounds = pl.ds(self.cut, (self.rows if self.by_rows else self.wide) - self.cut) if second else pl.ds(0, self.cut)
        return (bounds, slice(None)) if self.by_rows else (slice(None), bounds)

    def hold(self, z, x, y, *rest):
        if self.held is None:
            return (z, x, self.place.c, y) + rest
        return (z, x, y) + rest

    @property
    def home(self):
        return self.source if self.held is None else self.held

    def copy(self, src, dst, sem, peer):
        return pltpu.make_async_remote_copy(src_ref=src, dst_ref=dst, send_sem=self.send.at[sem], recv_sem=self.recv.at[sem], device_id=peer, device_id_type=MESH)

    def start(self, src, dst, sem, peer):
        def make():
            return self.copy(src(), dst() if callable(dst) else dst, sem, peer)

        make().start()
        self.started.append(make)

    def arrived(self, dst, sem):
        self.copy(dst, dst, sem, self.place.sides()[0]).wait_recv()

    def begin(self, own=None):
        p = self.place
        self.start(lambda: self.source.at[:, :, p.oc], self.core, 0, p.sides()[2])
        self.own = own
        if own is not None:
            own.start()

    def add_core(self, x, y):
        def body(z, _):
            spot = self.hold(z, x, y)
            self.home[spot] = self.home[spot] + self.core[z, x, y]
            return 0

        lax.fori_loop(0, 4, body, 0)

    def add(self, x, y, part, buffer):
        def body(z, _):
            spot = self.hold(z, x, y, *part)
            self.home[spot] = self.home[spot] + buffer[z]
            return 0

        lax.fori_loop(0, 4, body, 0)

    def step_core(self):
        p = self.place
        side_x, side_y, _ = p.sides()
        if self.own is not None:
            self.own.wait()
        self.arrived(self.core, 0)
        for x, y in ((p.ox, p.oy), (p.ox, p.y), (p.x, p.oy), (p.x, p.y)):
            self.add_core(x, y)

    def step_open(self):
        p = self.place
        side_x, side_y, _ = p.sides()
        every = slice(None)
        self.start(lambda: self.home.at[self.hold(every, p.ox, p.oy, *self.part(True))], self.diag_x, 1, side_x)
        self.start(lambda: self.home.at[self.hold(every, p.ox, p.oy, *self.part(False))], self.diag_y, 2, side_y)

    def step_diag(self):
        p = self.place
        side_x, side_y, _ = p.sides()
        every = slice(None)
        self.arrived(self.diag_y, 2)
        self.add(p.ox, p.y, self.part(False), self.diag_y)
        self.start(lambda: self.home.at[self.hold(every, p.ox, p.y)], self.side_x, 3, side_x)
        self.arrived(self.diag_x, 1)
        self.add(p.x, p.oy, self.part(True), self.diag_x)
        self.start(lambda: self.home.at[self.hold(every, p.x, p.oy)], self.side_y, 4, side_y)

    def step_sum(self):
        p = self.place
        whole = (slice(None), slice(None))
        self.arrived(self.side_x, 3)
        self.add(p.x, p.y, whole, self.side_x)
        self.arrived(self.side_y, 4)
        self.add(p.x, p.y, whole, self.side_y)

    def mine(self, z):
        if self.own4 is not None:
            return self.own4.at[z]
        return self.home.at[self.hold(z, self.place.x, self.place.y)]

    def step_send(self):
        p = self.place
        for k in (1, 2, 3):
            self.start(lambda k=k: self.mine(p.zs[k]), lambda k=k: self.line.at[k - 1], 4 + k, p.along[k])

    def step_side(self):
        self.step_sum()
        self.step_send()

    def step_line(self):
        p = self.place
        total = self.mine(p.z)[...].astype(F32)
        for k in (1, 2, 3):
            self.arrived(self.line.at[k - 1], 4 + k)
            total = total + self.line[k - 1].astype(F32)
        self.final[p.c, p.y] = total.astype(BF16)
        self.start(lambda: self.final.at[p.c, p.y], lambda: self.final.at[p.c, p.y], 8, p.sides()[1])

    def step_share(self):
        p = self.place
        self.arrived(self.final.at[p.c, p.oy], 8)
        self.start(lambda: self.final.at[p.c], lambda: self.final.at[p.c], 9, p.sides()[2])

    def finish(self):
        self.arrived(self.final.at[self.place.oc], 9)

    def drain(self):
        for make in self.started:
            make().wait_send()


class SmallReduce:
    def __init__(self, place, home, core, side_y, side_x, line, send, recv):
        self.place, self.home, self.core, self.side_y, self.side_x, self.line = place, home, core, side_y, side_x, line
        self.send, self.recv, self.started = send, recv, []

    copy, start, arrived, drain = Reduce.copy, Reduce.start, Reduce.arrived, Reduce.drain

    def begin(self):
        self.start(lambda: self.home, self.core, 0, self.place.sides()[2])

    def step_core(self, sent):
        p = self.place
        self.arrived(self.core, 0)
        sent[...] = self.home[...] + self.core[...]
        self.start(lambda: sent, self.side_y, 1, p.sides()[1])

    def step_y(self, sent, total):
        p = self.place
        self.arrived(self.side_y, 1)
        total[...] = sent[...] + self.side_y[...]
        self.start(lambda: total.at[:, p.ox], self.side_x, 2, p.sides()[0])

    def step_x(self, total):
        p = self.place
        self.arrived(self.side_x, 2)
        for z in range(4):
            self.side_x[z] = self.side_x[z] + total[z, p.x]
        for k in (1, 2, 3):
            self.start(lambda k=k: self.side_x.at[p.zs[k]], lambda k=k: self.line.at[k - 1], 2 + k, p.along[k])

    def step_line(self, out):
        total = self.side_x[self.place.z]
        for k in (1, 2, 3):
            self.arrived(self.line.at[k - 1], 2 + k)
            total = total + self.line[k - 1]
        out[...] = total


GATHER_PLAN = (
    (("k", "own"), ("v", "own"), ("o", "own"), ("p0", "own"), ("q", "z1"), ("k", "z1"), ("q", "z2"), ("k", "z2"), ("k", "z3"), ("q", "s1"), ("k", "s1"),),
    (("v", "z1"), ("q", "z3"), ("k", "c0"), ("k", "s3"),),
    (("v", "z2"), ("v", "z3"),),
    (),
    (("v", "s1"), ("q", "s2"), ("q", "c1"),),
    (("o", "zs"), ("k", "s2"), ("q", "s3"),),
    (("q", "own"), ("p0", "zs"), ("v", "c0"), ("v", "s2"), ("v", "s3"), ("k", "c2"), ("q", "c3"), ("k", "c3"),),
    (("q", "c0"), ("v", "c1"), ("q", "c2"), ("v", "c2"), ("v", "c3"),),
    (("k", "c1"), ("o", "spread"), ("q", "share"), ("k", "share"),),
    (("p1", "own"), ("p1", "zs"), ("o", "cross"), ("v", "share"),),
    (("p0", "spread"),),
    (),
    (),
    (("p2", "zs"), ("p1", "spread"), ("p0", "cross"), ("o", "share"),),
    (),
    (("p2", "own"),),
    (("p1", "cross"), ("p0", "share"),),
    (("p2", "spread"),),
    (),
    (),
    (("p1", "share"),),
    (("p2", "cross"),),
    (),
    (),
    (("p2", "share"),),
    (),
    (),
    (),
    (),
    (),
)
MERGE_PLAN = (22, 25, 26)
REDUCE_PLAN = (
    ("m0", (5, 21)),
    ("m1", (0, 4, 9, 14, 22)),
    ("m2", (2, 8, 13, 19, 21)),
    ("o", (7, 12, 15, 20, 21)),
    ("q", (13, 15, 17, 19, 21)),
    ("k", (14, 16, 19, 21, 21)),
    ("v", (14, 18, 19, 21, 22)),
)


VMEM = pl.BlockSpec(memory_space=pltpu.VMEM)
ANY = pl.BlockSpec(memory_space=pl.ANY)
LIMIT = 61 * 1024 * 1024
THIRD = 1024


def call(body, outs, scratch, args, name):
    return pl.pallas_call(
        body,
        out_shape=[jax.ShapeDtypeStruct(*o) for o in outs],
        in_specs=[VMEM] * len(args),
        out_specs=[VMEM] * len(outs),
        scratch_shapes=[pltpu.VMEM(*s) for s in scratch],
        compiler_params=pltpu.CompilerParams(vmem_limit_bytes=LIMIT),
        name=name,
    )(*args)


class Later:
    def __init__(self, sems):
        self.sems, self.flights = sems, {}

    def start(self, name, src, dst):
        self.plan(name, src, dst)
        self.flights[name]().start()

    def plan(self, name, src, dst):
        sem = len(self.flights)

        def make():
            return pltpu.make_async_copy(*(r() if callable(r) else r for r in (src, dst)), self.sems.at[sem])

        self.flights[name] = make

    def wait(self, *names):
        for name in names:
            self.flights[name]().wait()


def first_plain(
    images, slots, width, patches, keep, cot, vectors, w_qkv, w_out,
    token, n1t, dm, dmt, live, qkv, probs, att_t, middle, n2, n2t, stack, normed, mask, att, bias,
):
    bias[...] = jnp.concatenate([vectors[2:3, :], jnp.zeros((1, width), F32), vectors[3:4, :]], axis=1)
    stage_gather(images, slots, patches, keep, stack, live, mask, token)
    stage_norm(vectors[0:1, :], vectors[1:2, :], token, normed, n1t)
    stage_grads(images, slots, width, cot, stack, live, dm, dmt)
    stage_qkv(images, width, normed, w_qkv, bias, qkv, 0, 3 * width // TILE)
    for i in range(images):
        stage_attention(width, qkv, mask, probs.at[pl.ds(i * H, H)], stack, i)
    stage_out(width, stack, w_out, vectors.at[4:5, :], token, vectors.at[5:6, :], vectors.at[6:7, :], att, att_t, middle, n2, n2t)


def first_kernel(
    images, slots, width,
    patches, keep, cot, vec, s_qkv, s_out, s_up, s_down,
    vectors, g_b_up, h_token, h_n1t, h_dm, h_live, h_qkv, h_probs, h_att_t, h_middle, h_wqkv, h_wout, h_up, h_down, h_act, h_dh, h_gup, h_gdown, h_up1, h_down1, h_own_up, h_own_down,
    stack, normed, mask, token, n1t, dm, dmt, live, qkv, probs, att_t, middle, f_qkv, f_out, f_up, f_down, s_up3, act_, dh, g_up, g_down, up_core, down_core, up_dx, up_dy, up_sx, up_sy, dn_dx, dn_dy, dn_sx, dn_sy,
    vecs, bias, b_up, q_send, q_recv, m_send, m_recv, v_send, v_recv, own, saves, probs_sem, r_send, r_recv, w_send, w_recv,
):
    place = Place()
    _, side_y, side_c = place.sides()
    flat = [place.to(z=place.zs[k], x=x) for k in range(4) for x in (place.x, place.ox)][1:]
    later = Later(saves)

    def before():
        for t in range(3):
            for f in range(8):
                s_up3[t, :, f * 128 : f * 128 + 128] = s_up[:, f * 384 + t * 128 : f * 384 + t * 128 + 128]
        stage_gather(images, slots, patches, keep, stack, live, mask, token)
        later.start("live", live, h_live)
        later.start("token", token, h_token)
        stage_grads(images, slots, width, cot, stack, live, dm, dmt)
        later.start("dm", dm, h_dm)

    enter(flat + [side_y, side_c], before)
    columns = [slice(m * width, (m + 1) * width) for m in range(3)]
    g_qkv = [Gather(place, s_qkv.at[:, columns[m]], f_qkv.at[:, columns[m]], 128 if m == 2 else 256, q_send.at[m], q_recv.at[m]) for m in range(3)]
    g_out = Gather(place, s_out, f_out, 256, q_send.at[3], q_recv.at[3])
    g_ups = [Gather(place, s_up3.at[t], f_up.at[t], (256, 384, 256)[t], m_send.at[t], m_recv.at[t]) for t in range(3)]
    g_downs = [Gather(place, s_down.at[t * 128 : t * 128 + 128], f_down.at[t], 256, m_send.at[3 + t], m_recv.at[3 + t]) for t in range(3)]
    groups = {"q": g_qkv[:1], "k": g_qkv[1:2], "v": g_qkv[2:], "o": [g_out]}
    groups.update({f"p{t}": [g_ups[t], g_downs[t]] for t in range(3)})
    every = g_qkv + [g_out] + [g for t in range(3) for g in (g_ups[t], g_downs[t])]
    mine = place.z * 2 + place.x
    tiny = []
    for j, peer in enumerate(flat):
        copy = pltpu.make_async_remote_copy(src_ref=vec, dst_ref=vecs.at[mine], send_sem=v_send.at[j], recv_sem=v_recv.at[j], device_id=peer, device_id_type=MESH)
        copy.start()
        tiny.append(copy)
    vecs[mine] = vec[...]
    core = place.sides()[2]
    swaps = {
        (name, t): pltpu.make_async_remote_copy(
            src_ref=g.at[t, :, :, place.oc], dst_ref=buffer.at[t], send_sem=r_send.at[2 * t + j], recv_sem=r_recv.at[2 * t + j], device_id=core, device_id_type=MESH
        )
        for t in range(2)
        for j, (name, g, buffer) in enumerate((("up", g_up, up_core), ("down", g_down, down_core)))
    }
    early = (
        Reduce(place, None, up_core.at[0], None, up_dx, up_dy, up_sx, up_sy, None, None, w_send.at[0], w_recv.at[0]),
        Reduce(place, None, down_core.at[0], None, dn_dx, dn_dy, dn_sx, dn_sy, None, None, w_send.at[1], w_recv.at[1]),
    )

    def merge(t):
        for name, g, buffer in (("up", g_up, up_core), ("down", g_down, down_core)):
            swaps[name, t].wait_recv()

            def body(z, _, g=g, buffer=buffer):
                buffer[t, z] = buffer[t, z] + g[t, z, :, place.c]
                return 0

            lax.fori_loop(0, 4, body, 0)
        if t == 0:
            for r in early:
                r.step_open()
        else:
            later.start("up_sum1", lambda: up_core.at[1], h_up1)
            later.start("down_sum1", lambda: down_core.at[1], h_down1)

    def act(slot):
        for group, phase in GATHER_PLAN[slot]:
            for g in groups[group]:
                g.phase(phase)
        if slot == MERGE_PLAN[0]:
            merge(0)
        if slot == MERGE_PLAN[1]:
            for r in early:
                r.step_diag()
        if slot == MERGE_PLAN[2]:
            merge(1)

    act(0)
    locals_ = [g.own(own.at[j]) for j, g in enumerate(every)]
    for copy in locals_:
        copy.start()
    for slot in range(1, 5):
        act(slot)
    for copy in tiny:
        copy.wait_recv()
    vectors[...] = jnp.concatenate([vecs[f][:, :96] for f in range(8)], axis=1).astype(F32)
    act(5)
    stage_norm(vectors[0:1, :], vectors[1:2, :], token, normed, n1t)
    later.start("n1t", n1t, h_n1t)
    for f in range(8):
        row = jnp.concatenate([vecs[f][8 + j : 9 + j, :96] for j in range(4)], axis=1).astype(F32)
        for t in range(3):
            b_up[t, :, f * 128 : f * 128 + 128] = row[:, t * 128 : t * 128 + 128]
    bias[...] = jnp.concatenate([vectors[2:3, :], jnp.zeros((1, width), F32), vectors[3:4, :]], axis=1)
    act(6)
    act(7)
    for m in range(3):
        act(8 + m)
        locals_[m].wait()
        g_qkv[m].finish()
        stage_qkv(images, width, normed, f_qkv, bias, qkv, m * width // TILE, (m + 1) * width // TILE)
    later.start("w_qkv", f_qkv, h_wqkv)
    later.start("qkv", qkv, h_qkv)

    def save_probs(slot, i):
        return pltpu.make_async_copy(probs.at[slot], h_probs.at[pl.ds(i * H, H)], probs_sem.at[slot])

    def attend(i, _):
        slot = lax.rem(i, 2)
        for j in range(5):
            pl.when(i == j)(lambda j=j: act(11 + j))
        pl.when(i >= 2)(lambda: save_probs(slot, i - 2).wait())
        stage_attention(width, qkv, mask, probs.at[slot], stack, i)
        save_probs(slot, i).start()
        return 0

    lax.fori_loop(0, images, attend, 0)
    for i in range(images - 2, images):
        save_probs(i % 2, i).wait()
    act(16)
    locals_[3].wait()
    g_out.finish()
    later.start("w_out", f_out, h_wout)
    later.wait("n1t")
    n2t = n1t
    stage_out(width, stack, f_out, vectors.at[4:5, :], token, vectors.at[5:6, :], vectors.at[6:7, :], normed, att_t, middle, normed, n2t)
    later.start("att_t", att_t, h_att_t)
    later.start("middle", middle, h_middle)
    for t in range(3):
        for part in range(2):
            for name, src, dst in (("act", act_, h_act), ("dh", dh, h_dh)):
                cols = slice(part * 512, part * 512 + 512)
                later.plan(f"{name}{t}{part}", lambda src=src, cols=cols: src.at[:, cols], lambda dst=dst, t=t, cols=cols: dst.at[t, :, cols])

    def enter_third(t):
        locals_[4 + 2 * t].wait()
        locals_[5 + 2 * t].wait()
        g_ups[t].finish()
        g_downs[t].finish()
        later.start(f"up{t}", lambda: f_up.at[t], lambda: h_up.at[t])
        later.start(f"down{t}", lambda: f_down.at[t], lambda: h_down.at[t])
        if t:
            later.wait(f"act{t - 1}0", f"dh{t - 1}0")
        if t == 2:
            for name in ("up", "down"):
                swaps[name, 0].wait_send()

    def middle_third(t):
        if t:
            later.wait(f"act{t - 1}1", f"dh{t - 1}1")

    def save_part(t, part):
        later.flights[f"act{t}{part}"]().start()
        later.flights[f"dh{t}{part}"]().start()
        if part and t < 2:
            swaps["up", t].start()
            swaps["down", t].start()
        elif part:
            later.start("g_up2", lambda: g_up.at[0], h_gup)
            later.start("g_down2", lambda: g_down.at[0], h_gdown)

    def feed(step, _):
        t, c = step // 4, step % 4
        slot = t % 2
        for j in range(12):
            if GATHER_PLAN[17 + j] or 17 + j in MERGE_PLAN:
                pl.when(step == j)(lambda j=j: act(17 + j))
        for j in range(3):
            pl.when(step == 4 * j)(lambda j=j: enter_third(j))
            pl.when(step == 4 * j + 2)(lambda j=j: middle_third(j))

        def put_up(c, value):
            y, at = c // 2, tile_at(c % 2, TILE)
            g_up[slot, :, :, :, y, :, at] = value.reshape(4, 2, 2, 48, TILE)

        def put_down(c, value):
            for x in range(2):
                g_down[slot, c, x] = value[:, x * 128 : (x + 1) * 128].reshape(2, 2, 192, 128)

        stage_mlp(width, normed, n2t, dm, dmt, f_up.at[t], b_up.at[t], f_down.at[t], act_, dh, put_up, put_down, g_b_up.at[t], c)
        for j in range(3):
            for part in range(2):
                pl.when(step == 4 * j + 2 * part + 1)(lambda j=j, part=part: save_part(j, part))
        return 0

    lax.fori_loop(0, 12, feed, 0)
    act(29)
    for r, h, buffer in ((early[0], h_own_up, up_core), (early[1], h_own_down, down_core)):
        r.step_sum()
        later.start(f"own{h is h_own_up}", buffer.at[0, :, place.x, place.y], h)
    waited = {"n1t"} | {f"{n}{t}{p}" for n in ("act", "dh") for t in range(2) for p in range(2)}
    for name in ("up", "down"):
        swaps[name, 1].wait_send()
    later.wait(*(n for n in later.flights if n not in waited))
    for copy in tiny:
        copy.wait_send()
    for g in every + list(early):
        g.drain()


def second_plain(
    images, slots, width, hidden_width,
    n2, n2t, dm, dmt, w_up, b_up, w_down, b_d, middle_in, live, gain2,
    out, middle, d_low, g_up, g_down, g_b_up, g_g2, g_s2, g_bd, g_bo, act, dh, stack,
):
    middle[...] = middle_in[...]

    def put(ref, c, value):
        ref[:, tile_at(c, TILE)] = value

    feed = functools.partial(stage_mlp, width, n2, n2t, dm, dmt, w_up, b_up, w_down, act, dh, functools.partial(put, g_up), functools.partial(put, g_down), g_b_up)
    loop(0, hidden_width // TILE, lambda c, _: feed(c), 1)
    add_products(width, stack, True, lambda cols: dot(act[...], w_down[:, cols]))
    stage_final(images, slots, width, middle, live, b_d, stack, out)
    add_products(width, stack, True, lambda cols: dot_nt(dh[...], w_up[cols, :]))
    stage_middle_back(middle, gain2, dm, stack, d_low, g_g2, g_s2, g_bd, g_bo)


def third_plain(
    images, slots, width, d_low, att_t, w_out, qkv_in, probs, n1t, w_qkv, token, gain, mid, live, keep,
    g_out, g_qkv, g_b, g_g1, g_s1, gp, stack, tile, flat, qkv,
):
    def put(ref, c, value):
        ref[:, tile_at(c, TILE)] = value

    def put_patches(i, value):
        gp[i] = value

    qkv[...] = qkv_in[...]
    tile[...] = jnp.zeros_like(tile)
    stage_out_back(width, att_t, d_low, w_out, functools.partial(put, g_out), stack)
    for i in range(images):
        stage_attention_back(width, qkv, probs.at[pl.ds(i * H, H)], stack, i)
    back = functools.partial(stage_qkv_back, images, width, qkv, n1t, tile, flat, functools.partial(put, g_qkv), g_b)
    loop(0, 3 * width // TILE, lambda c, _: back(c), 1)
    stage_norm_back(width, flat, w_qkv, stack)
    stage_end(images, slots, width, keep, token, gain, mid, live, stack, g_g1, g_s1, put_patches)


def second_kernel(
    images, slots, width,
    keep, vectors, s_bup, h_token, h_n1t, h_dm, h_live, h_qkv, h_probs, h_att_t, h_middle, h_wqkv, h_wout, h_up, h_down, h_act, h_dh, h_gup, h_gdown, h_up1, h_down1, h_own_up, h_own_down,
    gp, out_tokens, o_qkv, o_out, o_up, o_down, e_small,
    e_up, e_down, e_out, e_q, e_k, e_v,
    stack, tile, flat, qkv, probs, t_a, t_b, r_a, r_b, mid, live, w_qkv, w_out, stage, g_b, g_g1, g_s1, g_g2, g_s2, g_bd, g_bo, g_attn,
    up_held, up_own, up_core, up_dx, up_dy, up_sx, up_sy, up_ln, dn_held, dn_own, dn_core, dn_dx, dn_dy, dn_sx, dn_sy, dn_ln,
    core4, dx4, dy4, sx4, sy4, ln4, v_home, v_core, v_sy, v_sx, v_ln, v_sent, v_total,
    send, recv, v_send, v_recv, own, loads, probs_sem, out_sem,
):
    place = Place()
    enter(place.along[1:] + list(place.sides()))
    def reduce_third(t, source, held, own4, core, dx, dy, sx, sy, ln, e, sem):
        sems = send.at[sem + t], recv.at[sem + t]
        if t == 0:
            r = Reduce(place, None, None, None, None, None, None, None, ln.at[0], e.at[0], *sems)
            r.own4 = own4
            return r
        return Reduce(place, source, held.at[t - 1], core, dx.at[t - 1], dy.at[t - 1], sx.at[t - 1], sy.at[t - 1], ln.at[t], e.at[t], *sems)

    r_up = [reduce_third(t, h_gup, up_held, up_own, up_core, up_dx, up_dy, up_sx, up_sy, up_ln, e_up, 0) for t in range(3)]
    r_down = [reduce_third(t, h_gdown, dn_held, dn_own, dn_core, dn_dx, dn_dy, dn_sx, dn_sy, dn_ln, e_down, 3) for t in range(3)]
    mlp = [(r_up[t], r_down[t]) for t in range(3)]
    r_q, r_k, r_v, r_out = (
        Reduce(place, g_attn.at[m], None, core4.at[m], dx4.at[m], dy4.at[m], sx4.at[m], sy4.at[m], ln4.at[m], e, send.at[6 + m], recv.at[6 + m])
        for m, e in enumerate((e_q, e_k, e_v, e_out))
    )
    small = SmallReduce(place, v_home, v_core, v_sy, v_sx, v_ln, v_send, v_recv)
    later = Later(loads)
    slots_ = [flat.at[:, 0:THIRD], flat.at[:, THIRD : 2 * THIRD]]
    groups = {"m0": mlp[0], "m1": mlp[1], "m2": mlp[2], "o": (r_out,), "q": (r_q,), "k": (r_k,), "v": (r_v,)}

    def act(slot):
        for phase in ("open", "core", "diag", "side", "line", "share"):
            for group, slots_of in REDUCE_PLAN:
                phases = {2: ("line", "share"), 5: ("open" if group == "m1" else "core", "diag", "side", "line", "share")}[len(slots_of)]
                if (phase, slot) in zip(phases, slots_of):
                    for r in groups[group]:
                        getattr(r, "step_" + phase)()
                        if phase == "core":
                            r.step_open()

    early = [
        pltpu.make_async_copy(h, into, own.at[j])
        for j, (h, into) in enumerate(((h_own_up, up_own), (h_own_down, dn_own), (h_up1, up_held.at[0]), (h_down1, dn_held.at[0])))
    ]
    for copy in early:
        copy.start()
    later.start("dh0", h_dh.at[0], slots_[0])
    later.start("up0", h_up.at[0], t_a)
    for j, (r, h, into) in enumerate(((r_up[2], h_gup, up_held), (r_down[2], h_gdown, dn_held))):
        r.begin(pltpu.make_async_copy(h.at[:, :, place.c], into.at[1], own.at[4 + j]))
    later.start("dh1", h_dh.at[1], slots_[1])
    later.start("up1", h_up.at[1], t_b)
    for copy, r in zip(early[:2], mlp[0]):
        copy.wait()
        r.step_send()
    for copy in early[2:]:
        copy.wait()
    act(0)
    for name, src, dst in (("mid", h_middle, mid), ("dm", h_dm, r_a), ("live", h_live, live), ("w_out", h_wout, w_out), ("qkv", h_qkv, qkv), ("w_qkv", h_wqkv, w_qkv)):
        later.start(name, src, dst)

    def load_probs(i):
        slot = i % 2
        return pltpu.make_async_copy(h_probs.at[pl.ds(i * H, H)], probs.at[slot], probs_sem.at[slot])

    load_probs(0).start()
    later.wait("dh0", "up0")
    act(1)
    add_products(width, stack, True, lambda cols: dot_nt(slots_[0][...], t_a[cols, :]))
    later.start("dh2", h_dh.at[2], slots_[0])
    later.start("up2", h_up.at[2], t_a)
    act(2)
    later.wait("dh1", "up1")
    add_products(width, stack, False, lambda cols: dot_nt(slots_[1][...], t_b[cols, :]))
    later.start("att_t", h_att_t, t_b)
    act(3)
    later.wait("dh2", "up2")
    add_products(width, stack, False, lambda cols: dot_nt(slots_[0][...], t_a[cols, :]))
    later.start("n1t", h_n1t, t_a)
    act(4)
    later.wait("mid", "dm")
    gain2 = vectors.at[5:6, :]
    stage_middle_back(mid, gain2, r_a, stack, r_b, g_g2, g_s2, g_bd, g_bo)
    later.start("token", h_token, r_a)

    def put(m, c, value):
        for j in range(2):
            col = 2 * c + j
            y, off = (col % 6) // 3, col % 3
            at = tile_at(off, 128)
            g_attn[col // 6 if m is None else m, :, :, :, y, :, at] = value[:, j * 128 : (j + 1) * 128].reshape(4, 2, 2, 48, 128)

    act(5)
    later.wait("att_t", "w_out", "qkv")
    stage_out_back(width, t_b, r_b, w_out, functools.partial(put, 3), stack)
    r_out.begin()

    def back(i, _):
        for j in range(5):
            pl.when(i == j)(lambda j=j: act(6 + j))
        load_probs(i).wait()
        pl.when(i + 1 < images)(lambda: load_probs(i + 1).start())
        stage_attention_back(width, qkv, probs.at[lax.rem(i, 2)], stack, i)
        return 0

    lax.fori_loop(0, images, back, 0)
    later.wait("n1t")
    tile[...] = jnp.zeros_like(tile)
    project = functools.partial(stage_qkv_back, images, width, qkv, t_a, tile, flat, functools.partial(put, None), g_b)
    third = width // TILE

    def project_tile(c, _):
        for m in range(3):
            pl.when(c == m * third)(lambda m=m: act(11 + m))
        project(c)
        for m, r in enumerate((r_q, r_k, r_v)):
            pl.when(c == m * third + third - 1)(lambda r=r: r.begin())
        return 0

    lax.fori_loop(0, 3 * third, project_tile, 0)
    act(14)
    later.wait("w_qkv")
    stage_norm_back(width, flat, w_qkv, stack)
    later.start("act0", h_act.at[0], slots_[0])
    later.start("act1", h_act.at[1], slots_[1])
    later.start("down0", h_down.at[0], r_b)
    act(15)
    later.wait("token", "live")
    flights = []

    def put_patches(i, value):
        if i >= 2:
            flights[i - 2].wait()
        stage[i % 2] = value
        copy = pltpu.make_async_copy(stage.at[i % 2], gp.at[i], out_sem.at[i % 2])
        copy.start()
        flights.append(copy)

    stage_end(images, slots, width, keep, r_a, vectors.at[0:1, :], mid, live, stack, g_g1, g_s1, put_patches)
    later.start("middle", h_middle, mid)
    later.start("down1", h_down.at[1], r_a)
    act(16)
    v_home[...] = jnp.zeros_like(v_home)
    for j, (ref, base) in enumerate(((g_g1, 0), (g_s1, 0), (g_b, 0), (g_b, 2 * width), (g_bo, 0), (g_g2, 0), (g_s2, 0), (g_bd, 0))):
        row = ref[:, base : base + width]
        for f in range(8):
            v_home[f // 2, f % 2, j : j + 1, :96] = row[:, 96 * f : 96 * f + 96]
    for f in range(8):
        row = jnp.concatenate([s_bup[t, :, f * 128 : f * 128 + 128] for t in range(3)], axis=1)
        for j in range(4):
            v_home[f // 2, f % 2, 8 + j : 9 + j, :96] = row[:, 96 * j : 96 * j + 96]
    small.begin()
    act(17)
    later.wait("act0", "down0")
    add_products(width, stack, True, lambda cols: dot(slots_[0][...], r_b[:, cols]))
    later.start("act2", h_act.at[2], slots_[0])
    later.start("down2", h_down.at[2], r_b)
    small.step_core(v_sent)
    act(18)
    later.wait("act1", "down1")
    add_products(width, stack, False, lambda cols: dot(slots_[1][...], r_a[:, cols]))
    small.step_y(v_sent, v_total)
    act(19)
    later.wait("act2", "down2", "middle")
    add_products(width, stack, False, lambda cols: dot(slots_[0][...], r_b[:, cols]))
    small.step_x(v_total)
    act(20)
    stage_final(images, slots, width, mid, live, vectors.at[7:8, :], stack, out_tokens)
    small.step_line(e_small)
    act(21)
    act(22)
    for r in r_up + r_down:
        r.finish()
    for t in range(3):
        for c in range(2):
            for y in range(2):
                for f in range(4):
                    col = (4 * y + f) * 384 + t * 128
                    o_up[48 * c : 48 * c + 48, col : col + 128] = e_up[t, c, y, :, f * 128 : f * 128 + 128]
        o_down[t * 128 : t * 128 + 128, :] = e_down[t].reshape(width, 128).T
    half = width // 2

    def place_blocks(ref, base, e):
        for c in range(2):
            for y in range(2):
                ref[48 * c : 48 * c + 48, base + y * half : base + y * half + half] = e[c, y]

    r_out.finish()
    place_blocks(o_out, 0, e_out)
    for m, (r, e) in enumerate(((r_q, e_q), (r_k, e_k), (r_v, e_v))):
        r.finish()
        place_blocks(o_qkv, m * width, e)
    for copy in flights[-2:]:
        copy.wait()
    for r in r_up + r_down + [r_out, r_q, r_k, r_v, small]:
        r.drain()


def shards(
    linked,
    patches, keep, ln1_gain, ln1_bias, w_qkv, b_query, b_value, w_out, b_out,
    ln2_gain, ln2_bias, w_up, b_up, w_down, b_down, cotangent,
):
    images, slots = keep.shape
    width = patches.shape[2]
    hidden_width = w_up.shape[1]
    keep_pad = jnp.pad(keep, ((0, 0), (0, SLOT - slots)), constant_values=-1).reshape(images, 1, SLOT)
    part = ln1_gain.shape[0]
    singles = [v.reshape(1, part) for v in (ln1_gain, ln1_bias, b_query, b_value, b_out, ln2_gain, ln2_bias, b_down)]
    rows_low, rows_wide = ((ROWS, width), BF16), ((ROWS, width), F32)
    cols_low = ((width, ROWS), BF16)
    live_like, mask_like = ((ROWS, BLOCK), F32), ((images, SLOT, SLOT), F32)
    heads_like = ((images, SLOT, 3 * width), BF16)
    probs_like = ((images * H, SLOT, SLOT), BF16)
    row_like = ((1, width), F32)

    if linked:
        half = width // 2
        vec = jnp.concatenate(singles + [b_up.reshape(4, part)], axis=0)
        vec = jnp.pad(vec, ((0, 4), (0, BLOCK - part)))
        full = lambda v: ((v.shape[0] * 8, v.shape[1]), BF16)
        up3, down3, hid3 = ((3, width, THIRD), BF16), ((3, THIRD, width), BF16), ((3, ROWS, THIRD), BF16)
        gup_like, gdown_like = (4, 2, 2, 2, 48, THIRD // 2), (4, 2, 2, 2, width // 4, 128)
        outs = [
            ((16, width), F32), ((3, 1, THIRD), F32), rows_low, cols_low, rows_low, live_like, heads_like, probs_like, cols_low, rows_wide,
            full(w_qkv), full(w_out), up3, down3, hid3, hid3, (gup_like, BF16), (gdown_like, BF16), ((4, 2) + gup_like[3:], BF16), ((4, 2) + gdown_like[3:], BF16),
            ((4,) + gup_like[4:], BF16), ((4,) + gdown_like[4:], BF16),
        ]
        scratch = [
            rows_wide, rows_low, mask_like, rows_low, cols_low, rows_low, cols_low, live_like, heads_like, ((2, H, SLOT, SLOT), BF16), cols_low,
            rows_wide, full(w_qkv), full(w_out), up3, down3, ((3, part, THIRD), BF16), hid3[0][1:], hid3[0][1:], (2,) + gup_like, (2,) + gdown_like,
            (2, 4, 2) + gup_like[3:], (2, 4, 2) + gdown_like[3:],
        ]
        for r, w, first, other in ((48, THIRD // 2, (4, 48, 128), (4, 48, THIRD // 2 - 128)), (width // 4, 128, (4, 64, 128), (4, width // 4 - 64, 128))):
            scratch += [other, first, (4, r, w), (4, r, w)]
        scratch += [((8, 16, BLOCK), BF16), ((1, 3 * width), F32), ((3, 1, THIRD), F32)]
        scratch = [s if isinstance(s[0], tuple) else (s, BF16) for s in scratch]
        vectors, g_b_up, token, n1t, dm, live, qkv, probs, att_t, middle, qkv_full, out_full, up_full, down_full, act, dh, g_up, g_down, up1, down1, own_up, own_down = pl.pallas_call(
            functools.partial(first_kernel, images, slots, width),
            out_shape=[jax.ShapeDtypeStruct(*o) for o in outs],
            in_specs=[VMEM] * 8,
            out_specs=[VMEM] * 2 + [ANY] * 20,
            scratch_shapes=[pltpu.VMEM(*s) for s in scratch]
            + [pltpu.SemaphoreType.DMA((4, 28))] * 2
            + [pltpu.SemaphoreType.DMA((6, 28))] * 2
            + [pltpu.SemaphoreType.DMA((7,))] * 2
            + [pltpu.SemaphoreType.DMA((10,)), pltpu.SemaphoreType.DMA((33,)), pltpu.SemaphoreType.DMA((2,))]
            + [pltpu.SemaphoreType.DMA((4,))] * 2
            + [pltpu.SemaphoreType.DMA((2, 10))] * 2,
            compiler_params=pltpu.CompilerParams(vmem_limit_bytes=LIMIT, collective_id=0, has_side_effects=True),
            name="first",
        )(patches, keep_pad, cotangent, vec, w_qkv, w_out, w_up, w_down)
        final = lambda r, w, lead=(): (lead + (2, 2, r, w), BF16)
        attn = final(48, half)
        outs = [((images, slots, width), F32), ((images, slots, width), BF16), ((part, 3 * width), BF16), ((part, width), BF16), ((part, hidden_width), BF16), ((half, width), BF16), ((16, BLOCK), F32)]

        def buffers(r, w, by_rows, cut, cores, lead, lines):
            other = (4, r - cut, w) if by_rows else (4, r, w - cut)
            first = (4, cut, w) if by_rows else (4, r, cut)
            return [(cores + (4, 2, 2, r, w), BF16)] + [(lead + s, BF16) for s in (other, first, (4, r, w), (4, r, w))] + [(lines + (3, r, w), BF16)]

        scratch = [final(48, THIRD // 2, (3,)), final(width // 4, 128, (3,)), attn, attn, attn, attn]
        scratch += [rows_wide, ((ROWS, TILE), F32), ((ROWS, 3 * width), BF16), heads_like, ((2, H, SLOT, SLOT), BF16), cols_low, cols_low, rows_low, rows_low]
        scratch += [rows_wide, live_like, ((width, 3 * width), BF16), ((width, width), BF16), ((2, slots, width), F32), ((1, 3 * width), F32)] + [row_like] * 6
        scratch += [((4, 4, 2, 2, 2, 48, half), BF16)]
        scratch += [((2, 4, 2, 2, 48, THIRD // 2), BF16), ((4, 48, THIRD // 2), BF16)] + buffers(48, THIRD // 2, False, 128, (), (2,), (3,))
        scratch += [((2, 4, 2, 2, width // 4, 128), BF16), ((4, width // 4, 128), BF16)] + buffers(width // 4, 128, True, 64, (), (2,), (3,))
        scratch += buffers(48, half, False, 128, (4,), (4,), (4,))
        small_like, line_like = ((4, 2, 16, BLOCK), F32), ((3, 16, BLOCK), F32)
        scratch += [small_like, small_like, small_like, ((4, 16, BLOCK), F32), line_like, small_like, small_like]
        grad_patches, out_tokens, o_qkv, o_out, o_up, o_down, small = pl.pallas_call(
            functools.partial(second_kernel, images, slots, width),
            out_shape=[jax.ShapeDtypeStruct(*o) for o in outs],
            in_specs=[VMEM] * 3 + [ANY] * 20,
            out_specs=[ANY] + [VMEM] * 6,
            scratch_shapes=[pltpu.VMEM(*s) for s in scratch]
            + [pltpu.SemaphoreType.DMA((10, 10))] * 2
            + [pltpu.SemaphoreType.DMA((6,))] * 2
            + [pltpu.SemaphoreType.DMA((6,)), pltpu.SemaphoreType.DMA((22,)), pltpu.SemaphoreType.DMA((2,)), pltpu.SemaphoreType.DMA((2,))],
            compiler_params=pltpu.CompilerParams(vmem_limit_bytes=LIMIT, collective_id=1, has_side_effects=True),
            name="second",
        )(keep_pad, vectors, g_b_up, token, n1t, dm, live, qkv, probs, att_t, middle, qkv_full, out_full, up_full, down_full, act, dh, g_up, g_down, up1, down1, own_up, own_down)
        rows = small[:8, :part]
        sum_qkv, sum_out, sum_up, sum_down = (o.astype(F32) for o in (o_qkv, o_out, o_up, o_down))
        b_up_sum = small[8:12, :part].reshape(-1)
    else:
        gather = lambda v: lax.all_gather(v, "fsdp", axis=0, tiled=True)
        vectors = jnp.pad(gather(jnp.concatenate(singles, axis=0).T).T.astype(F32), ((0, 8), (0, 0)))
        bias_up = gather(b_up).astype(F32).reshape(1, hidden_width)
        qkv_full, out_full, up_full, down_full = gather(w_qkv), gather(w_out), gather(w_up), gather(w_down)
        outs = [rows_low, cols_low, rows_low, cols_low, live_like, heads_like, probs_like, cols_low, rows_wide, rows_low, cols_low]
        scratch = [rows_wide, rows_low, mask_like, rows_low, ((1, 3 * width), F32)]
        token, n1t, dm, dmt, live, qkv, probs, att_t, middle, n2, n2t = call(
            functools.partial(first_plain, images, slots, width),
            outs, scratch, (patches, keep_pad, cotangent, vectors, qkv_full, out_full), "first",
        )
        gain1, gain2, b_d = vectors[0:1], vectors[5:6], vectors[7:8]
        hid = ((ROWS, hidden_width), BF16)
        out_tokens, d_mid, d_low, g_up, g_down, g_b_up, g_g2, g_s2, g_bd, g_bo = call(
            functools.partial(second_plain, images, slots, width, hidden_width),
            [((images, slots, width), BF16), rows_wide, rows_low] + [((width, hidden_width), BF16)] * 2 + [((1, hidden_width), F32)] + [row_like] * 4,
            [hid, hid, rows_wide],
            (n2, n2t, dm, dmt, up_full, bias_up, down_full, b_d, middle, live, gain2),
            "second",
        )
        g_out, g_qkv, g_b, g_g1, g_s1, grad_patches = call(
            functools.partial(third_plain, images, slots, width),
            [((width, width), BF16), ((width, 3 * width), BF16), ((1, 3 * width), F32), row_like, row_like, ((images, slots, width), F32)],
            [rows_wide, ((ROWS, TILE), F32), ((ROWS, 3 * width), BF16), heads_like],
            (d_low, att_t, out_full, qkv, probs, n1t, qkv_full, token, gain1, d_mid, live, keep_pad),
            "third",
        )
        scat = lambda v, dim=0: lax.psum(lax.psum_scatter(v, "fsdp", scatter_dimension=dim, tiled=True), "dp").astype(F32)
        rows = jnp.concatenate([g_g1, g_s1, g_b[:, :width], g_b[:, 2 * width :], g_bo, g_g2, g_s2, g_bd], axis=0).astype(BF16)
        rows = scat(rows, 1)
        b_up_sum = scat(g_b_up.astype(BF16), 1)[0]
        sum_qkv, sum_out, sum_up, sum_down = scat(g_qkv), scat(g_out), scat(g_up), scat(g_down, 1).T
    return (
        out_tokens, grad_patches, rows[0], rows[1], sum_qkv, rows[2], rows[3], sum_out, rows[4],
        rows[5], rows[6], sum_up, b_up_sum, sum_down, rows[7],
    )


def solution(mesh):
    linked = (mesh.shape["fsdp"], mesh.shape["dp"]) == (8, 4)
    many, one, two = P(("fsdp", "dp"), None, None), P("fsdp"), P("fsdp", None)
    in_specs = (many, P(("fsdp", "dp"), None), one, one, two, one, one, two, one, one, one, two, one, two, one, many)
    out_specs = (many, many, one, one, two, one, one, two, one, one, one, two, one, two, one)
    return jax.shard_map(functools.partial(shards, linked), mesh=mesh, in_specs=in_specs, out_specs=out_specs, check_vma=False)
```

```python
import functools
import math

import jax
import jax.numpy as jnp
from jax import lax
from jax.experimental import pallas as pl
from jax.experimental.pallas import tpu as pltpu
from jax.sharding import PartitionSpec as P

H = 12
HD = 64
EPSILON = 1e-06
F32 = jnp.float32
BF16 = jnp.bfloat16
SLOT = 200
ROWS = 1024
BLOCK = 128
TILE = 256
NT = (((1,), (1,)), ((), ()))


def dot(left, right):
    return jnp.dot(left, right, preferred_element_type=F32)


def dot_nt(left, right):
    return lax.dot_general(left, right, NT, preferred_element_type=F32)


def tile_at(index, size):
    if isinstance(index, int):
        return pl.ds(index * size, size)
    return pl.ds(pl.multiple_of(index * size, size), size)


def loop(begin, end, body, unroll):
    if (end - begin) == unroll:
        for j in range(begin, end):
            body(j, 0)
        return

    def group(t, _):
        for u in range(unroll):
            body(begin + t * unroll + u, 0)
        return 0

    lax.fori_loop(0, (end - begin) // unroll, group, 0)


def norm_parts(values):
    centre = values - jnp.mean(values, axis=-1, keepdims=True)
    spread = jnp.mean(centre * centre, axis=-1, keepdims=True)
    inverse = lax.rsqrt(spread + EPSILON)
    return centre * inverse, inverse


def norm_back(hat, inverse, gain, grad):
    scaled = grad * gain
    along = jnp.mean(scaled * hat, axis=-1, keepdims=True)
    return inverse * (scaled - jnp.mean(scaled, axis=-1, keepdims=True) - hat * along)


def gelu_parts(hidden):
    size = jnp.abs(hidden)
    bell = jnp.exp(hidden * hidden * -0.5)
    t = 1.0 / (1.0 + size * (0.3275911 / math.sqrt(2.0)))
    tail = 1.061405429 * 0.5
    for term in (-1.453152027, 1.421413741, -0.284496736, 0.254829592):
        tail = tail * t + term * 0.5
    tail = tail * t * bell
    below = jnp.where(hidden >= 0, 1.0 - tail, tail)
    slope = below + hidden * (bell * (1.0 / math.sqrt(2.0 * math.pi)))
    return hidden * below, slope


def first_lanes(rows):
    return lax.broadcasted_iota(jnp.int32, (rows, 2 * HD), 1) < HD


def pad_keep(keep, padded):
    padded[...] = jnp.full_like(padded, -1)
    for i in range(keep.shape[0]):
        padded[i, :, : keep.shape[1]] = keep[i : i + 1, :]


def stage_gather(images, slots, patches, keep, stack, live, mask, token):
    stack[...] = jnp.zeros_like(stack)
    live[...] = jnp.zeros_like(live)

    def gather(i, _):
        row = keep[i]
        column = jnp.broadcast_to(row, (SLOT, SLOT)).T
        mask[i] = jnp.where(column >= 0, 0.0, -1e30)
        alive = (column >= 0).astype(F32)
        chosen = (column[:, :slots] == lax.broadcasted_iota(jnp.int32, (SLOT, slots), 1)).astype(F32).astype(BF16)
        rows = pl.ds(pl.multiple_of(i * SLOT, 8), SLOT)
        stack[rows, :] = dot(chosen, patches[i])
        live[rows, :] = alive[:, :BLOCK]
        return 0

    loop(0, images, gather, 1)

    def narrow(b, _):
        rows = tile_at(b, BLOCK)
        token[rows, :] = stack[rows, :].astype(BF16)
        return 0

    loop(0, ROWS // BLOCK, narrow, 2)


def stage_norm(gain, shift, token, normed, normed_t):
    def norm(b, _):
        rows = tile_at(b, BLOCK)
        hat, _ = norm_parts(token[rows, :].astype(F32))
        low = (hat * gain + shift).astype(BF16)
        normed[rows, :] = low
        normed_t[:, rows] = low.T
        return 0

    loop(0, ROWS // BLOCK, norm, 4)


def stage_grads(images, slots, width, cot, stack, live, dm, dm_t):
    stack[...] = jnp.zeros_like(stack)
    for i in range(images):
        stack[i * SLOT : i * SLOT + slots, :] = cot[i].astype(F32)

    def grads(b, _):
        rows = tile_at(b, BLOCK)
        low = (stack[rows, :] * jnp.concatenate([live[rows, :]] * (width // BLOCK), axis=1)).astype(BF16)
        dm[rows, :] = low
        dm_t[:, rows] = low.T
        return 0

    loop(0, ROWS // BLOCK, grads, 2)


def stage_qkv(images, width, normed, w_qkv, bias, qkv, begin, end):
    def body(c, _):
        cols = tile_at(c, TILE)
        scale = jnp.where(c < width // TILE, 1.0 / math.sqrt(HD), 1.0)
        values = (dot(normed[...], w_qkv[:, cols]) + bias[:, cols]) * scale
        for i in range(images):
            qkv[i, :, cols] = values[i * SLOT : (i + 1) * SLOT].astype(BF16)
        return 0

    loop(begin, end, body, 1)


def stage_attention(width, qkv, mask, probs, stack, i):
    low = first_lanes(SLOT)
    for p in range(H // 2):
        q2 = qkv[i, :, p * 128 : (p + 1) * 128]
        k2 = qkv[i, :, width + p * 128 : width + (p + 1) * 128]
        v2_t = qkv[i, :, 2 * width + p * 128 : 2 * width + (p + 1) * 128].T
        outs = []
        for h in range(2):
            qh = jnp.where(low if h == 0 else ~low, q2, jnp.zeros_like(q2))
            scores = dot_nt(k2, qh) + mask[i]
            exponent = jnp.exp(scores - jnp.max(scores, axis=0, keepdims=True))
            share = 1.0 / jnp.sum(exponent, axis=0, keepdims=True)
            prob = (exponent * share).astype(BF16)
            probs[2 * p + h] = prob
            outs.append(dot(v2_t[h * HD : (h + 1) * HD], prob))
        stack[pl.ds(pl.multiple_of(i * SLOT, 8), SLOT), p * 128 : (p + 1) * 128] = jnp.concatenate(outs, axis=0).T


def stage_out(width, stack, w_out, bias, token, gain, shift, att, att_t, middle, normed, normed_t):
    def low(b, _):
        rows = tile_at(b, BLOCK)
        values = stack[rows, :].astype(BF16)
        att[rows, :] = values
        att_t[:, rows] = values.T
        return 0

    loop(0, ROWS // BLOCK, low, 4)

    def body(c, _):
        cols = tile_at(c, TILE)
        middle[:, cols] = token[:, cols].astype(F32) + (dot(att[...], w_out[:, cols]) + bias[:, cols])
        return 0

    loop(0, width // TILE, body, 1)

    def norm(b, _):
        rows = tile_at(b, BLOCK)
        hat, _ = norm_parts(middle[rows, :])
        values = (hat * gain[...] + shift[...]).astype(BF16)
        normed[rows, :] = values
        normed_t[:, rows] = values.T
        return 0

    loop(0, ROWS // BLOCK, norm, 4)


def stage_mlp(width, normed, normed_t, dm, dm_t, w_up, b_up, w_down, act, dh, put_up, put_down, g_b_up, c):
    cols = tile_at(c, TILE)
    up, down, bias = w_up[:, cols], w_down[cols, :], b_up[:, cols]
    total, waiting = 0.0, []
    for r in range(ROWS // TILE + 1):
        if r < ROWS // TILE:
            rows = slice(r * TILE, (r + 1) * TILE)
            waiting.append((rows, dot(normed[rows, :], up) + bias, dot_nt(dm[rows, :], down)))
        if r:
            rows, hidden, d_act = waiting.pop(0)
            value, slope = gelu_parts(hidden)
            grad = (d_act * slope).astype(BF16)
            act[rows, cols] = value.astype(BF16)
            dh[rows, cols] = grad
            total = total + jnp.sum(grad.astype(F32), axis=0, keepdims=True)
    g_b_up[:, cols] = total
    put_up(c, dot(normed_t[...], dh[:, cols]).astype(BF16))
    put_down(c, dot(dm_t[...], act[:, cols]).astype(BF16))


def add_products(width, stack, fresh, product):
    def body(c, _):
        cols = tile_at(c, TILE)
        value = product(cols)
        stack[:, cols] = value if fresh else stack[:, cols] + value
        return 0

    loop(0, width // TILE, body, 1)


def stage_final(images, slots, width, middle, live, b_down, stack, out):
    def final(b, _):
        rows = tile_at(b, BLOCK)
        stack[rows, :] = (middle[rows, :] + (stack[rows, :] + b_down[...])) * jnp.concatenate([live[rows, :]] * (width // BLOCK), axis=1)
        return 0

    loop(0, ROWS // BLOCK, final, 2)
    for i in range(images):
        out[i] = stack[i * SLOT : i * SLOT + slots, :].astype(BF16)


def stage_middle_back(middle, gain, dm, stack, d_mid_low, g_gain, g_shift, g_b_down, g_b_out):
    for ref in (g_gain, g_shift, g_b_down, g_b_out):
        ref[...] = jnp.zeros_like(ref)

    def back(b, _):
        rows = tile_at(b, BLOCK)
        grad = stack[rows, :]
        hat, inverse = norm_parts(middle[rows, :])
        g_gain[...] += jnp.sum(grad * hat, axis=0, keepdims=True)
        g_shift[...] += jnp.sum(grad, axis=0, keepdims=True)
        own = dm[rows, :].astype(F32)
        g_b_down[...] += jnp.sum(own, axis=0, keepdims=True)
        total = own + norm_back(hat, inverse, gain[...], grad)
        middle[rows, :] = total
        low = total.astype(BF16)
        d_mid_low[rows, :] = low
        g_b_out[...] += jnp.sum(low.astype(F32), axis=0, keepdims=True)
        return 0

    loop(0, ROWS // BLOCK, back, 2)


def stage_out_back(width, att_t, d_mid_low, w_out, put_out, stack):
    def body(c, _):
        cols = tile_at(c, TILE)
        put_out(c, dot(att_t[...], d_mid_low[:, cols]).astype(BF16))
        stack[:, cols] = dot_nt(d_mid_low[...], w_out[cols, :])
        return 0

    loop(0, width // TILE, body, 1)


def stage_attention_back(width, qkv, probs, stack, i):
    low = first_lanes(SLOT)
    for p in range(H // 2):
        at_q = slice(p * 128, (p + 1) * 128)
        at_k = slice(width + p * 128, width + (p + 1) * 128)
        at_v = slice(2 * width + p * 128, 2 * width + (p + 1) * 128)
        q2, k2, v2 = qkv[i, :, at_q], qkv[i, :, at_k], qkv[i, :, at_v]
        k2_t = k2.T
        da = stack[pl.ds(pl.multiple_of(i * SLOT, 8), SLOT), at_q].astype(BF16)
        dq, dk, dv = [], 0.0, 0.0
        for h in range(2):
            pick = lambda m: jnp.where(low if h == 0 else ~low, m, jnp.zeros_like(m))
            prob = probs[2 * p + h]
            d_prob = dot_nt(pick(v2), da)
            mixed = prob.astype(F32)
            moved = mixed * d_prob
            total = jnp.sum(moved, axis=0, keepdims=True)
            ds = (moved - mixed * total).astype(BF16)
            dq.append(dot(k2_t[h * HD : (h + 1) * HD], ds))
            dk = dk + dot(ds, pick(q2))
            dv = dv + dot(prob, pick(da))
        qkv[i, :, at_q] = (jnp.concatenate(dq, axis=0).T * (1.0 / math.sqrt(HD))).astype(BF16)
        qkv[i, :, at_k] = dk.astype(BF16)
        qkv[i, :, at_v] = dv.astype(BF16)


def stage_qkv_back(images, width, d_qkv, normed_t, tile, flat, put_qkv, g_b_qkv, c):
    cols = tile_at(c, TILE)
    for i in range(images):
        tile[i * SLOT : (i + 1) * SLOT, :] = d_qkv[i, :, cols].astype(F32)
    values = tile[...]
    g_b_qkv[:, cols] = jnp.sum(values, axis=0, keepdims=True)
    low = values.astype(BF16)
    flat[:, cols] = low
    put_qkv(c, dot(normed_t[...], low).astype(BF16))


def stage_norm_back(width, flat, w_qkv, stack):
    def body(c, _):
        cols = tile_at(c, TILE)
        stack[:, cols] = dot_nt(flat[...], w_qkv[cols, :])
        return 0

    loop(0, width // TILE, body, 1)


def stage_end(images, slots, width, keep, token, gain, middle, live, stack, g_gain, g_shift, put_patches):
    for ref in (g_gain, g_shift):
        ref[...] = jnp.zeros_like(ref)

    def back(b, _):
        rows = tile_at(b, BLOCK)
        grad = stack[rows, :]
        hat, inverse = norm_parts(token[rows, :].astype(F32))
        g_gain[...] += jnp.sum(grad * hat, axis=0, keepdims=True)
        g_shift[...] += jnp.sum(grad, axis=0, keepdims=True)
        total = middle[rows, :] + norm_back(hat, inverse, gain[...], grad)
        stack[rows, :] = total * jnp.concatenate([live[rows, :]] * (width // BLOCK), axis=1)
        return 0

    loop(0, ROWS // BLOCK, back, 2)

    def scatter(i, _):
        chosen = (lax.broadcasted_iota(jnp.int32, (slots, SLOT), 0) == keep[i]).astype(F32).astype(BF16)
        values = stack[pl.ds(pl.multiple_of(i * SLOT, 8), SLOT), :]
        high = values.astype(BF16)
        rest = (values - high.astype(F32)).astype(BF16)
        put_patches(i, dot(chosen, high) + dot(chosen, rest))
        return 0

    for i in range(images):
        scatter(i, 0)


MESH = pl.DeviceIdType.MESH


class Place:
    def __init__(self):
        f, d = lax.axis_index("fsdp"), lax.axis_index("dp")
        self.z, self.x = f // 2, lax.rem(f, 2)
        self.y, self.c = d // 2, lax.rem(d, 2)
        z = self.z
        self.zs = [z, z + 1 - 2 * lax.rem(z, 2), lax.rem(z + 2, 4), 3 - z]
        self.ox, self.oy, self.oc = 1 - self.x, 1 - self.y, 1 - self.c
        self.beside = self.to(x=self.ox), self.to(y=self.oy), self.to(c=self.oc)
        self.along = [self.to(z=k) for k in self.zs]

    def to(self, z=None, x=None, y=None, c=None):
        z, x, y, c = (own if new is None else new for new, own in ((z, self.z), (x, self.x), (y, self.y), (c, self.c)))
        return (z * 2 + x, y * 2 + c)

    def sides(self):
        return self.beside


def enter(peers, meanwhile=None):
    barrier = pltpu.get_barrier_semaphore()
    for peer in peers:
        pl.semaphore_signal(barrier, inc=1, device_id=peer, device_id_type=MESH)
    if meanwhile is not None:
        meanwhile()
    pl.semaphore_wait(barrier, len(peers))


class Gather:
    def __init__(self, place, shard, full, first_cols, send, recv):
        self.place, self.shard, self.full, self.send, self.recv = place, shard, full, send, recv
        self.rows, cols = shard.shape
        self.half, self.wide, self.cut = self.rows // 2, cols // 2, first_cols
        self.started = []

    def spot(self, *args):
        return lambda: self.place_of(*args)

    def place_of(self, z, x, y, part=None, local=False):
        p = self.place
        base = 0 if local else (z * 2 + x) * self.rows
        rows = pl.ds(pl.multiple_of(base + p.c * self.half, 16), self.half)
        if y is None:
            return rows, slice(None)
        start, size = (y * self.wide, self.wide) if part is None else ((y * self.wide, self.cut) if part == 0 else (y * self.wide + self.cut, self.wide - self.cut))
        return rows, pl.ds(pl.multiple_of(start, 128), size)

    def copy(self, spot, sem, peer, local=None):
        src = self.full.at[spot] if local is None else self.shard.at[local]
        return pltpu.make_async_remote_copy(
            src_ref=src, dst_ref=self.full.at[spot], send_sem=self.send.at[sem], recv_sem=self.recv.at[sem], device_id=peer, device_id_type=MESH
        )

    def start(self, spot, sem, peer, local=None):
        def make():
            return self.copy(spot(), sem, peer, None if local is None else local())

        make().start()
        self.started.append(make)

    def arrived(self, spot, sem):
        self.copy(spot(), sem, self.place.sides()[0]).wait_recv()

    def own(self, sem):
        p = self.place
        rows = pl.ds(pl.multiple_of((p.z * 2 + p.x) * self.rows, 16), self.rows)
        return pltpu.make_async_copy(self.shard, self.full.at[rows, :], sem)

    def lines(self, *ks):
        p = self.place
        spot, local = self.spot(p.z, p.x, p.y), self.spot(p.z, p.x, p.y, None, True)
        for k in ks:
            self.start(spot, k, p.along[k], local)

    def beside(self):
        p = self.place
        side_x, side_y, _ = p.sides()
        self.start(self.spot(p.z, p.x, p.y), 4, side_x, self.spot(p.z, p.x, p.y, None, True))
        self.start(self.spot(p.z, p.x, p.oy, 1), 16, side_x, self.spot(p.z, p.x, p.oy, 1, True))

    def phase(self, name):
        if name == "own":
            self.beside()
        elif name == "zs":
            self.lines(1, 2, 3)
        elif name[0] == "z":
            self.lines(int(name[1]))
        elif name in ("spread", "cross", "share"):
            for k in range(name == "spread", 4):
                getattr(self, name)(k)
        else:
            (self.spread if name[0] == "s" else self.cross)(int(name[1]))

    def spread(self, k):
        p = self.place
        side_x, side_y, _ = p.sides()
        spot = self.spot(p.zs[k], p.x, p.y)
        self.arrived(spot, k)
        self.start(spot, 4 + k, side_x)
        self.start(spot, 8 + k, side_y)

    def cross(self, k):
        p = self.place
        side_x, side_y, _ = p.sides()
        self.arrived(self.spot(p.zs[k], p.ox, p.y), 4 + k)
        self.start(self.spot(p.zs[k], p.ox, p.y, 0), 12 + k, side_y)
        if k:
            self.arrived(self.spot(p.zs[k], p.x, p.oy), 8 + k)
            self.start(self.spot(p.zs[k], p.x, p.oy, 1), 16 + k, side_x)

    def share(self, k):
        p = self.place
        core = p.sides()[2]
        if k:
            self.start(self.spot(p.zs[k], p.x, None), 20 + k, core)
        self.arrived(self.spot(p.zs[k], p.ox, p.oy, 0), 12 + k)
        self.arrived(self.spot(p.zs[k], p.ox, p.oy, 1), 16 + k)
        self.start(self.spot(p.zs[k], p.ox, None), 24 + k, core)

    def finish(self):
        p = self.place

        def other(z, x):
            return lambda: (pl.ds(pl.multiple_of((z * 2 + x) * self.rows + (p.oc) * self.half, 16), self.half), slice(None))

        for k in range(4):
            if k:
                self.arrived(other(p.zs[k], p.x), 20 + k)
            self.arrived(other(p.zs[k], p.ox), 24 + k)

    def drain(self):
        for make in self.started:
            make().wait_send()


class Reduce:
    def __init__(self, place, source, held, core, diag_x, diag_y, side_x, side_y, line, final, send, recv):
        self.place, self.source, self.held, self.core = place, source, held, core
        self.diag_x, self.diag_y, self.side_x, self.side_y, self.line, self.final = diag_x, diag_y, side_x, side_y, line, final
        self.send, self.recv, self.started = send, recv, []
        self.own4 = self.own = None
        if diag_y is not None:
            self.rows, self.wide = side_x.shape[1:]
            self.by_rows = diag_y.shape[2] == self.wide
            self.cut = diag_y.shape[1] if self.by_rows else diag_y.shape[2]

    def part(self, second):
        bounds = pl.ds(self.cut, (self.rows if self.by_rows else self.wide) - self.cut) if second else pl.ds(0, self.cut)
        return (bounds, slice(None)) if self.by_rows else (slice(None), bounds)

    def hold(self, z, x, y, *rest):
        if self.held is None:
            return (z, x, self.place.c, y) + rest
        return (z, x, y) + rest

    @property
    def home(self):
        return self.source if self.held is None else self.held

    def copy(self, src, dst, sem, peer):
        return pltpu.make_async_remote_copy(src_ref=src, dst_ref=dst, send_sem=self.send.at[sem], recv_sem=self.recv.at[sem], device_id=peer, device_id_type=MESH)

    def start(self, src, dst, sem, peer):
        def make():
            return self.copy(src(), dst() if callable(dst) else dst, sem, peer)

        make().start()
        self.started.append(make)

    def arrived(self, dst, sem):
        self.copy(dst, dst, sem, self.place.sides()[0]).wait_recv()

    def begin(self, own=None):
        p = self.place
        self.start(lambda: self.source.at[:, :, p.oc], self.core, 0, p.sides()[2])
        self.own = own
        if own is not None:
            own.start()

    def add_core(self, x, y):
        def body(z, _):
            spot = self.hold(z, x, y)
            self.home[spot] = self.home[spot] + self.core[z, x, y]
            return 0

        lax.fori_loop(0, 4, body, 0)

    def add(self, x, y, part, buffer):
        def body(z, _):
            spot = self.hold(z, x, y, *part)
            self.home[spot] = self.home[spot] + buffer[z]
            return 0

        lax.fori_loop(0, 4, body, 0)

    def step_core(self):
        p = self.place
        side_x, side_y, _ = p.sides()
        if self.own is not None:
            self.own.wait()
        self.arrived(self.core, 0)
        for x, y in ((p.ox, p.oy), (p.ox, p.y), (p.x, p.oy), (p.x, p.y)):
            self.add_core(x, y)

    def step_open(self):
        p = self.place
        side_x, side_y, _ = p.sides()
        every = slice(None)
        self.start(lambda: self.home.at[self.hold(every, p.ox, p.oy, *self.part(True))], self.diag_x, 1, side_x)
        self.start(lambda: self.home.at[self.hold(every, p.ox, p.oy, *self.part(False))], self.diag_y, 2, side_y)

    def step_diag(self):
        p = self.place
        side_x, side_y, _ = p.sides()
        every = slice(None)
        self.arrived(self.diag_y, 2)
        self.add(p.ox, p.y, self.part(False), self.diag_y)
        self.start(lambda: self.home.at[self.hold(every, p.ox, p.y)], self.side_x, 3, side_x)
        self.arrived(self.diag_x, 1)
        self.add(p.x, p.oy, self.part(True), self.diag_x)
        self.start(lambda: self.home.at[self.hold(every, p.x, p.oy)], self.side_y, 4, side_y)

    def step_sum(self):
        p = self.place
        whole = (slice(None), slice(None))
        self.arrived(self.side_x, 3)
        self.add(p.x, p.y, whole, self.side_x)
        self.arrived(self.side_y, 4)
        self.add(p.x, p.y, whole, self.side_y)

    def mine(self, z):
        if self.own4 is not None:
            return self.own4.at[z]
        return self.home.at[self.hold(z, self.place.x, self.place.y)]

    def step_send(self):
        p = self.place
        for k in (1, 2, 3):
            self.start(lambda k=k: self.mine(p.zs[k]), lambda k=k: self.line.at[k - 1], 4 + k, p.along[k])

    def step_side(self):
        self.step_sum()
        self.step_send()

    def step_line(self):
        p = self.place
        total = self.mine(p.z)[...].astype(F32)
        for k in (1, 2, 3):
            self.arrived(self.line.at[k - 1], 4 + k)
            total = total + self.line[k - 1].astype(F32)
        self.final[p.c, p.y] = total.astype(BF16)
        self.start(lambda: self.final.at[p.c, p.y], lambda: self.final.at[p.c, p.y], 8, p.sides()[1])

    def step_share(self):
        p = self.place
        self.arrived(self.final.at[p.c, p.oy], 8)
        self.start(lambda: self.final.at[p.c], lambda: self.final.at[p.c], 9, p.sides()[2])

    def finish(self):
        self.arrived(self.final.at[self.place.oc], 9)

    def drain(self):
        for make in self.started:
            make().wait_send()


class SmallReduce:
    def __init__(self, place, home, core, side_y, side_x, line, send, recv):
        self.place, self.home, self.core, self.side_y, self.side_x, self.line = place, home, core, side_y, side_x, line
        self.send, self.recv, self.started = send, recv, []

    copy, start, arrived, drain = Reduce.copy, Reduce.start, Reduce.arrived, Reduce.drain

    def begin(self):
        self.start(lambda: self.home, self.core, 0, self.place.sides()[2])

    def step_core(self, sent):
        p = self.place
        self.arrived(self.core, 0)
        sent[...] = self.home[...] + self.core[...]
        self.start(lambda: sent, self.side_y, 1, p.sides()[1])

    def step_y(self, sent, total):
        p = self.place
        self.arrived(self.side_y, 1)
        total[...] = sent[...] + self.side_y[...]
        self.start(lambda: total.at[:, p.ox], self.side_x, 2, p.sides()[0])

    def step_x(self, total):
        p = self.place
        self.arrived(self.side_x, 2)
        for z in range(4):
            self.side_x[z] = self.side_x[z] + total[z, p.x]
        for k in (1, 2, 3):
            self.start(lambda k=k: self.side_x.at[p.zs[k]], lambda k=k: self.line.at[k - 1], 2 + k, p.along[k])

    def step_line(self, out):
        total = self.side_x[self.place.z]
        for k in (1, 2, 3):
            self.arrived(self.line.at[k - 1], 2 + k)
            total = total + self.line[k - 1]
        out[...] = total


GATHER_PLAN = (
    (("k", "own"), ("v", "own"), ("o", "own"), ("p0", "own"), ("q", "z1"), ("k", "z1"), ("q", "z2"), ("k", "z2"), ("k", "z3"), ("q", "s1"), ("k", "s1"),),
    (("v", "z1"), ("q", "z3"), ("k", "c0"), ("k", "s3"),),
    (("v", "z2"), ("v", "z3"),),
    (),
    (("v", "s1"), ("q", "s2"), ("q", "c1"),),
    (("o", "zs"), ("k", "s2"), ("q", "s3"),),
    (("q", "own"), ("p0", "zs"), ("v", "c0"), ("v", "s2"), ("v", "s3"), ("k", "c2"), ("q", "c3"), ("k", "c3"),),
    (("q", "c0"), ("v", "c1"), ("q", "c2"), ("v", "c2"), ("v", "c3"),),
    (("k", "c1"), ("o", "spread"), ("q", "share"), ("k", "share"),),
    (("p1", "own"), ("p1", "zs"), ("o", "cross"), ("v", "share"),),
    (("p0", "spread"),),
    (),
    (),
    (("p2", "zs"), ("p1", "spread"), ("p0", "cross"), ("o", "share"),),
    (),
    (("p2", "own"),),
    (("p1", "cross"), ("p0", "share"),),
    (("p2", "spread"),),
    (),
    (),
    (("p1", "share"),),
    (("p2", "cross"),),
    (),
    (),
    (("p2", "share"),),
    (),
    (),
    (),
    (),
    (),
)
MERGE_PLAN = (22, 25, 26)
REDUCE_PLAN = (
    ("m0", (13, 14)),
    ("m1", (0, 4, 10, 20, 22)),
    ("m2", (3, 8, 13, 20, 22)),
    ("o", (12, 15, 18, 20, 22)),
    ("q", (13, 14, 16, 19, 21)),
    ("k", (14, 16, 19, 22, 22)),
    ("v", (14, 18, 20, 22, 22)),
)


VMEM = pl.BlockSpec(memory_space=pltpu.VMEM)
ANY = pl.BlockSpec(memory_space=pl.ANY)
LIMIT = 61 * 1024 * 1024
THIRD = 1024


def call(body, outs, scratch, args, name):
    return pl.pallas_call(
        body,
        out_shape=[jax.ShapeDtypeStruct(*o) for o in outs],
        in_specs=[VMEM] * len(args),
        out_specs=[VMEM] * len(outs),
        scratch_shapes=[pltpu.VMEM(*s) for s in scratch],
        compiler_params=pltpu.CompilerParams(vmem_limit_bytes=LIMIT),
        name=name,
    )(*args)


class Later:
    def __init__(self, sems):
        self.sems, self.flights = sems, {}

    def start(self, name, src, dst):
        self.plan(name, src, dst)
        self.flights[name]().start()

    def plan(self, name, src, dst):
        sem = len(self.flights)

        def make():
            return pltpu.make_async_copy(*(r() if callable(r) else r for r in (src, dst)), self.sems.at[sem])

        self.flights[name] = make

    def wait(self, *names):
        for name in names:
            self.flights[name]().wait()


def first_plain(
    images, slots, width, patches, keep, cot, vectors, w_qkv, w_out,
    token, n1t, dm, dmt, live, qkv, probs, att_t, middle, n2, n2t, stack, normed, mask, att, bias,
):
    bias[...] = jnp.concatenate([vectors[2:3, :], jnp.zeros((1, width), F32), vectors[3:4, :]], axis=1)
    stage_gather(images, slots, patches, keep, stack, live, mask, token)
    stage_norm(vectors[0:1, :], vectors[1:2, :], token, normed, n1t)
    stage_grads(images, slots, width, cot, stack, live, dm, dmt)
    stage_qkv(images, width, normed, w_qkv, bias, qkv, 0, 3 * width // TILE)
    for i in range(images):
        stage_attention(width, qkv, mask, probs.at[pl.ds(i * H, H)], stack, i)
    stage_out(width, stack, w_out, vectors.at[4:5, :], token, vectors.at[5:6, :], vectors.at[6:7, :], att, att_t, middle, n2, n2t)


def first_kernel(
    images, slots, width,
    h_patches, keep_in, h_cot, *rest,
):
    singles, rest = rest[:9], rest[9:]
    first_body(images, slots, width, h_patches, keep_in, h_cot, singles, *rest)


def first_body(
    images, slots, width,
    h_patches, keep_in, h_cot, singles, s_qkv, s_out, s_up, s_down,
    vectors, g_b_up, h_token, h_n1t, h_dm, h_live, h_qkv, h_probs, h_att_t, h_middle, h_wqkv, h_wout, h_up, h_down, h_act, h_dh, h_gup, h_gdown, h_up1, h_down1, h_own_up, h_own_down,
    patches, keep, cot, vec_wide, vec, stack, normed, mask, token, n1t, dm, dmt, live, qkv, probs, att_t, middle, f_qkv, f_out, f_up, f_down, s_up3, act_, dh, g_up, g_down, up_core, down_core, up_dx, up_dy, up_sx, up_sy, dn_dx, dn_dy, dn_sx, dn_sy,
    vecs, bias, b_up, q_send, q_recv, m_send, m_recv, v_send, v_recv, own, saves, probs_sem, r_send, r_recv, w_send, w_recv,
):
    place = Place()
    _, side_y, side_c = place.sides()
    flat = [place.to(z=place.zs[k], x=x) for k in range(4) for x in (place.x, place.ox)][1:]
    later = Later(saves)
    loads = [pltpu.make_async_copy(h_patches, patches, own.at[10]), pltpu.make_async_copy(h_cot, cot, own.at[11])]

    def before():
        for load in loads:
            load.start()
        pad_keep(keep_in, keep)
        vec_wide[...] = jnp.zeros_like(vec_wide)
        for j in range(8):
            vec_wide[j : j + 1, :96] = singles[j][...].astype(F32)
        for j in range(4):
            vec_wide[8 + j : 9 + j, :96] = singles[8][:, 96 * j : 96 * j + 96].astype(F32)
        vec[...] = vec_wide[...].astype(BF16)
        loads[0].wait()
        for t in range(3):
            for f in range(8):
                s_up3[t, :, f * 128 : f * 128 + 128] = s_up[:, f * 384 + t * 128 : f * 384 + t * 128 + 128]
        stage_gather(images, slots, patches, keep, stack, live, mask, token)
        later.start("live", live, h_live)
        later.start("token", token, h_token)
        loads[1].wait()
        stage_grads(images, slots, width, cot, stack, live, dm, dmt)
        later.start("dm", dm, h_dm)

    enter(flat + [side_y, side_c], before)
    columns = [slice(m * width, (m + 1) * width) for m in range(3)]
    g_qkv = [Gather(place, s_qkv.at[:, columns[m]], f_qkv.at[:, columns[m]], 128 if m == 2 else 256, q_send.at[m], q_recv.at[m]) for m in range(3)]
    g_out = Gather(place, s_out, f_out, 256, q_send.at[3], q_recv.at[3])
    g_ups = [Gather(place, s_up3.at[t], f_up.at[t], (256, 384, 256)[t], m_send.at[t], m_recv.at[t]) for t in range(3)]
    g_downs = [Gather(place, s_down.at[t * 128 : t * 128 + 128], f_down.at[t], 256, m_send.at[3 + t], m_recv.at[3 + t]) for t in range(3)]
    groups = {"q": g_qkv[:1], "k": g_qkv[1:2], "v": g_qkv[2:], "o": [g_out]}
    groups.update({f"p{t}": [g_ups[t], g_downs[t]] for t in range(3)})
    every = g_qkv + [g_out] + [g for t in range(3) for g in (g_ups[t], g_downs[t])]
    mine = place.z * 2 + place.x
    tiny = []
    for j, peer in enumerate(flat):
        copy = pltpu.make_async_remote_copy(src_ref=vec, dst_ref=vecs.at[mine], send_sem=v_send.at[j], recv_sem=v_recv.at[j], device_id=peer, device_id_type=MESH)
        copy.start()
        tiny.append(copy)
    vecs[mine] = vec[...]
    core = place.sides()[2]
    swaps = {
        (name, t): pltpu.make_async_remote_copy(
            src_ref=g.at[t, :, :, place.oc], dst_ref=buffer.at[t], send_sem=r_send.at[2 * t + j], recv_sem=r_recv.at[2 * t + j], device_id=core, device_id_type=MESH
        )
        for t in range(2)
        for j, (name, g, buffer) in enumerate((("up", g_up, up_core), ("down", g_down, down_core)))
    }
    early = (
        Reduce(place, None, up_core.at[0], None, up_dx, up_dy, up_sx, up_sy, None, None, w_send.at[0], w_recv.at[0]),
        Reduce(place, None, down_core.at[0], None, dn_dx, dn_dy, dn_sx, dn_sy, None, None, w_send.at[1], w_recv.at[1]),
    )

    def merge(t):
        for name, g, buffer in (("up", g_up, up_core), ("down", g_down, down_core)):
            swaps[name, t].wait_recv()

            def body(z, _, g=g, buffer=buffer):
                buffer[t, z] = buffer[t, z] + g[t, z, :, place.c]
                return 0

            lax.fori_loop(0, 4, body, 0)
        if t == 0:
            for r in early:
                r.step_open()
        else:
            later.start("up_sum1", lambda: up_core.at[1], h_up1)
            later.start("down_sum1", lambda: down_core.at[1], h_down1)

    def act(slot):
        for group, phase in GATHER_PLAN[slot]:
            for g in groups[group]:
                g.phase(phase)
        if slot == MERGE_PLAN[0]:
            merge(0)
        if slot == MERGE_PLAN[1]:
            for r in early:
                r.step_diag()
        if slot == MERGE_PLAN[2]:
            merge(1)

    act(0)
    locals_ = [g.own(own.at[j]) for j, g in enumerate(every)]
    for copy in locals_:
        copy.start()
    for slot in range(1, 5):
        act(slot)
    for copy in tiny:
        copy.wait_recv()
    vectors[...] = jnp.concatenate([vecs[f][:, :96] for f in range(8)], axis=1).astype(F32)
    act(5)
    stage_norm(vectors[0:1, :], vectors[1:2, :], token, normed, n1t)
    later.start("n1t", n1t, h_n1t)
    for f in range(8):
        row = jnp.concatenate([vecs[f][8 + j : 9 + j, :96] for j in range(4)], axis=1).astype(F32)
        for t in range(3):
            b_up[t, :, f * 128 : f * 128 + 128] = row[:, t * 128 : t * 128 + 128]
    bias[...] = jnp.concatenate([vectors[2:3, :], jnp.zeros((1, width), F32), vectors[3:4, :]], axis=1)
    act(6)
    act(7)
    for m in range(3):
        act(8 + m)
        locals_[m].wait()
        g_qkv[m].finish()
        stage_qkv(images, width, normed, f_qkv, bias, qkv, m * width // TILE, (m + 1) * width // TILE)
    later.start("w_qkv", f_qkv, h_wqkv)
    later.start("qkv", qkv, h_qkv)

    def save_probs(slot, i):
        return pltpu.make_async_copy(probs.at[slot], h_probs.at[pl.ds(i * H, H)], probs_sem.at[slot])

    def attend(i, _):
        slot = lax.rem(i, 2)
        for j in range(5):
            pl.when(i == j)(lambda j=j: act(11 + j))
        pl.when(i >= 2)(lambda: save_probs(slot, i - 2).wait())
        stage_attention(width, qkv, mask, probs.at[slot], stack, i)
        save_probs(slot, i).start()
        return 0

    lax.fori_loop(0, images, attend, 0)
    for i in range(images - 2, images):
        save_probs(i % 2, i).wait()
    act(16)
    locals_[3].wait()
    g_out.finish()
    later.start("w_out", f_out, h_wout)
    later.wait("n1t")
    n2t = n1t
    stage_out(width, stack, f_out, vectors.at[4:5, :], token, vectors.at[5:6, :], vectors.at[6:7, :], normed, att_t, middle, normed, n2t)
    later.start("att_t", att_t, h_att_t)
    later.start("middle", middle, h_middle)
    for t in range(3):
        for part in range(2):
            for name, src, dst in (("act", act_, h_act), ("dh", dh, h_dh)):
                cols = slice(part * 512, part * 512 + 512)
                later.plan(f"{name}{t}{part}", lambda src=src, cols=cols: src.at[:, cols], lambda dst=dst, t=t, cols=cols: dst.at[t, :, cols])

    def enter_third(t):
        locals_[4 + 2 * t].wait()
        locals_[5 + 2 * t].wait()
        g_ups[t].finish()
        g_downs[t].finish()
        later.start(f"up{t}", lambda: f_up.at[t], lambda: h_up.at[t])
        later.start(f"down{t}", lambda: f_down.at[t], lambda: h_down.at[t])
        if t:
            later.wait(f"act{t - 1}0", f"dh{t - 1}0")
        if t == 2:
            for name in ("up", "down"):
                swaps[name, 0].wait_send()

    def middle_third(t):
        if t:
            later.wait(f"act{t - 1}1", f"dh{t - 1}1")

    def save_part(t, part):
        later.flights[f"act{t}{part}"]().start()
        later.flights[f"dh{t}{part}"]().start()
        if part and t < 2:
            swaps["up", t].start()
            swaps["down", t].start()
        elif part:
            later.start("g_up2", lambda: g_up.at[0], h_gup)
            later.start("g_down2", lambda: g_down.at[0], h_gdown)

    def feed(step, _):
        t, c = step // 4, step % 4
        slot = t % 2
        for j in range(12):
            if GATHER_PLAN[17 + j] or 17 + j in MERGE_PLAN:
                pl.when(step == j)(lambda j=j: act(17 + j))
        for j in range(3):
            pl.when(step == 4 * j)(lambda j=j: enter_third(j))
            pl.when(step == 4 * j + 2)(lambda j=j: middle_third(j))

        def put_up(c, value):
            y, at = c // 2, tile_at(c % 2, TILE)
            g_up[slot, :, :, :, y, :, at] = value.reshape(4, 2, 2, 48, TILE)

        def put_down(c, value):
            for x in range(2):
                g_down[slot, c, x] = value[:, x * 128 : (x + 1) * 128].reshape(2, 2, 192, 128)

        stage_mlp(width, normed, n2t, dm, dmt, f_up.at[t], b_up.at[t], f_down.at[t], act_, dh, put_up, put_down, g_b_up.at[t], c)
        for j in range(3):
            for part in range(2):
                pl.when(step == 4 * j + 2 * part + 1)(lambda j=j, part=part: save_part(j, part))
        return 0

    lax.fori_loop(0, 12, feed, 0)
    act(29)
    for r, h, buffer in ((early[0], h_own_up, up_core), (early[1], h_own_down, down_core)):
        r.step_sum()
        later.start(f"own{h is h_own_up}", buffer.at[0, :, place.x, place.y], h)
    waited = {"n1t"} | {f"{n}{t}{p}" for n in ("act", "dh") for t in range(2) for p in range(2)}
    for name in ("up", "down"):
        swaps[name, 1].wait_send()
    later.wait(*(n for n in later.flights if n not in waited))
    for copy in tiny:
        copy.wait_send()
    for g in every + list(early):
        g.drain()


def second_plain(
    images, slots, width, hidden_width,
    n2, n2t, dm, dmt, w_up, b_up, w_down, b_d, middle_in, live, gain2,
    out, middle, d_low, g_up, g_down, g_b_up, g_g2, g_s2, g_bd, g_bo, act, dh, stack,
):
    middle[...] = middle_in[...]

    def put(ref, c, value):
        ref[:, tile_at(c, TILE)] = value

    feed = functools.partial(stage_mlp, width, n2, n2t, dm, dmt, w_up, b_up, w_down, act, dh, functools.partial(put, g_up), functools.partial(put, g_down), g_b_up)
    loop(0, hidden_width // TILE, lambda c, _: feed(c), 1)
    add_products(width, stack, True, lambda cols: dot(act[...], w_down[:, cols]))
    stage_final(images, slots, width, middle, live, b_d, stack, out)
    add_products(width, stack, True, lambda cols: dot_nt(dh[...], w_up[cols, :]))
    stage_middle_back(middle, gain2, dm, stack, d_low, g_g2, g_s2, g_bd, g_bo)


def third_plain(
    images, slots, width, d_low, att_t, w_out, qkv_in, probs, n1t, w_qkv, token, gain, mid, live, keep,
    g_out, g_qkv, g_b, g_g1, g_s1, gp, stack, tile, flat, qkv,
):
    def put(ref, c, value):
        ref[:, tile_at(c, TILE)] = value

    def put_patches(i, value):
        gp[i] = value

    qkv[...] = qkv_in[...]
    tile[...] = jnp.zeros_like(tile)
    stage_out_back(width, att_t, d_low, w_out, functools.partial(put, g_out), stack)
    for i in range(images):
        stage_attention_back(width, qkv, probs.at[pl.ds(i * H, H)], stack, i)
    back = functools.partial(stage_qkv_back, images, width, qkv, n1t, tile, flat, functools.partial(put, g_qkv), g_b)
    loop(0, 3 * width // TILE, lambda c, _: back(c), 1)
    stage_norm_back(width, flat, w_qkv, stack)
    stage_end(images, slots, width, keep, token, gain, mid, live, stack, g_g1, g_s1, put_patches)


def second_kernel(
    images, slots, width,
    keep_in, vectors, s_bup, h_token, h_n1t, h_dm, h_live, h_qkv, h_probs, h_att_t, h_middle, h_wqkv, h_wout, h_up, h_down, h_act, h_dh, h_gup, h_gdown, h_up1, h_down1, h_own_up, h_own_down,
    gp, out_tokens, o_wide, o_down, e_small,
    out_vm, keep,
    e_up, e_down, e_out, e_q, e_k, e_v,
    stack, tile, flat, qkv, probs, t_a, t_b, r_a, r_b, mid, live, w_qkv, w_out, stage, g_b, g_g1, g_s1, g_g2, g_s2, g_bd, g_bo, g_attn,
    up_held, up_own, up_core, up_dx, up_dy, up_sx, up_sy, up_ln, dn_held, dn_own, dn_core, dn_dx, dn_dy, dn_sx, dn_sy, dn_ln,
    core4, dx4, dy4, sx4, sy4, ln4, v_home, v_core, v_sy, v_sx, v_ln, v_sent, v_total,
    send, recv, v_send, v_recv, own, loads, probs_sem, out_sem,
):
    place = Place()
    pad_keep(keep_in, keep)
    enter(place.along[1:] + list(place.sides()))
    def reduce_third(t, source, held, own4, core, dx, dy, sx, sy, ln, e, sem):
        sems = send.at[sem + t], recv.at[sem + t]
        if t == 0:
            r = Reduce(place, None, None, None, None, None, None, None, ln.at[0], e.at[0], *sems)
            r.own4 = own4
            return r
        return Reduce(place, source, held.at[t - 1], core, dx.at[t - 1], dy.at[t - 1], sx.at[t - 1], sy.at[t - 1], ln.at[t], e.at[t], *sems)

    r_up = [reduce_third(t, h_gup, up_held, up_own, up_core, up_dx, up_dy, up_sx, up_sy, up_ln, e_up, 0) for t in range(3)]
    r_down = [reduce_third(t, h_gdown, dn_held, dn_own, dn_core, dn_dx, dn_dy, dn_sx, dn_sy, dn_ln, e_down, 3) for t in range(3)]
    mlp = [(r_up[t], r_down[t]) for t in range(3)]
    r_q, r_k, r_v, r_out = (
        Reduce(place, g_attn.at[m], None, core4.at[m], dx4.at[m], dy4.at[m], sx4.at[m], sy4.at[m], ln4.at[m], e, send.at[6 + m], recv.at[6 + m])
        for m, e in enumerate((e_q, e_k, e_v, e_out))
    )
    small = SmallReduce(place, v_home, v_core, v_sy, v_sx, v_ln, v_send, v_recv)
    later = Later(loads)
    slots_ = [flat.at[:, 0:THIRD], flat.at[:, THIRD : 2 * THIRD]]
    groups = {"m0": mlp[0], "m1": mlp[1], "m2": mlp[2], "o": (r_out,), "q": (r_q,), "k": (r_k,), "v": (r_v,)}

    def act(slot):
        for phase in ("open", "core", "diag", "side", "line", "share"):
            for group, slots_of in REDUCE_PLAN:
                phases = {2: ("line", "share"), 5: ("open" if group == "m1" else "core", "diag", "side", "line", "share")}[len(slots_of)]
                if (phase, slot) in zip(phases, slots_of):
                    for r in groups[group]:
                        getattr(r, "step_" + phase)()
                        if phase == "core":
                            r.step_open()

    early = [
        pltpu.make_async_copy(h, into, own.at[j])
        for j, (h, into) in enumerate(((h_own_up, up_own), (h_own_down, dn_own), (h_up1, up_held.at[0]), (h_down1, dn_held.at[0])))
    ]
    for copy in early:
        copy.start()
    later.start("dh0", h_dh.at[0], slots_[0])
    later.start("up0", h_up.at[0], t_a)
    for j, (r, h, into) in enumerate(((r_up[2], h_gup, up_held), (r_down[2], h_gdown, dn_held))):
        r.begin(pltpu.make_async_copy(h.at[:, :, place.c], into.at[1], own.at[4 + j]))
    later.start("dh1", h_dh.at[1], slots_[1])
    later.start("up1", h_up.at[1], t_b)
    for copy, r in zip(early[:2], mlp[0]):
        copy.wait()
        r.step_send()
    for copy in early[2:]:
        copy.wait()
    act(0)
    for name, src, dst in (("mid", h_middle, mid), ("dm", h_dm, r_a), ("live", h_live, live), ("w_out", h_wout, w_out), ("qkv", h_qkv, qkv), ("w_qkv", h_wqkv, w_qkv)):
        later.start(name, src, dst)

    def load_probs(i):
        slot = i % 2
        return pltpu.make_async_copy(h_probs.at[pl.ds(i * H, H)], probs.at[slot], probs_sem.at[slot])

    load_probs(0).start()
    later.wait("dh0", "up0")
    act(1)
    add_products(width, stack, True, lambda cols: dot_nt(slots_[0][...], t_a[cols, :]))
    later.start("dh2", h_dh.at[2], slots_[0])
    later.start("up2", h_up.at[2], t_a)
    act(2)
    later.wait("dh1", "up1")
    add_products(width, stack, False, lambda cols: dot_nt(slots_[1][...], t_b[cols, :]))
    later.start("att_t", h_att_t, t_b)
    act(3)
    later.wait("dh2", "up2")
    add_products(width, stack, False, lambda cols: dot_nt(slots_[0][...], t_a[cols, :]))
    later.start("n1t", h_n1t, t_a)
    act(4)
    later.wait("mid", "dm")
    gain2 = vectors.at[5:6, :]
    stage_middle_back(mid, gain2, r_a, stack, r_b, g_g2, g_s2, g_bd, g_bo)
    later.start("token", h_token, r_a)

    def put(m, c, value):
        for j in range(2):
            col = 2 * c + j
            y, off = (col % 6) // 3, col % 3
            at = tile_at(off, 128)
            g_attn[col // 6 if m is None else m, :, :, :, y, :, at] = value[:, j * 128 : (j + 1) * 128].reshape(4, 2, 2, 48, 128)

    act(5)
    later.wait("att_t", "w_out", "qkv")
    stage_out_back(width, t_b, r_b, w_out, functools.partial(put, 3), stack)
    r_out.begin()

    def back(i, _):
        for j in range(5):
            pl.when(i == j)(lambda j=j: act(6 + j))
        load_probs(i).wait()
        pl.when(i + 1 < images)(lambda: load_probs(i + 1).start())
        stage_attention_back(width, qkv, probs.at[lax.rem(i, 2)], stack, i)
        return 0

    lax.fori_loop(0, images, back, 0)
    later.wait("n1t")
    tile[...] = jnp.zeros_like(tile)
    project = functools.partial(stage_qkv_back, images, width, qkv, t_a, tile, flat, functools.partial(put, None), g_b)
    third = width // TILE

    def project_tile(c, _):
        for m in range(3):
            pl.when(c == m * third)(lambda m=m: act(11 + m))
        project(c)
        for m, r in enumerate((r_q, r_k, r_v)):
            pl.when(c == m * third + third - 1)(lambda r=r: r.begin())
        return 0

    lax.fori_loop(0, 3 * third, project_tile, 0)
    act(14)
    later.wait("w_qkv")
    stage_norm_back(width, flat, w_qkv, stack)
    later.start("act0", h_act.at[0], slots_[0])
    later.start("act1", h_act.at[1], slots_[1])
    later.start("down0", h_down.at[0], r_b)
    act(15)
    later.wait("token", "live")
    flights = []

    def put_patches(i, value):
        if i >= 2:
            flights[i - 2].wait()
        stage[i % 2] = value
        copy = pltpu.make_async_copy(stage.at[i % 2], gp.at[i], out_sem.at[i % 2])
        copy.start()
        flights.append(copy)

    stage_end(images, slots, width, keep, r_a, vectors.at[0:1, :], mid, live, stack, g_g1, g_s1, put_patches)
    later.start("middle", h_middle, mid)
    later.start("down1", h_down.at[1], r_a)
    act(16)
    v_home[...] = jnp.zeros_like(v_home)
    for j, (ref, base) in enumerate(((g_g1, 0), (g_s1, 0), (g_b, 0), (g_b, 2 * width), (g_bo, 0), (g_g2, 0), (g_s2, 0), (g_bd, 0))):
        row = ref[:, base : base + width]
        for f in range(8):
            v_home[f // 2, f % 2, j : j + 1, :96] = row[:, 96 * f : 96 * f + 96]
    for f in range(8):
        row = jnp.concatenate([s_bup[t, :, f * 128 : f * 128 + 128] for t in range(3)], axis=1)
        for j in range(4):
            v_home[f // 2, f % 2, 8 + j : 9 + j, :96] = row[:, 96 * j : 96 * j + 96]
    small.begin()
    act(17)
    later.wait("act0", "down0")
    add_products(width, stack, True, lambda cols: dot(slots_[0][...], r_b[:, cols]))
    later.start("act2", h_act.at[2], slots_[0])
    later.start("down2", h_down.at[2], r_b)
    small.step_core(v_sent)
    act(18)
    later.wait("act1", "down1")
    add_products(width, stack, False, lambda cols: dot(slots_[1][...], r_a[:, cols]))
    small.step_y(v_sent, v_total)
    act(19)
    later.wait("act2", "down2", "middle")
    add_products(width, stack, False, lambda cols: dot(slots_[0][...], r_b[:, cols]))
    small.step_x(v_total)
    act(20)
    stage_final(images, slots, width, mid, live, vectors.at[7:8, :], stack, out_vm)
    later.start("tokens", out_vm, out_tokens)
    small.step_line(e_small)
    act(21)
    act(22)
    for r in r_up + r_down:
        r.finish()
    for t in range(3):
        for c in range(2):
            for y in range(2):
                for f in range(4):
                    col = (4 * y + f) * 384 + t * 128
                    o_wide[48 * c : 48 * c + 48, 3 * width + col : 3 * width + col + 128] = e_up[t, c, y, :, f * 128 : f * 128 + 128]
        o_down[t * 128 : t * 128 + 128, :] = e_down[t].reshape(width, 128).T
    half = width // 2

    def place_blocks(ref, base, e):
        for c in range(2):
            for y in range(2):
                ref[48 * c : 48 * c + 48, base + y * half : base + y * half + half] = e[c, y]

    r_out.finish()
    place_blocks(o_wide, 7 * width, e_out)
    for m, (r, e) in enumerate(((r_q, e_q), (r_k, e_k), (r_v, e_v))):
        r.finish()
        place_blocks(o_wide, m * width, e)
    later.wait("tokens")
    for copy in flights[-2:]:
        copy.wait()
    for r in r_up + r_down + [r_out, r_q, r_k, r_v, small]:
        r.drain()


def last_kernel(images, width, h_patches, h_tokens, small, wide, down, patches, tokens, o_qkv, o_up, o_out, o_down, o_b_up, *rest):
    vectors, (held_p, held_t, loads, stores) = rest[:8], rest[8:]
    copies = []
    for i in range(images):
        for j, (src, held, dst) in enumerate(((h_patches, held_p, patches), (h_tokens, held_t, tokens))):
            load = pltpu.make_async_copy(src.at[i], held.at[i], loads.at[2 * i + j])
            load.start()
            copies.append((load, pltpu.make_async_copy(held.at[i], dst.at[i], stores.at[2 * i + j])))
    for load, store in copies:
        load.wait()
        store.start()
    o_qkv[...] = wide[:, : 3 * width].astype(F32)
    o_up[...] = wide[:, 3 * width : 7 * width].astype(F32)
    o_out[...] = wide[:, 7 * width :].astype(F32)
    o_down[...] = down[...].astype(F32)
    for j, ref in enumerate(vectors):
        ref[...] = small[j : j + 1, :96]
    o_b_up[...] = jnp.concatenate([small[8 + j : 9 + j, :96] for j in range(4)], axis=1)
    for _, store in copies:
        store.wait()


def shards(
    linked,
    patches, keep, ln1_gain, ln1_bias, w_qkv, b_query, b_value, w_out, b_out,
    ln2_gain, ln2_bias, w_up, b_up, w_down, b_down, cotangent,
):
    images, slots = keep.shape
    width = patches.shape[2]
    hidden_width = w_up.shape[1]
    keep_pad = jnp.pad(keep, ((0, 0), (0, SLOT - slots)), constant_values=-1).reshape(images, 1, SLOT)
    part = ln1_gain.shape[0]
    singles = [v.reshape(1, part) for v in (ln1_gain, ln1_bias, b_query, b_value, b_out, ln2_gain, ln2_bias, b_down)]
    rows_low, rows_wide = ((ROWS, width), BF16), ((ROWS, width), F32)
    cols_low = ((width, ROWS), BF16)
    live_like, mask_like = ((ROWS, BLOCK), F32), ((images, SLOT, SLOT), F32)
    heads_like = ((images, SLOT, 3 * width), BF16)
    probs_like = ((images * H, SLOT, SLOT), BF16)
    row_like = ((1, width), F32)

    if linked:
        half = width // 2
        full = lambda v: ((v.shape[0] * 8, v.shape[1]), BF16)
        up3, down3, hid3 = ((3, width, THIRD), BF16), ((3, THIRD, width), BF16), ((3, ROWS, THIRD), BF16)
        gup_like, gdown_like = (4, 2, 2, 2, 48, THIRD // 2), (4, 2, 2, 2, width // 4, 128)
        outs = [
            ((16, width), F32), ((3, 1, THIRD), F32), rows_low, cols_low, rows_low, live_like, heads_like, probs_like, cols_low, rows_wide,
            full(w_qkv), full(w_out), up3, down3, hid3, hid3, (gup_like, BF16), (gdown_like, BF16), ((4, 2) + gup_like[3:], BF16), ((4, 2) + gdown_like[3:], BF16),
            ((4,) + gup_like[4:], BF16), ((4,) + gdown_like[4:], BF16),
        ]
        scratch = [
            (patches.shape, BF16), ((images, 1, SLOT), jnp.int32), (patches.shape, BF16), ((16, BLOCK), F32), ((16, BLOCK), BF16),
            rows_wide, rows_low, mask_like, rows_low, cols_low, rows_low, cols_low, live_like, heads_like, ((2, H, SLOT, SLOT), BF16), cols_low,
            rows_wide, full(w_qkv), full(w_out), up3, down3, ((3, part, THIRD), BF16), hid3[0][1:], hid3[0][1:], (2,) + gup_like, (2,) + gdown_like,
            (2, 4, 2) + gup_like[3:], (2, 4, 2) + gdown_like[3:],
        ]
        for r, w, first, other in ((48, THIRD // 2, (4, 48, 128), (4, 48, THIRD // 2 - 128)), (width // 4, 128, (4, 64, 128), (4, width // 4 - 64, 128))):
            scratch += [other, first, (4, r, w), (4, r, w)]
        scratch += [((8, 16, BLOCK), BF16), ((1, 3 * width), F32), ((3, 1, THIRD), F32)]
        scratch = [s if isinstance(s[0], tuple) else (s, BF16) for s in scratch]
        vectors, g_b_up, token, n1t, dm, live, qkv, probs, att_t, middle, qkv_full, out_full, up_full, down_full, act, dh, g_up, g_down, up1, down1, own_up, own_down = pl.pallas_call(
            functools.partial(first_kernel, images, slots, width),
            out_shape=[jax.ShapeDtypeStruct(*o) for o in outs],
            in_specs=[ANY, VMEM, ANY] + [VMEM] * 13,
            out_specs=[VMEM] * 2 + [ANY] * 20,
            scratch_shapes=[pltpu.VMEM(*s) for s in scratch]
            + [pltpu.SemaphoreType.DMA((4, 28))] * 2
            + [pltpu.SemaphoreType.DMA((6, 28))] * 2
            + [pltpu.SemaphoreType.DMA((7,))] * 2
            + [pltpu.SemaphoreType.DMA((12,)), pltpu.SemaphoreType.DMA((33,)), pltpu.SemaphoreType.DMA((2,))]
            + [pltpu.SemaphoreType.DMA((4,))] * 2
            + [pltpu.SemaphoreType.DMA((2, 10))] * 2,
            compiler_params=pltpu.CompilerParams(vmem_limit_bytes=LIMIT, collective_id=0, has_side_effects=True),
            name="first",
        )(patches, keep, cotangent, *singles, b_up.reshape(1, -1), w_qkv, w_out, w_up, w_down)
        final = lambda r, w, lead=(): (lead + (2, 2, r, w), BF16)
        attn = final(48, half)
        outs = [((images, slots, width), F32), ((images, slots, width), BF16), ((part, 8 * width), BF16), ((half, width), BF16), ((16, BLOCK), F32)]

        def buffers(r, w, by_rows, cut, cores, lead, lines):
            other = (4, r - cut, w) if by_rows else (4, r, w - cut)
            first = (4, cut, w) if by_rows else (4, r, cut)
            return [(cores + (4, 2, 2, r, w), BF16)] + [(lead + s, BF16) for s in (other, first, (4, r, w), (4, r, w))] + [(lines + (3, r, w), BF16)]

        scratch = [((images, slots, width), BF16), ((images, 1, SLOT), jnp.int32), final(48, THIRD // 2, (3,)), final(width // 4, 128, (3,)), attn, attn, attn, attn]
        scratch += [rows_wide, ((ROWS, TILE), F32), ((ROWS, 3 * width), BF16), heads_like, ((2, H, SLOT, SLOT), BF16), cols_low, cols_low, rows_low, rows_low]
        scratch += [rows_wide, live_like, ((width, 3 * width), BF16), ((width, width), BF16), ((2, slots, width), F32), ((1, 3 * width), F32)] + [row_like] * 6
        scratch += [((4, 4, 2, 2, 2, 48, half), BF16)]
        scratch += [((2, 4, 2, 2, 48, THIRD // 2), BF16), ((4, 48, THIRD // 2), BF16)] + buffers(48, THIRD // 2, False, 128, (), (2,), (3,))
        scratch += [((2, 4, 2, 2, width // 4, 128), BF16), ((4, width // 4, 128), BF16)] + buffers(width // 4, 128, True, 64, (), (2,), (3,))
        scratch += buffers(48, half, False, 128, (4,), (4,), (4,))
        small_like, line_like = ((4, 2, 16, BLOCK), F32), ((3, 16, BLOCK), F32)
        scratch += [small_like, small_like, small_like, ((4, 16, BLOCK), F32), line_like, small_like, small_like]
        grad_patches, out_tokens, o_wide, o_down, small = pl.pallas_call(
            functools.partial(second_kernel, images, slots, width),
            out_shape=[jax.ShapeDtypeStruct(*o) for o in outs],
            in_specs=[VMEM] * 3 + [ANY] * 20,
            out_specs=[ANY] * 2 + [VMEM] * 3,
            scratch_shapes=[pltpu.VMEM(*s) for s in scratch]
            + [pltpu.SemaphoreType.DMA((10, 10))] * 2
            + [pltpu.SemaphoreType.DMA((6,))] * 2
            + [pltpu.SemaphoreType.DMA((6,)), pltpu.SemaphoreType.DMA((23,)), pltpu.SemaphoreType.DMA((2,)), pltpu.SemaphoreType.DMA((2,))],
            compiler_params=pltpu.CompilerParams(vmem_limit_bytes=LIMIT, collective_id=1, has_side_effects=True),
            name="second",
        )(keep, vectors, g_b_up, token, n1t, dm, live, qkv, probs, att_t, middle, qkv_full, out_full, up_full, down_full, act, dh, g_up, g_down, up1, down1, own_up, own_down)
        outs = [
            ((images, slots, width), F32), ((images, slots, width), BF16), ((part, 3 * width), F32), ((part, 4 * width), F32), ((part, width), F32),
            ((half, width), F32), ((1, half), F32),
        ] + [((1, part), F32)] * 8
        grad_patches, out_tokens, sum_qkv, sum_up, sum_out, sum_down, b_up_sum, *rows = pl.pallas_call(
            functools.partial(last_kernel, images, width),
            out_shape=[jax.ShapeDtypeStruct(*o) for o in outs],
            in_specs=[ANY, ANY, VMEM, VMEM, VMEM],
            out_specs=[ANY, ANY] + [VMEM] * 13,
            scratch_shapes=[pltpu.VMEM((images, slots, width), F32), pltpu.VMEM((images, slots, width), BF16)] + [pltpu.SemaphoreType.DMA((2 * images,))] * 2,
            compiler_params=pltpu.CompilerParams(vmem_limit_bytes=LIMIT),
            name="last",
        )(grad_patches, out_tokens, small, o_wide, o_down)
        rows = [row.reshape(part) for row in rows]
        b_up_sum = b_up_sum.reshape(half)
    else:
        gather = lambda v: lax.all_gather(v, "fsdp", axis=0, tiled=True)
        vectors = jnp.pad(gather(jnp.concatenate(singles, axis=0).T).T.astype(F32), ((0, 8), (0, 0)))
        bias_up = gather(b_up).astype(F32).reshape(1, hidden_width)
        qkv_full, out_full, up_full, down_full = gather(w_qkv), gather(w_out), gather(w_up), gather(w_down)
        outs = [rows_low, cols_low, rows_low, cols_low, live_like, heads_like, probs_like, cols_low, rows_wide, rows_low, cols_low]
        scratch = [rows_wide, rows_low, mask_like, rows_low, ((1, 3 * width), F32)]
        token, n1t, dm, dmt, live, qkv, probs, att_t, middle, n2, n2t = call(
            functools.partial(first_plain, images, slots, width),
            outs, scratch, (patches, keep_pad, cotangent, vectors, qkv_full, out_full), "first",
        )
        gain1, gain2, b_d = vectors[0:1], vectors[5:6], vectors[7:8]
        hid = ((ROWS, hidden_width), BF16)
        out_tokens, d_mid, d_low, g_up, g_down, g_b_up, g_g2, g_s2, g_bd, g_bo = call(
            functools.partial(second_plain, images, slots, width, hidden_width),
            [((images, slots, width), BF16), rows_wide, rows_low] + [((width, hidden_width), BF16)] * 2 + [((1, hidden_width), F32)] + [row_like] * 4,
            [hid, hid, rows_wide],
            (n2, n2t, dm, dmt, up_full, bias_up, down_full, b_d, middle, live, gain2),
            "second",
        )
        g_out, g_qkv, g_b, g_g1, g_s1, grad_patches = call(
            functools.partial(third_plain, images, slots, width),
            [((width, width), BF16), ((width, 3 * width), BF16), ((1, 3 * width), F32), row_like, row_like, ((images, slots, width), F32)],
            [rows_wide, ((ROWS, TILE), F32), ((ROWS, 3 * width), BF16), heads_like],
            (d_low, att_t, out_full, qkv, probs, n1t, qkv_full, token, gain1, d_mid, live, keep_pad),
            "third",
        )
        scat = lambda v, dim=0: lax.psum(lax.psum_scatter(v, "fsdp", scatter_dimension=dim, tiled=True), "dp").astype(F32)
        rows = jnp.concatenate([g_g1, g_s1, g_b[:, :width], g_b[:, 2 * width :], g_bo, g_g2, g_s2, g_bd], axis=0).astype(BF16)
        rows = scat(rows, 1)
        b_up_sum = scat(g_b_up.astype(BF16), 1)[0]
        sum_qkv, sum_out, sum_up, sum_down = scat(g_qkv), scat(g_out), scat(g_up), scat(g_down, 1).T
    return (
        out_tokens, grad_patches, rows[0], rows[1], sum_qkv, rows[2], rows[3], sum_out, rows[4],
        rows[5], rows[6], sum_up, b_up_sum, sum_down, rows[7],
    )


def solution(mesh):
    linked = (mesh.shape["fsdp"], mesh.shape["dp"]) == (8, 4)
    many, one, two = P(("fsdp", "dp"), None, None), P("fsdp"), P("fsdp", None)
    in_specs = (many, P(("fsdp", "dp"), None), one, one, two, one, one, two, one, one, one, two, one, two, one, many)
    out_specs = (many, many, one, one, two, one, one, two, one, one, one, two, one, two, one)
    return jax.shard_map(functools.partial(shards, linked), mesh=mesh, in_specs=in_specs, out_specs=out_specs, check_vma=False)
```

```python
import functools
import math

import jax
import jax.numpy as jnp
from jax import lax
from jax.experimental import pallas as pl
from jax.experimental.pallas import tpu as pltpu
from jax.sharding import PartitionSpec as P

H = 12
HD = 64
EPSILON = 1e-06
F32 = jnp.float32
BF16 = jnp.bfloat16
SLOT = 200
ROWS = 1024
BLOCK = 128
TILE = 256
NT = (((1,), (1,)), ((), ()))


def dot(left, right):
    return jnp.dot(left, right, preferred_element_type=F32)


def dot_nt(left, right):
    return lax.dot_general(left, right, NT, preferred_element_type=F32)


def tile_at(index, size):
    if isinstance(index, int):
        return pl.ds(index * size, size)
    return pl.ds(pl.multiple_of(index * size, size), size)


def loop(begin, end, body, unroll):
    if (end - begin) == unroll:
        for j in range(begin, end):
            body(j, 0)
        return

    def group(t, _):
        for u in range(unroll):
            body(begin + t * unroll + u, 0)
        return 0

    lax.fori_loop(0, (end - begin) // unroll, group, 0)


def norm_parts(values):
    centre = values - jnp.mean(values, axis=-1, keepdims=True)
    spread = jnp.mean(centre * centre, axis=-1, keepdims=True)
    inverse = lax.rsqrt(spread + EPSILON)
    return centre * inverse, inverse


def norm_back(hat, inverse, gain, grad):
    scaled = grad * gain
    along = jnp.mean(scaled * hat, axis=-1, keepdims=True)
    return inverse * (scaled - jnp.mean(scaled, axis=-1, keepdims=True) - hat * along)


def gelu_parts(hidden):
    size = jnp.abs(hidden)
    bell = jnp.exp(hidden * hidden * -0.5)
    t = 1.0 / (1.0 + size * (0.3275911 / math.sqrt(2.0)))
    tail = 1.061405429 * 0.5
    for term in (-1.453152027, 1.421413741, -0.284496736, 0.254829592):
        tail = tail * t + term * 0.5
    tail = tail * t * bell
    below = jnp.where(hidden >= 0, 1.0 - tail, tail)
    slope = below + hidden * (bell * (1.0 / math.sqrt(2.0 * math.pi)))
    return hidden * below, slope


def first_lanes(rows):
    return lax.broadcasted_iota(jnp.int32, (rows, 2 * HD), 1) < HD


def pad_keep(keep, padded):
    padded[...] = jnp.full_like(padded, -1)
    for i in range(keep.shape[0]):
        padded[i, :, : keep.shape[1]] = keep[i : i + 1, :]


def stage_gather(images, slots, patches, keep, stack, live, mask, token):
    stack[...] = jnp.zeros_like(stack)
    live[...] = jnp.zeros_like(live)

    def gather(i, _):
        row = keep[i]
        column = jnp.broadcast_to(row, (SLOT, SLOT)).T
        mask[i] = jnp.where(column >= 0, 0.0, -1e30)
        alive = (column >= 0).astype(F32)
        chosen = (column[:, :slots] == lax.broadcasted_iota(jnp.int32, (SLOT, slots), 1)).astype(F32).astype(BF16)
        rows = pl.ds(pl.multiple_of(i * SLOT, 8), SLOT)
        stack[rows, :] = dot(chosen, patches[i])
        live[rows, :] = alive[:, :BLOCK]
        return 0

    loop(0, images, gather, 1)

    def narrow(b, _):
        rows = tile_at(b, BLOCK)
        token[rows, :] = stack[rows, :].astype(BF16)
        return 0

    loop(0, ROWS // BLOCK, narrow, 2)


def stage_norm(gain, shift, token, normed, normed_t):
    def norm(b, _):
        rows = tile_at(b, BLOCK)
        hat, _ = norm_parts(token[rows, :].astype(F32))
        low = (hat * gain + shift).astype(BF16)
        normed[rows, :] = low
        normed_t[:, rows] = low.T
        return 0

    loop(0, ROWS // BLOCK, norm, 4)


def stage_grads(images, slots, width, cot, stack, live, dm, dm_t):
    stack[...] = jnp.zeros_like(stack)
    for i in range(images):
        stack[i * SLOT : i * SLOT + slots, :] = cot[i].astype(F32)

    def grads(b, _):
        rows = tile_at(b, BLOCK)
        low = (stack[rows, :] * jnp.concatenate([live[rows, :]] * (width // BLOCK), axis=1)).astype(BF16)
        dm[rows, :] = low
        dm_t[:, rows] = low.T
        return 0

    loop(0, ROWS // BLOCK, grads, 2)


def stage_qkv(images, width, normed, w_qkv, bias, qkv, begin, end):
    def body(c, _):
        cols = tile_at(c, TILE)
        scale = jnp.where(c < width // TILE, 1.0 / math.sqrt(HD), 1.0)
        values = (dot(normed[...], w_qkv[:, cols]) + bias[:, cols]) * scale
        for i in range(images):
            qkv[i, :, cols] = values[i * SLOT : (i + 1) * SLOT].astype(BF16)
        return 0

    loop(begin, end, body, 1)


def stage_attention(width, qkv, mask, probs, stack, i):
    low = first_lanes(SLOT)
    for p in range(H // 2):
        q2 = qkv[i, :, p * 128 : (p + 1) * 128]
        k2 = qkv[i, :, width + p * 128 : width + (p + 1) * 128]
        v2_t = qkv[i, :, 2 * width + p * 128 : 2 * width + (p + 1) * 128].T
        outs = []
        for h in range(2):
            qh = jnp.where(low if h == 0 else ~low, q2, jnp.zeros_like(q2))
            scores = dot_nt(k2, qh) + mask[i]
            exponent = jnp.exp(scores - jnp.max(scores, axis=0, keepdims=True))
            share = 1.0 / jnp.sum(exponent, axis=0, keepdims=True)
            prob = (exponent * share).astype(BF16)
            probs[2 * p + h] = prob
            outs.append(dot(v2_t[h * HD : (h + 1) * HD], prob))
        stack[pl.ds(pl.multiple_of(i * SLOT, 8), SLOT), p * 128 : (p + 1) * 128] = jnp.concatenate(outs, axis=0).T


def stage_out(width, stack, w_out, bias, token, gain, shift, att, att_t, middle, normed, normed_t):
    def low(b, _):
        rows = tile_at(b, BLOCK)
        values = stack[rows, :].astype(BF16)
        att[rows, :] = values
        att_t[:, rows] = values.T
        return 0

    loop(0, ROWS // BLOCK, low, 4)

    def body(c, _):
        cols = tile_at(c, TILE)
        middle[:, cols] = token[:, cols].astype(F32) + (dot(att[...], w_out[:, cols]) + bias[:, cols])
        return 0

    loop(0, width // TILE, body, 1)

    def norm(b, _):
        rows = tile_at(b, BLOCK)
        hat, _ = norm_parts(middle[rows, :])
        values = (hat * gain[...] + shift[...]).astype(BF16)
        normed[rows, :] = values
        normed_t[:, rows] = values.T
        return 0

    loop(0, ROWS // BLOCK, norm, 4)


def stage_mlp(width, normed, normed_t, dm, dm_t, w_up, b_up, w_down, act, dh, put_up, put_down, g_b_up, c):
    cols = tile_at(c, TILE)
    up, down, bias = w_up[:, cols], w_down[cols, :], b_up[:, cols]
    total, waiting = 0.0, []
    for r in range(ROWS // TILE + 1):
        if r < ROWS // TILE:
            rows = slice(r * TILE, (r + 1) * TILE)
            waiting.append((rows, dot(normed[rows, :], up) + bias, dot_nt(dm[rows, :], down)))
        if r:
            rows, hidden, d_act = waiting.pop(0)
            value, slope = gelu_parts(hidden)
            grad = (d_act * slope).astype(BF16)
            act[rows, cols] = value.astype(BF16)
            dh[rows, cols] = grad
            total = total + jnp.sum(grad.astype(F32), axis=0, keepdims=True)
    g_b_up[:, cols] = total
    put_up(c, dot(normed_t[...], dh[:, cols]).astype(BF16))
    put_down(c, dot(dm_t[...], act[:, cols]).astype(BF16))


def add_products(width, stack, fresh, product):
    def body(c, _):
        cols = tile_at(c, TILE)
        value = product(cols)
        stack[:, cols] = value if fresh else stack[:, cols] + value
        return 0

    loop(0, width // TILE, body, 1)


def stage_final(images, slots, width, middle, live, b_down, stack, out):
    def final(b, _):
        rows = tile_at(b, BLOCK)
        stack[rows, :] = (middle[rows, :] + (stack[rows, :] + b_down[...])) * jnp.concatenate([live[rows, :]] * (width // BLOCK), axis=1)
        return 0

    loop(0, ROWS // BLOCK, final, 2)
    for i in range(images):
        out[i] = stack[i * SLOT : i * SLOT + slots, :].astype(BF16)


def stage_middle_back(middle, gain, dm, stack, d_mid_low, g_gain, g_shift, g_b_down, g_b_out):
    for ref in (g_gain, g_shift, g_b_down, g_b_out):
        ref[...] = jnp.zeros_like(ref)

    def back(b, _):
        rows = tile_at(b, BLOCK)
        grad = stack[rows, :]
        hat, inverse = norm_parts(middle[rows, :])
        g_gain[...] += jnp.sum(grad * hat, axis=0, keepdims=True)
        g_shift[...] += jnp.sum(grad, axis=0, keepdims=True)
        own = dm[rows, :].astype(F32)
        g_b_down[...] += jnp.sum(own, axis=0, keepdims=True)
        total = own + norm_back(hat, inverse, gain[...], grad)
        middle[rows, :] = total
        low = total.astype(BF16)
        d_mid_low[rows, :] = low
        g_b_out[...] += jnp.sum(low.astype(F32), axis=0, keepdims=True)
        return 0

    loop(0, ROWS // BLOCK, back, 2)


def stage_out_back(width, att_t, d_mid_low, w_out, put_out, stack):
    def body(c, _):
        cols = tile_at(c, TILE)
        put_out(c, dot(att_t[...], d_mid_low[:, cols]).astype(BF16))
        stack[:, cols] = dot_nt(d_mid_low[...], w_out[cols, :])
        return 0

    loop(0, width // TILE, body, 1)


def stage_attention_back(width, qkv, probs, stack, i):
    low = first_lanes(SLOT)
    for p in range(H // 2):
        at_q = slice(p * 128, (p + 1) * 128)
        at_k = slice(width + p * 128, width + (p + 1) * 128)
        at_v = slice(2 * width + p * 128, 2 * width + (p + 1) * 128)
        q2, k2, v2 = qkv[i, :, at_q], qkv[i, :, at_k], qkv[i, :, at_v]
        k2_t = k2.T
        da = stack[pl.ds(pl.multiple_of(i * SLOT, 8), SLOT), at_q].astype(BF16)
        dq, dk, dv = [], 0.0, 0.0
        for h in range(2):
            pick = lambda m: jnp.where(low if h == 0 else ~low, m, jnp.zeros_like(m))
            prob = probs[2 * p + h]
            d_prob = dot_nt(pick(v2), da)
            mixed = prob.astype(F32)
            moved = mixed * d_prob
            total = jnp.sum(moved, axis=0, keepdims=True)
            ds = (moved - mixed * total).astype(BF16)
            dq.append(dot(k2_t[h * HD : (h + 1) * HD], ds))
            dk = dk + dot(ds, pick(q2))
            dv = dv + dot(prob, pick(da))
        qkv[i, :, at_q] = (jnp.concatenate(dq, axis=0).T * (1.0 / math.sqrt(HD))).astype(BF16)
        qkv[i, :, at_k] = dk.astype(BF16)
        qkv[i, :, at_v] = dv.astype(BF16)


def stage_qkv_back(images, width, d_qkv, normed_t, tile, flat, put_qkv, g_b_qkv, c):
    cols = tile_at(c, TILE)
    for i in range(images):
        tile[i * SLOT : (i + 1) * SLOT, :] = d_qkv[i, :, cols].astype(F32)
    values = tile[...]
    g_b_qkv[:, cols] = jnp.sum(values, axis=0, keepdims=True)
    low = values.astype(BF16)
    flat[:, cols] = low
    put_qkv(c, dot(normed_t[...], low).astype(BF16))


def stage_norm_back(width, flat, w_qkv, stack):
    def body(c, _):
        cols = tile_at(c, TILE)
        stack[:, cols] = dot_nt(flat[...], w_qkv[cols, :])
        return 0

    loop(0, width // TILE, body, 1)


def stage_end(images, slots, width, keep, token, gain, middle, live, stack, g_gain, g_shift, put_patches):
    for ref in (g_gain, g_shift):
        ref[...] = jnp.zeros_like(ref)

    def back(b, _):
        rows = tile_at(b, BLOCK)
        grad = stack[rows, :]
        hat, inverse = norm_parts(token[rows, :].astype(F32))
        g_gain[...] += jnp.sum(grad * hat, axis=0, keepdims=True)
        g_shift[...] += jnp.sum(grad, axis=0, keepdims=True)
        total = middle[rows, :] + norm_back(hat, inverse, gain[...], grad)
        stack[rows, :] = total * jnp.concatenate([live[rows, :]] * (width // BLOCK), axis=1)
        return 0

    loop(0, ROWS // BLOCK, back, 2)

    def scatter(i, _):
        chosen = (lax.broadcasted_iota(jnp.int32, (slots, SLOT), 0) == keep[i]).astype(F32).astype(BF16)
        values = stack[pl.ds(pl.multiple_of(i * SLOT, 8), SLOT), :]
        high = values.astype(BF16)
        rest = (values - high.astype(F32)).astype(BF16)
        put_patches(i, dot(chosen, high) + dot(chosen, rest))
        return 0

    for i in range(images):
        scatter(i, 0)


MESH = pl.DeviceIdType.MESH


class Place:
    def __init__(self):
        f, d = lax.axis_index("fsdp"), lax.axis_index("dp")
        self.z, self.x = f // 2, lax.rem(f, 2)
        self.y, self.c = d // 2, lax.rem(d, 2)
        z = self.z
        self.zs = [z, z + 1 - 2 * lax.rem(z, 2), lax.rem(z + 2, 4), 3 - z]
        self.ox, self.oy, self.oc = 1 - self.x, 1 - self.y, 1 - self.c
        self.beside = self.to(x=self.ox), self.to(y=self.oy), self.to(c=self.oc)
        self.along = [self.to(z=k) for k in self.zs]

    def to(self, z=None, x=None, y=None, c=None):
        z, x, y, c = (own if new is None else new for new, own in ((z, self.z), (x, self.x), (y, self.y), (c, self.c)))
        return (z * 2 + x, y * 2 + c)

    def sides(self):
        return self.beside


def enter(peers, meanwhile=None):
    barrier = pltpu.get_barrier_semaphore()
    for peer in peers:
        pl.semaphore_signal(barrier, inc=1, device_id=peer, device_id_type=MESH)
    if meanwhile is not None:
        meanwhile()
    pl.semaphore_wait(barrier, len(peers))


class Gather:
    def __init__(self, place, shard, full, first_cols, send, recv):
        self.place, self.shard, self.full, self.send, self.recv = place, shard, full, send, recv
        self.rows, cols = shard.shape
        self.half, self.wide, self.cut = self.rows // 2, cols // 2, first_cols
        self.started = []

    def spot(self, *args):
        return lambda: self.place_of(*args)

    def place_of(self, z, x, y, part=None, local=False):
        p = self.place
        base = 0 if local else (z * 2 + x) * self.rows
        rows = pl.ds(pl.multiple_of(base + p.c * self.half, 16), self.half)
        if y is None:
            return rows, slice(None)
        start, size = (y * self.wide, self.wide) if part is None else ((y * self.wide, self.cut) if part == 0 else (y * self.wide + self.cut, self.wide - self.cut))
        return rows, pl.ds(pl.multiple_of(start, 128), size)

    def copy(self, spot, sem, peer, local=None):
        src = self.full.at[spot] if local is None else self.shard.at[local]
        return pltpu.make_async_remote_copy(
            src_ref=src, dst_ref=self.full.at[spot], send_sem=self.send.at[sem], recv_sem=self.recv.at[sem], device_id=peer, device_id_type=MESH
        )

    def start(self, spot, sem, peer, local=None):
        def make():
            return self.copy(spot(), sem, peer, None if local is None else local())

        make().start()
        self.started.append(make)

    def arrived(self, spot, sem):
        self.copy(spot(), sem, self.place.sides()[0]).wait_recv()

    def own(self, sem):
        p = self.place
        rows = pl.ds(pl.multiple_of((p.z * 2 + p.x) * self.rows, 16), self.rows)
        return pltpu.make_async_copy(self.shard, self.full.at[rows, :], sem)

    def lines(self, *ks):
        p = self.place
        spot, local = self.spot(p.z, p.x, p.y), self.spot(p.z, p.x, p.y, None, True)
        for k in ks:
            self.start(spot, k, p.along[k], local)

    def beside(self):
        p = self.place
        side_x, side_y, _ = p.sides()
        self.start(self.spot(p.z, p.x, p.y), 4, side_x, self.spot(p.z, p.x, p.y, None, True))
        self.start(self.spot(p.z, p.x, p.oy, 1), 16, side_x, self.spot(p.z, p.x, p.oy, 1, True))

    def phase(self, name):
        if name == "own":
            self.beside()
        elif name == "zs":
            self.lines(1, 2, 3)
        elif name[0] == "z":
            self.lines(int(name[1]))
        elif name in ("spread", "cross", "share"):
            for k in range(name == "spread", 4):
                getattr(self, name)(k)
        else:
            (self.spread if name[0] == "s" else self.cross)(int(name[1]))

    def spread(self, k):
        p = self.place
        side_x, side_y, _ = p.sides()
        spot = self.spot(p.zs[k], p.x, p.y)
        self.arrived(spot, k)
        self.start(spot, 4 + k, side_x)
        self.start(spot, 8 + k, side_y)

    def cross(self, k):
        p = self.place
        side_x, side_y, _ = p.sides()
        self.arrived(self.spot(p.zs[k], p.ox, p.y), 4 + k)
        self.start(self.spot(p.zs[k], p.ox, p.y, 0), 12 + k, side_y)
        if k:
            self.arrived(self.spot(p.zs[k], p.x, p.oy), 8 + k)
            self.start(self.spot(p.zs[k], p.x, p.oy, 1), 16 + k, side_x)

    def share(self, k):
        p = self.place
        core = p.sides()[2]
        if k:
            self.start(self.spot(p.zs[k], p.x, None), 20 + k, core)
        self.arrived(self.spot(p.zs[k], p.ox, p.oy, 0), 12 + k)
        self.arrived(self.spot(p.zs[k], p.ox, p.oy, 1), 16 + k)
        self.start(self.spot(p.zs[k], p.ox, None), 24 + k, core)

    def finish(self):
        p = self.place

        def other(z, x):
            return lambda: (pl.ds(pl.multiple_of((z * 2 + x) * self.rows + (p.oc) * self.half, 16), self.half), slice(None))

        for k in range(4):
            if k:
                self.arrived(other(p.zs[k], p.x), 20 + k)
            self.arrived(other(p.zs[k], p.ox), 24 + k)

    def drain(self):
        for make in self.started:
            make().wait_send()


class Reduce:
    def __init__(self, place, source, held, core, diag_x, diag_y, side_x, side_y, line, final, send, recv):
        self.place, self.source, self.held, self.core = place, source, held, core
        self.diag_x, self.diag_y, self.side_x, self.side_y, self.line, self.final = diag_x, diag_y, side_x, side_y, line, final
        self.send, self.recv, self.started = send, recv, []
        self.own4 = self.own = None
        if diag_y is not None:
            self.rows, self.wide = side_x.shape[1:]
            self.by_rows = diag_y.shape[2] == self.wide
            self.cut = diag_y.shape[1] if self.by_rows else diag_y.shape[2]

    def part(self, second):
        bounds = pl.ds(self.cut, (self.rows if self.by_rows else self.wide) - self.cut) if second else pl.ds(0, self.cut)
        return (bounds, slice(None)) if self.by_rows else (slice(None), bounds)

    def hold(self, z, x, y, *rest):
        if self.held is None:
            return (z, x, self.place.c, y) + rest
        return (z, x, y) + rest

    @property
    def home(self):
        return self.source if self.held is None else self.held

    def copy(self, src, dst, sem, peer):
        return pltpu.make_async_remote_copy(src_ref=src, dst_ref=dst, send_sem=self.send.at[sem], recv_sem=self.recv.at[sem], device_id=peer, device_id_type=MESH)

    def start(self, src, dst, sem, peer):
        def make():
            return self.copy(src(), dst() if callable(dst) else dst, sem, peer)

        make().start()
        self.started.append(make)

    def arrived(self, dst, sem):
        self.copy(dst, dst, sem, self.place.sides()[0]).wait_recv()

    def begin(self, own=None):
        p = self.place
        self.start(lambda: self.source.at[:, :, p.oc], self.core, 0, p.sides()[2])
        self.own = own
        if own is not None:
            own.start()

    def add_core(self, x, y):
        def body(z, _):
            spot = self.hold(z, x, y)
            self.home[spot] = self.home[spot] + self.core[z, x, y]
            return 0

        lax.fori_loop(0, 4, body, 0)

    def add(self, x, y, part, buffer):
        def body(z, _):
            spot = self.hold(z, x, y, *part)
            self.home[spot] = self.home[spot] + buffer[z]
            return 0

        lax.fori_loop(0, 4, body, 0)

    def step_core(self):
        p = self.place
        side_x, side_y, _ = p.sides()
        if self.own is not None:
            self.own.wait()
        self.arrived(self.core, 0)
        for x, y in ((p.ox, p.oy), (p.ox, p.y), (p.x, p.oy), (p.x, p.y)):
            self.add_core(x, y)

    def step_open(self):
        p = self.place
        side_x, side_y, _ = p.sides()
        every = slice(None)
        self.start(lambda: self.home.at[self.hold(every, p.ox, p.oy, *self.part(True))], self.diag_x, 1, side_x)
        self.start(lambda: self.home.at[self.hold(every, p.ox, p.oy, *self.part(False))], self.diag_y, 2, side_y)

    def step_diag(self):
        p = self.place
        side_x, side_y, _ = p.sides()
        every = slice(None)
        self.arrived(self.diag_y, 2)
        self.add(p.ox, p.y, self.part(False), self.diag_y)
        self.start(lambda: self.home.at[self.hold(every, p.ox, p.y)], self.side_x, 3, side_x)
        self.arrived(self.diag_x, 1)
        self.add(p.x, p.oy, self.part(True), self.diag_x)
        self.start(lambda: self.home.at[self.hold(every, p.x, p.oy)], self.side_y, 4, side_y)

    def step_sum(self):
        p = self.place
        whole = (slice(None), slice(None))
        self.arrived(self.side_x, 3)
        self.add(p.x, p.y, whole, self.side_x)
        self.arrived(self.side_y, 4)
        self.add(p.x, p.y, whole, self.side_y)

    def mine(self, z):
        if self.own4 is not None:
            return self.own4.at[z]
        return self.home.at[self.hold(z, self.place.x, self.place.y)]

    def step_send(self):
        p = self.place
        for k in (1, 2, 3):
            self.start(lambda k=k: self.mine(p.zs[k]), lambda k=k: self.line.at[k - 1], 4 + k, p.along[k])

    def step_side(self):
        self.step_sum()
        self.step_send()

    def step_line(self):
        p = self.place
        total = self.mine(p.z)[...].astype(F32)
        for k in (1, 2, 3):
            self.arrived(self.line.at[k - 1], 4 + k)
            total = total + self.line[k - 1].astype(F32)
        self.final[p.c, p.y] = total.astype(BF16)
        self.start(lambda: self.final.at[p.c, p.y], lambda: self.final.at[p.c, p.y], 8, p.sides()[1])

    def step_share(self):
        p = self.place
        self.arrived(self.final.at[p.c, p.oy], 8)
        self.start(lambda: self.final.at[p.c], lambda: self.final.at[p.c], 9, p.sides()[2])

    def finish(self):
        self.arrived(self.final.at[self.place.oc], 9)

    def drain(self):
        for make in self.started:
            make().wait_send()


class SmallReduce:
    def __init__(self, place, home, core, side_y, side_x, line, send, recv):
        self.place, self.home, self.core, self.side_y, self.side_x, self.line = place, home, core, side_y, side_x, line
        self.send, self.recv, self.started = send, recv, []

    copy, start, arrived, drain = Reduce.copy, Reduce.start, Reduce.arrived, Reduce.drain

    def begin(self):
        self.start(lambda: self.home, self.core, 0, self.place.sides()[2])

    def step_core(self, sent):
        p = self.place
        self.arrived(self.core, 0)
        sent[...] = self.home[...] + self.core[...]
        self.start(lambda: sent, self.side_y, 1, p.sides()[1])

    def step_y(self, sent, total):
        p = self.place
        self.arrived(self.side_y, 1)
        total[...] = sent[...] + self.side_y[...]
        self.start(lambda: total.at[:, p.ox], self.side_x, 2, p.sides()[0])

    def step_x(self, total):
        p = self.place
        self.arrived(self.side_x, 2)
        for z in range(4):
            self.side_x[z] = self.side_x[z] + total[z, p.x]
        for k in (1, 2, 3):
            self.start(lambda k=k: self.side_x.at[p.zs[k]], lambda k=k: self.line.at[k - 1], 2 + k, p.along[k])

    def step_line(self, out):
        total = self.side_x[self.place.z]
        for k in (1, 2, 3):
            self.arrived(self.line.at[k - 1], 2 + k)
            total = total + self.line[k - 1]
        out[...] = total


GATHER_PLAN = (
    (("k", "own"), ("v", "own"), ("o", "own"), ("p0", "own"), ("q", "z1"), ("k", "z1"), ("q", "z2"), ("k", "z2"), ("k", "z3"), ("q", "s1"), ("k", "s1"),),
    (("v", "z1"), ("q", "z3"), ("k", "c0"), ("k", "s3"),),
    (("v", "z2"), ("v", "z3"),),
    (),
    (("v", "s1"), ("q", "s2"), ("q", "c1"),),
    (("o", "zs"), ("k", "s2"), ("q", "s3"),),
    (("q", "own"), ("p0", "zs"), ("v", "c0"), ("v", "s2"), ("v", "s3"), ("k", "c2"), ("q", "c3"), ("k", "c3"),),
    (("q", "c0"), ("v", "c1"), ("q", "c2"), ("v", "c2"), ("v", "c3"),),
    (("k", "c1"), ("o", "spread"), ("q", "share"), ("k", "share"),),
    (("p1", "own"), ("p1", "zs"), ("o", "cross"), ("v", "share"),),
    (("p0", "spread"),),
    (),
    (),
    (("p2", "zs"), ("p1", "spread"), ("p0", "cross"), ("o", "share"),),
    (),
    (("p2", "own"),),
    (("p1", "cross"), ("p0", "share"),),
    (("p2", "spread"),),
    (),
    (),
    (("p1", "share"),),
    (("p2", "cross"),),
    (),
    (),
    (("p2", "share"),),
    (),
    (),
    (),
    (),
    (),
)
MERGE_PLAN = (22, 25, 26)
REDUCE_PLAN = (
    ("m0", (13, 14)),
    ("m1", (0, 4, 10, 20, 22)),
    ("m2", (3, 8, 13, 20, 22)),
    ("o", (12, 15, 18, 20, 22)),
    ("q", (13, 14, 16, 19, 21)),
    ("k", (14, 16, 19, 22, 22)),
    ("v", (14, 18, 20, 22, 22)),
)


VMEM = pl.BlockSpec(memory_space=pltpu.VMEM)
ANY = pl.BlockSpec(memory_space=pl.ANY)
LIMIT = 61 * 1024 * 1024
THIRD = 1024


def call(body, outs, scratch, args, name):
    return pl.pallas_call(
        body,
        out_shape=[jax.ShapeDtypeStruct(*o) for o in outs],
        in_specs=[VMEM] * len(args),
        out_specs=[VMEM] * len(outs),
        scratch_shapes=[pltpu.VMEM(*s) for s in scratch],
        compiler_params=pltpu.CompilerParams(vmem_limit_bytes=LIMIT),
        name=name,
    )(*args)


class Later:
    def __init__(self, sems):
        self.sems, self.flights = sems, {}

    def start(self, name, src, dst):
        self.plan(name, src, dst)
        self.flights[name]().start()

    def plan(self, name, src, dst):
        sem = len(self.flights)

        def make():
            return pltpu.make_async_copy(*(r() if callable(r) else r for r in (src, dst)), self.sems.at[sem])

        self.flights[name] = make

    def wait(self, *names):
        for name in names:
            self.flights[name]().wait()


def first_plain(
    images, slots, width, patches, keep, cot, vectors, w_qkv, w_out,
    token, n1t, dm, dmt, live, qkv, probs, att_t, middle, n2, n2t, stack, normed, mask, att, bias,
):
    bias[...] = jnp.concatenate([vectors[2:3, :], jnp.zeros((1, width), F32), vectors[3:4, :]], axis=1)
    stage_gather(images, slots, patches, keep, stack, live, mask, token)
    stage_norm(vectors[0:1, :], vectors[1:2, :], token, normed, n1t)
    stage_grads(images, slots, width, cot, stack, live, dm, dmt)
    stage_qkv(images, width, normed, w_qkv, bias, qkv, 0, 3 * width // TILE)
    for i in range(images):
        stage_attention(width, qkv, mask, probs.at[pl.ds(i * H, H)], stack, i)
    stage_out(width, stack, w_out, vectors.at[4:5, :], token, vectors.at[5:6, :], vectors.at[6:7, :], att, att_t, middle, n2, n2t)


def first_kernel(
    images, slots, width,
    h_patches, keep_in, h_cot, *rest,
):
    singles, rest = rest[:9], rest[9:]
    first_body(images, slots, width, h_patches, keep_in, h_cot, singles, *rest)


def first_body(
    images, slots, width,
    h_patches, keep_in, h_cot, singles, s_qkv, s_out, s_up, s_down,
    vectors, g_b_up, h_token, h_n1t, h_dm, h_live, h_qkv, h_probs, h_att_t, h_middle, h_wqkv, h_wout, h_up, h_down, h_act, h_dh, h_gup, h_gdown, h_up1, h_down1, h_own_up, h_own_down,
    patches, keep, cot, vec_wide, vec, stack, normed, mask, token, n1t, dm, dmt, live, qkv, probs, att_t, middle, f_qkv, f_out, f_up, f_down, s_up3, act_, dh, g_up, g_down, up_core, down_core, up_dx, up_dy, up_sx, up_sy, dn_dx, dn_dy, dn_sx, dn_sy,
    vecs, bias, b_up, q_send, q_recv, m_send, m_recv, v_send, v_recv, own, saves, probs_sem, r_send, r_recv, w_send, w_recv,
):
    place = Place()
    _, side_y, side_c = place.sides()
    flat = [place.to(z=place.zs[k], x=x) for k in range(4) for x in (place.x, place.ox)][1:]
    later = Later(saves)
    loads = [pltpu.make_async_copy(h_patches, patches, own.at[10]), pltpu.make_async_copy(h_cot, cot, own.at[11])]

    def before():
        for load in loads:
            load.start()
        pad_keep(keep_in, keep)
        vec_wide[...] = jnp.zeros_like(vec_wide)
        for j in range(8):
            vec_wide[j : j + 1, :96] = singles[j][...].astype(F32)
        row = jnp.concatenate([singles[8][...].astype(F32)[j : j + 1] for j in range(3)], axis=1)
        for j in range(4):
            vec_wide[8 + j : 9 + j, :96] = row[:, 96 * j : 96 * j + 96]
        vec[...] = vec_wide[...].astype(BF16)
        loads[0].wait()
        for t in range(3):
            for f in range(8):
                s_up3[t, :, f * 128 : f * 128 + 128] = s_up[:, f * 384 + t * 128 : f * 384 + t * 128 + 128]
        stage_gather(images, slots, patches, keep, stack, live, mask, token)
        later.start("live", live, h_live)
        later.start("token", token, h_token)
        loads[1].wait()
        stage_grads(images, slots, width, cot, stack, live, dm, dmt)
        later.start("dm", dm, h_dm)

    enter(flat + [side_y, side_c], before)
    columns = [slice(m * width, (m + 1) * width) for m in range(3)]
    g_qkv = [Gather(place, s_qkv.at[:, columns[m]], f_qkv.at[:, columns[m]], 128 if m == 2 else 256, q_send.at[m], q_recv.at[m]) for m in range(3)]
    g_out = Gather(place, s_out, f_out, 256, q_send.at[3], q_recv.at[3])
    g_ups = [Gather(place, s_up3.at[t], f_up.at[t], (256, 384, 256)[t], m_send.at[t], m_recv.at[t]) for t in range(3)]
    g_downs = [Gather(place, s_down.at[t * 128 : t * 128 + 128], f_down.at[t], 256, m_send.at[3 + t], m_recv.at[3 + t]) for t in range(3)]
    groups = {"q": g_qkv[:1], "k": g_qkv[1:2], "v": g_qkv[2:], "o": [g_out]}
    groups.update({f"p{t}": [g_ups[t], g_downs[t]] for t in range(3)})
    every = g_qkv + [g_out] + [g for t in range(3) for g in (g_ups[t], g_downs[t])]
    mine = place.z * 2 + place.x
    tiny = []
    for j, peer in enumerate(flat):
        copy = pltpu.make_async_remote_copy(src_ref=vec, dst_ref=vecs.at[mine], send_sem=v_send.at[j], recv_sem=v_recv.at[j], device_id=peer, device_id_type=MESH)
        copy.start()
        tiny.append(copy)
    vecs[mine] = vec[...]
    core = place.sides()[2]
    swaps = {
        (name, t): pltpu.make_async_remote_copy(
            src_ref=g.at[t, :, :, place.oc], dst_ref=buffer.at[t], send_sem=r_send.at[2 * t + j], recv_sem=r_recv.at[2 * t + j], device_id=core, device_id_type=MESH
        )
        for t in range(2)
        for j, (name, g, buffer) in enumerate((("up", g_up, up_core), ("down", g_down, down_core)))
    }
    early = (
        Reduce(place, None, up_core.at[0], None, up_dx, up_dy, up_sx, up_sy, None, None, w_send.at[0], w_recv.at[0]),
        Reduce(place, None, down_core.at[0], None, dn_dx, dn_dy, dn_sx, dn_sy, None, None, w_send.at[1], w_recv.at[1]),
    )

    def merge(t):
        for name, g, buffer in (("up", g_up, up_core), ("down", g_down, down_core)):
            swaps[name, t].wait_recv()

            def body(z, _, g=g, buffer=buffer):
                buffer[t, z] = buffer[t, z] + g[t, z, :, place.c]
                return 0

            lax.fori_loop(0, 4, body, 0)
        if t == 0:
            for r in early:
                r.step_open()
        else:
            later.start("up_sum1", lambda: up_core.at[1], h_up1)
            later.start("down_sum1", lambda: down_core.at[1], h_down1)

    def act(slot):
        for group, phase in GATHER_PLAN[slot]:
            for g in groups[group]:
                g.phase(phase)
        if slot == MERGE_PLAN[0]:
            merge(0)
        if slot == MERGE_PLAN[1]:
            for r in early:
                r.step_diag()
        if slot == MERGE_PLAN[2]:
            merge(1)

    act(0)
    locals_ = [g.own(own.at[j]) for j, g in enumerate(every)]
    for copy in locals_:
        copy.start()
    for slot in range(1, 5):
        act(slot)
    for copy in tiny:
        copy.wait_recv()
    vectors[...] = jnp.concatenate([vecs[f][:, :96] for f in range(8)], axis=1).astype(F32)
    act(5)
    stage_norm(vectors[0:1, :], vectors[1:2, :], token, normed, n1t)
    later.start("n1t", n1t, h_n1t)
    for f in range(8):
        row = jnp.concatenate([vecs[f][8 + j : 9 + j, :96] for j in range(4)], axis=1).astype(F32)
        for t in range(3):
            b_up[t, :, f * 128 : f * 128 + 128] = row[:, t * 128 : t * 128 + 128]
    bias[...] = jnp.concatenate([vectors[2:3, :], jnp.zeros((1, width), F32), vectors[3:4, :]], axis=1)
    act(6)
    act(7)
    for m in range(3):
        act(8 + m)
        locals_[m].wait()
        g_qkv[m].finish()
        stage_qkv(images, width, normed, f_qkv, bias, qkv, m * width // TILE, (m + 1) * width // TILE)
    later.start("w_qkv", f_qkv, h_wqkv)
    later.start("qkv", qkv, h_qkv)

    def save_probs(slot, i):
        return pltpu.make_async_copy(probs.at[slot], h_probs.at[pl.ds(i * H, H)], probs_sem.at[slot])

    def attend(i, _):
        slot = lax.rem(i, 2)
        for j in range(5):
            pl.when(i == j)(lambda j=j: act(11 + j))
        pl.when(i >= 2)(lambda: save_probs(slot, i - 2).wait())
        stage_attention(width, qkv, mask, probs.at[slot], stack, i)
        save_probs(slot, i).start()
        return 0

    lax.fori_loop(0, images, attend, 0)
    for i in range(images - 2, images):
        save_probs(i % 2, i).wait()
    act(16)
    locals_[3].wait()
    g_out.finish()
    later.start("w_out", f_out, h_wout)
    later.wait("n1t")
    n2t = n1t
    stage_out(width, stack, f_out, vectors.at[4:5, :], token, vectors.at[5:6, :], vectors.at[6:7, :], normed, att_t, middle, normed, n2t)
    later.start("att_t", att_t, h_att_t)
    later.start("middle", middle, h_middle)
    for t in range(3):
        for part in range(2):
            for name, src, dst in (("act", act_, h_act), ("dh", dh, h_dh)):
                cols = slice(part * 512, part * 512 + 512)
                later.plan(f"{name}{t}{part}", lambda src=src, cols=cols: src.at[:, cols], lambda dst=dst, t=t, cols=cols: dst.at[t, :, cols])

    def enter_third(t):
        locals_[4 + 2 * t].wait()
        locals_[5 + 2 * t].wait()
        g_ups[t].finish()
        g_downs[t].finish()
        later.start(f"up{t}", lambda: f_up.at[t], lambda: h_up.at[t])
        later.start(f"down{t}", lambda: f_down.at[t], lambda: h_down.at[t])
        if t:
            later.wait(f"act{t - 1}0", f"dh{t - 1}0")
        if t == 2:
            for name in ("up", "down"):
                swaps[name, 0].wait_send()

    def middle_third(t):
        if t:
            later.wait(f"act{t - 1}1", f"dh{t - 1}1")

    def save_part(t, part):
        later.flights[f"act{t}{part}"]().start()
        later.flights[f"dh{t}{part}"]().start()
        if part and t < 2:
            swaps["up", t].start()
            swaps["down", t].start()
        elif part:
            later.start("g_up2", lambda: g_up.at[0], h_gup)
            later.start("g_down2", lambda: g_down.at[0], h_gdown)

    def feed(step, _):
        t, c = step // 4, step % 4
        slot = t % 2
        for j in range(12):
            if GATHER_PLAN[17 + j] or 17 + j in MERGE_PLAN:
                pl.when(step == j)(lambda j=j: act(17 + j))
        for j in range(3):
            pl.when(step == 4 * j)(lambda j=j: enter_third(j))
            pl.when(step == 4 * j + 2)(lambda j=j: middle_third(j))

        def put_up(c, value):
            y, at = c // 2, tile_at(c % 2, TILE)
            g_up[slot, :, :, :, y, :, at] = value.reshape(4, 2, 2, 48, TILE)

        def put_down(c, value):
            for x in range(2):
                g_down[slot, c, x] = value[:, x * 128 : (x + 1) * 128].reshape(2, 2, 192, 128)

        stage_mlp(width, normed, n2t, dm, dmt, f_up.at[t], b_up.at[t], f_down.at[t], act_, dh, put_up, put_down, g_b_up.at[t], c)
        for j in range(3):
            for part in range(2):
                pl.when(step == 4 * j + 2 * part + 1)(lambda j=j, part=part: save_part(j, part))
        return 0

    lax.fori_loop(0, 12, feed, 0)
    act(29)
    for r, h, buffer in ((early[0], h_own_up, up_core), (early[1], h_own_down, down_core)):
        r.step_sum()
        later.start(f"own{h is h_own_up}", buffer.at[0, :, place.x, place.y], h)
    waited = {"n1t"} | {f"{n}{t}{p}" for n in ("act", "dh") for t in range(2) for p in range(2)}
    for name in ("up", "down"):
        swaps[name, 1].wait_send()
    later.wait(*(n for n in later.flights if n not in waited))
    for copy in tiny:
        copy.wait_send()
    for g in every + list(early):
        g.drain()


def second_plain(
    images, slots, width, hidden_width,
    n2, n2t, dm, dmt, w_up, b_up, w_down, b_d, middle_in, live, gain2,
    out, middle, d_low, g_up, g_down, g_b_up, g_g2, g_s2, g_bd, g_bo, act, dh, stack,
):
    middle[...] = middle_in[...]

    def put(ref, c, value):
        ref[:, tile_at(c, TILE)] = value

    feed = functools.partial(stage_mlp, width, n2, n2t, dm, dmt, w_up, b_up, w_down, act, dh, functools.partial(put, g_up), functools.partial(put, g_down), g_b_up)
    loop(0, hidden_width // TILE, lambda c, _: feed(c), 1)
    add_products(width, stack, True, lambda cols: dot(act[...], w_down[:, cols]))
    stage_final(images, slots, width, middle, live, b_d, stack, out)
    add_products(width, stack, True, lambda cols: dot_nt(dh[...], w_up[cols, :]))
    stage_middle_back(middle, gain2, dm, stack, d_low, g_g2, g_s2, g_bd, g_bo)


def third_plain(
    images, slots, width, d_low, att_t, w_out, qkv_in, probs, n1t, w_qkv, token, gain, mid, live, keep,
    g_out, g_qkv, g_b, g_g1, g_s1, gp, stack, tile, flat, qkv,
):
    def put(ref, c, value):
        ref[:, tile_at(c, TILE)] = value

    def put_patches(i, value):
        gp[i] = value

    qkv[...] = qkv_in[...]
    tile[...] = jnp.zeros_like(tile)
    stage_out_back(width, att_t, d_low, w_out, functools.partial(put, g_out), stack)
    for i in range(images):
        stage_attention_back(width, qkv, probs.at[pl.ds(i * H, H)], stack, i)
    back = functools.partial(stage_qkv_back, images, width, qkv, n1t, tile, flat, functools.partial(put, g_qkv), g_b)
    loop(0, 3 * width // TILE, lambda c, _: back(c), 1)
    stage_norm_back(width, flat, w_qkv, stack)
    stage_end(images, slots, width, keep, token, gain, mid, live, stack, g_g1, g_s1, put_patches)


def second_kernel(
    images, slots, width,
    keep_in, vectors, s_bup, h_token, h_n1t, h_dm, h_live, h_qkv, h_probs, h_att_t, h_middle, h_wqkv, h_wout, h_up, h_down, h_act, h_dh, h_gup, h_gdown, h_up1, h_down1, h_own_up, h_own_down,
    gp, out_tokens, o_wide, o_down, e_small,
    out_vm, keep,
    e_up, e_down, e_out, e_q, e_k, e_v,
    stack, tile, flat, qkv, probs, t_a, t_b, r_a, r_b, mid, live, w_qkv, w_out, stage, g_b, g_g1, g_s1, g_g2, g_s2, g_bd, g_bo, g_attn,
    up_held, up_own, up_core, up_dx, up_dy, up_sx, up_sy, up_ln, dn_held, dn_own, dn_core, dn_dx, dn_dy, dn_sx, dn_sy, dn_ln,
    core4, dx4, dy4, sx4, sy4, ln4, v_home, v_core, v_sy, v_sx, v_ln, v_sent, v_total,
    send, recv, v_send, v_recv, own, loads, probs_sem, out_sem,
):
    place = Place()
    pad_keep(keep_in, keep)
    enter(place.along[1:] + list(place.sides()))
    def reduce_third(t, source, held, own4, core, dx, dy, sx, sy, ln, e, sem):
        sems = send.at[sem + t], recv.at[sem + t]
        if t == 0:
            r = Reduce(place, None, None, None, None, None, None, None, ln.at[0], e.at[0], *sems)
            r.own4 = own4
            return r
        return Reduce(place, source, held.at[t - 1], core, dx.at[t - 1], dy.at[t - 1], sx.at[t - 1], sy.at[t - 1], ln.at[t], e.at[t], *sems)

    r_up = [reduce_third(t, h_gup, up_held, up_own, up_core, up_dx, up_dy, up_sx, up_sy, up_ln, e_up, 0) for t in range(3)]
    r_down = [reduce_third(t, h_gdown, dn_held, dn_own, dn_core, dn_dx, dn_dy, dn_sx, dn_sy, dn_ln, e_down, 3) for t in range(3)]
    mlp = [(r_up[t], r_down[t]) for t in range(3)]
    r_q, r_k, r_v, r_out = (
        Reduce(place, g_attn.at[m], None, core4.at[m], dx4.at[m], dy4.at[m], sx4.at[m], sy4.at[m], ln4.at[m], e, send.at[6 + m], recv.at[6 + m])
        for m, e in enumerate((e_q, e_k, e_v, e_out))
    )
    small = SmallReduce(place, v_home, v_core, v_sy, v_sx, v_ln, v_send, v_recv)
    later = Later(loads)
    slots_ = [flat.at[:, 0:THIRD], flat.at[:, THIRD : 2 * THIRD]]
    groups = {"m0": mlp[0], "m1": mlp[1], "m2": mlp[2], "o": (r_out,), "q": (r_q,), "k": (r_k,), "v": (r_v,)}

    def act(slot):
        for phase in ("open", "core", "diag", "side", "line", "share"):
            for group, slots_of in REDUCE_PLAN:
                phases = {2: ("line", "share"), 5: ("open" if group == "m1" else "core", "diag", "side", "line", "share")}[len(slots_of)]
                if (phase, slot) in zip(phases, slots_of):
                    for r in groups[group]:
                        getattr(r, "step_" + phase)()
                        if phase == "core":
                            r.step_open()

    early = [
        pltpu.make_async_copy(h, into, own.at[j])
        for j, (h, into) in enumerate(((h_own_up, up_own), (h_own_down, dn_own), (h_up1, up_held.at[0]), (h_down1, dn_held.at[0])))
    ]
    for copy in early:
        copy.start()
    later.start("dh0", h_dh.at[0], slots_[0])
    later.start("up0", h_up.at[0], t_a)
    for j, (r, h, into) in enumerate(((r_up[2], h_gup, up_held), (r_down[2], h_gdown, dn_held))):
        r.begin(pltpu.make_async_copy(h.at[:, :, place.c], into.at[1], own.at[4 + j]))
    later.start("dh1", h_dh.at[1], slots_[1])
    later.start("up1", h_up.at[1], t_b)
    for copy, r in zip(early[:2], mlp[0]):
        copy.wait()
        r.step_send()
    for copy in early[2:]:
        copy.wait()
    act(0)
    for name, src, dst in (("mid", h_middle, mid), ("dm", h_dm, r_a), ("live", h_live, live), ("w_out", h_wout, w_out), ("qkv", h_qkv, qkv), ("w_qkv", h_wqkv, w_qkv)):
        later.start(name, src, dst)

    def load_probs(i):
        slot = i % 2
        return pltpu.make_async_copy(h_probs.at[pl.ds(i * H, H)], probs.at[slot], probs_sem.at[slot])

    load_probs(0).start()
    later.wait("dh0", "up0")
    act(1)
    add_products(width, stack, True, lambda cols: dot_nt(slots_[0][...], t_a[cols, :]))
    later.start("dh2", h_dh.at[2], slots_[0])
    later.start("up2", h_up.at[2], t_a)
    act(2)
    later.wait("dh1", "up1")
    add_products(width, stack, False, lambda cols: dot_nt(slots_[1][...], t_b[cols, :]))
    later.start("att_t", h_att_t, t_b)
    act(3)
    later.wait("dh2", "up2")
    add_products(width, stack, False, lambda cols: dot_nt(slots_[0][...], t_a[cols, :]))
    later.start("n1t", h_n1t, t_a)
    act(4)
    later.wait("mid", "dm")
    gain2 = vectors.at[5:6, :]
    stage_middle_back(mid, gain2, r_a, stack, r_b, g_g2, g_s2, g_bd, g_bo)
    later.start("token", h_token, r_a)

    def put(m, c, value):
        for j in range(2):
            col = 2 * c + j
            y, off = (col % 6) // 3, col % 3
            at = tile_at(off, 128)
            g_attn[col // 6 if m is None else m, :, :, :, y, :, at] = value[:, j * 128 : (j + 1) * 128].reshape(4, 2, 2, 48, 128)

    act(5)
    later.wait("att_t", "w_out", "qkv")
    stage_out_back(width, t_b, r_b, w_out, functools.partial(put, 3), stack)
    r_out.begin()

    def back(i, _):
        for j in range(5):
            pl.when(i == j)(lambda j=j: act(6 + j))
        load_probs(i).wait()
        pl.when(i + 1 < images)(lambda: load_probs(i + 1).start())
        stage_attention_back(width, qkv, probs.at[lax.rem(i, 2)], stack, i)
        return 0

    lax.fori_loop(0, images, back, 0)
    later.wait("n1t")
    tile[...] = jnp.zeros_like(tile)
    project = functools.partial(stage_qkv_back, images, width, qkv, t_a, tile, flat, functools.partial(put, None), g_b)
    third = width // TILE

    def project_tile(c, _):
        for m in range(3):
            pl.when(c == m * third)(lambda m=m: act(11 + m))
        project(c)
        for m, r in enumerate((r_q, r_k, r_v)):
            pl.when(c == m * third + third - 1)(lambda r=r: r.begin())
        return 0

    lax.fori_loop(0, 3 * third, project_tile, 0)
    act(14)
    later.wait("w_qkv")
    stage_norm_back(width, flat, w_qkv, stack)
    later.start("act0", h_act.at[0], slots_[0])
    later.start("act1", h_act.at[1], slots_[1])
    later.start("down0", h_down.at[0], r_b)
    act(15)
    later.wait("token", "live")
    flights = []

    def put_patches(i, value):
        if i >= 2:
            flights[i - 2].wait()
        stage[i % 2] = value
        copy = pltpu.make_async_copy(stage.at[i % 2], gp.at[i], out_sem.at[i % 2])
        copy.start()
        flights.append(copy)

    stage_end(images, slots, width, keep, r_a, vectors.at[0:1, :], mid, live, stack, g_g1, g_s1, put_patches)
    later.start("middle", h_middle, mid)
    later.start("down1", h_down.at[1], r_a)
    act(16)
    v_home[...] = jnp.zeros_like(v_home)
    for j, (ref, base) in enumerate(((g_g1, 0), (g_s1, 0), (g_b, 0), (g_b, 2 * width), (g_bo, 0), (g_g2, 0), (g_s2, 0), (g_bd, 0))):
        row = ref[:, base : base + width]
        for f in range(8):
            v_home[f // 2, f % 2, j : j + 1, :96] = row[:, 96 * f : 96 * f + 96]
    for f in range(8):
        row = jnp.concatenate([s_bup[t, :, f * 128 : f * 128 + 128] for t in range(3)], axis=1)
        for j in range(4):
            v_home[f // 2, f % 2, 8 + j : 9 + j, :96] = row[:, 96 * j : 96 * j + 96]
    small.begin()
    act(17)
    later.wait("act0", "down0")
    add_products(width, stack, True, lambda cols: dot(slots_[0][...], r_b[:, cols]))
    later.start("act2", h_act.at[2], slots_[0])
    later.start("down2", h_down.at[2], r_b)
    small.step_core(v_sent)
    act(18)
    later.wait("act1", "down1")
    add_products(width, stack, False, lambda cols: dot(slots_[1][...], r_a[:, cols]))
    small.step_y(v_sent, v_total)
    act(19)
    later.wait("act2", "down2", "middle")
    add_products(width, stack, False, lambda cols: dot(slots_[0][...], r_b[:, cols]))
    small.step_x(v_total)
    act(20)
    stage_final(images, slots, width, mid, live, vectors.at[7:8, :], stack, out_vm)
    later.start("tokens", out_vm, out_tokens)
    small.step_line(e_small)
    act(21)
    act(22)
    for r in r_up + r_down:
        r.finish()
    for t in range(3):
        for c in range(2):
            for y in range(2):
                for f in range(4):
                    col = (4 * y + f) * 384 + t * 128
                    o_wide[48 * c : 48 * c + 48, 3 * width + col : 3 * width + col + 128] = e_up[t, c, y, :, f * 128 : f * 128 + 128]
        o_down[t * 128 : t * 128 + 128, :] = e_down[t].reshape(width, 128).T
    half = width // 2

    def place_blocks(ref, base, e):
        for c in range(2):
            for y in range(2):
                ref[48 * c : 48 * c + 48, base + y * half : base + y * half + half] = e[c, y]

    r_out.finish()
    place_blocks(o_wide, 7 * width, e_out)
    for m, (r, e) in enumerate(((r_q, e_q), (r_k, e_k), (r_v, e_v))):
        r.finish()
        place_blocks(o_wide, m * width, e)
    later.wait("tokens")
    for copy in flights[-2:]:
        copy.wait()
    for r in r_up + r_down + [r_out, r_q, r_k, r_v, small]:
        r.drain()


def last_kernel(images, width, h_patches, h_tokens, small, h_wide, h_down, patches, tokens, o_qkv, o_up, o_out, o_down, o_b_up, *rest):
    vectors, (held_p, held_t, wide, down, f_wide, f_down, loads, stores, own) = rest[:8], rest[8:]
    first = [pltpu.make_async_copy(h_wide, wide, own.at[0]), pltpu.make_async_copy(h_down, down, own.at[1])]
    for load in first:
        load.start()
    copies = []
    for i in range(images):
        for j, (src, held, dst) in enumerate(((h_patches, held_p, patches), (h_tokens, held_t, tokens))):
            load = pltpu.make_async_copy(src.at[i], held.at[i], loads.at[2 * i + j])
            load.start()
            copies.append((load, pltpu.make_async_copy(held.at[i], dst.at[i], stores.at[2 * i + j])))
    for j, ref in enumerate(vectors):
        ref[...] = small[j : j + 1, :96]
    row = jnp.concatenate([small[8 + j : 9 + j, :96] for j in range(4)], axis=1)
    for j in range(3):
        o_b_up[j : j + 1, :] = row[:, j * 128 : (j + 1) * 128]
    stored = []
    first[1].wait()
    f_down[...] = down[...].astype(F32)
    stored.append(pltpu.make_async_copy(f_down, o_down, own.at[2]))
    stored[-1].start()
    first[0].wait()
    for j, (dst, begin, end) in enumerate(((o_qkv, 0, 3), (o_up, 3, 7), (o_out, 7, 8))):
        cols = slice(begin * width, end * width)
        f_wide[:, cols] = wide[:, cols].astype(F32)
        stored.append(pltpu.make_async_copy(f_wide.at[:, cols], dst, own.at[3 + j]))
        stored[-1].start()
    for load, store in copies:
        load.wait()
        store.start()
    for store in stored + [store for _, store in copies]:
        store.wait()


def shards(
    linked,
    patches, keep, ln1_gain, ln1_bias, w_qkv, b_query, b_value, w_out, b_out,
    ln2_gain, ln2_bias, w_up, b_up, w_down, b_down, cotangent,
):
    images, slots = keep.shape
    width = patches.shape[2]
    hidden_width = w_up.shape[1]
    keep_pad = jnp.pad(keep, ((0, 0), (0, SLOT - slots)), constant_values=-1).reshape(images, 1, SLOT)
    part = ln1_gain.shape[0]
    singles = [v.reshape(1, part) for v in (ln1_gain, ln1_bias, b_query, b_value, b_out, ln2_gain, ln2_bias, b_down)]
    rows_low, rows_wide = ((ROWS, width), BF16), ((ROWS, width), F32)
    cols_low = ((width, ROWS), BF16)
    live_like, mask_like = ((ROWS, BLOCK), F32), ((images, SLOT, SLOT), F32)
    heads_like = ((images, SLOT, 3 * width), BF16)
    probs_like = ((images * H, SLOT, SLOT), BF16)
    row_like = ((1, width), F32)

    if linked:
        half = width // 2
        full = lambda v: ((v.shape[0] * 8, v.shape[1]), BF16)
        up3, down3, hid3 = ((3, width, THIRD), BF16), ((3, THIRD, width), BF16), ((3, ROWS, THIRD), BF16)
        gup_like, gdown_like = (4, 2, 2, 2, 48, THIRD // 2), (4, 2, 2, 2, width // 4, 128)
        outs = [
            ((16, width), F32), ((3, 1, THIRD), F32), rows_low, cols_low, rows_low, live_like, heads_like, probs_like, cols_low, rows_wide,
            full(w_qkv), full(w_out), up3, down3, hid3, hid3, (gup_like, BF16), (gdown_like, BF16), ((4, 2) + gup_like[3:], BF16), ((4, 2) + gdown_like[3:], BF16),
            ((4,) + gup_like[4:], BF16), ((4,) + gdown_like[4:], BF16),
        ]
        scratch = [
            (patches.shape, BF16), ((images, 1, SLOT), jnp.int32), (patches.shape, BF16), ((16, BLOCK), F32), ((16, BLOCK), BF16),
            rows_wide, rows_low, mask_like, rows_low, cols_low, rows_low, cols_low, live_like, heads_like, ((2, H, SLOT, SLOT), BF16), cols_low,
            rows_wide, full(w_qkv), full(w_out), up3, down3, ((3, part, THIRD), BF16), hid3[0][1:], hid3[0][1:], (2,) + gup_like, (2,) + gdown_like,
            (2, 4, 2) + gup_like[3:], (2, 4, 2) + gdown_like[3:],
        ]
        for r, w, first, other in ((48, THIRD // 2, (4, 48, 128), (4, 48, THIRD // 2 - 128)), (width // 4, 128, (4, 64, 128), (4, width // 4 - 64, 128))):
            scratch += [other, first, (4, r, w), (4, r, w)]
        scratch += [((8, 16, BLOCK), BF16), ((1, 3 * width), F32), ((3, 1, THIRD), F32)]
        scratch = [s if isinstance(s[0], tuple) else (s, BF16) for s in scratch]
        vectors, g_b_up, token, n1t, dm, live, qkv, probs, att_t, middle, qkv_full, out_full, up_full, down_full, act, dh, g_up, g_down, up1, down1, own_up, own_down = pl.pallas_call(
            functools.partial(first_kernel, images, slots, width),
            out_shape=[jax.ShapeDtypeStruct(*o) for o in outs],
            in_specs=[ANY, VMEM, ANY] + [VMEM] * 13,
            out_specs=[VMEM] * 2 + [ANY] * 20,
            scratch_shapes=[pltpu.VMEM(*s) for s in scratch]
            + [pltpu.SemaphoreType.DMA((4, 28))] * 2
            + [pltpu.SemaphoreType.DMA((6, 28))] * 2
            + [pltpu.SemaphoreType.DMA((7,))] * 2
            + [pltpu.SemaphoreType.DMA((12,)), pltpu.SemaphoreType.DMA((33,)), pltpu.SemaphoreType.DMA((2,))]
            + [pltpu.SemaphoreType.DMA((4,))] * 2
            + [pltpu.SemaphoreType.DMA((2, 10))] * 2,
            compiler_params=pltpu.CompilerParams(vmem_limit_bytes=LIMIT, collective_id=0, has_side_effects=True),
            name="first",
        )(patches, keep, cotangent, *singles, b_up.reshape(3, -1), w_qkv, w_out, w_up, w_down)
        final = lambda r, w, lead=(): (lead + (2, 2, r, w), BF16)
        attn = final(48, half)
        outs = [((images, slots, width), F32), ((images, slots, width), BF16), ((part, 8 * width), BF16), ((half, width), BF16), ((16, BLOCK), F32)]

        def buffers(r, w, by_rows, cut, cores, lead, lines):
            other = (4, r - cut, w) if by_rows else (4, r, w - cut)
            first = (4, cut, w) if by_rows else (4, r, cut)
            return [(cores + (4, 2, 2, r, w), BF16)] + [(lead + s, BF16) for s in (other, first, (4, r, w), (4, r, w))] + [(lines + (3, r, w), BF16)]

        scratch = [((images, slots, width), BF16), ((images, 1, SLOT), jnp.int32), final(48, THIRD // 2, (3,)), final(width // 4, 128, (3,)), attn, attn, attn, attn]
        scratch += [rows_wide, ((ROWS, TILE), F32), ((ROWS, 3 * width), BF16), heads_like, ((2, H, SLOT, SLOT), BF16), cols_low, cols_low, rows_low, rows_low]
        scratch += [rows_wide, live_like, ((width, 3 * width), BF16), ((width, width), BF16), ((2, slots, width), F32), ((1, 3 * width), F32)] + [row_like] * 6
        scratch += [((4, 4, 2, 2, 2, 48, half), BF16)]
        scratch += [((2, 4, 2, 2, 48, THIRD // 2), BF16), ((4, 48, THIRD // 2), BF16)] + buffers(48, THIRD // 2, False, 128, (), (2,), (3,))
        scratch += [((2, 4, 2, 2, width // 4, 128), BF16), ((4, width // 4, 128), BF16)] + buffers(width // 4, 128, True, 64, (), (2,), (3,))
        scratch += buffers(48, half, False, 128, (4,), (4,), (4,))
        small_like, line_like = ((4, 2, 16, BLOCK), F32), ((3, 16, BLOCK), F32)
        scratch += [small_like, small_like, small_like, ((4, 16, BLOCK), F32), line_like, small_like, small_like]
        grad_patches, out_tokens, o_wide, o_down, small = pl.pallas_call(
            functools.partial(second_kernel, images, slots, width),
            out_shape=[jax.ShapeDtypeStruct(*o) for o in outs],
            in_specs=[VMEM] * 3 + [ANY] * 20,
            out_specs=[ANY] * 2 + [VMEM] * 3,
            scratch_shapes=[pltpu.VMEM(*s) for s in scratch]
            + [pltpu.SemaphoreType.DMA((10, 10))] * 2
            + [pltpu.SemaphoreType.DMA((6,))] * 2
            + [pltpu.SemaphoreType.DMA((6,)), pltpu.SemaphoreType.DMA((23,)), pltpu.SemaphoreType.DMA((2,)), pltpu.SemaphoreType.DMA((2,))],
            compiler_params=pltpu.CompilerParams(vmem_limit_bytes=LIMIT, collective_id=1, has_side_effects=True),
            name="second",
        )(keep, vectors, g_b_up, token, n1t, dm, live, qkv, probs, att_t, middle, qkv_full, out_full, up_full, down_full, act, dh, g_up, g_down, up1, down1, own_up, own_down)
        outs = [
            ((images, slots, width), F32), ((images, slots, width), BF16), ((part, 3 * width), F32), ((part, 4 * width), F32), ((part, width), F32),
            ((half, width), F32), ((3, 128), F32),
        ] + [((1, part), F32)] * 8
        grad_patches, out_tokens, sum_qkv, sum_up, sum_out, sum_down, b_up_sum, *rows = pl.pallas_call(
            functools.partial(last_kernel, images, width),
            out_shape=[jax.ShapeDtypeStruct(*o) for o in outs],
            in_specs=[ANY, ANY, VMEM, ANY, ANY],
            out_specs=[ANY] * 6 + [VMEM] * 9,
            scratch_shapes=[
                pltpu.VMEM(*s)
                for s in (((images, slots, width), F32), ((images, slots, width), BF16), ((part, 8 * width), BF16), ((half, width), BF16), ((part, 8 * width), F32), ((half, width), F32))
            ]
            + [pltpu.SemaphoreType.DMA((2 * images,))] * 2
            + [pltpu.SemaphoreType.DMA((6,))],
            compiler_params=pltpu.CompilerParams(vmem_limit_bytes=LIMIT),
            name="last",
        )(grad_patches, out_tokens, small, o_wide, o_down)
        rows = [row.reshape(part) for row in rows]
        b_up_sum = b_up_sum.reshape(half)
    else:
        gather = lambda v: lax.all_gather(v, "fsdp", axis=0, tiled=True)
        vectors = jnp.pad(gather(jnp.concatenate(singles, axis=0).T).T.astype(F32), ((0, 8), (0, 0)))
        bias_up = gather(b_up).astype(F32).reshape(1, hidden_width)
        qkv_full, out_full, up_full, down_full = gather(w_qkv), gather(w_out), gather(w_up), gather(w_down)
        outs = [rows_low, cols_low, rows_low, cols_low, live_like, heads_like, probs_like, cols_low, rows_wide, rows_low, cols_low]
        scratch = [rows_wide, rows_low, mask_like, rows_low, ((1, 3 * width), F32)]
        token, n1t, dm, dmt, live, qkv, probs, att_t, middle, n2, n2t = call(
            functools.partial(first_plain, images, slots, width),
            outs, scratch, (patches, keep_pad, cotangent, vectors, qkv_full, out_full), "first",
        )
        gain1, gain2, b_d = vectors[0:1], vectors[5:6], vectors[7:8]
        hid = ((ROWS, hidden_width), BF16)
        out_tokens, d_mid, d_low, g_up, g_down, g_b_up, g_g2, g_s2, g_bd, g_bo = call(
            functools.partial(second_plain, images, slots, width, hidden_width),
            [((images, slots, width), BF16), rows_wide, rows_low] + [((width, hidden_width), BF16)] * 2 + [((1, hidden_width), F32)] + [row_like] * 4,
            [hid, hid, rows_wide],
            (n2, n2t, dm, dmt, up_full, bias_up, down_full, b_d, middle, live, gain2),
            "second",
        )
        g_out, g_qkv, g_b, g_g1, g_s1, grad_patches = call(
            functools.partial(third_plain, images, slots, width),
            [((width, width), BF16), ((width, 3 * width), BF16), ((1, 3 * width), F32), row_like, row_like, ((images, slots, width), F32)],
            [rows_wide, ((ROWS, TILE), F32), ((ROWS, 3 * width), BF16), heads_like],
            (d_low, att_t, out_full, qkv, probs, n1t, qkv_full, token, gain1, d_mid, live, keep_pad),
            "third",
        )
        scat = lambda v, dim=0: lax.psum(lax.psum_scatter(v, "fsdp", scatter_dimension=dim, tiled=True), "dp").astype(F32)
        rows = jnp.concatenate([g_g1, g_s1, g_b[:, :width], g_b[:, 2 * width :], g_bo, g_g2, g_s2, g_bd], axis=0).astype(BF16)
        rows = scat(rows, 1)
        b_up_sum = scat(g_b_up.astype(BF16), 1)[0]
        sum_qkv, sum_out, sum_up, sum_down = scat(g_qkv), scat(g_out), scat(g_up), scat(g_down, 1).T
    return (
        out_tokens, grad_patches, rows[0], rows[1], sum_qkv, rows[2], rows[3], sum_out, rows[4],
        rows[5], rows[6], sum_up, b_up_sum, sum_down, rows[7],
    )


def solution(mesh):
    linked = (mesh.shape["fsdp"], mesh.shape["dp"]) == (8, 4)
    many, one, two = P(("fsdp", "dp"), None, None), P("fsdp"), P("fsdp", None)
    in_specs = (many, P(("fsdp", "dp"), None), one, one, two, one, one, two, one, one, one, two, one, two, one, many)
    out_specs = (many, many, one, one, two, one, one, two, one, one, one, two, one, two, one)
    return jax.shard_map(functools.partial(shards, linked), mesh=mesh, in_specs=in_specs, out_specs=out_specs, check_vma=False)
```

```python
import functools
import math

import jax
import jax.numpy as jnp
from jax import lax
from jax.experimental import pallas as pl
from jax.experimental.pallas import tpu as pltpu
from jax.sharding import PartitionSpec as P

H = 12
HD = 64
EPSILON = 1e-06
F32 = jnp.float32
BF16 = jnp.bfloat16
SLOT = 200
ROWS = 1024
BLOCK = 128
TILE = 256
NT = (((1,), (1,)), ((), ()))


def dot(left, right):
    return jnp.dot(left, right, preferred_element_type=F32)


def dot_nt(left, right):
    return lax.dot_general(left, right, NT, preferred_element_type=F32)


def tile_at(index, size):
    if isinstance(index, int):
        return pl.ds(index * size, size)
    return pl.ds(pl.multiple_of(index * size, size), size)


def loop(begin, end, body, unroll):
    if (end - begin) == unroll:
        for j in range(begin, end):
            body(j, 0)
        return

    def group(t, _):
        for u in range(unroll):
            body(begin + t * unroll + u, 0)
        return 0

    lax.fori_loop(0, (end - begin) // unroll, group, 0)


def norm_parts(values):
    centre = values - jnp.mean(values, axis=-1, keepdims=True)
    spread = jnp.mean(centre * centre, axis=-1, keepdims=True)
    inverse = lax.rsqrt(spread + EPSILON)
    return centre * inverse, inverse


def norm_back(hat, inverse, gain, grad):
    scaled = grad * gain
    along = jnp.mean(scaled * hat, axis=-1, keepdims=True)
    return inverse * (scaled - jnp.mean(scaled, axis=-1, keepdims=True) - hat * along)


def gelu_parts(hidden):
    size = jnp.abs(hidden)
    bell = jnp.exp(hidden * hidden * -0.5)
    t = 1.0 / (1.0 + size * (0.3275911 / math.sqrt(2.0)))
    tail = 1.061405429 * 0.5
    for term in (-1.453152027, 1.421413741, -0.284496736, 0.254829592):
        tail = tail * t + term * 0.5
    tail = tail * t * bell
    below = jnp.where(hidden >= 0, 1.0 - tail, tail)
    slope = below + hidden * (bell * (1.0 / math.sqrt(2.0 * math.pi)))
    return hidden * below, slope


def first_lanes(rows):
    return lax.broadcasted_iota(jnp.int32, (rows, 2 * HD), 1) < HD


def pad_keep(keep, padded):
    padded[...] = jnp.full_like(padded, -1)
    for i in range(keep.shape[0]):
        padded[i, :, : keep.shape[1]] = keep[i : i + 1, :]


def stage_gather(images, slots, patches, keep, stack, live, mask, token):
    stack[...] = jnp.zeros_like(stack)
    live[...] = jnp.zeros_like(live)

    def gather(i, _):
        row = keep[i]
        column = jnp.broadcast_to(row, (SLOT, SLOT)).T
        mask[i] = jnp.where(column >= 0, 0.0, -1e30)
        alive = (column >= 0).astype(F32)
        chosen = (column[:, :slots] == lax.broadcasted_iota(jnp.int32, (SLOT, slots), 1)).astype(F32).astype(BF16)
        rows = pl.ds(pl.multiple_of(i * SLOT, 8), SLOT)
        stack[rows, :] = dot(chosen, patches[i])
        live[rows, :] = alive[:, :BLOCK]
        return 0

    loop(0, images, gather, 1)

    def narrow(b, _):
        rows = tile_at(b, BLOCK)
        token[rows, :] = stack[rows, :].astype(BF16)
        return 0

    loop(0, ROWS // BLOCK, narrow, 2)


def stage_norm(gain, shift, token, normed, normed_t):
    def norm(b, _):
        rows = tile_at(b, BLOCK)
        hat, _ = norm_parts(token[rows, :].astype(F32))
        low = (hat * gain + shift).astype(BF16)
        normed[rows, :] = low
        normed_t[:, rows] = low.T
        return 0

    loop(0, ROWS // BLOCK, norm, 4)


def stage_grads(images, slots, width, cot, stack, live, dm, dm_t):
    stack[...] = jnp.zeros_like(stack)
    for i in range(images):
        stack[i * SLOT : i * SLOT + slots, :] = cot[i].astype(F32)

    def grads(b, _):
        rows = tile_at(b, BLOCK)
        low = (stack[rows, :] * jnp.concatenate([live[rows, :]] * (width // BLOCK), axis=1)).astype(BF16)
        dm[rows, :] = low
        dm_t[:, rows] = low.T
        return 0

    loop(0, ROWS // BLOCK, grads, 2)


def stage_qkv(images, width, normed, w_qkv, bias, qkv, begin, end):
    def body(c, _):
        cols = tile_at(c, TILE)
        scale = jnp.where(c < width // TILE, 1.0 / math.sqrt(HD), 1.0)
        values = (dot(normed[...], w_qkv[:, cols]) + bias[:, cols]) * scale
        for i in range(images):
            qkv[i, :, cols] = values[i * SLOT : (i + 1) * SLOT].astype(BF16)
        return 0

    loop(begin, end, body, 1)


def stage_attention(width, qkv, mask, probs, stack, i):
    low = first_lanes(SLOT)
    for p in range(H // 2):
        q2 = qkv[i, :, p * 128 : (p + 1) * 128]
        k2 = qkv[i, :, width + p * 128 : width + (p + 1) * 128]
        v2_t = qkv[i, :, 2 * width + p * 128 : 2 * width + (p + 1) * 128].T
        outs = []
        for h in range(2):
            qh = jnp.where(low if h == 0 else ~low, q2, jnp.zeros_like(q2))
            scores = dot_nt(k2, qh) + mask[i]
            exponent = jnp.exp(scores - jnp.max(scores, axis=0, keepdims=True))
            share = 1.0 / jnp.sum(exponent, axis=0, keepdims=True)
            prob = (exponent * share).astype(BF16)
            probs[2 * p + h] = prob
            outs.append(dot(v2_t[h * HD : (h + 1) * HD], prob))
        stack[pl.ds(pl.multiple_of(i * SLOT, 8), SLOT), p * 128 : (p + 1) * 128] = jnp.concatenate(outs, axis=0).T


def stage_out(width, stack, w_out, bias, token, gain, shift, att, att_t, middle, normed, normed_t):
    def low(b, _):
        rows = tile_at(b, BLOCK)
        values = stack[rows, :].astype(BF16)
        att[rows, :] = values
        att_t[:, rows] = values.T
        return 0

    loop(0, ROWS // BLOCK, low, 4)

    def body(c, _):
        cols = tile_at(c, TILE)
        middle[:, cols] = token[:, cols].astype(F32) + (dot(att[...], w_out[:, cols]) + bias[:, cols])
        return 0

    loop(0, width // TILE, body, 1)

    def norm(b, _):
        rows = tile_at(b, BLOCK)
        hat, _ = norm_parts(middle[rows, :])
        values = (hat * gain[...] + shift[...]).astype(BF16)
        normed[rows, :] = values
        normed_t[:, rows] = values.T
        return 0

    loop(0, ROWS // BLOCK, norm, 4)


def stage_mlp(width, normed, normed_t, dm, dm_t, w_up, b_up, w_down, act, dh, put_up, put_down, g_b_up, c):
    cols = tile_at(c, TILE)
    up, down, bias = w_up[:, cols], w_down[cols, :], b_up[:, cols]
    total, waiting = 0.0, []
    for r in range(ROWS // TILE + 1):
        if r < ROWS // TILE:
            rows = slice(r * TILE, (r + 1) * TILE)
            waiting.append((rows, dot(normed[rows, :], up) + bias, dot_nt(dm[rows, :], down)))
        if r:
            rows, hidden, d_act = waiting.pop(0)
            value, slope = gelu_parts(hidden)
            grad = (d_act * slope).astype(BF16)
            act[rows, cols] = value.astype(BF16)
            dh[rows, cols] = grad
            total = total + jnp.sum(grad.astype(F32), axis=0, keepdims=True)
    g_b_up[:, cols] = total
    put_up(c, dot(normed_t[...], dh[:, cols]).astype(BF16))
    put_down(c, dot(dm_t[...], act[:, cols]).astype(BF16))


def add_products(width, stack, fresh, product):
    def body(c, _):
        cols = tile_at(c, TILE)
        value = product(cols)
        stack[:, cols] = value if fresh else stack[:, cols] + value
        return 0

    loop(0, width // TILE, body, 1)


def stage_final(images, slots, width, middle, live, b_down, stack, out):
    def final(b, _):
        rows = tile_at(b, BLOCK)
        stack[rows, :] = (middle[rows, :] + (stack[rows, :] + b_down[...])) * jnp.concatenate([live[rows, :]] * (width // BLOCK), axis=1)
        return 0

    loop(0, ROWS // BLOCK, final, 2)
    for i in range(images):
        out[i] = stack[i * SLOT : i * SLOT + slots, :].astype(BF16)


def stage_middle_back(middle, gain, dm, stack, d_mid_low, g_gain, g_shift, g_b_down, g_b_out):
    for ref in (g_gain, g_shift, g_b_down, g_b_out):
        ref[...] = jnp.zeros_like(ref)

    def back(b, _):
        rows = tile_at(b, BLOCK)
        grad = stack[rows, :]
        hat, inverse = norm_parts(middle[rows, :])
        g_gain[...] += jnp.sum(grad * hat, axis=0, keepdims=True)
        g_shift[...] += jnp.sum(grad, axis=0, keepdims=True)
        own = dm[rows, :].astype(F32)
        g_b_down[...] += jnp.sum(own, axis=0, keepdims=True)
        total = own + norm_back(hat, inverse, gain[...], grad)
        middle[rows, :] = total
        low = total.astype(BF16)
        d_mid_low[rows, :] = low
        g_b_out[...] += jnp.sum(low.astype(F32), axis=0, keepdims=True)
        return 0

    loop(0, ROWS // BLOCK, back, 2)


def stage_out_back(width, att_t, d_mid_low, w_out, put_out, stack):
    def body(c, _):
        cols = tile_at(c, TILE)
        put_out(c, dot(att_t[...], d_mid_low[:, cols]).astype(BF16))
        stack[:, cols] = dot_nt(d_mid_low[...], w_out[cols, :])
        return 0

    loop(0, width // TILE, body, 1)


def stage_attention_back(width, qkv, probs, stack, i):
    low = first_lanes(SLOT)
    for p in range(H // 2):
        at_q = slice(p * 128, (p + 1) * 128)
        at_k = slice(width + p * 128, width + (p + 1) * 128)
        at_v = slice(2 * width + p * 128, 2 * width + (p + 1) * 128)
        q2, k2, v2 = qkv[i, :, at_q], qkv[i, :, at_k], qkv[i, :, at_v]
        k2_t = k2.T
        da = stack[pl.ds(pl.multiple_of(i * SLOT, 8), SLOT), at_q].astype(BF16)
        dq, dk, dv = [], 0.0, 0.0
        for h in range(2):
            pick = lambda m: jnp.where(low if h == 0 else ~low, m, jnp.zeros_like(m))
            prob = probs[2 * p + h]
            d_prob = dot_nt(pick(v2), da)
            mixed = prob.astype(F32)
            moved = mixed * d_prob
            total = jnp.sum(moved, axis=0, keepdims=True)
            ds = (moved - mixed * total).astype(BF16)
            dq.append(dot(k2_t[h * HD : (h + 1) * HD], ds))
            dk = dk + dot(ds, pick(q2))
            dv = dv + dot(prob, pick(da))
        qkv[i, :, at_q] = (jnp.concatenate(dq, axis=0).T * (1.0 / math.sqrt(HD))).astype(BF16)
        qkv[i, :, at_k] = dk.astype(BF16)
        qkv[i, :, at_v] = dv.astype(BF16)


def stage_qkv_back(images, width, d_qkv, normed_t, tile, flat, put_qkv, g_b_qkv, c):
    cols = tile_at(c, TILE)
    for i in range(images):
        tile[i * SLOT : (i + 1) * SLOT, :] = d_qkv[i, :, cols].astype(F32)
    values = tile[...]
    g_b_qkv[:, cols] = jnp.sum(values, axis=0, keepdims=True)
    low = values.astype(BF16)
    flat[:, cols] = low
    put_qkv(c, dot(normed_t[...], low).astype(BF16))


def stage_norm_back(width, flat, w_qkv, stack):
    def body(c, _):
        cols = tile_at(c, TILE)
        stack[:, cols] = dot_nt(flat[...], w_qkv[cols, :])
        return 0

    loop(0, width // TILE, body, 1)


def stage_end(images, slots, width, keep, token, gain, middle, live, stack, g_gain, g_shift, put_patches):
    for ref in (g_gain, g_shift):
        ref[...] = jnp.zeros_like(ref)

    def back(b, _):
        rows = tile_at(b, BLOCK)
        grad = stack[rows, :]
        hat, inverse = norm_parts(token[rows, :].astype(F32))
        g_gain[...] += jnp.sum(grad * hat, axis=0, keepdims=True)
        g_shift[...] += jnp.sum(grad, axis=0, keepdims=True)
        total = middle[rows, :] + norm_back(hat, inverse, gain[...], grad)
        stack[rows, :] = total * jnp.concatenate([live[rows, :]] * (width // BLOCK), axis=1)
        return 0

    loop(0, ROWS // BLOCK, back, 2)

    def scatter(i, _):
        chosen = (lax.broadcasted_iota(jnp.int32, (slots, SLOT), 0) == keep[i]).astype(F32).astype(BF16)
        values = stack[pl.ds(pl.multiple_of(i * SLOT, 8), SLOT), :]
        high = values.astype(BF16)
        rest = (values - high.astype(F32)).astype(BF16)
        put_patches(i, dot(chosen, high) + dot(chosen, rest))
        return 0

    for i in range(images):
        scatter(i, 0)


MESH = pl.DeviceIdType.MESH


class Place:
    def __init__(self):
        f, d = lax.axis_index("fsdp"), lax.axis_index("dp")
        self.z, self.x = f // 2, lax.rem(f, 2)
        self.y, self.c = d // 2, lax.rem(d, 2)
        z = self.z
        self.zs = [z, z + 1 - 2 * lax.rem(z, 2), lax.rem(z + 2, 4), 3 - z]
        self.ox, self.oy, self.oc = 1 - self.x, 1 - self.y, 1 - self.c
        self.beside = self.to(x=self.ox), self.to(y=self.oy), self.to(c=self.oc)
        self.along = [self.to(z=k) for k in self.zs]

    def to(self, z=None, x=None, y=None, c=None):
        z, x, y, c = (own if new is None else new for new, own in ((z, self.z), (x, self.x), (y, self.y), (c, self.c)))
        return (z * 2 + x, y * 2 + c)

    def sides(self):
        return self.beside


def enter(peers, meanwhile=None):
    barrier = pltpu.get_barrier_semaphore()
    for peer in peers:
        pl.semaphore_signal(barrier, inc=1, device_id=peer, device_id_type=MESH)
    if meanwhile is not None:
        meanwhile()
    pl.semaphore_wait(barrier, len(peers))


class Gather:
    def __init__(self, place, shard, full, first_cols, send, recv):
        self.place, self.shard, self.full, self.send, self.recv = place, shard, full, send, recv
        self.rows, cols = shard.shape
        self.half, self.wide, self.cut = self.rows // 2, cols // 2, first_cols
        self.started = []

    def spot(self, *args):
        return lambda: self.place_of(*args)

    def place_of(self, z, x, y, part=None, local=False):
        p = self.place
        base = 0 if local else (z * 2 + x) * self.rows
        rows = pl.ds(pl.multiple_of(base + p.c * self.half, 16), self.half)
        if y is None:
            return rows, slice(None)
        start, size = (y * self.wide, self.wide) if part is None else ((y * self.wide, self.cut) if part == 0 else (y * self.wide + self.cut, self.wide - self.cut))
        return rows, pl.ds(pl.multiple_of(start, 128), size)

    def copy(self, spot, sem, peer, local=None):
        src = self.full.at[spot] if local is None else self.shard.at[local]
        return pltpu.make_async_remote_copy(
            src_ref=src, dst_ref=self.full.at[spot], send_sem=self.send.at[sem], recv_sem=self.recv.at[sem], device_id=peer, device_id_type=MESH
        )

    def start(self, spot, sem, peer, local=None):
        def make():
            return self.copy(spot(), sem, peer, None if local is None else local())

        make().start()
        self.started.append(make)

    def arrived(self, spot, sem):
        self.copy(spot(), sem, self.place.sides()[0]).wait_recv()

    def own(self, sem):
        p = self.place
        rows = pl.ds(pl.multiple_of((p.z * 2 + p.x) * self.rows, 16), self.rows)
        return pltpu.make_async_copy(self.shard, self.full.at[rows, :], sem)

    def lines(self, *ks):
        p = self.place
        spot, local = self.spot(p.z, p.x, p.y), self.spot(p.z, p.x, p.y, None, True)
        for k in ks:
            self.start(spot, k, p.along[k], local)

    def beside(self):
        p = self.place
        side_x, side_y, _ = p.sides()
        self.start(self.spot(p.z, p.x, p.y), 4, side_x, self.spot(p.z, p.x, p.y, None, True))
        self.start(self.spot(p.z, p.x, p.oy, 1), 16, side_x, self.spot(p.z, p.x, p.oy, 1, True))

    def phase(self, name):
        if name == "own":
            self.beside()
        elif name == "zs":
            self.lines(1, 2, 3)
        elif name[0] == "z":
            self.lines(int(name[1]))
        elif name in ("spread", "cross", "share"):
            for k in range(name == "spread", 4):
                getattr(self, name)(k)
        else:
            (self.spread if name[0] == "s" else self.cross)(int(name[1]))

    def spread(self, k):
        p = self.place
        side_x, side_y, _ = p.sides()
        spot = self.spot(p.zs[k], p.x, p.y)
        self.arrived(spot, k)
        self.start(spot, 4 + k, side_x)
        self.start(spot, 8 + k, side_y)

    def cross(self, k):
        p = self.place
        side_x, side_y, _ = p.sides()
        self.arrived(self.spot(p.zs[k], p.ox, p.y), 4 + k)
        self.start(self.spot(p.zs[k], p.ox, p.y, 0), 12 + k, side_y)
        if k:
            self.arrived(self.spot(p.zs[k], p.x, p.oy), 8 + k)
            self.start(self.spot(p.zs[k], p.x, p.oy, 1), 16 + k, side_x)

    def share(self, k):
        p = self.place
        core = p.sides()[2]
        if k:
            self.start(self.spot(p.zs[k], p.x, None), 20 + k, core)
        self.arrived(self.spot(p.zs[k], p.ox, p.oy, 0), 12 + k)
        self.arrived(self.spot(p.zs[k], p.ox, p.oy, 1), 16 + k)
        self.start(self.spot(p.zs[k], p.ox, None), 24 + k, core)

    def finish(self):
        p = self.place

        def other(z, x):
            return lambda: (pl.ds(pl.multiple_of((z * 2 + x) * self.rows + (p.oc) * self.half, 16), self.half), slice(None))

        for k in range(4):
            if k:
                self.arrived(other(p.zs[k], p.x), 20 + k)
            self.arrived(other(p.zs[k], p.ox), 24 + k)

    def drain(self):
        for make in self.started:
            make().wait_send()


class Reduce:
    def __init__(self, place, source, held, core, diag_x, diag_y, side_x, side_y, line, final, send, recv):
        self.place, self.source, self.held, self.core = place, source, held, core
        self.diag_x, self.diag_y, self.side_x, self.side_y, self.line, self.final = diag_x, diag_y, side_x, side_y, line, final
        self.send, self.recv, self.started = send, recv, []
        self.own4 = self.own = None
        if diag_y is not None:
            self.rows, self.wide = side_x.shape[1:]
            self.by_rows = diag_y.shape[2] == self.wide
            self.cut = diag_y.shape[1] if self.by_rows else diag_y.shape[2]

    def part(self, second):
        bounds = pl.ds(self.cut, (self.rows if self.by_rows else self.wide) - self.cut) if second else pl.ds(0, self.cut)
        return (bounds, slice(None)) if self.by_rows else (slice(None), bounds)

    def hold(self, z, x, y, *rest):
        if self.held is None:
            return (z, x, self.place.c, y) + rest
        return (z, x, y) + rest

    @property
    def home(self):
        return self.source if self.held is None else self.held

    def copy(self, src, dst, sem, peer):
        return pltpu.make_async_remote_copy(src_ref=src, dst_ref=dst, send_sem=self.send.at[sem], recv_sem=self.recv.at[sem], device_id=peer, device_id_type=MESH)

    def start(self, src, dst, sem, peer):
        def make():
            return self.copy(src(), dst() if callable(dst) else dst, sem, peer)

        make().start()
        self.started.append(make)

    def arrived(self, dst, sem):
        self.copy(dst, dst, sem, self.place.sides()[0]).wait_recv()

    def begin(self, own=None):
        p = self.place
        self.start(lambda: self.source.at[:, :, p.oc], self.core, 0, p.sides()[2])
        self.own = own
        if own is not None:
            own.start()

    def add_core(self, x, y):
        def body(z, _):
            spot = self.hold(z, x, y)
            self.home[spot] = self.home[spot] + self.core[z, x, y]
            return 0

        lax.fori_loop(0, 4, body, 0)

    def add(self, x, y, part, buffer):
        def body(z, _):
            spot = self.hold(z, x, y, *part)
            self.home[spot] = self.home[spot] + buffer[z]
            return 0

        lax.fori_loop(0, 4, body, 0)

    def step_core(self):
        p = self.place
        side_x, side_y, _ = p.sides()
        if self.own is not None:
            self.own.wait()
        self.arrived(self.core, 0)
        for x, y in ((p.ox, p.oy), (p.ox, p.y), (p.x, p.oy), (p.x, p.y)):
            self.add_core(x, y)

    def step_open(self):
        p = self.place
        side_x, side_y, _ = p.sides()
        every = slice(None)
        self.start(lambda: self.home.at[self.hold(every, p.ox, p.oy, *self.part(True))], self.diag_x, 1, side_x)
        self.start(lambda: self.home.at[self.hold(every, p.ox, p.oy, *self.part(False))], self.diag_y, 2, side_y)

    def step_diag(self):
        p = self.place
        side_x, side_y, _ = p.sides()
        every = slice(None)
        self.arrived(self.diag_y, 2)
        self.add(p.ox, p.y, self.part(False), self.diag_y)
        self.start(lambda: self.home.at[self.hold(every, p.ox, p.y)], self.side_x, 3, side_x)
        self.arrived(self.diag_x, 1)
        self.add(p.x, p.oy, self.part(True), self.diag_x)
        self.start(lambda: self.home.at[self.hold(every, p.x, p.oy)], self.side_y, 4, side_y)

    def step_sum(self):
        p = self.place
        whole = (slice(None), slice(None))
        self.arrived(self.side_x, 3)
        self.add(p.x, p.y, whole, self.side_x)
        self.arrived(self.side_y, 4)
        self.add(p.x, p.y, whole, self.side_y)

    def mine(self, z):
        if self.own4 is not None:
            return self.own4.at[z]
        return self.home.at[self.hold(z, self.place.x, self.place.y)]

    def step_send(self):
        p = self.place
        for k in (1, 2, 3):
            self.start(lambda k=k: self.mine(p.zs[k]), lambda k=k: self.line.at[k - 1], 4 + k, p.along[k])

    def step_side(self):
        self.step_sum()
        self.step_send()

    def step_line(self):
        p = self.place
        total = self.mine(p.z)[...].astype(F32)
        for k in (1, 2, 3):
            self.arrived(self.line.at[k - 1], 4 + k)
            total = total + self.line[k - 1].astype(F32)
        self.final[p.c, p.y] = total.astype(BF16)
        self.start(lambda: self.final.at[p.c, p.y], lambda: self.final.at[p.c, p.y], 8, p.sides()[1])

    def step_share(self):
        p = self.place
        self.arrived(self.final.at[p.c, p.oy], 8)
        self.start(lambda: self.final.at[p.c], lambda: self.final.at[p.c], 9, p.sides()[2])

    def finish(self):
        self.arrived(self.final.at[self.place.oc], 9)

    def drain(self):
        for make in self.started:
            make().wait_send()


class SmallReduce:
    def __init__(self, place, home, core, side_y, side_x, line, send, recv):
        self.place, self.home, self.core, self.side_y, self.side_x, self.line = place, home, core, side_y, side_x, line
        self.send, self.recv, self.started = send, recv, []

    copy, start, arrived, drain = Reduce.copy, Reduce.start, Reduce.arrived, Reduce.drain

    def begin(self):
        self.start(lambda: self.home, self.core, 0, self.place.sides()[2])

    def step_core(self, sent):
        p = self.place
        self.arrived(self.core, 0)
        sent[...] = self.home[...] + self.core[...]
        self.start(lambda: sent, self.side_y, 1, p.sides()[1])

    def step_y(self, sent, total):
        p = self.place
        self.arrived(self.side_y, 1)
        total[...] = sent[...] + self.side_y[...]
        self.start(lambda: total.at[:, p.ox], self.side_x, 2, p.sides()[0])

    def step_x(self, total):
        p = self.place
        self.arrived(self.side_x, 2)
        for z in range(4):
            self.side_x[z] = self.side_x[z] + total[z, p.x]
        for k in (1, 2, 3):
            self.start(lambda k=k: self.side_x.at[p.zs[k]], lambda k=k: self.line.at[k - 1], 2 + k, p.along[k])

    def step_line(self, out):
        total = self.side_x[self.place.z]
        for k in (1, 2, 3):
            self.arrived(self.line.at[k - 1], 2 + k)
            total = total + self.line[k - 1]
        out[...] = total


GATHER_PLAN = (
    (("k", "own"), ("v", "own"), ("o", "own"), ("p0", "own"), ("q", "z1"), ("k", "z1"), ("q", "z2"), ("k", "z2"), ("k", "z3"), ("q", "s1"), ("k", "s1"),),
    (("v", "z1"), ("q", "z3"), ("k", "c0"), ("k", "s3"),),
    (("v", "z2"), ("v", "z3"),),
    (),
    (("v", "s1"), ("q", "s2"), ("q", "c1"),),
    (("o", "zs"), ("k", "s2"), ("q", "s3"),),
    (("q", "own"), ("p0", "zs"), ("v", "c0"), ("v", "s2"), ("v", "s3"), ("k", "c2"), ("q", "c3"), ("k", "c3"),),
    (("q", "c0"), ("v", "c1"), ("q", "c2"), ("v", "c2"), ("v", "c3"),),
    (("k", "c1"), ("o", "spread"), ("q", "share"), ("k", "share"),),
    (("p1", "own"), ("p1", "zs"), ("o", "cross"), ("v", "share"),),
    (("p0", "spread"),),
    (),
    (),
    (("p2", "zs"), ("p1", "spread"), ("p0", "cross"), ("o", "share"),),
    (),
    (("p2", "own"),),
    (("p1", "cross"), ("p0", "share"),),
    (("p2", "spread"),),
    (),
    (),
    (("p1", "share"),),
    (("p2", "cross"),),
    (),
    (),
    (("p2", "share"),),
    (),
    (),
    (),
    (),
    (),
)
MERGE_PLAN = (22, 25, 26)
REDUCE_PLAN = (
    ("m0", (13, 14)),
    ("m1", (0, 4, 10, 20, 22)),
    ("m2", (3, 8, 13, 20, 22)),
    ("o", (12, 15, 18, 20, 22)),
    ("q", (13, 14, 16, 19, 21)),
    ("k", (14, 16, 19, 22, 22)),
    ("v", (14, 18, 20, 22, 22)),
)


VMEM = pl.BlockSpec(memory_space=pltpu.VMEM)
ANY = pl.BlockSpec(memory_space=pl.ANY)
LIMIT = 61 * 1024 * 1024
THIRD = 1024


def call(body, outs, scratch, args, name):
    return pl.pallas_call(
        body,
        out_shape=[jax.ShapeDtypeStruct(*o) for o in outs],
        in_specs=[VMEM] * len(args),
        out_specs=[VMEM] * len(outs),
        scratch_shapes=[pltpu.VMEM(*s) for s in scratch],
        compiler_params=pltpu.CompilerParams(vmem_limit_bytes=LIMIT),
        name=name,
    )(*args)


class Later:
    def __init__(self, sems):
        self.sems, self.flights = sems, {}

    def start(self, name, src, dst):
        self.plan(name, src, dst)
        self.flights[name]().start()

    def plan(self, name, src, dst):
        sem = len(self.flights)

        def make():
            return pltpu.make_async_copy(*(r() if callable(r) else r for r in (src, dst)), self.sems.at[sem])

        self.flights[name] = make

    def wait(self, *names):
        for name in names:
            self.flights[name]().wait()


def first_plain(
    images, slots, width, patches, keep, cot, vectors, w_qkv, w_out,
    token, n1t, dm, dmt, live, qkv, probs, att_t, middle, n2, n2t, stack, normed, mask, att, bias,
):
    bias[...] = jnp.concatenate([vectors[2:3, :], jnp.zeros((1, width), F32), vectors[3:4, :]], axis=1)
    stage_gather(images, slots, patches, keep, stack, live, mask, token)
    stage_norm(vectors[0:1, :], vectors[1:2, :], token, normed, n1t)
    stage_grads(images, slots, width, cot, stack, live, dm, dmt)
    stage_qkv(images, width, normed, w_qkv, bias, qkv, 0, 3 * width // TILE)
    for i in range(images):
        stage_attention(width, qkv, mask, probs.at[pl.ds(i * H, H)], stack, i)
    stage_out(width, stack, w_out, vectors.at[4:5, :], token, vectors.at[5:6, :], vectors.at[6:7, :], att, att_t, middle, n2, n2t)


def first_kernel(
    images, slots, width,
    h_patches, keep_in, h_cot, *rest,
):
    singles, rest = rest[:9], rest[9:]
    first_body(images, slots, width, h_patches, keep_in, h_cot, singles, *rest)


def first_body(
    images, slots, width,
    h_patches, keep_in, h_cot, singles, s_qkv, s_out, s_up, s_down,
    vectors, g_b_up, h_token, h_n1t, h_dm, h_live, h_qkv, h_probs, h_att_t, h_middle, h_wqkv, h_wout, h_up, h_down, h_act, h_dh, h_gup, h_gdown, h_up1, h_down1, h_own_up, h_own_down,
    patches, keep, cot, vec_wide, vec, stack, normed, mask, token, n1t, dm, dmt, live, qkv, probs, att_t, middle, f_qkv, f_out, f_up, f_down, s_up3, act_, dh, g_up, g_down, up_core, down_core, up_dx, up_dy, up_sx, up_sy, dn_dx, dn_dy, dn_sx, dn_sy,
    vecs, bias, b_up, q_send, q_recv, m_send, m_recv, v_send, v_recv, own, saves, probs_sem, r_send, r_recv, w_send, w_recv,
):
    place = Place()
    _, side_y, side_c = place.sides()
    flat = [place.to(z=place.zs[k], x=x) for k in range(4) for x in (place.x, place.ox)][1:]
    later = Later(saves)
    loads = [pltpu.make_async_copy(h_patches, patches, own.at[10]), pltpu.make_async_copy(h_cot, cot, own.at[11])]

    def before():
        for load in loads:
            load.start()
        pad_keep(keep_in, keep)
        vec_wide[...] = jnp.zeros_like(vec_wide)
        for j in range(8):
            vec_wide[j : j + 1, :96] = singles[j][...].astype(F32)
        row = jnp.concatenate([singles[8][...].astype(F32)[j : j + 1] for j in range(3)], axis=1)
        for j in range(4):
            vec_wide[8 + j : 9 + j, :96] = row[:, 96 * j : 96 * j + 96]
        vec[...] = vec_wide[...].astype(BF16)
        loads[0].wait()
        for t in range(3):
            for f in range(8):
                s_up3[t, :, f * 128 : f * 128 + 128] = s_up[:, f * 384 + t * 128 : f * 384 + t * 128 + 128]
        stage_gather(images, slots, patches, keep, stack, live, mask, token)
        later.start("live", live, h_live)
        later.start("token", token, h_token)
        loads[1].wait()
        stage_grads(images, slots, width, cot, stack, live, dm, dmt)
        later.start("dm", dm, h_dm)

    enter(flat + [side_y, side_c], before)
    columns = [slice(m * width, (m + 1) * width) for m in range(3)]
    g_qkv = [Gather(place, s_qkv.at[:, columns[m]], f_qkv.at[:, columns[m]], 128 if m == 2 else 256, q_send.at[m], q_recv.at[m]) for m in range(3)]
    g_out = Gather(place, s_out, f_out, 256, q_send.at[3], q_recv.at[3])
    g_ups = [Gather(place, s_up3.at[t], f_up.at[t], (256, 256, 256)[t], m_send.at[t], m_recv.at[t]) for t in range(3)]
    g_downs = [Gather(place, s_down.at[t * 128 : t * 128 + 128], f_down.at[t], 256, m_send.at[3 + t], m_recv.at[3 + t]) for t in range(3)]
    groups = {"q": g_qkv[:1], "k": g_qkv[1:2], "v": g_qkv[2:], "o": [g_out]}
    groups.update({f"p{t}": [g_ups[t], g_downs[t]] for t in range(3)})
    every = g_qkv + [g_out] + [g for t in range(3) for g in (g_ups[t], g_downs[t])]
    mine = place.z * 2 + place.x
    tiny = []
    for j, peer in enumerate(flat):
        copy = pltpu.make_async_remote_copy(src_ref=vec, dst_ref=vecs.at[mine], send_sem=v_send.at[j], recv_sem=v_recv.at[j], device_id=peer, device_id_type=MESH)
        copy.start()
        tiny.append(copy)
    vecs[mine] = vec[...]
    core = place.sides()[2]
    swaps = {
        (name, t): pltpu.make_async_remote_copy(
            src_ref=g.at[t, :, :, place.oc], dst_ref=buffer.at[t], send_sem=r_send.at[2 * t + j], recv_sem=r_recv.at[2 * t + j], device_id=core, device_id_type=MESH
        )
        for t in range(2)
        for j, (name, g, buffer) in enumerate((("up", g_up, up_core), ("down", g_down, down_core)))
    }
    early = (
        Reduce(place, None, up_core.at[0], None, up_dx, up_dy, up_sx, up_sy, None, None, w_send.at[0], w_recv.at[0]),
        Reduce(place, None, down_core.at[0], None, dn_dx, dn_dy, dn_sx, dn_sy, None, None, w_send.at[1], w_recv.at[1]),
    )

    def merge(t):
        for name, g, buffer in (("up", g_up, up_core), ("down", g_down, down_core)):
            swaps[name, t].wait_recv()

            def body(z, _, g=g, buffer=buffer):
                buffer[t, z] = buffer[t, z] + g[t, z, :, place.c]
                return 0

            lax.fori_loop(0, 4, body, 0)
        if t == 0:
            for r in early:
                r.step_open()
        else:
            later.start("up_sum1", lambda: up_core.at[1], h_up1)
            later.start("down_sum1", lambda: down_core.at[1], h_down1)

    def act(slot):
        for group, phase in GATHER_PLAN[slot]:
            for g in groups[group]:
                g.phase(phase)
        if slot == MERGE_PLAN[0]:
            merge(0)
        if slot == MERGE_PLAN[1]:
            for r in early:
                r.step_diag()
        if slot == MERGE_PLAN[2]:
            merge(1)

    act(0)
    locals_ = [g.own(own.at[j]) for j, g in enumerate(every)]
    for copy in locals_:
        copy.start()
    for slot in range(1, 5):
        act(slot)
    for copy in tiny:
        copy.wait_recv()
    vectors[...] = jnp.concatenate([vecs[f][:, :96] for f in range(8)], axis=1).astype(F32)
    act(5)
    stage_norm(vectors[0:1, :], vectors[1:2, :], token, normed, n1t)
    later.start("n1t", n1t, h_n1t)
    for f in range(8):
        row = jnp.concatenate([vecs[f][8 + j : 9 + j, :96] for j in range(4)], axis=1).astype(F32)
        for t in range(3):
            b_up[t, :, f * 128 : f * 128 + 128] = row[:, t * 128 : t * 128 + 128]
    bias[...] = jnp.concatenate([vectors[2:3, :], jnp.zeros((1, width), F32), vectors[3:4, :]], axis=1)
    act(6)
    act(7)
    for m in range(3):
        act(8 + m)
        locals_[m].wait()
        g_qkv[m].finish()
        stage_qkv(images, width, normed, f_qkv, bias, qkv, m * width // TILE, (m + 1) * width // TILE)
    later.start("w_qkv", f_qkv, h_wqkv)
    later.start("qkv", qkv, h_qkv)

    def save_probs(slot, i):
        return pltpu.make_async_copy(probs.at[slot], h_probs.at[pl.ds(i * H, H)], probs_sem.at[slot])

    def attend(i, _):
        slot = lax.rem(i, 2)
        for j in range(5):
            pl.when(i == j)(lambda j=j: act(11 + j))
        pl.when(i >= 2)(lambda: save_probs(slot, i - 2).wait())
        stage_attention(width, qkv, mask, probs.at[slot], stack, i)
        save_probs(slot, i).start()
        return 0

    lax.fori_loop(0, images, attend, 0)
    for i in range(images - 2, images):
        save_probs(i % 2, i).wait()
    act(16)
    locals_[3].wait()
    g_out.finish()
    later.start("w_out", f_out, h_wout)
    later.wait("n1t")
    n2t = n1t
    stage_out(width, stack, f_out, vectors.at[4:5, :], token, vectors.at[5:6, :], vectors.at[6:7, :], normed, att_t, middle, normed, n2t)
    later.start("att_t", att_t, h_att_t)
    later.start("middle", middle, h_middle)
    for t in range(3):
        for part in range(2):
            for name, src, dst in (("act", act_, h_act), ("dh", dh, h_dh)):
                cols = slice(part * 512, part * 512 + 512)
                later.plan(f"{name}{t}{part}", lambda src=src, cols=cols: src.at[:, cols], lambda dst=dst, t=t, cols=cols: dst.at[t, :, cols])

    def enter_third(t):
        locals_[4 + 2 * t].wait()
        locals_[5 + 2 * t].wait()
        g_ups[t].finish()
        g_downs[t].finish()
        later.start(f"up{t}", lambda: f_up.at[t], lambda: h_up.at[t])
        later.start(f"down{t}", lambda: f_down.at[t], lambda: h_down.at[t])
        if t:
            later.wait(f"act{t - 1}0", f"dh{t - 1}0")
        if t == 2:
            for name in ("up", "down"):
                swaps[name, 0].wait_send()

    def middle_third(t):
        if t:
            later.wait(f"act{t - 1}1", f"dh{t - 1}1")

    def save_part(t, part):
        later.flights[f"act{t}{part}"]().start()
        later.flights[f"dh{t}{part}"]().start()
        if part and t < 2:
            swaps["up", t].start()
            swaps["down", t].start()
        elif t == 2:
            later.start(f"g_up2{part}", lambda: g_up.at[0, :, :, :, part], lambda: h_gup.at[:, :, :, part])
            later.start(f"g_down2{part}", lambda: g_down.at[0, 2 * part : 2 * part + 2], lambda: h_gdown.at[2 * part : 2 * part + 2])

    def feed(step, _):
        t, c = step // 4, step % 4
        slot = t % 2
        for j in range(12):
            if GATHER_PLAN[17 + j] or 17 + j in MERGE_PLAN:
                pl.when(step == j)(lambda j=j: act(17 + j))
        for j in range(3):
            pl.when(step == 4 * j)(lambda j=j: enter_third(j))
            pl.when(step == 4 * j + 2)(lambda j=j: middle_third(j))

        def put_up(c, value):
            y, at = c // 2, tile_at(c % 2, TILE)
            g_up[slot, :, :, :, y, :, at] = value.reshape(4, 2, 2, 48, TILE)

        def put_down(c, value):
            for x in range(2):
                g_down[slot, c, x] = value[:, x * 128 : (x + 1) * 128].reshape(2, 2, 192, 128)

        stage_mlp(width, normed, n2t, dm, dmt, f_up.at[t], b_up.at[t], f_down.at[t], act_, dh, put_up, put_down, g_b_up.at[t], c)
        for j in range(3):
            for part in range(2):
                pl.when(step == 4 * j + 2 * part + 1)(lambda j=j, part=part: save_part(j, part))
        return 0

    lax.fori_loop(0, 12, feed, 0)
    act(29)
    for r, h, buffer in ((early[0], h_own_up, up_core), (early[1], h_own_down, down_core)):
        r.step_sum()
        later.start(f"own{h is h_own_up}", buffer.at[0, :, place.x, place.y], h)
    waited = {"n1t"} | {f"{n}{t}{p}" for n in ("act", "dh") for t in range(2) for p in range(2)}
    for name in ("up", "down"):
        swaps[name, 1].wait_send()
    later.wait(*(n for n in later.flights if n not in waited))
    for copy in tiny:
        copy.wait_send()
    for g in every + list(early):
        g.drain()


def second_plain(
    images, slots, width, hidden_width,
    n2, n2t, dm, dmt, w_up, b_up, w_down, b_d, middle_in, live, gain2,
    out, middle, d_low, g_up, g_down, g_b_up, g_g2, g_s2, g_bd, g_bo, act, dh, stack,
):
    middle[...] = middle_in[...]

    def put(ref, c, value):
        ref[:, tile_at(c, TILE)] = value

    feed = functools.partial(stage_mlp, width, n2, n2t, dm, dmt, w_up, b_up, w_down, act, dh, functools.partial(put, g_up), functools.partial(put, g_down), g_b_up)
    loop(0, hidden_width // TILE, lambda c, _: feed(c), 1)
    add_products(width, stack, True, lambda cols: dot(act[...], w_down[:, cols]))
    stage_final(images, slots, width, middle, live, b_d, stack, out)
    add_products(width, stack, True, lambda cols: dot_nt(dh[...], w_up[cols, :]))
    stage_middle_back(middle, gain2, dm, stack, d_low, g_g2, g_s2, g_bd, g_bo)


def third_plain(
    images, slots, width, d_low, att_t, w_out, qkv_in, probs, n1t, w_qkv, token, gain, mid, live, keep,
    g_out, g_qkv, g_b, g_g1, g_s1, gp, stack, tile, flat, qkv,
):
    def put(ref, c, value):
        ref[:, tile_at(c, TILE)] = value

    def put_patches(i, value):
        gp[i] = value

    qkv[...] = qkv_in[...]
    tile[...] = jnp.zeros_like(tile)
    stage_out_back(width, att_t, d_low, w_out, functools.partial(put, g_out), stack)
    for i in range(images):
        stage_attention_back(width, qkv, probs.at[pl.ds(i * H, H)], stack, i)
    back = functools.partial(stage_qkv_back, images, width, qkv, n1t, tile, flat, functools.partial(put, g_qkv), g_b)
    loop(0, 3 * width // TILE, lambda c, _: back(c), 1)
    stage_norm_back(width, flat, w_qkv, stack)
    stage_end(images, slots, width, keep, token, gain, mid, live, stack, g_g1, g_s1, put_patches)


def second_kernel(
    images, slots, width,
    keep_in, vectors, s_bup, h_token, h_n1t, h_dm, h_live, h_qkv, h_probs, h_att_t, h_middle, h_wqkv, h_wout, h_up, h_down, h_act, h_dh, h_gup, h_gdown, h_up1, h_down1, h_own_up, h_own_down,
    gp, out_tokens, o_wide, o_down, e_small,
    out_vm, keep,
    e_up, e_down, e_out, e_q, e_k, e_v,
    stack, tile, flat, qkv, probs, t_a, t_b, r_a, r_b, mid, live, w_qkv, w_out, stage, g_b, g_g1, g_s1, g_g2, g_s2, g_bd, g_bo, g_attn,
    up_held, up_own, up_core, up_dx, up_dy, up_sx, up_sy, up_ln, dn_held, dn_own, dn_core, dn_dx, dn_dy, dn_sx, dn_sy, dn_ln,
    core4, dx4, dy4, sx4, sy4, ln4, v_home, v_core, v_sy, v_sx, v_ln, v_sent, v_total,
    send, recv, v_send, v_recv, own, loads, probs_sem, out_sem,
):
    place = Place()
    pad_keep(keep_in, keep)
    enter(place.along[1:] + list(place.sides()))
    def reduce_third(t, source, held, own4, core, dx, dy, sx, sy, ln, e, sem):
        sems = send.at[sem + t], recv.at[sem + t]
        if t == 0:
            r = Reduce(place, None, None, None, None, None, None, None, ln.at[0], e.at[0], *sems)
            r.own4 = own4
            return r
        return Reduce(place, source, held.at[t - 1], core, dx.at[t - 1], dy.at[t - 1], sx.at[t - 1], sy.at[t - 1], ln.at[t], e.at[t], *sems)

    r_up = [reduce_third(t, h_gup, up_held, up_own, up_core, up_dx, up_dy, up_sx, up_sy, up_ln, e_up, 0) for t in range(3)]
    r_down = [reduce_third(t, h_gdown, dn_held, dn_own, dn_core, dn_dx, dn_dy, dn_sx, dn_sy, dn_ln, e_down, 3) for t in range(3)]
    mlp = [(r_up[t], r_down[t]) for t in range(3)]
    r_q, r_k, r_v, r_out = (
        Reduce(place, g_attn.at[m], None, core4.at[m], dx4.at[m], dy4.at[m], sx4.at[m], sy4.at[m], ln4.at[m], e, send.at[6 + m], recv.at[6 + m])
        for m, e in enumerate((e_q, e_k, e_v, e_out))
    )
    small = SmallReduce(place, v_home, v_core, v_sy, v_sx, v_ln, v_send, v_recv)
    later = Later(loads)
    slots_ = [flat.at[:, 0:THIRD], flat.at[:, THIRD : 2 * THIRD]]
    groups = {"m0": mlp[0], "m1": mlp[1], "m2": mlp[2], "o": (r_out,), "q": (r_q,), "k": (r_k,), "v": (r_v,)}

    def act(slot):
        for phase in ("open", "core", "diag", "side", "line", "share"):
            for group, slots_of in REDUCE_PLAN:
                phases = {2: ("line", "share"), 5: ("open" if group == "m1" else "core", "diag", "side", "line", "share")}[len(slots_of)]
                if (phase, slot) in zip(phases, slots_of):
                    for r in groups[group]:
                        getattr(r, "step_" + phase)()
                        if phase == "core":
                            r.step_open()

    early = [
        pltpu.make_async_copy(h, into, own.at[j])
        for j, (h, into) in enumerate(((h_own_up, up_own), (h_own_down, dn_own), (h_up1, up_held.at[0]), (h_down1, dn_held.at[0])))
    ]
    for copy in early:
        copy.start()
    later.start("dh0", h_dh.at[0], slots_[0])
    later.start("up0", h_up.at[0], t_a)
    for j, (r, h, into) in enumerate(((r_up[2], h_gup, up_held), (r_down[2], h_gdown, dn_held))):
        r.begin(pltpu.make_async_copy(h.at[:, :, place.c], into.at[1], own.at[4 + j]))
    later.start("dh1", h_dh.at[1], slots_[1])
    later.start("up1", h_up.at[1], t_b)
    for copy, r in zip(early[:2], mlp[0]):
        copy.wait()
        r.step_send()
    for copy in early[2:]:
        copy.wait()
    act(0)
    for name, src, dst in (("mid", h_middle, mid), ("dm", h_dm, r_a), ("live", h_live, live), ("w_out", h_wout, w_out), ("qkv", h_qkv, qkv), ("w_qkv", h_wqkv, w_qkv)):
        later.start(name, src, dst)

    def load_probs(i):
        slot = i % 2
        return pltpu.make_async_copy(h_probs.at[pl.ds(i * H, H)], probs.at[slot], probs_sem.at[slot])

    load_probs(0).start()
    later.wait("dh0", "up0")
    act(1)
    add_products(width, stack, True, lambda cols: dot_nt(slots_[0][...], t_a[cols, :]))
    later.start("dh2", h_dh.at[2], slots_[0])
    later.start("up2", h_up.at[2], t_a)
    act(2)
    later.wait("dh1", "up1")
    add_products(width, stack, False, lambda cols: dot_nt(slots_[1][...], t_b[cols, :]))
    later.start("att_t", h_att_t, t_b)
    act(3)
    later.wait("dh2", "up2")
    add_products(width, stack, False, lambda cols: dot_nt(slots_[0][...], t_a[cols, :]))
    later.start("n1t", h_n1t, t_a)
    act(4)
    later.wait("mid", "dm")
    gain2 = vectors.at[5:6, :]
    stage_middle_back(mid, gain2, r_a, stack, r_b, g_g2, g_s2, g_bd, g_bo)
    later.start("token", h_token, r_a)

    def put(m, c, value):
        for j in range(2):
            col = 2 * c + j
            y, off = (col % 6) // 3, col % 3
            at = tile_at(off, 128)
            g_attn[col // 6 if m is None else m, :, :, :, y, :, at] = value[:, j * 128 : (j + 1) * 128].reshape(4, 2, 2, 48, 128)

    act(5)
    later.wait("att_t", "w_out", "qkv")
    stage_out_back(width, t_b, r_b, w_out, functools.partial(put, 3), stack)
    r_out.begin()

    def back(i, _):
        for j in range(5):
            pl.when(i == j)(lambda j=j: act(6 + j))
        load_probs(i).wait()
        pl.when(i + 1 < images)(lambda: load_probs(i + 1).start())
        stage_attention_back(width, qkv, probs.at[lax.rem(i, 2)], stack, i)
        return 0

    lax.fori_loop(0, images, back, 0)
    later.wait("n1t")
    tile[...] = jnp.zeros_like(tile)
    project = functools.partial(stage_qkv_back, images, width, qkv, t_a, tile, flat, functools.partial(put, None), g_b)
    third = width // TILE

    def project_tile(c, _):
        for m in range(3):
            pl.when(c == m * third)(lambda m=m: act(11 + m))
        project(c)
        for m, r in enumerate((r_q, r_k, r_v)):
            pl.when(c == m * third + third - 1)(lambda r=r: r.begin())
        return 0

    lax.fori_loop(0, 3 * third, project_tile, 0)
    act(14)
    later.wait("w_qkv")
    stage_norm_back(width, flat, w_qkv, stack)
    later.start("act0", h_act.at[0], slots_[0])
    later.start("act1", h_act.at[1], slots_[1])
    later.start("down0", h_down.at[0], r_b)
    act(15)
    later.wait("token", "live")
    flights = []

    def put_patches(i, value):
        if i >= 2:
            flights[i - 2].wait()
        stage[i % 2] = value
        copy = pltpu.make_async_copy(stage.at[i % 2], gp.at[i], out_sem.at[i % 2])
        copy.start()
        flights.append(copy)

    stage_end(images, slots, width, keep, r_a, vectors.at[0:1, :], mid, live, stack, g_g1, g_s1, put_patches)
    later.start("middle", h_middle, mid)
    later.start("down1", h_down.at[1], r_a)
    act(16)
    v_home[...] = jnp.zeros_like(v_home)
    for j, (ref, base) in enumerate(((g_g1, 0), (g_s1, 0), (g_b, 0), (g_b, 2 * width), (g_bo, 0), (g_g2, 0), (g_s2, 0), (g_bd, 0))):
        row = ref[:, base : base + width]
        for f in range(8):
            v_home[f // 2, f % 2, j : j + 1, :96] = row[:, 96 * f : 96 * f + 96]
    for f in range(8):
        row = jnp.concatenate([s_bup[t, :, f * 128 : f * 128 + 128] for t in range(3)], axis=1)
        for j in range(4):
            v_home[f // 2, f % 2, 8 + j : 9 + j, :96] = row[:, 96 * j : 96 * j + 96]
    small.begin()
    act(17)
    later.wait("act0", "down0")
    add_products(width, stack, True, lambda cols: dot(slots_[0][...], r_b[:, cols]))
    later.start("act2", h_act.at[2], slots_[0])
    later.start("down2", h_down.at[2], r_b)
    small.step_core(v_sent)
    act(18)
    later.wait("act1", "down1")
    add_products(width, stack, False, lambda cols: dot(slots_[1][...], r_a[:, cols]))
    small.step_y(v_sent, v_total)
    act(19)
    later.wait("act2", "down2", "middle")
    add_products(width, stack, False, lambda cols: dot(slots_[0][...], r_b[:, cols]))
    small.step_x(v_total)
    act(20)
    stage_final(images, slots, width, mid, live, vectors.at[7:8, :], stack, out_vm)
    later.start("tokens", out_vm, out_tokens)
    small.step_line(e_small)
    act(21)
    act(22)
    for r in r_up + r_down:
        r.finish()
    for t in range(3):
        for c in range(2):
            for y in range(2):
                for f in range(4):
                    col = (4 * y + f) * 384 + t * 128
                    o_wide[48 * c : 48 * c + 48, 3 * width + col : 3 * width + col + 128] = e_up[t, c, y, :, f * 128 : f * 128 + 128]
        o_down[t * 128 : t * 128 + 128, :] = e_down[t].reshape(width, 128).T
    half = width // 2

    def place_blocks(ref, base, e):
        for c in range(2):
            for y in range(2):
                ref[48 * c : 48 * c + 48, base + y * half : base + y * half + half] = e[c, y]

    r_out.finish()
    place_blocks(o_wide, 7 * width, e_out)
    for m, (r, e) in enumerate(((r_q, e_q), (r_k, e_k), (r_v, e_v))):
        r.finish()
        place_blocks(o_wide, m * width, e)
    later.wait("tokens")
    for copy in flights[-2:]:
        copy.wait()
    for r in r_up + r_down + [r_out, r_q, r_k, r_v, small]:
        r.drain()


def last_kernel(images, width, h_patches, h_tokens, small, h_wide, h_down, patches, tokens, o_qkv, o_up, o_out, o_down, o_b_up, *rest):
    vectors, (held_p, held_t, wide, down, f_wide, f_down, loads, stores, own) = rest[:8], rest[8:]
    first = [pltpu.make_async_copy(h_wide, wide, own.at[0]), pltpu.make_async_copy(h_down, down, own.at[1])]
    for load in first:
        load.start()
    copies = []
    for i in range(images):
        for j, (src, held, dst) in enumerate(((h_patches, held_p, patches), (h_tokens, held_t, tokens))):
            load = pltpu.make_async_copy(src.at[i], held.at[i], loads.at[2 * i + j])
            load.start()
            copies.append((load, pltpu.make_async_copy(held.at[i], dst.at[i], stores.at[2 * i + j])))
    for j, ref in enumerate(vectors):
        ref[...] = small[j : j + 1, :96]
    row = jnp.concatenate([small[8 + j : 9 + j, :96] for j in range(4)], axis=1)
    for j in range(3):
        o_b_up[j : j + 1, :] = row[:, j * 128 : (j + 1) * 128]
    stored = []
    first[1].wait()
    f_down[...] = down[...].astype(F32)
    stored.append(pltpu.make_async_copy(f_down, o_down, own.at[2]))
    stored[-1].start()
    first[0].wait()
    for j, (dst, begin, end) in enumerate(((o_qkv, 0, 3), (o_up, 3, 7), (o_out, 7, 8))):
        cols = slice(begin * width, end * width)
        f_wide[:, cols] = wide[:, cols].astype(F32)
        stored.append(pltpu.make_async_copy(f_wide.at[:, cols], dst, own.at[3 + j]))
        stored[-1].start()
    for load, store in copies:
        load.wait()
        store.start()
    for store in stored + [store for _, store in copies]:
        store.wait()


def shards(
    linked,
    patches, keep, ln1_gain, ln1_bias, w_qkv, b_query, b_value, w_out, b_out,
    ln2_gain, ln2_bias, w_up, b_up, w_down, b_down, cotangent,
):
    images, slots = keep.shape
    width = patches.shape[2]
    hidden_width = w_up.shape[1]
    keep_pad = jnp.pad(keep, ((0, 0), (0, SLOT - slots)), constant_values=-1).reshape(images, 1, SLOT)
    part = ln1_gain.shape[0]
    singles = [v.reshape(1, part) for v in (ln1_gain, ln1_bias, b_query, b_value, b_out, ln2_gain, ln2_bias, b_down)]
    rows_low, rows_wide = ((ROWS, width), BF16), ((ROWS, width), F32)
    cols_low = ((width, ROWS), BF16)
    live_like, mask_like = ((ROWS, BLOCK), F32), ((images, SLOT, SLOT), F32)
    heads_like = ((images, SLOT, 3 * width), BF16)
    probs_like = ((images * H, SLOT, SLOT), BF16)
    row_like = ((1, width), F32)

    if linked:
        half = width // 2
        full = lambda v: ((v.shape[0] * 8, v.shape[1]), BF16)
        up3, down3, hid3 = ((3, width, THIRD), BF16), ((3, THIRD, width), BF16), ((3, ROWS, THIRD), BF16)
        gup_like, gdown_like = (4, 2, 2, 2, 48, THIRD // 2), (4, 2, 2, 2, width // 4, 128)
        outs = [
            ((16, width), F32), ((3, 1, THIRD), F32), rows_low, cols_low, rows_low, live_like, heads_like, probs_like, cols_low, rows_wide,
            full(w_qkv), full(w_out), up3, down3, hid3, hid3, (gup_like, BF16), (gdown_like, BF16), ((4, 2) + gup_like[3:], BF16), ((4, 2) + gdown_like[3:], BF16),
            ((4,) + gup_like[4:], BF16), ((4,) + gdown_like[4:], BF16),
        ]
        scratch = [
            (patches.shape, BF16), ((images, 1, SLOT), jnp.int32), (patches.shape, BF16), ((16, BLOCK), F32), ((16, BLOCK), BF16),
            rows_wide, rows_low, mask_like, rows_low, cols_low, rows_low, cols_low, live_like, heads_like, ((2, H, SLOT, SLOT), BF16), cols_low,
            rows_wide, full(w_qkv), full(w_out), up3, down3, ((3, part, THIRD), BF16), hid3[0][1:], hid3[0][1:], (2,) + gup_like, (2,) + gdown_like,
            (2, 4, 2) + gup_like[3:], (2, 4, 2) + gdown_like[3:],
        ]
        for r, w, first, other in ((48, THIRD // 2, (4, 48, 128), (4, 48, THIRD // 2 - 128)), (width // 4, 128, (4, 64, 128), (4, width // 4 - 64, 128))):
            scratch += [other, first, (4, r, w), (4, r, w)]
        scratch += [((8, 16, BLOCK), BF16), ((1, 3 * width), F32), ((3, 1, THIRD), F32)]
        scratch = [s if isinstance(s[0], tuple) else (s, BF16) for s in scratch]
        vectors, g_b_up, token, n1t, dm, live, qkv, probs, att_t, middle, qkv_full, out_full, up_full, down_full, act, dh, g_up, g_down, up1, down1, own_up, own_down = pl.pallas_call(
            functools.partial(first_kernel, images, slots, width),
            out_shape=[jax.ShapeDtypeStruct(*o) for o in outs],
            in_specs=[ANY, VMEM, ANY] + [VMEM] * 13,
            out_specs=[VMEM] * 2 + [ANY] * 20,
            scratch_shapes=[pltpu.VMEM(*s) for s in scratch]
            + [pltpu.SemaphoreType.DMA((4, 28))] * 2
            + [pltpu.SemaphoreType.DMA((6, 28))] * 2
            + [pltpu.SemaphoreType.DMA((7,))] * 2
            + [pltpu.SemaphoreType.DMA((12,)), pltpu.SemaphoreType.DMA((35,)), pltpu.SemaphoreType.DMA((2,))]
            + [pltpu.SemaphoreType.DMA((4,))] * 2
            + [pltpu.SemaphoreType.DMA((2, 10))] * 2,
            compiler_params=pltpu.CompilerParams(vmem_limit_bytes=LIMIT, collective_id=0, has_side_effects=True),
            name="first",
        )(patches, keep, cotangent, *singles, b_up.reshape(3, -1), w_qkv, w_out, w_up, w_down)
        final = lambda r, w, lead=(): (lead + (2, 2, r, w), BF16)
        attn = final(48, half)
        outs = [((images, slots, width), F32), ((images, slots, width), BF16), ((part, 8 * width), BF16), ((half, width), BF16), ((16, BLOCK), F32)]

        def buffers(r, w, by_rows, cut, cores, lead, lines):
            other = (4, r - cut, w) if by_rows else (4, r, w - cut)
            first = (4, cut, w) if by_rows else (4, r, cut)
            return [(cores + (4, 2, 2, r, w), BF16)] + [(lead + s, BF16) for s in (other, first, (4, r, w), (4, r, w))] + [(lines + (3, r, w), BF16)]

        scratch = [((images, slots, width), BF16), ((images, 1, SLOT), jnp.int32), final(48, THIRD // 2, (3,)), final(width // 4, 128, (3,)), attn, attn, attn, attn]
        scratch += [rows_wide, ((ROWS, TILE), F32), ((ROWS, 3 * width), BF16), heads_like, ((2, H, SLOT, SLOT), BF16), cols_low, cols_low, rows_low, rows_low]
        scratch += [rows_wide, live_like, ((width, 3 * width), BF16), ((width, width), BF16), ((2, slots, width), F32), ((1, 3 * width), F32)] + [row_like] * 6
        scratch += [((4, 4, 2, 2, 2, 48, half), BF16)]
        scratch += [((2, 4, 2, 2, 48, THIRD // 2), BF16), ((4, 48, THIRD // 2), BF16)] + buffers(48, THIRD // 2, False, 128, (), (2,), (3,))
        scratch += [((2, 4, 2, 2, width // 4, 128), BF16), ((4, width // 4, 128), BF16)] + buffers(width // 4, 128, True, 64, (), (2,), (3,))
        scratch += buffers(48, half, False, 128, (4,), (4,), (4,))
        small_like, line_like = ((4, 2, 16, BLOCK), F32), ((3, 16, BLOCK), F32)
        scratch += [small_like, small_like, small_like, ((4, 16, BLOCK), F32), line_like, small_like, small_like]
        grad_patches, out_tokens, o_wide, o_down, small = pl.pallas_call(
            functools.partial(second_kernel, images, slots, width),
            out_shape=[jax.ShapeDtypeStruct(*o) for o in outs],
            in_specs=[VMEM] * 3 + [ANY] * 20,
            out_specs=[ANY] * 2 + [VMEM] * 3,
            scratch_shapes=[pltpu.VMEM(*s) for s in scratch]
            + [pltpu.SemaphoreType.DMA((10, 10))] * 2
            + [pltpu.SemaphoreType.DMA((6,))] * 2
            + [pltpu.SemaphoreType.DMA((6,)), pltpu.SemaphoreType.DMA((23,)), pltpu.SemaphoreType.DMA((2,)), pltpu.SemaphoreType.DMA((2,))],
            compiler_params=pltpu.CompilerParams(vmem_limit_bytes=LIMIT, collective_id=1, has_side_effects=True),
            name="second",
        )(keep, vectors, g_b_up, token, n1t, dm, live, qkv, probs, att_t, middle, qkv_full, out_full, up_full, down_full, act, dh, g_up, g_down, up1, down1, own_up, own_down)
        outs = [
            ((images, slots, width), F32), ((images, slots, width), BF16), ((part, 3 * width), F32), ((part, 4 * width), F32), ((part, width), F32),
            ((half, width), F32), ((3, 128), F32),
        ] + [((1, part), F32)] * 8
        grad_patches, out_tokens, sum_qkv, sum_up, sum_out, sum_down, b_up_sum, *rows = pl.pallas_call(
            functools.partial(last_kernel, images, width),
            out_shape=[jax.ShapeDtypeStruct(*o) for o in outs],
            in_specs=[ANY, ANY, VMEM, ANY, ANY],
            out_specs=[ANY] * 6 + [VMEM] * 9,
            scratch_shapes=[
                pltpu.VMEM(*s)
                for s in (((images, slots, width), F32), ((images, slots, width), BF16), ((part, 8 * width), BF16), ((half, width), BF16), ((part, 8 * width), F32), ((half, width), F32))
            ]
            + [pltpu.SemaphoreType.DMA((2 * images,))] * 2
            + [pltpu.SemaphoreType.DMA((6,))],
            compiler_params=pltpu.CompilerParams(vmem_limit_bytes=LIMIT),
            name="last",
        )(grad_patches, out_tokens, small, o_wide, o_down)
        rows = [row.reshape(part) for row in rows]
        b_up_sum = b_up_sum.reshape(half)
    else:
        gather = lambda v: lax.all_gather(v, "fsdp", axis=0, tiled=True)
        vectors = jnp.pad(gather(jnp.concatenate(singles, axis=0).T).T.astype(F32), ((0, 8), (0, 0)))
        bias_up = gather(b_up).astype(F32).reshape(1, hidden_width)
        qkv_full, out_full, up_full, down_full = gather(w_qkv), gather(w_out), gather(w_up), gather(w_down)
        outs = [rows_low, cols_low, rows_low, cols_low, live_like, heads_like, probs_like, cols_low, rows_wide, rows_low, cols_low]
        scratch = [rows_wide, rows_low, mask_like, rows_low, ((1, 3 * width), F32)]
        token, n1t, dm, dmt, live, qkv, probs, att_t, middle, n2, n2t = call(
            functools.partial(first_plain, images, slots, width),
            outs, scratch, (patches, keep_pad, cotangent, vectors, qkv_full, out_full), "first",
        )
        gain1, gain2, b_d = vectors[0:1], vectors[5:6], vectors[7:8]
        hid = ((ROWS, hidden_width), BF16)
        out_tokens, d_mid, d_low, g_up, g_down, g_b_up, g_g2, g_s2, g_bd, g_bo = call(
            functools.partial(second_plain, images, slots, width, hidden_width),
            [((images, slots, width), BF16), rows_wide, rows_low] + [((width, hidden_width), BF16)] * 2 + [((1, hidden_width), F32)] + [row_like] * 4,
            [hid, hid, rows_wide],
            (n2, n2t, dm, dmt, up_full, bias_up, down_full, b_d, middle, live, gain2),
            "second",
        )
        g_out, g_qkv, g_b, g_g1, g_s1, grad_patches = call(
            functools.partial(third_plain, images, slots, width),
            [((width, width), BF16), ((width, 3 * width), BF16), ((1, 3 * width), F32), row_like, row_like, ((images, slots, width), F32)],
            [rows_wide, ((ROWS, TILE), F32), ((ROWS, 3 * width), BF16), heads_like],
            (d_low, att_t, out_full, qkv, probs, n1t, qkv_full, token, gain1, d_mid, live, keep_pad),
            "third",
        )
        scat = lambda v, dim=0: lax.psum(lax.psum_scatter(v, "fsdp", scatter_dimension=dim, tiled=True), "dp").astype(F32)
        rows = jnp.concatenate([g_g1, g_s1, g_b[:, :width], g_b[:, 2 * width :], g_bo, g_g2, g_s2, g_bd], axis=0).astype(BF16)
        rows = scat(rows, 1)
        b_up_sum = scat(g_b_up.astype(BF16), 1)[0]
        sum_qkv, sum_out, sum_up, sum_down = scat(g_qkv), scat(g_out), scat(g_up), scat(g_down, 1).T
    return (
        out_tokens, grad_patches, rows[0], rows[1], sum_qkv, rows[2], rows[3], sum_out, rows[4],
        rows[5], rows[6], sum_up, b_up_sum, sum_down, rows[7],
    )


def solution(mesh):
    linked = (mesh.shape["fsdp"], mesh.shape["dp"]) == (8, 4)
    many, one, two = P(("fsdp", "dp"), None, None), P("fsdp"), P("fsdp", None)
    in_specs = (many, P(("fsdp", "dp"), None), one, one, two, one, one, two, one, one, one, two, one, two, one, many)
    out_specs = (many, many, one, one, two, one, one, two, one, one, one, two, one, two, one)
    return jax.shard_map(functools.partial(shards, linked), mesh=mesh, in_specs=in_specs, out_specs=out_specs, check_vma=False)
```
